32 devices in a mesh: dp: 8 (over z, y), tensor: 4 (over x, core).
Axes of the slice: x: 2, y: 2, z: 4, core: 2. Of those that a mesh axis runs over, the one named last changes fastest.
Arguments:
- hidden_in: bfloat16 [8192, 1536], P('dp'), may hold values from -6 to 6
- pre_gain: float32 [1536], replicated, may hold values from 0.1 to 1.9
- w_gate: bfloat16 [1536, 3072], P(None, 'tensor'), may hold values from -0.15625 to 0.15625
- w_value: bfloat16 [1536, 3072], P(None, 'tensor'), may hold values from -0.15625 to 0.15625
- w_bc: bfloat16 [1536, 256], replicated, may hold values from -0.15625 to 0.15625
- w_dt: bfloat16 [1536, 48], P(None, 'tensor'), may hold values from -0.15625 to 0.15625
- conv_x: float32 [4, 3072], P(None, 'tensor'), may hold values from -3 to 3
- conv_x_bias: float32 [3072], P('tensor'), may hold values from -2 to 2
- conv_bc: float32 [4, 256], replicated, may hold values from -3 to 3
- conv_bc_bias: float32 [256], replicated, may hold values from -2 to 2
- dt_bias: float32 [48], P('tensor'), may hold values from -7 to -3
- a_log: float32 [48], P('tensor'), may hold values from 0 to 2.77
- d_skip: float32 [48], P('tensor'), may hold values from 0.5 to 1.5
- gate_gain: float32 [3072], P('tensor'), may hold values from 0.1 to 1.9
- w_out: bfloat16 [3072, 1536], P('tensor'), may hold values from -0.109375 to 0.109375
- cotangent: bfloat16 [8192, 1536], P('dp'), may hold values from -6 to 6
- segments: int32 [8, 1024], P('dp'), may hold values from 0 to 31, never falling along the last dimension, each value on 1 to 512 neighbouring positions
Outputs:
- block_out: bfloat16 [8192, 1536], P(('dp', 'tensor'))
- hidden_grad: float32 [8192, 1536], P(('dp', 'tensor'))
- pre_gain_grad: float32 [1536], replicated
- w_gate_grad: float32 [1536, 3072], P(None, 'tensor')
- w_value_grad: float32 [1536, 3072], P(None, 'tensor')
- w_bc_grad: float32 [1536, 256], P(None, 'tensor')
- w_dt_grad: float32 [1536, 48], P(None, 'tensor')
- conv_x_grad: float32 [4, 3072], P(None, 'tensor')
- conv_x_bias_grad: float32 [3072], P('tensor')
- conv_bc_grad: float32 [4, 256], replicated
- conv_bc_bias_grad: float32 [256], replicated
- dt_bias_grad: float32 [48], P('tensor')
- a_log_grad: float32 [48], P('tensor')
- d_skip_grad: float32 [48], P('tensor')
- gate_gain_grad: float32 [3072], P('tensor')
- w_out_grad: float32 [3072, 1536], P('tensor')
The draws below stay inside these ranges and needn't reach their ends.
Inputs may be any that keep to these rules, and one draw needn't show every extreme that they name: `segments`: within a sequence document numbers never fall; a document has at most 512 tokens.
All inputs are finite; a program needn't handle non-finite values.
Results may differ from the reference program's by a relative error of at most 0.02.
Values may be sent and summed in bfloat16 or wider, within the bound.
No kernel may reach another device: no remote copies, remote signals or barrier semaphores. Data moves between devices by JAX's collectives and lax.ppermute only.
A program may use at most 192 MiB of HBM per device.

```python
import math
import jax
import jax.numpy as jnp
import numpy as np
from jax import lax

D = 1536
HEADS = 48
STATE = 128
CONV = 4
SPAN = 256
SEQ_LEN = 1024
INNER = 3072
SEQS = 8
TOKENS = 8192
N_TENSOR = 4


def level_of(own_key, extent, cuts, smallest, largest):
    level = 1.0
    for axis_at, shards_of in cuts:
        heights = jax.random.uniform(jax.random.fold_in(jax.random.fold_in(own_key, 6), axis_at), (shards_of,), jnp.float32, smallest / len(cuts), largest / len(cuts))
        level = level * jnp.repeat(jnp.exp(heights), extent[axis_at] // shards_of).reshape((-1,) + (1,) * (len(extent) - 1 - axis_at))
    return level


def length_profile(amount, total, reach, slope):
    weights = [(1 << 20) // math.isqrt(rank ** slope) + 1 for rank in range(2, amount + 1)]
    rest, counts = total - reach - (amount - 1), [1] * (amount - 1)
    while rest > 0:
        free = [i for i in range(amount - 1) if counts[i] < reach]
        whole, remaining = sum([weights[i] for i in free]), rest
        for i in free:
            extra = min(reach - counts[i], max(1, remaining * weights[i] // whole), rest)
            counts[i] = counts[i] + extra
            rest = rest - extra
    return np.array([reach] + counts)


def uneven_parts(stream_key, amount, total, most, slope):
    if amount == 2:
        one = jax.random.randint(stream_key, (), max(1, total - most), min(most, total - 1) + 1)
        return jnp.stack([one, total - one])
    lengths = jnp.asarray(length_profile(amount, total, most, slope), jnp.int32)
    couples = (amount - 1) // 2
    source_of, receiver = lengths[1:1 + 2 * couples:2], lengths[2:2 + 2 * couples:2]
    margin = jnp.minimum(source_of - 1, most - receiver)
    moved = jax.random.randint(jax.random.fold_in(stream_key, 1), (couples,), 0, 1 << 20) % (margin + 1)
    lengths = lengths.at[1:1 + 2 * couples:2].set(source_of - moved).at[2:2 + 2 * couples:2].set(receiver + moved)
    return lengths[jax.random.permutation(jax.random.fold_in(stream_key, 2), amount)]


def scatter_about(stream_key, extent, spread, reach, split=(), held_as=jnp.bfloat16):
    entries = jax.random.normal(stream_key, extent, jnp.float32) * spread
    if len(split) > 0:
        entries = level_of(stream_key, extent, split, -0.22, 0.18) * entries
    return jnp.clip(entries, min=-reach, max=reach).astype(held_as)


def setup_inputs(seed: int = 0) -> dict:
    seeds = jax.random.split(jax.random.key(seed), 18)
    hidden_in = scatter_about(seeds[0], (TOKENS, D), 1.0, 6.0, ((0, 8),))
    pre_gain = jnp.clip(1.0 + 0.18 * jax.random.normal(seeds[1], (D,), jnp.float32), 0.1, 1.9)
    w_gate = scatter_about(seeds[2], (D, INNER), D ** -0.5, 0.15625, ((1, 4),))
    w_value = scatter_about(seeds[3], (D, INNER), D ** -0.5, 0.15625, ((1, 4),))
    w_bc = scatter_about(seeds[4], (D, 2 * STATE), D ** -0.5, 0.15625)
    w_dt = scatter_about(seeds[5], (D, HEADS), D ** -0.5, 0.15625, ((1, 4),))
    conv_x = scatter_about(seeds[6], (CONV, INNER), CONV ** -0.5, 3.0, ((1, 4),), jnp.float32)
    conv_x_bias = scatter_about(seeds[7], (INNER,), 0.3, 2.0, ((0, 4),), jnp.float32)
    conv_bc = scatter_about(seeds[8], (CONV, 2 * STATE), CONV ** -0.5, 3.0, (), jnp.float32)
    conv_bc_bias = scatter_about(seeds[9], (2 * STATE,), 0.3, 2.0, (), jnp.float32)
    dt_bias = jnp.clip(-7.0 + 4.0 * jax.random.uniform(seeds[10], (HEADS,), jnp.float32) ** level_of(seeds[10], (HEADS,), ((0, 4),), -0.2, 0.2), -7.0, -3.0)
    a_log = jnp.clip(2.77 * jax.random.uniform(seeds[11], (HEADS,), jnp.float32) ** level_of(seeds[11], (HEADS,), ((0, 4),), -0.2, 0.2), 0.0, 2.77)
    d_skip = jnp.clip(0.5 + 1.0 * jax.random.uniform(seeds[12], (HEADS,), jnp.float32) ** level_of(seeds[12], (HEADS,), ((0, 4),), -0.2, 0.2), 0.5, 1.5)
    gate_gain = jnp.clip(1.0 + 0.18 * jax.random.normal(seeds[13], (INNER,), jnp.float32), 0.1, 1.9)
    w_out = scatter_about(seeds[14], (INNER, D), INNER ** -0.5, 0.109375, ((0, 4),))
    cotangent = scatter_about(seeds[15], (TOKENS, D), 1.0, 6.0, ((0, 8),))
    segments = jax.vmap(lambda own: jnp.searchsorted(jnp.cumsum(uneven_parts(own, SEQ_LEN // 32, SEQ_LEN, SEQ_LEN // 2, 2)), jnp.arange(SEQ_LEN), side="right"))(jax.random.split(seeds[16], SEQS)).reshape((SEQS, SEQ_LEN)).astype(jnp.int32)
    return {"hidden_in": hidden_in, "pre_gain": pre_gain, "w_gate": w_gate, "w_value": w_value, "w_bc": w_bc, "w_dt": w_dt, "conv_x": conv_x, "conv_x_bias": conv_x_bias, "conv_bc": conv_bc, "conv_bc_bias": conv_bc_bias, "dt_bias": dt_bias, "a_log": a_log, "d_skip": d_skip, "gate_gain": gate_gain, "w_out": w_out, "cotangent": cotangent, "segments": segments}


EPS = 1e-05
HIGH = lax.Precision.HIGHEST

@jax.custom_vjp
def low(v):
    return lax.optimization_barrier(v.astype(jnp.bfloat16)).astype(jnp.float32)

@jax.custom_vjp
def low_back(v):
    return v

def low_keep(v):
    return (low(v), None)

def low_pass(kept, grad):
    return (grad,)

def back_keep(v):
    return (v, None)

def back_low(kept, grad):
    return (low(grad),)
low.defvjp(low_keep, low_pass)
low_back.defvjp(back_keep, back_low)

def causal_conv(inputs, segments, weight, conv_bias):
    result = conv_bias + weight[CONV - 1] * inputs
    for offset in range(1, CONV):
        shifted = jnp.pad(inputs, ((0, 0), (offset, 0), (0, 0)))[:, :-offset]
        earlier = jnp.pad(segments, ((0, 0), (offset, 0)), constant_values=-1)[:, :-offset]
        same_doc = (earlier == segments).astype(jnp.float32)[..., None]
        result = result + weight[CONV - 1 - offset] * shifted * same_doc
    return jax.nn.silu(result)

def scan_sequence(values, step_sizes, log_rates, bmat, cmat, segments):
    span_count = SEQ_LEN // SPAN
    head_count = log_rates.shape[1]
    values = values.reshape(span_count, SPAN, head_count, -1)
    step_sizes = step_sizes.reshape(span_count, SPAN, head_count)
    log_rates = log_rates.reshape(span_count, SPAN, head_count)
    bmat = bmat.reshape(span_count, SPAN, -1)
    cmat = cmat.reshape(span_count, SPAN, -1)
    blocks = segments.reshape(span_count, SPAN).astype(jnp.int32)
    before = jnp.concatenate([jnp.full((1,), -1, jnp.int32), blocks[:-1, -1].astype(jnp.int32)])
    cumulative = jnp.cumsum(log_rates, axis=1)
    row_index = lax.broadcasted_iota(jnp.int32, (SPAN, SPAN), 0)
    col_index = lax.broadcasted_iota(jnp.int32, (SPAN, SPAN), 1)
    inside = (blocks[:, :, None] == blocks[:, None, :]) & (row_index >= col_index)[None]
    gaps = cumulative[:, :, None, :] - cumulative[:, None, :, :]
    decays = jnp.exp(jnp.where(inside[..., None], gaps, 0.0)) * inside.astype(jnp.float32)[..., None]
    scores = jnp.einsum('cin,cjn->cij', cmat, bmat, precision=HIGH)
    weights = scores[..., None] * decays * step_sizes[:, None, :, :]
    inside_part = jnp.einsum('cijh,cjhp->cihp', weights, values, precision=HIGH)
    same_last = (blocks == blocks[:, -1:]).astype(jnp.float32)[..., None]
    tail_weight = same_last * jnp.exp(cumulative[:, -1:, :] - cumulative) * step_sizes
    span_states = jnp.einsum('cjhp,cjn->chpn', tail_weight[..., None] * values, bmat, precision=HIGH)
    kept_mask = (blocks == before[:, None]).astype(jnp.float32)
    carry_rate = jnp.exp(cumulative[:, -1, :]) * kept_mask[:, -1:]
    carried_state = jnp.zeros(span_states.shape[1:], jnp.float32)
    entering = []
    for position in range(span_count):
        entering.append(carried_state)
        carried_state = carry_rate[position][:, None, None] * carried_state + span_states[position]
    entering = jnp.stack(entering)
    reach_gain = jnp.exp(cumulative) * kept_mask[..., None]
    carried = jnp.einsum('cin,chpn->cihp', cmat, entering, precision=HIGH) * reach_gain[..., None]
    return (inside_part + carried).reshape(SEQ_LEN, head_count, -1)

def mix_heads(gate_pre, inner_pre, step_raw, state_io, segments, conv_x, conv_x_bias, dt_bias, a_log, d_skip):
    values = causal_conv(inner_pre, segments, conv_x, conv_x_bias)
    step_sizes = jax.nn.softplus(step_raw + dt_bias)
    log_rates = -jnp.exp(a_log) * step_sizes
    seq_count, length, channels = values.shape
    head_count = step_sizes.shape[-1]
    head_values = values.reshape(seq_count, length, head_count, channels // head_count)

    def per_sequence(packed):
        vals, sizes, rates_in, states_in, segs_in = packed
        return scan_sequence(vals, sizes, rates_in, states_in[:, :STATE], states_in[:, STATE:], segs_in)
    scanned = lax.map(jax.checkpoint(per_sequence), (head_values, step_sizes, log_rates, state_io, segments))
    scanned = scanned + d_skip[:, None] * head_values
    return scanned.reshape(seq_count, length, channels) * jax.nn.silu(gate_pre)

def forward(hidden, pre_gain, w_gate, w_value, w_bc, w_dt, conv_x, conv_x_bias, conv_bc, conv_bc_bias, dt_bias, a_log, d_skip, gate_gain, w_out, segments):
    row_count = hidden.shape[0]
    seq_count = segments.shape[0]
    inv_rms = lax.rsqrt(lax.optimization_barrier(jnp.mean(hidden * hidden, axis=-1, keepdims=True)) + EPS)
    normed = low(hidden * inv_rms * pre_gain)
    gate_pre = low_back(jnp.dot(normed, w_gate, precision=HIGH))
    inner_pre = low_back(jnp.dot(normed, w_value, precision=HIGH))
    state_pre = low_back(jnp.dot(normed, w_bc, precision=HIGH))
    step_raw = low_back(jnp.dot(normed, w_dt, precision=HIGH))
    state_io = causal_conv(state_pre.reshape(seq_count, SEQ_LEN, -1), segments, conv_bc, conv_bc_bias)
    mixed_out = mix_heads(gate_pre.reshape(seq_count, SEQ_LEN, -1), inner_pre.reshape(seq_count, SEQ_LEN, -1), step_raw.reshape(seq_count, SEQ_LEN, -1), state_io, segments, conv_x, conv_x_bias, dt_bias, a_log, d_skip).reshape(row_count, INNER)
    square_sum = lax.optimization_barrier(jnp.sum(mixed_out * mixed_out, axis=-1, keepdims=True))
    gated = low(mixed_out * lax.rsqrt(square_sum / INNER + EPS) * gate_gain)
    terms = jnp.einsum('tri,rid->trd', gated.reshape(row_count, N_TENSOR, -1), w_out.reshape(N_TENSOR, -1, D), precision=HIGH)
    return hidden + lax.optimization_barrier(jnp.sum(low(terms), axis=1))

def reference(hidden_in, pre_gain, w_gate, w_value, w_bc, w_dt, conv_x, conv_x_bias, conv_bc, conv_bc_bias, dt_bias, a_log, d_skip, gate_gain, w_out, cotangent, segments):
    params = tuple((argument.astype(jnp.float32) for argument in (pre_gain, w_gate, w_value, w_bc, w_dt, conv_x, conv_x_bias, conv_bc, conv_bc_bias, dt_bias, a_log, d_skip, gate_gain, w_out)))
    group_size = 4
    seq_count = segments.shape[0]
    group_count = seq_count // group_size
    hidden_groups = hidden_in.astype(jnp.float32).reshape(group_count, group_size * SEQ_LEN, D)
    cotan_groups = cotangent.astype(jnp.float32).reshape(group_count, group_size * SEQ_LEN, D)
    seg_groups = segments.reshape(group_count, group_size, SEQ_LEN)

    def group_step(totals, packed):
        hidden_part, cotan_part, seg_part = packed

        def apply_block(hidden_arg, *weights):
            return forward(hidden_arg, *weights, seg_part)
        result, pullback = jax.vjp(apply_block, hidden_part, *params)
        gradients = pullback(cotan_part)
        totals = jax.tree.map(lambda summed, added: summed + added, totals, tuple(gradients[1:]))
        return (totals, (result.astype(jnp.bfloat16), gradients[0]))
    zero_grads = tuple((jnp.zeros_like(param_arr) for param_arr in params))
    totals, (outputs, hidden_grads) = lax.scan(group_step, zero_grads, (hidden_groups, cotan_groups, seg_groups))
    block_out = outputs.reshape(seq_count * SEQ_LEN, D)
    hidden_grad = hidden_grads.reshape(seq_count * SEQ_LEN, D)
    return (block_out, hidden_grad, totals[0], totals[1], totals[2], totals[3], totals[4], totals[5], totals[6], totals[7], totals[8], totals[9], totals[10], totals[11], totals[12], totals[13])
```

```python
import jax
import jax.numpy as jnp
from jax import lax
from jax.sharding import PartitionSpec as P

D = 1536
STATE = 128
CONV = 4
SPAN = 256
SEQ_LEN = 1024
INNER = 3072


EPS = 1e-05
HIGH = lax.Precision.HIGHEST


def causal_conv(inputs, segments, weight, conv_bias):
    result = conv_bias + weight[CONV - 1] * inputs
    for offset in range(1, CONV):
        shifted = jnp.pad(inputs, ((0, 0), (offset, 0), (0, 0)))[:, :-offset]
        earlier = jnp.pad(segments, ((0, 0), (offset, 0)), constant_values=-1)[:, :-offset]
        same_doc = (earlier == segments).astype(jnp.float32)[..., None]
        result = result + weight[CONV - 1 - offset] * shifted * same_doc
    return jax.nn.silu(result)


def scan_sequence(values, step_sizes, log_rates, bmat, cmat, segments):
    span_count = SEQ_LEN // SPAN
    head_count = log_rates.shape[1]
    values = values.reshape(span_count, SPAN, head_count, -1)
    step_sizes = step_sizes.reshape(span_count, SPAN, head_count)
    log_rates = log_rates.reshape(span_count, SPAN, head_count)
    bmat = bmat.reshape(span_count, SPAN, -1)
    cmat = cmat.reshape(span_count, SPAN, -1)
    blocks = segments.reshape(span_count, SPAN)
    before = jnp.concatenate([jnp.full((1,), -1, jnp.int32), blocks[:-1, -1]])
    cumulative = jnp.cumsum(log_rates, axis=1)
    row_index = lax.broadcasted_iota(jnp.int32, (SPAN, SPAN), 0)
    col_index = lax.broadcasted_iota(jnp.int32, (SPAN, SPAN), 1)
    inside = (blocks[:, :, None] == blocks[:, None, :]) & (row_index >= col_index)[None]
    gaps = cumulative[:, :, None, :] - cumulative[:, None, :, :]
    decays = (
        jnp.exp(jnp.where(inside[..., None], gaps, 0.0)) * inside.astype(jnp.float32)[..., None]
    )
    scores = jnp.einsum("cin,cjn->cij", cmat, bmat, precision=HIGH)
    weights = scores[..., None] * decays * step_sizes[:, None, :, :]
    inside_part = jnp.einsum("cijh,cjhp->cihp", weights, values, precision=HIGH)
    same_last = (blocks == blocks[:, -1:]).astype(jnp.float32)[..., None]
    tail_weight = same_last * jnp.exp(cumulative[:, -1:, :] - cumulative) * step_sizes
    span_states = jnp.einsum(
        "cjhp,cjn->chpn", tail_weight[..., None] * values, bmat, precision=HIGH
    )
    kept_mask = (blocks == before[:, None]).astype(jnp.float32)
    carry_rate = jnp.exp(cumulative[:, -1, :]) * kept_mask[:, -1:]
    carried_state = jnp.zeros(span_states.shape[1:], jnp.float32)
    entering = []
    for position in range(span_count):
        entering.append(carried_state)
        carried_state = carry_rate[position][:, None, None] * carried_state + span_states[position]
    entering = jnp.stack(entering)
    reach_gain = jnp.exp(cumulative) * kept_mask[..., None]
    carried = jnp.einsum("cin,chpn->cihp", cmat, entering, precision=HIGH) * reach_gain[..., None]
    return (inside_part + carried).reshape(SEQ_LEN, head_count, -1)


def mix_heads(
    gate_pre, inner_pre, step_raw, state_io, segments, conv_x, conv_x_bias, dt_bias, a_log, d_skip
):
    values = causal_conv(inner_pre, segments, conv_x, conv_x_bias)
    step_sizes = jax.nn.softplus(step_raw + dt_bias)
    log_rates = -jnp.exp(a_log) * step_sizes
    seq_count, length, channels = values.shape
    head_count = step_sizes.shape[-1]
    head_values = values.reshape(seq_count, length, head_count, channels // head_count)

    def per_sequence(packed):
        vals, sizes, rates_in, states_in, segs_in = packed
        return scan_sequence(
            vals, sizes, rates_in, states_in[:, :STATE], states_in[:, STATE:], segs_in
        )

    scanned = lax.map(
        jax.checkpoint(per_sequence), (head_values, step_sizes, log_rates, state_io, segments)
    )
    scanned = scanned + d_skip[:, None] * head_values
    return scanned.reshape(seq_count, length, channels) * jax.nn.silu(gate_pre)


def swap(array, axis, bit):
    size = lax.axis_size(axis)
    return lax.ppermute(array, axis, [(source, source ^ bit) for source in range(size)])


def half_of(array, which):
    half = array.shape[0] // 2
    return lax.dynamic_slice_in_dim(array, which * half, half, 0)


def axis_bits(axis):
    size = lax.axis_size(axis)
    return [1 << place for place in range(size.bit_length() - 1)]


def sum_over(array, axis, order):
    place = lax.axis_index(axis)
    part = array
    for bit in order:
        mine = (place // bit) % 2
        sent = half_of(part, 1 - mine).astype(jnp.bfloat16)
        part = half_of(part, mine).astype(jnp.float32) + swap(sent, axis, bit).astype(jnp.float32)
    part = part.astype(jnp.bfloat16)
    for bit in reversed(order):
        mine = (place // bit) % 2
        other = swap(part, axis, bit)
        first = jnp.where(mine == 0, part, other)
        second = jnp.where(mine == 0, other, part)
        part = jnp.concatenate([first, second], axis=0)
    return part


def sum_rows(array):
    bits = axis_bits("dp")
    swapped = [bits[1], bits[0]] + bits[2:]
    cut = array.shape[0] * 3 // 4
    first = sum_over(array[:cut], "dp", bits)
    second = sum_over(array[cut:], "dp", swapped)
    return jnp.concatenate([first, second], axis=0).astype(jnp.float32)


def scatter_tensor(array, dim):
    part = array.astype(jnp.bfloat16)
    rank = lax.axis_index("tensor")
    bits = axis_bits("tensor")
    count = 1 << len(bits)
    shape = part.shape
    grouped = part.reshape(shape[:dim] + (2,) * len(bits) + (shape[dim] // count,) + shape[dim + 1 :])
    for place, bit in enumerate(bits):
        mine = (rank // bit) % 2
        axis_at = dim + len(bits) - 1 - place
        sent = lax.dynamic_index_in_dim(grouped, 1 - mine, axis_at, keepdims=False)
        kept = lax.dynamic_index_in_dim(grouped, mine, axis_at, keepdims=False)
        grouped = kept.astype(jnp.float32) + swap(sent.astype(jnp.bfloat16), "tensor", bit).astype(jnp.float32)
    return grouped


def sum_tensor(array):
    for bit in axis_bits("tensor"):
        array = array + swap(array, "tensor", bit)
    return array


def shards(
    hidden_in,
    pre_gain,
    w_gate,
    w_value,
    w_bc,
    w_dt,
    conv_x,
    conv_x_bias,
    conv_bc,
    conv_bc_bias,
    dt_bias,
    a_log,
    d_skip,
    gate_gain,
    w_out,
    cotangent,
    segments,
):
    row_count = hidden_in.shape[0]
    seq_count = segments.shape[0]
    ranks = lax.axis_size("tensor")
    my_rank = lax.axis_index("tensor")
    own_rows = row_count // ranks
    row_start = my_rank * own_rows
    pair_width = w_bc.shape[1] // ranks
    pair_start = my_rank * pair_width
    contract_first = (((0,), (0,)), ((), ()))
    contract_last = (((1,), (1,)), ((), ()))
    hidden32 = hidden_in.astype(jnp.float32)
    inv_rms = lax.rsqrt(jnp.mean(hidden32 * hidden32, axis=-1, keepdims=True) + EPS)
    normed = (hidden32 * inv_rms * pre_gain).astype(jnp.bfloat16)
    gate_pre = jnp.dot(normed, w_gate, preferred_element_type=jnp.float32)
    inner_pre = jnp.dot(normed, w_value, preferred_element_type=jnp.float32)
    state_pre = jnp.dot(normed, w_bc, preferred_element_type=jnp.float32)
    step_raw = jnp.dot(normed, w_dt, preferred_element_type=jnp.float32)

    def conv_states(state_flat, conv_weight, conv_offset):
        return causal_conv(
            state_flat.reshape(seq_count, SEQ_LEN, -1), segments, conv_weight, conv_offset
        )

    state_io = conv_states(state_pre, conv_bc, conv_bc_bias)

    def heads_part(
        gate_flat,
        inner_flat,
        step_flat,
        states_in,
        conv_weight,
        conv_offset,
        bias_step,
        log_decay,
        skip_weight,
    ):
        return mix_heads(
            gate_flat.reshape(seq_count, SEQ_LEN, -1),
            inner_flat.reshape(seq_count, SEQ_LEN, -1),
            step_flat.reshape(seq_count, SEQ_LEN, -1),
            states_in,
            segments,
            conv_weight,
            conv_offset,
            bias_step,
            log_decay,
            skip_weight,
        ).reshape(row_count, -1)

    mixed_out, heads_back = jax.vjp(
        heads_part,
        gate_pre,
        inner_pre,
        step_raw,
        state_io,
        conv_x,
        conv_x_bias,
        dt_bias,
        a_log,
        d_skip,
    )
    gated_grad = lax.dot_general(
        cotangent, w_out, contract_last, preferred_element_type=jnp.float32
    )
    scaled_grad = gated_grad * gate_gain
    token_sums = sum_tensor(
        jnp.stack([jnp.sum(mixed_out * mixed_out, axis=-1), jnp.sum(scaled_grad * mixed_out, axis=-1)])
    )
    square_sum = token_sums[0][:, None]
    scale_dot = token_sums[1][:, None]
    inv_gate = lax.rsqrt(square_sum / INNER + EPS)
    gated = (mixed_out * inv_gate * gate_gain).astype(jnp.bfloat16)
    own_hidden = lax.dynamic_slice_in_dim(hidden32, row_start, own_rows, 0)
    w_out_grad = lax.dot_general(
        gated, cotangent, contract_first, preferred_element_type=jnp.float32
    )
    w_out_sum = sum_rows(w_out_grad)
    branch_own = scatter_tensor(jnp.dot(gated, w_out, preferred_element_type=jnp.float32), 0)
    block_out = (own_hidden + branch_own).astype(jnp.bfloat16)
    gate_gain_grad = jnp.sum(gated_grad * mixed_out * inv_gate, axis=0)
    mixed_grad = (
        scaled_grad * inv_gate - mixed_out * (inv_gate * inv_gate * inv_gate) * scale_dot / INNER
    )
    (
        gate_grad,
        inner_grad,
        step_grad,
        state_part,
        conv_x_grad,
        conv_x_bias_grad,
        dt_bias_grad,
        a_log_grad,
        d_skip_grad,
    ) = heads_back(mixed_grad)
    gate_low = gate_grad.astype(jnp.bfloat16)
    w_gate_sum = sum_rows(
        lax.dot_general(normed, gate_low, contract_first, preferred_element_type=jnp.float32)
    )
    inner_low = inner_grad.astype(jnp.bfloat16)
    w_value_sum = sum_rows(
        lax.dot_general(normed, inner_low, contract_first, preferred_element_type=jnp.float32)
    )
    state_own = scatter_tensor(state_part.reshape(row_count, -1), 1)
    _, state_back = jax.vjp(
        conv_states,
        lax.dynamic_slice_in_dim(state_pre, pair_start, pair_width, 1),
        lax.dynamic_slice_in_dim(conv_bc, pair_start, pair_width, 1),
        lax.dynamic_slice_in_dim(conv_bc_bias, pair_start, pair_width, 0),
    )
    pair_grad, pair_conv_grad, pair_bias_grad = state_back(
        state_own.reshape(seq_count, SEQ_LEN, -1)
    )
    pair_low = pair_grad.astype(jnp.bfloat16)
    step_low = step_grad.astype(jnp.bfloat16)
    pair_weight = lax.dynamic_slice_in_dim(w_bc, pair_start, pair_width, 1)
    total = lax.dot_general(gate_low, w_gate, contract_last, preferred_element_type=jnp.float32)
    total = total + lax.dot_general(
        inner_low, w_value, contract_last, preferred_element_type=jnp.float32
    )
    total = total + lax.dot_general(
        pair_low, pair_weight, contract_last, preferred_element_type=jnp.float32
    )
    total = total + lax.dot_general(step_low, w_dt, contract_last, preferred_element_type=jnp.float32)
    normed_own = scatter_tensor(total, 0)
    own_inv = lax.dynamic_slice_in_dim(inv_rms, row_start, own_rows, 0)
    own_cotan = lax.dynamic_slice_in_dim(cotangent, row_start, own_rows, 0).astype(jnp.float32)
    gain_scaled = normed_own * pre_gain
    own_dot = jnp.sum(gain_scaled * own_hidden, axis=-1, keepdims=True)
    hidden_grad = (
        own_cotan + own_inv * gain_scaled - own_hidden * (own_inv * own_inv * own_inv) * own_dot / D
    )
    w_bc_rows = lax.dot_general(pair_low, normed, contract_first, preferred_element_type=jnp.float32)
    w_dt_rows = lax.dot_general(step_low, normed, contract_first, preferred_element_type=jnp.float32)
    spread = jnp.zeros((CONV + 1, w_bc.shape[1]), jnp.float32)
    spread = lax.dynamic_update_slice_in_dim(
        spread, jnp.concatenate([pair_conv_grad, pair_bias_grad[None]]), pair_start, 1
    )
    gain_part = jnp.sum(total * hidden32 * inv_rms, axis=0)
    shared = sum_tensor(jnp.concatenate([gain_part, spread.reshape(-1)]))
    small = jnp.concatenate(
        [
            conv_x_grad.reshape(-1),
            conv_x_bias_grad,
            gate_gain_grad,
            shared,
            dt_bias_grad,
            a_log_grad,
            d_skip_grad,
        ]
    )
    small_rows = -(-small.shape[0] // D)
    used_rows = w_bc_rows.shape[0] + w_dt_rows.shape[0] + small_rows
    all_rows = -(-used_rows // 128) * 128
    packed = jnp.concatenate(
        [
            w_bc_rows,
            w_dt_rows,
            jnp.pad(small, (0, small_rows * D - small.shape[0])).reshape(small_rows, D),
            jnp.zeros((all_rows - used_rows, D), jnp.float32),
        ]
    )
    packed = sum_over(packed, "dp", axis_bits("dp")).astype(jnp.float32)
    channels = conv_x.shape[1]
    heads = dt_bias.shape[0]
    w_bc_sum = packed[:pair_width].T
    w_dt_sum = packed[pair_width : pair_width + heads].T
    small = packed[pair_width + heads : used_rows].reshape(-1)
    pieces = []
    at = 0
    for length in (
        CONV * channels,
        channels,
        channels,
        D,
        CONV * w_bc.shape[1],
        w_bc.shape[1],
        heads,
        heads,
        heads,
    ):
        pieces.append(small[at : at + length])
        at += length
    return (
        block_out,
        hidden_grad,
        pieces[3],
        w_gate_sum,
        w_value_sum,
        w_bc_sum,
        w_dt_sum,
        pieces[0].reshape(CONV, channels),
        pieces[1],
        pieces[4].reshape(CONV, -1),
        pieces[5],
        pieces[6],
        pieces[7],
        pieces[8],
        pieces[2],
        w_out_sum,
    )


def solution(mesh):
    in_specs = (
        P("dp", None),
        P(),
        P(None, "tensor"),
        P(None, "tensor"),
        P(),
        P(None, "tensor"),
        P(None, "tensor"),
        P("tensor"),
        P(),
        P(),
        P("tensor"),
        P("tensor"),
        P("tensor"),
        P("tensor"),
        P("tensor", None),
        P("dp", None),
        P("dp", None),
    )
    out_specs = (
        P(("dp", "tensor"), None),
        P(("dp", "tensor"), None),
        P(),
        P(None, "tensor"),
        P(None, "tensor"),
        P(None, "tensor"),
        P(None, "tensor"),
        P(None, "tensor"),
        P("tensor"),
        P(),
        P(),
        P("tensor"),
        P("tensor"),
        P("tensor"),
        P("tensor"),
        P("tensor", None),
    )
    return jax.shard_map(shards, mesh=mesh, in_specs=in_specs, out_specs=out_specs, check_vma=False)
```

```python
import functools
import math

import jax
import jax.numpy as jnp
from jax import lax
from jax.experimental import pallas as pl
from jax.experimental.pallas import tpu as pltpu
from jax.sharding import PartitionSpec as P

STATE = 128
CONV = 4
BLOCK = 256
PIECE = 128
LANES = 128
EPS = 1e-05
HIGH = lax.Precision.HIGHEST
LOG2E = math.log2(math.e)
BF16 = jnp.bfloat16
F32 = jnp.float32


def dot(left, right):
    return jnp.dot(left, right, preferred_element_type=F32)


def dot_last(left, right):
    return lax.dot_general(left, right, (((1,), (1,)), ((), ())), preferred_element_type=F32)


def dot_first(left, right):
    return lax.dot_general(left, right, (((0,), (0,)), ((), ())), preferred_element_type=F32)


def two_terms(array):
    upper = array.astype(BF16)
    return upper, (array - upper.astype(F32)).astype(BF16)


def sigmoid(array):
    return 0.5 * jnp.tanh(0.5 * array) + 0.5


def spread_heads(array, heads_twice):
    upper, rest = two_terms(array)
    return dot(jnp.concatenate([upper, rest], axis=1), heads_twice)


def sum_heads(array, heads):
    upper, rest = two_terms(array)
    return dot_last(upper, heads) + dot_last(rest, heads)


def triangle(rows, columns):
    return rows >= columns


def forward_kernel(
    hidden_ref,
    cotan_ref,
    gain_ref,
    w_gate_ref,
    w_value_ref,
    w_bc_ref,
    w_dt_ref,
    w_out_ref,
    channel_ref,
    conv_bc_ref,
    head_ref,
    side_ref,
    seg_row_ref,
    heads_ref,
    normed_ref,
    gate_ref,
    scan_ref,
    value_ref,
    slope_ref,
    inner_ref,
    grad_ref,
    step_ref,
    cum_ref,
    bc_ref,
    state_ref,
    enter_ref,
    sums_ref,
    tail_x,
    tail_bc,
    carried,
):
    block = pl.program_id(0)

    @pl.when(block == 0)
    def _():
        tail_x[0:8, :] = jnp.zeros((8, tail_x.shape[1]), F32)
        tail_bc[0:8, :] = jnp.zeros((8, tail_bc.shape[1]), F32)
        carried[...] = jnp.zeros(carried.shape, F32)

    hidden = hidden_ref[...].astype(F32)
    inv_rms = lax.rsqrt(jnp.mean(hidden * hidden, axis=-1, keepdims=True) + EPS)
    normed = (hidden * inv_rms * gain_ref[0:1, :]).astype(BF16)
    normed_ref[...] = normed
    tail_x[8:, :] = dot(normed, w_value_ref[...])
    tail_bc[8:, :] = dot(normed, w_bc_ref[...])
    step_in = dot(normed, w_dt_ref[...]) + head_ref[0:1, :]
    step_ref[...] = step_in
    step = jnp.maximum(step_in, 0.0) + jnp.log1p(jnp.exp(-jnp.abs(step_in)))
    rate = head_ref[1:2, :] * step * LOG2E
    gate_ref[...] = dot(normed, w_gate_ref[...])
    grad_ref[...] = dot_last(cotan_ref[...], w_out_ref[...])
    masks = [None] + [side_ref[:, k : k + 1] for k in range(1, CONV)]

    def conv(tail, taps_ref, lanes):
        result = taps_ref[CONV : CONV + 1, lanes] + taps_ref[CONV - 1 : CONV, lanes] * tail[8:, lanes]
        for k in range(1, CONV):
            shifted = tail[8 - k : 8 - k + BLOCK, lanes]
            result = result + taps_ref[CONV - 1 - k : CONV - k, lanes] * shifted * masks[k]
        return result

    channels = tail_x.shape[1]
    for at in range(0, channels, LANES):
        lanes = slice(at, at + LANES)
        before = conv(tail_x, channel_ref, lanes)
        half = sigmoid(before)
        value_ref[:, lanes] = before * half
        slope_ref[:, lanes] = half * (1.0 + before * (1.0 - half))
        inner_ref[:, lanes] = tail_x[8:, lanes]
    for at in range(0, 2 * STATE, LANES):
        lanes = slice(at, at + LANES)
        before = conv(tail_bc, conv_bc_ref, lanes)
        bc_ref[:, lanes] = (before * sigmoid(before)).astype(BF16)
        state_ref[:, lanes] = tail_bc[8:, lanes]
    tail_x[0:8, :] = tail_x[BLOCK:, :]
    tail_bc[0:8, :] = tail_bc[BLOCK:, :]

    row_at = lax.broadcasted_iota(jnp.int32, (PIECE, PIECE), 0)
    col_at = lax.broadcasted_iota(jnp.int32, (PIECE, PIECE), 1)
    lower = (row_at >= col_at).astype(F32)
    first_half = lax.broadcasted_iota(jnp.int32, (PIECE, LANES), 1) < LANES // 2
    heads = heads_ref[...]
    heads_twice = jnp.concatenate([heads, heads], axis=0)
    for piece in range(BLOCK // PIECE):
        rows = slice(piece * PIECE, (piece + 1) * PIECE)
        cum = jnp.dot(lower, rate[rows], precision=HIGH, preferred_element_type=F32)
        cum_ref[rows, :] = cum
        cum_t = cum.T
        same = (side_ref[rows, 0:1] == seg_row_ref[0:1, rows]) & (row_at >= col_at)
        bias = jnp.where(same, 0.0, -1e30)
        reach = jnp.exp2(cum) * side_ref[rows, 4:5]
        tail = jnp.exp2(cum[PIECE - 1 : PIECE, :] - cum) * side_ref[rows, 5:6]
        wide = spread_heads(jnp.concatenate([step[rows], reach, tail], axis=0), heads_twice)
        b_low = bc_ref[rows, 0:STATE]
        c_low = bc_ref[rows, STATE : 2 * STATE]
        scores = dot_last(c_low, b_low)
        enter = carried[...].astype(BF16)
        enter_ref[piece] = enter
        for pair in range(channels // LANES):
            lanes = slice(pair * LANES, (pair + 1) * LANES)
            values = value_ref[rows, lanes]
            scaled = wide[0:PIECE, lanes] * values
            low = scaled.astype(BF16)
            weights = []
            for head in (2 * pair, 2 * pair + 1):
                gaps = (cum[:, head : head + 1] - cum_t[head : head + 1, :]) + bias
                weights.append((scores * jnp.exp2(gaps)).astype(BF16))
            zero = jnp.zeros_like(low)
            both = jnp.concatenate(
                [jnp.where(first_half, low, zero), jnp.where(first_half, zero, low)], axis=0
            )
            out = dot(jnp.concatenate(weights, axis=1), both)
            out = out + dot(c_low, enter[:, lanes]) * wide[PIECE : 2 * PIECE, lanes]
            scan_ref[rows, lanes] = out + channel_ref[5:6, lanes] * values
            tailed = (wide[2 * PIECE :, lanes] * scaled).astype(BF16)
            kept = wide[2 * PIECE - 1 : 2 * PIECE, lanes]
            carried[:, lanes] = kept * carried[:, lanes] + dot_first(b_low, tailed)

    squares = jnp.zeros((8, BLOCK), F32)
    crosses = jnp.zeros((8, BLOCK), F32)
    ones = jnp.ones((8, LANES), BF16)
    square_part = jnp.zeros((BLOCK, LANES), F32)
    cross_part = jnp.zeros((BLOCK, LANES), F32)
    for at in range(0, channels, LANES):
        lanes = slice(at, at + LANES)
        gate = gate_ref[:, lanes]
        mixed = scan_ref[:, lanes] * (gate * sigmoid(gate))
        square_part = square_part + mixed * mixed
        cross_part = cross_part + mixed * (grad_ref[:, lanes] * channel_ref[6:7, lanes])
    upper, rest = two_terms(square_part)
    squares = dot_last(ones, upper) + dot_last(ones, rest)
    upper, rest = two_terms(cross_part)
    crosses = dot_last(ones, upper) + dot_last(ones, rest)
    is_first = lax.broadcasted_iota(jnp.int32, (8, BLOCK), 0) == 0
    sums_ref[...] = jnp.where(is_first, squares, crosses)


def gate_kernel(
    gate_ref,
    scan_ref,
    grad_ref,
    sums_ref,
    channel_ref,
    gated_ref,
    gate_low_ref,
    dscan_ref,
    gain_ref,
):
    @pl.when(pl.program_id(0) == 0)
    def _():
        gain_ref[...] = jnp.zeros(gain_ref.shape, F32)

    row_at = lax.broadcasted_iota(jnp.int32, (8, LANES), 0)

    def column(which):
        pick = (row_at == which).astype(F32)
        return lax.dot_general(
            sums_ref[...], pick, (((0,), (0,)), ((), ())), precision=HIGH, preferred_element_type=F32
        )

    channels = gate_ref.shape[1]
    inv_gate = lax.rsqrt(column(0) + EPS)
    pull = inv_gate * inv_gate * column(1)
    for at in range(0, channels, LANES):
        lanes = slice(at, at + LANES)
        gate = gate_ref[:, lanes]
        scan = scan_ref[:, lanes]
        half = sigmoid(gate)
        act = gate * half
        mixed = scan * act
        gain = channel_ref[6:7, lanes]
        normal = mixed * inv_gate
        gated_ref[:, lanes] = (normal * gain).astype(BF16)
        grad = grad_ref[:, lanes]
        gain_ref[:, lanes] += jnp.sum((grad * normal).reshape(-1, 8, LANES), axis=0)
        mixed_grad = inv_gate * (grad * gain - mixed * pull)
        gate_low_ref[:, lanes] = (mixed_grad * scan * (half * (1.0 + gate * (1.0 - half)))).astype(BF16)
        dscan_ref[:, lanes] = (mixed_grad * act).astype(BF16)


def backward_kernel(
    dscan_ref,
    scan_ref,
    value_ref,
    slope_ref,
    inner_ref,
    step_ref,
    cum_ref,
    bc_ref,
    enter_ref,
    channel_ref,
    head_ref,
    side_ref,
    seg_row_ref,
    heads_ref,
    inner_low_ref,
    step_low_ref,
    state_part_ref,
    channel_grad_ref,
    head_grad_ref,
    later,
    leaving,
):
    @pl.when(pl.program_id(0) == 0)
    def _():
        later[PIECE:, :] = jnp.zeros((8, later.shape[1]), F32)
        leaving[...] = jnp.zeros(leaving.shape, F32)
        channel_grad_ref[...] = jnp.zeros(channel_grad_ref.shape, F32)
        head_grad_ref[...] = jnp.zeros(head_grad_ref.shape, F32)

    channels = inner_ref.shape[1]
    row_at = lax.broadcasted_iota(jnp.int32, (PIECE, PIECE), 0)
    col_at = lax.broadcasted_iota(jnp.int32, (PIECE, PIECE), 1)
    upper_ones = (row_at <= col_at).astype(F32)
    first_half = lax.broadcasted_iota(jnp.int32, (PIECE, LANES), 1) < LANES // 2
    heads = heads_ref[...]
    heads_twice = jnp.concatenate([heads, heads], axis=0)
    step_in = step_ref[...]
    step = jnp.maximum(step_in, 0.0) + jnp.log1p(jnp.exp(-jnp.abs(step_in)))
    cum = cum_ref[...]
    cum_t = cum.T
    same = (side_ref[:, 0:1] == seg_row_ref[0:1, :]) & (row_at <= col_at)
    bias = jnp.where(same, 0.0, -1e30)
    reach = jnp.exp2(cum) * side_ref[:, 4:5]
    tail = jnp.exp2(cum[PIECE - 1 : PIECE, :] - cum) * side_ref[:, 5:6]
    wide = spread_heads(jnp.concatenate([step, reach, tail], axis=0), heads_twice)
    b_low = bc_ref[:, 0:STATE]
    c_low = bc_ref[:, STATE : 2 * STATE]
    scores = dot_last(b_low, c_low)
    score_grad = jnp.zeros((PIECE, PIECE), F32)
    b_grad = jnp.zeros((PIECE, STATE), F32)
    c_grad = jnp.zeros((PIECE, STATE), F32)
    row_sum = jnp.zeros((PIECE, LANES), F32)
    value_sum = jnp.zeros((PIECE, LANES), F32)
    last_sum = jnp.zeros((8, LANES), F32)
    masks = [None] + [side_ref[:, 5 + k : 6 + k] for k in range(1, CONV)]
    for pair in range(channels // LANES):
        lanes = slice(pair * LANES, (pair + 1) * LANES)
        own_heads = heads[:, lanes]
        values = value_ref[:, lanes]
        dy_low = dscan_ref[:, lanes]
        dy = dy_low.astype(F32)
        wide_step = wide[0:PIECE, lanes]
        wide_reach = wide[PIECE : 2 * PIECE, lanes]
        wide_tail = wide[2 * PIECE :, lanes]
        low = (wide_step * values).astype(BF16)
        low_wide = low.astype(F32)
        leave = leaving[:, lanes]
        leave_low = leave.astype(BF16)
        enter = enter_ref[0, :, lanes]
        reached = (wide_reach * dy).astype(BF16)
        tailed = (wide_tail * low_wide).astype(BF16)
        c_grad = c_grad + dot_last(reached, enter)
        b_grad = b_grad + dot_last(tailed, leave_low)
        from_state = wide_tail * dot(b_low, leave_low)
        zero = jnp.zeros_like(low)
        dy_first = jnp.where(first_half, dy_low, zero)
        dy_second = jnp.where(first_half, zero, dy_low)
        weights = []
        for head, own in ((2 * pair, dy_first), (2 * pair + 1, dy_second)):
            gaps = (cum_t[head : head + 1, :] - cum[:, head : head + 1]) + bias
            decay = jnp.exp2(gaps)
            weights.append((scores * decay).astype(BF16))
            score_grad = score_grad + dot_last(low, own) * decay
        dx = dot(jnp.concatenate(weights, axis=1), jnp.concatenate([dy_first, dy_second], axis=0))
        dx = dx + from_state
        out = scan_ref[:, lanes] - channel_ref[5:6, lanes] * values
        row_sum = row_sum + sum_heads(dy * out - low_wide * dx, own_heads)
        value_sum = value_sum + sum_heads(values * dx, own_heads)
        kept = wide[2 * PIECE - 1 : 2 * PIECE, lanes]
        last = jnp.sum(low_wide * from_state, axis=0, keepdims=True) + kept * jnp.sum(
            enter.astype(F32) * leave, axis=0, keepdims=True
        )
        last_sum = last_sum + sum_heads(jnp.broadcast_to(last, (8, LANES)), own_heads)
        leaving[:, lanes] = kept * leave + dot_first(c_low, reached)
        dvalue = wide_step * dx + channel_ref[5:6, lanes] * dy
        dbefore = dvalue * slope_ref[:, lanes]
        later[0:PIECE, lanes] = dbefore
        inner = inner_ref[:, lanes]
        inner_grad = channel_ref[CONV - 1 : CONV, lanes] * dbefore
        channel_grad_ref[CONV - 1 : CONV, lanes] += jnp.sum(inner * dbefore, axis=0, keepdims=True)
        channel_grad_ref[CONV : CONV + 1, lanes] += jnp.sum(dbefore, axis=0, keepdims=True)
        channel_grad_ref[CONV + 1 : CONV + 2, lanes] += jnp.sum(dy * values, axis=0, keepdims=True)
        for k in range(1, CONV):
            shifted = later[k : k + PIECE, lanes] * masks[k]
            inner_grad = inner_grad + channel_ref[CONV - 1 - k : CONV - k, lanes] * shifted
            channel_grad_ref[CONV - 1 - k : CONV - k, lanes] += jnp.sum(
                inner * shifted, axis=0, keepdims=True
            )
        inner_low_ref[:, lanes] = inner_grad.astype(BF16)
    later[PIECE:, :] = later[0:8, :]
    grad_low = score_grad.astype(BF16)
    state_part_ref[:, 0:STATE] = (b_grad + dot(grad_low, c_low)).astype(BF16)
    state_part_ref[:, STATE:] = (c_grad + dot_first(grad_low, b_low)).astype(BF16)
    rate_grad = (
        jnp.dot(upper_ones, row_sum, precision=HIGH, preferred_element_type=F32) + last_sum[0:1, :]
    )
    coefficient = head_ref[1:2, :]
    step_grad = (value_sum + coefficient * rate_grad) / (1.0 + jnp.exp(-step_in))
    step_low_ref[...] = step_grad.astype(BF16)
    head_grad_ref[0:1, :] += jnp.sum(step_grad, axis=0, keepdims=True)
    head_grad_ref[1:2, :] += jnp.sum(rate_grad * step, axis=0, keepdims=True) * coefficient


def whole(shape):
    return pl.BlockSpec(shape, lambda i: (0,) * len(shape), pipeline_mode=pl.Buffered(1))


def run_forward(hidden_in, cotangent, gain, weights, tables, side, doc_row):
    rows, width = hidden_in.shape
    w_gate, w_value, w_bc, w_dt, w_out = weights
    channel_table, conv_table, head_table, heads = tables
    channels = w_gate.shape[1]
    states = w_bc.shape[1]

    def block(columns):
        return pl.BlockSpec((BLOCK, columns), lambda i: (i, 0))

    def out(columns, kind=F32):
        return jax.ShapeDtypeStruct((rows, columns), kind)

    per_block = BLOCK // PIECE
    return pl.pallas_call(
        forward_kernel,
        grid=(rows // BLOCK,),
        in_specs=[
            block(width),
            block(width),
            whole(gain.shape),
            whole(w_gate.shape),
            whole(w_value.shape),
            whole(w_bc.shape),
            whole(w_dt.shape),
            whole(w_out.shape),
            whole(channel_table.shape),
            whole(conv_table.shape),
            whole(head_table.shape),
            block(LANES),
            pl.BlockSpec((8, BLOCK), lambda i: (0, i)),
            whole(heads.shape),
        ],
        out_specs=[
            block(width),
            block(channels),
            block(channels),
            block(channels),
            block(channels),
            block(channels),
            block(channels),
            block(LANES),
            block(LANES),
            block(states),
            block(states),
            pl.BlockSpec((per_block, STATE, channels), lambda i: (i, 0, 0)),
            pl.BlockSpec((8, BLOCK), lambda i: (0, i)),
        ],
        out_shape=[
            out(width, BF16),
            out(channels),
            out(channels),
            out(channels),
            out(channels),
            out(channels),
            out(channels),
            out(LANES),
            out(LANES),
            out(states, BF16),
            out(states),
            jax.ShapeDtypeStruct((rows // PIECE, STATE, channels), BF16),
            jax.ShapeDtypeStruct((8, rows), F32),
        ],
        scratch_shapes=[
            pltpu.VMEM((BLOCK + 8, channels), F32),
            pltpu.VMEM((BLOCK + 8, states), F32),
            pltpu.VMEM((STATE, channels), F32),
        ],
        compiler_params=pltpu.CompilerParams(vmem_limit_bytes=56 << 20),
        name="forward",
    )(
        hidden_in,
        cotangent,
        gain,
        w_gate,
        w_value,
        w_bc,
        w_dt,
        w_out,
        channel_table,
        conv_table,
        head_table,
        side,
        doc_row,
        heads,
    )


def run_gate(gate_pre, scan, grad, sums, channel_table):
    rows, channels = gate_pre.shape
    block = pl.BlockSpec((BLOCK, channels), lambda i: (i, 0))
    low = jax.ShapeDtypeStruct((rows, channels), BF16)
    return pl.pallas_call(
        gate_kernel,
        grid=(rows // BLOCK,),
        in_specs=[
            block,
            block,
            block,
            pl.BlockSpec((8, BLOCK), lambda i: (0, i)),
            whole(channel_table.shape),
        ],
        out_specs=[block, block, block, whole((8, channels))],
        out_shape=[low, low, low, jax.ShapeDtypeStruct((8, channels), F32)],
        compiler_params=pltpu.CompilerParams(vmem_limit_bytes=32 << 20),
        name="gate",
    )(gate_pre, scan, grad, sums, channel_table)


def run_backward(dscan, scan, values, slope, inner, step_in, cum, bc_low, enter, tables, side, doc_row):
    rows, channels = scan.shape
    channel_table, _, head_table, heads = tables
    count = rows // PIECE
    states = bc_low.shape[1]

    def block(columns):
        return pl.BlockSpec((PIECE, columns), lambda i: (count - 1 - i, 0))

    return pl.pallas_call(
        backward_kernel,
        grid=(count,),
        in_specs=[
            block(channels),
            block(channels),
            block(channels),
            block(channels),
            block(channels),
            block(LANES),
            block(LANES),
            block(states),
            pl.BlockSpec((1, STATE, channels), lambda i: (count - 1 - i, 0, 0)),
            whole(channel_table.shape),
            whole(head_table.shape),
            block(LANES),
            pl.BlockSpec((8, PIECE), lambda i: (0, count - 1 - i)),
            whole(heads.shape),
        ],
        out_specs=[
            block(channels),
            block(LANES),
            block(states),
            whole((8, channels)),
            whole((8, LANES)),
        ],
        out_shape=[
            jax.ShapeDtypeStruct((rows, channels), BF16),
            jax.ShapeDtypeStruct((rows, LANES), BF16),
            jax.ShapeDtypeStruct((rows, states), BF16),
            jax.ShapeDtypeStruct((8, channels), F32),
            jax.ShapeDtypeStruct((8, LANES), F32),
        ],
        scratch_shapes=[
            pltpu.VMEM((PIECE + 8, channels), F32),
            pltpu.VMEM((STATE, channels), F32),
        ],
        compiler_params=pltpu.CompilerParams(vmem_limit_bytes=48 << 20),
        name="backward",
    )(
        dscan,
        scan,
        values,
        slope,
        inner,
        step_in,
        cum,
        bc_low,
        enter,
        channel_table,
        head_table,
        side,
        doc_row,
        heads,
    )


def document_tables(segments):
    seq_count, length = segments.shape
    documents = (segments + 64 * jnp.arange(seq_count, dtype=segments.dtype)[:, None]).reshape(-1)
    rows = documents.shape[0]
    padded = jnp.pad(documents, (CONV, CONV), constant_values=-1)
    columns = [documents.astype(F32)]
    for k in range(1, CONV):
        columns.append((padded[CONV - k : CONV - k + rows] == documents).astype(F32))
    pieces = documents.reshape(-1, PIECE)
    before = jnp.concatenate([jnp.full((1,), -1, documents.dtype), pieces[:-1, -1]])
    columns.append((pieces == before[:, None]).astype(F32).reshape(-1))
    columns.append((pieces == pieces[:, -1:]).astype(F32).reshape(-1))
    for k in range(1, CONV):
        columns.append((padded[CONV + k : CONV + k + rows] == documents).astype(F32))
    side = jnp.pad(jnp.stack(columns, axis=1), ((0, 0), (0, LANES - len(columns))))
    return side, jnp.broadcast_to(documents.astype(F32)[None], (8, rows))


def conv_silu(inputs, masks, weight, conv_bias):
    result = conv_bias + weight[CONV - 1] * inputs
    for k in range(1, CONV):
        shifted = jnp.pad(inputs, ((k, 0), (0, 0)))[:-k]
        result = result + weight[CONV - 1 - k] * shifted * masks[:, k : k + 1]
    return jax.nn.silu(result)


def swap(array, axis, bit):
    size = lax.axis_size(axis)
    return lax.ppermute(array, axis, [(source, source ^ bit) for source in range(size)])


def half_of(array, which):
    half = array.shape[0] // 2
    return lax.dynamic_slice_in_dim(array, which * half, half, 0)


def axis_bits(axis):
    size = lax.axis_size(axis)
    return [1 << place for place in range(size.bit_length() - 1)]


def sum_over(array, axis, order):
    place = lax.axis_index(axis)
    part = array
    for bit in order:
        mine = (place // bit) % 2
        sent = half_of(part, 1 - mine).astype(jnp.bfloat16)
        part = half_of(part, mine).astype(jnp.float32) + swap(sent, axis, bit).astype(jnp.float32)
    part = part.astype(jnp.bfloat16)
    for bit in reversed(order):
        mine = (place // bit) % 2
        other = swap(part, axis, bit)
        first = jnp.where(mine == 0, part, other)
        second = jnp.where(mine == 0, other, part)
        part = jnp.concatenate([first, second], axis=0)
    return part


def sum_rows(array):
    bits = axis_bits("dp")
    swapped = [bits[1], bits[0]] + bits[2:]
    cut = array.shape[0] * 3 // 4
    first = sum_over(array[:cut], "dp", bits)
    second = sum_over(array[cut:], "dp", swapped)
    return jnp.concatenate([first, second], axis=0).astype(jnp.float32)


def scatter_tensor(array, dim):
    part = array.astype(jnp.bfloat16)
    rank = lax.axis_index("tensor")
    bits = axis_bits("tensor")
    count = 1 << len(bits)
    shape = part.shape
    grouped = part.reshape(shape[:dim] + (2,) * len(bits) + (shape[dim] // count,) + shape[dim + 1 :])
    for place, bit in enumerate(bits):
        mine = (rank // bit) % 2
        axis_at = dim + len(bits) - 1 - place
        sent = lax.dynamic_index_in_dim(grouped, 1 - mine, axis_at, keepdims=False)
        kept = lax.dynamic_index_in_dim(grouped, mine, axis_at, keepdims=False)
        grouped = kept.astype(jnp.float32) + swap(sent.astype(jnp.bfloat16), "tensor", bit).astype(jnp.float32)
    return grouped


def sum_tensor(array):
    for bit in axis_bits("tensor"):
        array = array + swap(array, "tensor", bit)
    return array


def shards(
    hidden_in,
    pre_gain,
    w_gate,
    w_value,
    w_bc,
    w_dt,
    conv_x,
    conv_x_bias,
    conv_bc,
    conv_bc_bias,
    dt_bias,
    a_log,
    d_skip,
    gate_gain,
    w_out,
    cotangent,
    segments,
):
    row_count, width = hidden_in.shape
    channels = w_gate.shape[1]
    head_count = dt_bias.shape[0]
    head_width = channels // head_count
    ranks = lax.axis_size("tensor")
    my_rank = lax.axis_index("tensor")
    own_rows = row_count // ranks
    row_start = my_rank * own_rows
    pair_width = w_bc.shape[1] // ranks
    pair_start = my_rank * pair_width
    contract_first = (((0,), (0,)), ((), ()))
    contract_last = (((1,), (1,)), ((), ()))

    def pad_heads(array):
        return jnp.pad(array, [(0, 0)] * (array.ndim - 1) + [(0, LANES - head_count)])

    side, doc_row = document_tables(segments)
    channel_table = jnp.concatenate(
        [
            conv_x,
            conv_x_bias[None],
            jnp.repeat(d_skip, head_width)[None],
            gate_gain[None],
            jnp.zeros((1, channels), F32),
        ]
    )
    conv_table = jnp.concatenate([conv_bc, conv_bc_bias[None], jnp.zeros((3, w_bc.shape[1]), F32)])
    head_table = jnp.pad(
        jnp.stack([dt_bias, -jnp.exp(a_log)]), ((0, 6), (0, LANES - head_count))
    )
    heads = (
        lax.broadcasted_iota(jnp.int32, (LANES, channels), 1) // head_width
        == lax.broadcasted_iota(jnp.int32, (LANES, channels), 0)
    ).astype(BF16)
    tables = (channel_table, conv_table, head_table, heads)
    wide_dt = pad_heads(w_dt)
    (
        normed,
        gate_pre,
        scan,
        values,
        slope,
        inner_pre,
        gated_grad,
        step_in,
        cum,
        bc_low,
        state_pre,
        enter,
        sums,
    ) = run_forward(
        hidden_in,
        cotangent,
        jnp.broadcast_to(pre_gain[None], (8, width)),
        (w_gate, w_value, w_bc, wide_dt, w_out),
        tables,
        side,
        doc_row,
    )
    sums = sum_tensor(sums) / (channels * ranks)
    gated, gate_low, dscan, gain_rows = run_gate(gate_pre, scan, gated_grad, sums, channel_table)
    gate_gain_grad = jnp.sum(gain_rows, axis=0)
    w_out_sum = sum_rows(
        lax.dot_general(gated, cotangent, contract_first, preferred_element_type=F32)
    )
    w_gate_sum = sum_rows(
        lax.dot_general(normed, gate_low, contract_first, preferred_element_type=F32)
    )
    own_hidden = lax.dynamic_slice_in_dim(hidden_in, row_start, own_rows, 0).astype(F32)
    branch_own = scatter_tensor(jnp.dot(gated, w_out, preferred_element_type=F32), 0)
    block_out = (own_hidden + branch_own).astype(BF16)
    inner_low, step_low, state_part, channel_grads, head_grads = run_backward(
        dscan, scan, values, slope, inner_pre, step_in, cum, bc_low, enter, tables, side, doc_row
    )
    w_value_sum = sum_rows(
        lax.dot_general(normed, inner_low, contract_first, preferred_element_type=F32)
    )
    d_skip_grad = jnp.sum(channel_grads[CONV + 1].reshape(head_count, head_width), axis=-1)
    state_own = scatter_tensor(state_part, 1)
    _, state_back = jax.vjp(
        lambda inputs, weight, bias: conv_silu(inputs, side, weight, bias),
        lax.dynamic_slice_in_dim(state_pre, pair_start, pair_width, 1),
        lax.dynamic_slice_in_dim(conv_bc, pair_start, pair_width, 1),
        lax.dynamic_slice_in_dim(conv_bc_bias, pair_start, pair_width, 0),
    )
    pair_grad, pair_conv_grad, pair_bias_grad = state_back(state_own)
    pair_low = pair_grad.astype(BF16)
    pair_weight = lax.dynamic_slice_in_dim(w_bc, pair_start, pair_width, 1)
    total = lax.dot_general(gate_low, w_gate, contract_last, preferred_element_type=F32)
    total = total + lax.dot_general(
        inner_low, w_value, contract_last, preferred_element_type=F32
    )
    total = total + lax.dot_general(
        pair_low, pair_weight, contract_last, preferred_element_type=F32
    )
    total = total + lax.dot_general(step_low, wide_dt, contract_last, preferred_element_type=F32)
    normed_own = scatter_tensor(total, 0)
    hidden32 = hidden_in.astype(F32)
    inv_rms = lax.rsqrt(jnp.mean(hidden32 * hidden32, axis=-1, keepdims=True) + EPS)
    own_inv = lax.rsqrt(jnp.mean(own_hidden * own_hidden, axis=-1, keepdims=True) + EPS)
    own_cotan = lax.dynamic_slice_in_dim(cotangent, row_start, own_rows, 0).astype(F32)
    gain_scaled = normed_own * pre_gain
    own_dot = jnp.sum(gain_scaled * own_hidden, axis=-1, keepdims=True)
    hidden_grad = (
        own_cotan
        + own_inv * gain_scaled
        - own_hidden * (own_inv * own_inv * own_inv) * own_dot / width
    )
    w_bc_rows = lax.dot_general(pair_low, normed, contract_first, preferred_element_type=F32)
    w_dt_rows = lax.dot_general(step_low, normed, contract_first, preferred_element_type=F32)
    w_dt_rows = w_dt_rows[:16]
    spread = jnp.zeros((CONV + 1, w_bc.shape[1]), F32)
    spread = lax.dynamic_update_slice_in_dim(
        spread, jnp.concatenate([pair_conv_grad, pair_bias_grad[None]]), pair_start, 1
    )
    gain_part = jnp.sum(total * hidden32 * inv_rms, axis=0)
    shared = sum_tensor(jnp.concatenate([gain_part, spread.reshape(-1)]))
    small = jnp.concatenate(
        [
            channel_grads[: CONV + 1].reshape(-1),
            gate_gain_grad,
            shared,
            head_grads[0, :head_count],
            head_grads[1, :head_count],
            d_skip_grad,
        ]
    )
    small_rows = -(-small.shape[0] // width)
    dt_rows = w_dt_rows.shape[0]
    used_rows = pair_width + dt_rows + small_rows
    all_rows = -(-used_rows // 64) * 64
    packed = jnp.concatenate(
        [
            w_bc_rows,
            w_dt_rows,
            jnp.pad(small, (0, small_rows * width - small.shape[0])).reshape(small_rows, width),
            jnp.zeros((all_rows - used_rows, width), F32),
        ]
    )
    packed = sum_over(packed, "dp", axis_bits("dp")).astype(F32)
    w_bc_sum = packed[:pair_width].T
    w_dt_sum = packed[pair_width : pair_width + head_count].T
    small = packed[pair_width + dt_rows : used_rows].reshape(-1)
    pieces = []
    at = 0
    for length in (
        CONV * channels,
        channels,
        channels,
        width,
        CONV * w_bc.shape[1],
        w_bc.shape[1],
        head_count,
        head_count,
        head_count,
    ):
        pieces.append(small[at : at + length])
        at += length
    return (
        block_out,
        hidden_grad,
        pieces[3],
        w_gate_sum,
        w_value_sum,
        w_bc_sum,
        w_dt_sum,
        pieces[0].reshape(CONV, channels),
        pieces[1],
        pieces[4].reshape(CONV, -1),
        pieces[5],
        pieces[6],
        pieces[7],
        pieces[8],
        pieces[2],
        w_out_sum,
    )


def solution(mesh):
    in_specs = (
        P("dp", None),
        P(),
        P(None, "tensor"),
        P(None, "tensor"),
        P(),
        P(None, "tensor"),
        P(None, "tensor"),
        P("tensor"),
        P(),
        P(),
        P("tensor"),
        P("tensor"),
        P("tensor"),
        P("tensor"),
        P("tensor", None),
        P("dp", None),
        P("dp", None),
    )
    out_specs = (
        P(("dp", "tensor"), None),
        P(("dp", "tensor"), None),
        P(),
        P(None, "tensor"),
        P(None, "tensor"),
        P(None, "tensor"),
        P(None, "tensor"),
        P(None, "tensor"),
        P("tensor"),
        P(),
        P(),
        P("tensor"),
        P("tensor"),
        P("tensor"),
        P("tensor"),
        P("tensor", None),
    )
    return jax.shard_map(shards, mesh=mesh, in_specs=in_specs, out_specs=out_specs, check_vma=False)
```

```python
import functools
import math

import jax
import jax.numpy as jnp
from jax import lax
from jax.experimental import pallas as pl
from jax.experimental.pallas import tpu as pltpu
from jax.sharding import PartitionSpec as P

STATE = 128
CONV = 4
BLOCK = 256
PIECE = 128
PACKED = 128
LANES = 128
EPS = 1e-05
HIGH = lax.Precision.HIGHEST
LOG2E = math.log2(math.e)
BF16 = jnp.bfloat16
F32 = jnp.float32


def dot(left, right):
    return jnp.dot(left, right, preferred_element_type=F32)


def dot_last(left, right):
    return lax.dot_general(left, right, (((1,), (1,)), ((), ())), preferred_element_type=F32)


def dot_first(left, right):
    return lax.dot_general(left, right, (((0,), (0,)), ((), ())), preferred_element_type=F32)


def two_terms(array):
    upper = array.astype(BF16)
    return upper, (array - upper.astype(F32)).astype(BF16)


def sigmoid(array):
    return 0.5 * jnp.tanh(0.5 * array) + 0.5


def spread_heads(array, heads_twice):
    upper, rest = two_terms(array)
    return dot(jnp.concatenate([upper, rest], axis=1), heads_twice)


def sum_heads(array, heads):
    upper, rest = two_terms(array)
    return dot_last(upper, heads) + dot_last(rest, heads)


def head_table(channels, head_count):
    head_width = channels // head_count
    channel = lax.broadcasted_iota(jnp.int32, (LANES, channels), 1)
    head = lax.broadcasted_iota(jnp.int32, (LANES, channels), 0)
    first = head * head_width
    return ((channel >= first) & (channel < first + head_width)).astype(F32).astype(BF16)


def head_rows(head_ref, heads):
    upper, rest = two_terms(head_ref[...])
    return dot(upper, heads) + dot(rest, heads)


def table_kernel(
    segment_ref,
    pre_gain_ref,
    bias_x_ref,
    gate_gain_ref,
    bias_bc_ref,
    dt_bias_ref,
    a_log_ref,
    d_skip_ref,
    token_ref,
    row_ref,
    head_ref,
):
    seq_count, length = segment_ref.shape
    place = lax.broadcasted_iota(jnp.int32, (8, length), 1)
    at_row = lax.broadcasted_iota(jnp.int32, (8, length), 0)
    for seq in range(seq_count):
        documents = jnp.broadcast_to(segment_ref[seq : seq + 1, :], (8, length)).astype(F32)
        padded = jnp.where(at_row == 0, documents, 0.0)

        def moved(by):
            other = pltpu.roll(documents, by % length, 1)
            return other, (place >= by) & (place < length + by)

        for k in range(1, CONV):
            before, inside = moved(k)
            padded = jnp.where((at_row == k) & inside & (before == documents), 1.0, padded)
        ends = []
        for piece in range(length // PIECE):
            here = slice(piece * PIECE, (piece + 1) * PIECE)
            ends.append(jnp.broadcast_to(documents[:, (piece + 1) * PIECE - 1 : (piece + 1) * PIECE], (8, PIECE)))
        starts = [jnp.full((8, PIECE), -1.0, F32)] + ends[:-1]
        padded = jnp.where((at_row == 4) & (jnp.concatenate(starts, axis=1) == documents), 1.0, padded)
        padded = jnp.where((at_row == 5) & (jnp.concatenate(ends, axis=1) == documents), 1.0, padded)
        lower = jnp.zeros((8, length), F32)
        for k in range(1, CONV):
            after, inside = moved(-k)
            hit = inside & (after == documents)
            if 5 + k < 8:
                padded = jnp.where((at_row == 5 + k) & hit, 1.0, padded)
            else:
                lower = jnp.where((at_row == 5 + k - 8) & hit, 1.0, lower)
        columns = slice(seq * length, (seq + 1) * length)
        token_ref[0:8, columns] = padded + jnp.where(at_row == 0, 64.0 * seq, 0.0)
        token_ref[8:16, columns] = lower
    row_ref[...] = jnp.zeros(row_ref.shape, F32)
    for at, ref in enumerate((pre_gain_ref, bias_x_ref, gate_gain_ref, bias_bc_ref)):
        row_ref[at : at + 1, 0 : ref.shape[0]] = ref[...].reshape(1, -1)
    head_ref[...] = jnp.zeros(head_ref.shape, F32)
    count = dt_bias_ref.shape[0]
    head_ref[0:1, 0:count] = dt_bias_ref[...].reshape(1, -1)
    head_ref[1:2, 0:count] = -jnp.exp(a_log_ref[...].reshape(1, -1))
    head_ref[2:3, 0:count] = d_skip_ref[...].reshape(1, -1)


def forward_kernel(
    hidden_ref,
    cotan_ref,
    w_gate_ref,
    w_value_ref,
    w_bc_ref,
    w_dt_ref,
    w_out_ref,
    conv_x_ref,
    conv_bc_ref,
    row_ref,
    head_ref,
    token_ref,
    normed_ref,
    mixed_ref,
    act_ref,
    turn_ref,
    grad_ref,
    scan_ref,
    value_ref,
    slope_ref,
    inner_ref,
    step_ref,
    cum_ref,
    bc_ref,
    bc_slope_ref,
    state_ref,
    enter_ref,
    sums_ref,
    tail_x,
    tail_bc,
    carried,
    wide_dt,
    gate_all,
    grad_all,
):
    block = pl.program_id(0)

    @pl.when(block == 0)
    def _():
        tail_x[0:8, :] = jnp.zeros((8, tail_x.shape[1]), F32)
        tail_bc[0:8, :] = jnp.zeros((8, tail_bc.shape[1]), F32)
        carried[...] = jnp.zeros(carried.shape, F32)
        wide_dt[...] = jnp.zeros(wide_dt.shape, BF16)
        wide_dt[0 : w_dt_ref.shape[0], :] = w_dt_ref[...]

    channels = tail_x.shape[1]
    heads = head_table(channels, w_dt_ref.shape[0])
    skips = head_rows(head_ref, heads)[2:3, :]
    side = token_ref[...].T
    hidden = hidden_ref[...].astype(F32)
    inv_rms = lax.rsqrt(jnp.mean(hidden * hidden, axis=-1, keepdims=True) + EPS)
    normed = (hidden * inv_rms * row_ref[0:1, :]).astype(BF16)
    normed_ref[...] = normed
    tail_x[8:, :] = dot(normed, w_value_ref[...])
    tail_bc[8:, :] = dot(normed, w_bc_ref[...])
    step_in = dot_last(normed, wide_dt[...]) + head_ref[0:1, :]
    step_ref[...] = step_in
    step = jnp.maximum(step_in, 0.0) + jnp.log1p(jnp.exp(-jnp.abs(step_in)))
    rate = head_ref[1:2, :] * step * LOG2E
    gate_all[...] = dot(normed, w_gate_ref[...])
    grad_all[...] = dot_last(cotan_ref[...], w_out_ref[...])
    masks = [None] + [side[:, k : k + 1] for k in range(1, CONV)]

    def conv(tail, taps_ref, bias_at, lanes):
        result = row_ref[bias_at : bias_at + 1, lanes] + taps_ref[CONV - 1 : CONV, lanes] * tail[8:, lanes]
        for k in range(1, CONV):
            shifted = tail[8 - k : 8 - k + BLOCK, lanes]
            result = result + taps_ref[CONV - 1 - k : CONV - k, lanes] * shifted * masks[k]
        return result

    for at in range(0, channels, LANES):
        lanes = slice(at, at + LANES)
        before = conv(tail_x, conv_x_ref, 1, lanes)
        half = sigmoid(before)
        value_ref[:, lanes] = (before * half).astype(BF16)
        slope_ref[:, lanes] = (half * (1.0 + before * (1.0 - half))).astype(BF16)
        inner_ref[:, lanes] = tail_x[8:, lanes].astype(BF16)
    for at in range(0, 2 * STATE, LANES):
        lanes = slice(at, at + LANES)
        before = conv(tail_bc, conv_bc_ref, 3, lanes)
        half = sigmoid(before)
        bc_ref[:, lanes] = (before * half).astype(BF16)
        bc_slope_ref[:, lanes] = (half * (1.0 + before * (1.0 - half))).astype(BF16)
        state_ref[:, lanes] = tail_bc[8:, lanes].astype(BF16)
    tail_x[0:8, :] = tail_x[BLOCK:, :]
    tail_bc[0:8, :] = tail_bc[BLOCK:, :]

    row_at = lax.broadcasted_iota(jnp.int32, (PIECE, PIECE), 0)
    col_at = lax.broadcasted_iota(jnp.int32, (PIECE, PIECE), 1)
    lower = (row_at >= col_at).astype(F32)
    first_half = lax.broadcasted_iota(jnp.int32, (PIECE, LANES), 1) < LANES // 2
    heads_twice = jnp.concatenate([heads, heads], axis=0)
    for piece in range(BLOCK // PIECE):
        rows = slice(piece * PIECE, (piece + 1) * PIECE)
        cum = jnp.dot(lower, rate[rows], precision=HIGH, preferred_element_type=F32)
        cum_ref[rows, :] = cum
        cum_t = cum.T
        same = (side[rows, 0:1] == token_ref[0:1, rows]) & (row_at >= col_at)
        bias = jnp.where(same, 0.0, -1e30)
        reach = jnp.exp2(cum) * side[rows, 4:5]
        tail = jnp.exp2(cum[PIECE - 1 : PIECE, :] - cum) * side[rows, 5:6]
        wide = spread_heads(jnp.concatenate([step[rows], reach, tail], axis=0), heads_twice)
        b_low = bc_ref[rows, 0:STATE]
        c_low = bc_ref[rows, STATE : 2 * STATE]
        scores = dot_last(c_low, b_low)
        enter = carried[...].astype(BF16)
        enter_ref[piece] = enter
        for pair in range(channels // LANES):
            lanes = slice(pair * LANES, (pair + 1) * LANES)
            values = value_ref[rows, lanes].astype(F32)
            scaled = wide[0:PIECE, lanes] * values
            low = scaled.astype(BF16)
            weights = []
            for head in (2 * pair, 2 * pair + 1):
                gaps = (cum[:, head : head + 1] - cum_t[head : head + 1, :]) + bias
                weights.append((scores * jnp.exp2(gaps)).astype(BF16))
            zero = jnp.zeros_like(low)
            both = jnp.concatenate(
                [jnp.where(first_half, low, zero), jnp.where(first_half, zero, low)], axis=0
            )
            out = dot(jnp.concatenate(weights, axis=1), both)
            out = out + dot(c_low, enter[:, lanes]) * wide[PIECE : 2 * PIECE, lanes]
            scan_ref[rows, lanes] = out + skips[:, lanes] * values
            tailed = (wide[2 * PIECE :, lanes] * scaled).astype(BF16)
            kept = wide[2 * PIECE - 1 : 2 * PIECE, lanes]
            carried[:, lanes] = kept * carried[:, lanes] + dot_first(b_low, tailed)

    ones = jnp.ones((8, LANES), BF16)
    square_part = jnp.zeros((BLOCK, LANES), F32)
    cross_part = jnp.zeros((BLOCK, LANES), F32)
    for at in range(0, channels, LANES):
        lanes = slice(at, at + LANES)
        gate = gate_all[:, lanes]
        scan = scan_ref[:, lanes]
        grad = grad_all[:, lanes]
        half = sigmoid(gate)
        act = gate * half
        mixed = scan * act
        mixed_ref[:, lanes] = mixed.astype(BF16)
        act_ref[:, lanes] = act.astype(BF16)
        turn_ref[:, lanes] = (scan * (half * (1.0 + gate * (1.0 - half)))).astype(BF16)
        grad_ref[:, lanes] = grad.astype(BF16)
        square_part = square_part + mixed * mixed
        cross_part = cross_part + mixed * (grad * row_ref[2:3, lanes])
    upper, rest = two_terms(square_part)
    squares = dot_last(ones, upper) + dot_last(ones, rest)
    upper, rest = two_terms(cross_part)
    crosses = dot_last(ones, upper) + dot_last(ones, rest)
    is_first = lax.broadcasted_iota(jnp.int32, (8, BLOCK), 0) == 0
    sums_ref[...] = jnp.where(is_first, squares, crosses)


def store_halves(total, start, rows, mine, sent_ref, kept_ref):
    half = rows // 2
    sent_ref[...] = total[pl.ds(pl.multiple_of(start + (1 - mine) * half, 8), half), :].astype(BF16)
    kept_ref[...] = total[pl.ds(pl.multiple_of(start + mine * half, 8), half), :].astype(BF16)


def gate_kernel(
    low_ref,
    mixed_ref,
    act_ref,
    turn_ref,
    grad_ref,
    sums_ref,
    row_ref,
    cotan_ref,
    gated_ref,
    gate_low_ref,
    dscan_ref,
    gain_ref,
    sent_ref,
    kept_ref,
    out_total,
):
    block = pl.program_id(0)

    @pl.when(block == 0)
    def _():
        gain_ref[...] = jnp.zeros(gain_ref.shape, F32)
        out_total[...] = jnp.zeros(out_total.shape, F32)

    row_at = lax.broadcasted_iota(jnp.int32, (8, LANES), 0)

    def column(which):
        pick = (row_at == which).astype(F32)
        return lax.dot_general(
            sums_ref[...], pick, (((0,), (0,)), ((), ())), precision=HIGH, preferred_element_type=F32
        )

    channels = mixed_ref.shape[1]
    inv_gate = lax.rsqrt(column(0) + EPS)
    pull = inv_gate * inv_gate * column(1)
    for at in range(0, channels, LANES):
        lanes = slice(at, at + LANES)
        mixed = mixed_ref[:, lanes].astype(F32)
        grad = grad_ref[:, lanes].astype(F32)
        gain = row_ref[2:3, lanes]
        normal = mixed * inv_gate
        gated_ref[:, lanes] = (normal * gain).astype(BF16)
        gain_ref[:, lanes] += jnp.sum((grad * normal).reshape(-1, 8, LANES), axis=0)
        mixed_grad = inv_gate * (grad * gain - mixed * pull)
        gate_low_ref[:, lanes] = (mixed_grad * turn_ref[:, lanes].astype(F32)).astype(BF16)
        dscan_ref[:, lanes] = (mixed_grad * act_ref[:, lanes].astype(F32)).astype(BF16)
    out_total[...] += dot_first(gated_ref[...], cotan_ref[...])

    @pl.when(block == pl.num_programs(0) - 1)
    def _():
        store_halves(out_total, 0, out_total.shape[0], low_ref[0], sent_ref, kept_ref)


def weight_kernel(low_ref, normed_ref, grad_ref, sent_ref, kept_ref, total):
    block = pl.program_id(0)
    part = dot_first(normed_ref[...], grad_ref[...])

    @pl.when(block == 0)
    def _():
        total[...] = part

    @pl.when(block > 0)
    def _():
        total[...] += part

    @pl.when(block == pl.num_programs(0) - 1)
    def _():
        store_halves(total, 0, total.shape[0], low_ref[1], sent_ref, kept_ref)


def backward_kernel(
    head_count,
    low_ref,
    dscan_ref,
    scan_ref,
    value_ref,
    slope_ref,
    inner_ref,
    step_ref,
    cum_ref,
    bc_ref,
    enter_ref,
    normed_ref,
    conv_x_ref,
    head_ref,
    token_ref,
    state_part_ref,
    inner_low_ref,
    step_low_ref,
    channel_grad_ref,
    head_grad_ref,
    step_rows_ref,
    first_sent_ref,
    first_kept_ref,
    second_sent_ref,
    second_kept_ref,
    later,
    leaving,
    value_total,
    step_total,
):
    block = pl.program_id(0)

    @pl.when(block == 0)
    def _():
        later[PIECE:, :] = jnp.zeros((8, later.shape[1]), F32)
        leaving[...] = jnp.zeros(leaving.shape, F32)
        channel_grad_ref[...] = jnp.zeros(channel_grad_ref.shape, F32)
        head_grad_ref[...] = jnp.zeros(head_grad_ref.shape, F32)
        value_total[...] = jnp.zeros(value_total.shape, F32)
        step_total[...] = jnp.zeros(step_total.shape, F32)

    channels = inner_ref.shape[1]
    row_at = lax.broadcasted_iota(jnp.int32, (PIECE, PIECE), 0)
    col_at = lax.broadcasted_iota(jnp.int32, (PIECE, PIECE), 1)
    upper_ones = (row_at <= col_at).astype(F32)
    first_half = lax.broadcasted_iota(jnp.int32, (PIECE, LANES), 1) < LANES // 2
    heads = head_table(channels, head_count)
    skips = head_rows(head_ref, heads)[2:3, :]
    side_all = token_ref[...].T
    heads_twice = jnp.concatenate([heads, heads], axis=0)
    for piece in reversed(range(BLOCK // PIECE)):
        rows = slice(piece * PIECE, (piece + 1) * PIECE)
        side = side_all[rows]
        step_in = step_ref[rows, :]
        step = jnp.maximum(step_in, 0.0) + jnp.log1p(jnp.exp(-jnp.abs(step_in)))
        cum = cum_ref[rows, :]
        cum_t = cum.T
        same = (side[:, 0:1] == token_ref[0:1, rows]) & (row_at <= col_at)
        bias = jnp.where(same, 0.0, -1e30)
        reach = jnp.exp2(cum) * side[:, 4:5]
        tail = jnp.exp2(cum[PIECE - 1 : PIECE, :] - cum) * side[:, 5:6]
        wide = spread_heads(jnp.concatenate([step, reach, tail], axis=0), heads_twice)
        b_low = bc_ref[rows, 0:STATE]
        c_low = bc_ref[rows, STATE : 2 * STATE]
        scores = dot_last(b_low, c_low)
        score_grad = jnp.zeros((PIECE, PIECE), F32)
        b_grad = jnp.zeros((PIECE, STATE), F32)
        c_grad = jnp.zeros((PIECE, STATE), F32)
        row_sum = jnp.zeros((PIECE, LANES), F32)
        value_sum = jnp.zeros((PIECE, LANES), F32)
        last_sum = jnp.zeros((8, LANES), F32)
        masks = [None] + [side[:, 5 + k : 6 + k] for k in range(1, CONV)]
        for pair in range(channels // LANES):
            lanes = slice(pair * LANES, (pair + 1) * LANES)
            own_heads = heads[:, lanes]
            values = value_ref[rows, lanes].astype(F32)
            dy_low = dscan_ref[rows, lanes]
            dy = dy_low.astype(F32)
            wide_step = wide[0:PIECE, lanes]
            wide_reach = wide[PIECE : 2 * PIECE, lanes]
            wide_tail = wide[2 * PIECE :, lanes]
            low = (wide_step * values).astype(BF16)
            low_wide = low.astype(F32)
            leave = leaving[:, lanes]
            leave_low = leave.astype(BF16)
            enter = enter_ref[piece, :, lanes]
            reached = (wide_reach * dy).astype(BF16)
            tailed = (wide_tail * low_wide).astype(BF16)
            c_grad = c_grad + dot_last(reached, enter)
            b_grad = b_grad + dot_last(tailed, leave_low)
            from_state = wide_tail * dot(b_low, leave_low)
            zero = jnp.zeros_like(low)
            dy_first = jnp.where(first_half, dy_low, zero)
            dy_second = jnp.where(first_half, zero, dy_low)
            weights = []
            for head, own in ((2 * pair, dy_first), (2 * pair + 1, dy_second)):
                gaps = (cum_t[head : head + 1, :] - cum[:, head : head + 1]) + bias
                decay = jnp.exp2(gaps)
                weights.append((scores * decay).astype(BF16))
                score_grad = score_grad + dot_last(low, own) * decay
            dx = dot(jnp.concatenate(weights, axis=1), jnp.concatenate([dy_first, dy_second], axis=0))
            dx = dx + from_state
            out = scan_ref[rows, lanes] - skips[:, lanes] * values
            row_sum = row_sum + sum_heads(dy * out - low_wide * dx, own_heads)
            value_sum = value_sum + sum_heads(values * dx, own_heads)
            kept = wide[2 * PIECE - 1 : 2 * PIECE, lanes]
            last = jnp.sum(low_wide * from_state, axis=0, keepdims=True) + kept * jnp.sum(
                enter.astype(F32) * leave, axis=0, keepdims=True
            )
            last_sum = last_sum + sum_heads(jnp.broadcast_to(last, (8, LANES)), own_heads)
            leaving[:, lanes] = kept * leave + dot_first(c_low, reached)
            dvalue = wide_step * dx + skips[:, lanes] * dy
            dbefore = dvalue * slope_ref[rows, lanes].astype(F32)
            later[0:PIECE, lanes] = dbefore
            inner = inner_ref[rows, lanes].astype(F32)
            inner_grad = conv_x_ref[CONV - 1 : CONV, lanes] * dbefore
            channel_grad_ref[CONV - 1 : CONV, lanes] += jnp.sum(inner * dbefore, axis=0, keepdims=True)
            channel_grad_ref[CONV : CONV + 1, lanes] += jnp.sum(dbefore, axis=0, keepdims=True)
            channel_grad_ref[CONV + 1 : CONV + 2, lanes] += jnp.sum(dy * values, axis=0, keepdims=True)
            for k in range(1, CONV):
                shifted = later[k : k + PIECE, lanes] * masks[k]
                inner_grad = inner_grad + conv_x_ref[CONV - 1 - k : CONV - k, lanes] * shifted
                channel_grad_ref[CONV - 1 - k : CONV - k, lanes] += jnp.sum(
                    inner * shifted, axis=0, keepdims=True
                )
            inner_low_ref[rows, lanes] = inner_grad.astype(BF16)
        later[PIECE:, :] = later[0:8, :]
        grad_low = score_grad.astype(BF16)
        state_part_ref[rows, 0:STATE] = (b_grad + dot(grad_low, c_low)).astype(BF16)
        state_part_ref[rows, STATE:] = (c_grad + dot_first(grad_low, b_low)).astype(BF16)
        rate_grad = (
            jnp.dot(upper_ones, row_sum, precision=HIGH, preferred_element_type=F32) + last_sum[0:1, :]
        )
        coefficient = head_ref[1:2, :]
        step_grad = (value_sum + coefficient * rate_grad) / (1.0 + jnp.exp(-step_in))
        step_low_ref[rows, :] = step_grad.astype(BF16)
        head_grad_ref[0:1, :] += jnp.sum(step_grad, axis=0, keepdims=True)
        head_grad_ref[1:2, :] += jnp.sum(rate_grad * step, axis=0, keepdims=True) * coefficient
    value_total[...] += dot_first(normed_ref[...], inner_low_ref[...])
    step_total[...] += dot_first(step_low_ref[...], normed_ref[...])

    @pl.when(block == pl.num_programs(0) - 1)
    def _():
        half = value_total.shape[0] // 2
        store_halves(value_total, 0, half, low_ref[0], first_sent_ref, first_kept_ref)
        store_halves(value_total, half, half, low_ref[1], second_sent_ref, second_kept_ref)
        step_rows_ref[...] = step_total[0 : step_rows_ref.shape[0], :]


def merge_kernel(
    gate_low_ref,
    inner_low_ref,
    step_low_ref,
    gated_ref,
    normed_ref,
    w_gate_ref,
    w_value_ref,
    w_dt_ref,
    w_out_ref,
    both_ref,
    gain_ref,
    wide_dt,
):
    @pl.when(pl.program_id(0) == 0)
    def _():
        gain_ref[...] = jnp.zeros(gain_ref.shape, F32)
        wide_dt[...] = jnp.zeros(wide_dt.shape, BF16)
        wide_dt[0 : w_dt_ref.shape[0], :] = w_dt_ref[...]

    width = normed_ref.shape[1]
    total = dot_last(inner_low_ref[...], w_value_ref[...]) + dot_last(gate_low_ref[...], w_gate_ref[...])
    total = total + dot(step_low_ref[...], wide_dt[...])
    both_ref[:, 0:width] = total.astype(BF16)
    gain_ref[...] += jnp.sum((total * normed_ref[...].astype(F32)).reshape(-1, 8, width), axis=0)
    both_ref[:, width:] = dot(gated_ref[...], w_out_ref[...]).astype(BF16)


def state_kernel(
    rank_ref,
    total_ref,
    slope_ref,
    state_ref,
    conv_bc_ref,
    token_ref,
    w_bc_ref,
    normed_ref,
    own_part_ref,
    rows_ref,
    conv_grad_ref,
    gain_ref,
    later,
):
    rank = rank_ref[0]
    count, columns = total_ref.shape
    side = token_ref[...].T
    later[count:, :] = jnp.zeros((8, columns), F32)
    dbefore = total_ref[...].astype(F32) * slope_ref[...].astype(F32)
    later[0:count, :] = dbefore
    state = state_ref[...].astype(F32)
    grad = conv_bc_ref[CONV - 1 : CONV, :] * dbefore
    conv_grad_ref[...] = jnp.zeros(conv_grad_ref.shape, F32)
    conv_grad_ref[CONV - 1 : CONV, :] = jnp.sum(state * dbefore, axis=0, keepdims=True)
    conv_grad_ref[CONV : CONV + 1, :] = jnp.sum(dbefore, axis=0, keepdims=True)
    for k in range(1, CONV):
        shifted = later[k : k + count, :] * side[:, 5 + k : 6 + k]
        grad = grad + conv_bc_ref[CONV - 1 - k : CONV - k, :] * shifted
        conv_grad_ref[CONV - 1 - k : CONV - k, :] = jnp.sum(state * shifted, axis=0, keepdims=True)
    later[0:count, :] = grad
    own_columns = rows_ref.shape[0]
    picked = lax.broadcasted_iota(jnp.int32, (columns, own_columns), 0) == (
        lax.broadcasted_iota(jnp.int32, (columns, own_columns), 1) + rank * own_columns
    )
    own = dot(grad.astype(BF16), picked.astype(F32).astype(BF16)).astype(BF16)
    rows_ref[...] = dot_first(own, normed_ref[...])
    own_rows = own_part_ref.shape[0]
    start = pl.multiple_of(rank * own_rows, 8)
    own_part = dot_last(later[pl.ds(start, own_rows), :].astype(BF16), w_bc_ref[...])
    own_part_ref[...] = own_part
    own_normed = normed_ref[pl.ds(pl.multiple_of(start, 16), own_rows), :].astype(F32)
    gain_ref[...] = jnp.sum((own_part * own_normed).reshape(-1, 8, own_part.shape[1]), axis=0)


def pack_kernel(
    head_count,
    low_ref,
    bc_rows_ref,
    step_rows_ref,
    channel_ref,
    gate_gain_ref,
    shared_ref,
    conv_bc_ref,
    head_ref,
    sent_ref,
    kept_ref,
    packed,
):
    channels = channel_ref.shape[1]
    packed[...] = jnp.zeros(packed.shape, F32)
    at = bc_rows_ref.shape[0]
    packed[0:at, :] = bc_rows_ref[...]
    packed[at : at + 16, :] = step_rows_ref[...]
    at += 16
    for k in range(CONV):
        packed[at + k : at + k + 1, 0:channels] = channel_ref[k : k + 1, :]
    at += CONV
    packed[at : at + 1, 0:channels] = channel_ref[CONV : CONV + 1, :]
    packed[at + 1 : at + 2, 0:channels] = jnp.sum(gate_gain_ref[...], axis=0, keepdims=True)
    packed[at + 2 : at + 3, :] = shared_ref[0:1, :]
    at += 3
    states = conv_bc_ref.shape[1]
    packed[at : at + CONV + 1, 0:states] = conv_bc_ref[0 : CONV + 1, :]
    at += CONV + 1
    skips = sum_heads(channel_ref[...], head_table(channels, head_count))
    packed[at : at + 2, 0:LANES] = head_ref[0:2, :]
    packed[at + 2 : at + 3, 0:LANES] = skips[CONV + 1 : CONV + 2, :]
    store_halves(packed, 0, packed.shape[0], low_ref[0], sent_ref, kept_ref)


def whole(shape):
    return pl.BlockSpec(shape, lambda i: (0,) * len(shape), pipeline_mode=pl.Buffered(1))


def no_cost():
    return pl.CostEstimate(flops=0, bytes_accessed=0, transcendentals=0)


def params():
    return pltpu.CompilerParams(vmem_limit_bytes=60 << 20)


def run_tables(segments, pre_gain, bias_x, gate_gain, bias_bc, dt_bias, a_log, d_skip):
    inputs = (segments, pre_gain, bias_x, gate_gain, bias_bc, dt_bias, a_log, d_skip)
    in_vmem = pl.BlockSpec(memory_space=pltpu.VMEM)
    return pl.pallas_call(
        table_kernel,
        in_specs=[in_vmem] * len(inputs),
        out_specs=[in_vmem] * 3,
        out_shape=[
            jax.ShapeDtypeStruct((16, segments.size), F32),
            jax.ShapeDtypeStruct((8, pre_gain.shape[0]), F32),
            jax.ShapeDtypeStruct((8, LANES), F32),
        ],
        compiler_params=params(),
        name="tables",
    )(*inputs)


def run_forward(hidden_in, cotangent, weights, tables, tokens):
    rows, width = hidden_in.shape
    channels = weights[0].shape[1]
    states = weights[2].shape[1]
    constants = (*weights, *tables)

    def block(columns):
        return pl.BlockSpec((BLOCK, columns), lambda i: (i, 0))

    def out(columns, kind=BF16):
        return jax.ShapeDtypeStruct((rows, columns), kind)

    return pl.pallas_call(
        forward_kernel,
        grid=(rows // BLOCK,),
        in_specs=[block(width), block(width)]
        + [whole(array.shape) for array in constants]
        + [pl.BlockSpec((tokens.shape[0], BLOCK), lambda i: (0, i))],
        out_specs=[block(width)]
        + [block(channels)] * 8
        + [block(LANES)] * 2
        + [block(states)] * 3
        + [
            pl.BlockSpec((BLOCK // PIECE, STATE, channels), lambda i: (i, 0, 0)),
            pl.BlockSpec((8, BLOCK), lambda i: (0, i)),
        ],
        out_shape=[
            out(width),
            out(channels),
            out(channels),
            out(channels),
            out(channels),
            out(channels, F32),
            out(channels),
            out(channels),
            out(channels),
            out(LANES, F32),
            out(LANES, F32),
            out(states),
            out(states),
            out(states),
            jax.ShapeDtypeStruct((rows // PIECE, STATE, channels), BF16),
            jax.ShapeDtypeStruct((8, rows), F32),
        ],
        scratch_shapes=[
            pltpu.VMEM((BLOCK + 8, channels), F32),
            pltpu.VMEM((BLOCK + 8, states), F32),
            pltpu.VMEM((STATE, channels), F32),
            pltpu.VMEM((LANES, width), BF16),
            pltpu.VMEM((BLOCK, channels), F32),
            pltpu.VMEM((BLOCK, channels), F32),
        ],
        compiler_params=params(),
        cost_estimate=no_cost(),
        name="forward",
    )(hidden_in, cotangent, *constants, tokens)


def scalar_spec():
    return pl.BlockSpec(memory_space=pltpu.SMEM)


def half_shapes(rows, columns):
    return [jax.ShapeDtypeStruct((rows // 2, columns), BF16)] * 2


def run_gate(low, forward, sums, rows_table, cotangent):
    rows, channels = forward[0].shape
    width = cotangent.shape[1]

    def block(columns):
        return pl.BlockSpec((BLOCK, columns), lambda i: (i, 0))

    shape = jax.ShapeDtypeStruct((rows, channels), BF16)
    halves = half_shapes(channels, width)
    out = pl.pallas_call(
        gate_kernel,
        grid=(rows // BLOCK,),
        in_specs=[scalar_spec()]
        + [block(channels)] * 4
        + [pl.BlockSpec((8, BLOCK), lambda i: (0, i)), whole(rows_table.shape), block(width)],
        out_specs=[block(channels)] * 3
        + [whole((8, channels))]
        + [whole(half.shape) for half in halves],
        out_shape=[shape, shape, shape, jax.ShapeDtypeStruct((8, channels), F32)] + halves,
        scratch_shapes=[pltpu.VMEM((channels, width), F32)],
        compiler_params=params(),
        cost_estimate=no_cost(),
        name="gate",
    )(low, *forward, sums, rows_table, cotangent)
    return out[:4], out[4:]


def run_weight(low, normed, grad):
    rows, width = normed.shape
    channels = grad.shape[1]
    size = 2 * BLOCK
    halves = half_shapes(width, channels)
    return pl.pallas_call(
        weight_kernel,
        grid=(rows // size,),
        in_specs=[
            scalar_spec(),
            pl.BlockSpec((size, width), lambda i: (i, 0)),
            pl.BlockSpec((size, channels), lambda i: (i, 0)),
        ],
        out_specs=[whole(half.shape) for half in halves],
        out_shape=halves,
        scratch_shapes=[pltpu.VMEM((width, channels), F32)],
        compiler_params=params(),
        cost_estimate=no_cost(),
        name="weight",
    )(low, normed, grad)


def run_backward(low, by_channel, step_in, cum, bc_low, enter, normed, conv_x, head_values, tokens, head_count):
    rows, channels = by_channel[0].shape
    width = normed.shape[1]
    count = rows // BLOCK
    states = bc_low.shape[1]

    def block(columns):
        return pl.BlockSpec((BLOCK, columns), lambda i: (count - 1 - i, 0))

    def low_rows(columns):
        return jax.ShapeDtypeStruct((rows, columns), BF16)

    halves = half_shapes(width // 2, channels) * 2
    step_rows = jax.ShapeDtypeStruct((16, width), F32)
    out = pl.pallas_call(
        functools.partial(backward_kernel, head_count),
        grid=(count,),
        in_specs=[scalar_spec()]
        + [block(channels)] * 5
        + [block(LANES), block(LANES), block(states)]
        + [pl.BlockSpec((BLOCK // PIECE, STATE, channels), lambda i: (count - 1 - i, 0, 0))]
        + [block(width), whole(conv_x.shape), whole(head_values.shape)]
        + [pl.BlockSpec((tokens.shape[0], BLOCK), lambda i: (0, count - 1 - i))],
        out_specs=[block(states), block(channels), block(LANES)]
        + [whole((8, channels)), whole((8, LANES)), whole(step_rows.shape)]
        + [whole(half.shape) for half in halves],
        out_shape=[
            low_rows(states),
            low_rows(channels),
            low_rows(LANES),
            jax.ShapeDtypeStruct((8, channels), F32),
            jax.ShapeDtypeStruct((8, LANES), F32),
            step_rows,
        ]
        + halves,
        scratch_shapes=[
            pltpu.VMEM((PIECE + 8, channels), F32),
            pltpu.VMEM((STATE, channels), F32),
            pltpu.VMEM((width, channels), F32),
            pltpu.VMEM((LANES, width), F32),
        ],
        compiler_params=params(),
        cost_estimate=no_cost(),
        name="backward",
    )(low, *by_channel, step_in, cum, bc_low, enter, normed, conv_x, head_values, tokens)
    return out[:6], out[6:]


def run_merge(gate_low, inner_low, step_low, gated, normed, weights):
    rows, width = normed.shape
    blocked = (gate_low, inner_low, step_low, gated, normed)

    def block(columns):
        return pl.BlockSpec((BLOCK, columns), lambda i: (i, 0))

    return pl.pallas_call(
        merge_kernel,
        grid=(rows // BLOCK,),
        in_specs=[block(array.shape[1]) for array in blocked] + [whole(weight.shape) for weight in weights],
        out_specs=[block(2 * width), whole((8, width))],
        out_shape=[
            jax.ShapeDtypeStruct((rows, 2 * width), BF16),
            jax.ShapeDtypeStruct((8, width), F32),
        ],
        scratch_shapes=[pltpu.VMEM((LANES, width), BF16)],
        compiler_params=params(),
        cost_estimate=no_cost(),
        name="merge",
    )(*blocked, *weights)


def run_states(rank, total, slope, state_pre, conv_bc, tokens, w_bc, normed, ranks):
    rows, columns = total.shape
    width = normed.shape[1]
    in_vmem = pl.BlockSpec(memory_space=pltpu.VMEM)
    return pl.pallas_call(
        state_kernel,
        in_specs=[scalar_spec()] + [in_vmem] * 7,
        out_specs=[in_vmem] * 4,
        out_shape=[
            jax.ShapeDtypeStruct((rows // ranks, width), F32),
            jax.ShapeDtypeStruct((columns // ranks, width), F32),
            jax.ShapeDtypeStruct((8, columns), F32),
            jax.ShapeDtypeStruct((8, width), F32),
        ],
        scratch_shapes=[pltpu.VMEM((rows + 8, columns), F32)],
        compiler_params=params(),
        cost_estimate=no_cost(),
        name="states",
    )(rank, total, slope, state_pre, conv_bc, tokens, w_bc, normed)


def run_pack(low, bc_rows, step_rows, channel_grads, gain_rows, shared, conv_bc_grads, head_grads, head_count):
    width = bc_rows.shape[1]
    in_vmem = pl.BlockSpec(memory_space=pltpu.VMEM)
    return pl.pallas_call(
        functools.partial(pack_kernel, head_count),
        in_specs=[scalar_spec()] + [in_vmem] * 7,
        out_specs=[in_vmem] * 2,
        out_shape=half_shapes(PACKED, width),
        scratch_shapes=[pltpu.VMEM((PACKED, width), F32)],
        compiler_params=params(),
        cost_estimate=no_cost(),
        name="pack",
    )(low, bc_rows, step_rows, channel_grads, gain_rows, shared, conv_bc_grads, head_grads)


def swap(array, axis, bit):
    size = lax.axis_size(axis)
    return lax.ppermute(array, axis, [(source, source ^ bit) for source in range(size)])


def axis_bits(axis):
    size = lax.axis_size(axis)
    return [1 << place for place in range(size.bit_length() - 1)]


def half_of(array, which):
    half = array.shape[0] // 2
    return lax.dynamic_slice_in_dim(array, which * half, half, 0)


def sum_tensor_low_steps(array):
    size = lax.axis_size("tensor")
    for bit in axis_bits("tensor"):
        got = yield array, "tensor", [(i, i ^ bit) for i in range(size)]
        array = (array.astype(F32) + got.astype(F32)).astype(BF16)
    return array


def sum_tensor(array):
    for bit in axis_bits("tensor"):
        array = array + swap(array, "tensor", bit)
    return array


def sum_tensor_steps(array):
    size = lax.axis_size("tensor")
    for bit in axis_bits("tensor"):
        got = yield array, "tensor", [(i, i ^ bit) for i in range(size)]
        array = array + got
    return array


def sum_steps(sent, kept, bits):
    size = lax.axis_size("dp")
    place = lax.axis_index("dp")
    mine = [(place // bit) % 2 for bit in bits]
    moves = [[(i, i ^ bit) for i in range(size)] for bit in bits]
    got = yield sent, "dp", moves[0]
    part = kept.astype(F32) + got.astype(F32)
    for which, pairs in zip(mine[1:], moves[1:]):
        got = yield half_of(part, 1 - which).astype(BF16), "dp", pairs
        part = half_of(part, which) + got.astype(F32)
    part = part.astype(BF16)
    for which, pairs in reversed(list(zip(mine[1:], moves[1:]))):
        got = yield part, "dp", pairs
        part = jnp.concatenate([jnp.where(which == 0, part, got), jnp.where(which == 0, got, part)])
    got = yield part, "dp", moves[0]
    return jnp.where(mine[0] == 0, part, got), jnp.where(mine[0] == 0, got, part)


class Order:
    def __init__(self, token):
        self.token = token
        self.waiting = {}
        self.flying = {}
        self.results = {}

    def mark(self, *arrays):
        out = lax.optimization_barrier((self.token, *arrays))
        self.token = out[0]
        return out[1] if len(arrays) == 1 else out[1:]

    def run(self, function, *arrays):
        out = function(*(self.mark(*arrays) if len(arrays) > 1 else [self.mark(*arrays)]))
        return self.mark(*out) if isinstance(out, (tuple, list)) else self.mark(out)

    def advance(self, name, steps, got):
        try:
            self.waiting[name] = (steps, steps.send(got))
        except StopIteration as end:
            self.results[name] = end.value

    def add(self, name, steps):
        self.advance(name, steps, None)

    def go(self, *names):
        for name in names:
            if name in self.waiting:
                steps, (sent, axis, moves) = self.waiting.pop(name)
                self.flying[name] = (steps, lax.ppermute(self.mark(sent), axis, moves))

    def land(self, *names):
        names = [name for name in names if name in self.flying]
        if names:
            found = [self.flying.pop(name) for name in names]
            marked = lax.optimization_barrier((self.token, *[got for _, got in found]))
            self.token = marked[0]
            for name, (steps, _), got in zip(names, found, marked[1:]):
                self.advance(name, steps, got)

    def step(self, *names):
        for name in names:
            self.land(name)
            self.go(name)

    def follow(self, *moves):
        for move in moves:
            (self.go if move[0] == "+" else self.land)(move[1:])

    def finish_all(self):
        while self.flying or self.waiting:
            self.go(*list(self.waiting))
            self.land(*list(self.flying))


MOVES = (
    ("+o", "+w", "+g", "+st"),
    ("-st", "-o", "+st", "+v", "-g", "+o", "+g", "-w", "-st"),
    ("-v", "+v", "-o", "+w", "+o", "-g", "+g"),
    ("+sh", "-v", "-sh", "+sh", "-w", "-o", "+o", "-sh"),
    ("+sm", "+v", "-g", "-sm", "+w", "-o", "+g", "+sm", "-v", "+v", "+o", "-sm", "+sm", "-w", "+w", "-v", "+v", "-sm", "-g", "+sm", "+g", "-v", "-w", "+w", "+v", "-sm", "+sm", "-w", "+w"),
    ("-sm", "+sm", "-v", "-g", "-sm", "-o", "-w"),
)


def shards(
    hidden_in,
    pre_gain,
    w_gate,
    w_value,
    w_bc,
    w_dt,
    conv_x,
    conv_x_bias,
    conv_bc,
    conv_bc_bias,
    dt_bias,
    a_log,
    d_skip,
    gate_gain,
    w_out,
    cotangent,
    segments,
):
    row_count, width = hidden_in.shape
    channels = w_gate.shape[1]
    head_count = dt_bias.shape[0]
    head_width = channels // head_count
    ranks = lax.axis_size("tensor")
    my_rank = lax.axis_index("tensor")
    own_rows = row_count // ranks
    row_start = my_rank * own_rows
    pair_width = w_bc.shape[1] // ranks
    bits = axis_bits("dp")
    crossed = [bits[1], bits[0]] + bits[2:]
    place = lax.axis_index("dp").astype(jnp.int32)
    low_bits = jnp.stack([place % 2, (place // 2) % 2])
    w_dt_rows = w_dt.T
    tokens, rows_table, head_values = run_tables(
        segments, pre_gain, conv_x_bias, gate_gain, conv_bc_bias, dt_bias, a_log, d_skip
    )
    (
        normed,
        mixed,
        act,
        turn,
        gated_grad,
        scan,
        values,
        slope,
        inner_pre,
        step_in,
        cum,
        bc_low,
        bc_slope,
        state_pre,
        enter,
        sums,
    ) = run_forward(
        hidden_in,
        cotangent,
        (w_gate, w_value, w_bc, w_dt_rows, w_out),
        (conv_x, conv_bc, rows_table, head_values),
        tokens,
    )
    sums = sum_tensor(sums) / (channels * ranks)
    (gated, gate_low, dscan, gain_rows), out_halves = run_gate(
        low_bits, (mixed, act, turn, gated_grad), sums, rows_table, cotangent
    )
    order = Order(sums[0, 0])
    order.add("o", sum_steps(*out_halves, bits))
    order.go("o")
    order.add("g", sum_steps(*order.mark(*run_weight(low_bits, normed, order.mark(gate_low))), crossed))
    order.go("g")
    (state_part, inner_low, step_low, channel_grads, head_grads, step_rows), value_halves = run_backward(
        low_bits,
        (order.mark(dscan), scan, values, slope, inner_pre),
        step_in,
        cum,
        bc_low,
        enter,
        normed,
        conv_x,
        head_values,
        tokens,
        head_count,
    )
    state_part, *value_halves = order.mark(state_part, *value_halves)
    order.land("o", "g")
    order.add("v", sum_steps(*value_halves[:2], bits))
    order.add("w", sum_steps(*value_halves[2:], crossed))
    order.add("st", sum_tensor_low_steps(state_part))
    order.follow(*MOVES[0])
    both, gain_first = order.mark(
        *run_merge(
            *order.mark(gate_low, inner_low, step_low, gated),
            normed,
            (w_gate, w_value, w_dt_rows, w_out),
        )
    )
    both_own = lax.psum_scatter(both, "tensor", scatter_dimension=0, tiled=True)
    order.follow(*MOVES[1])
    pair_part, bc_rows, conv_bc_grads, gain_second = order.mark(
        *run_states(
            jnp.reshape(my_rank.astype(jnp.int32), (1,)),
            order.mark(order.results["st"]),
            bc_slope,
            state_pre,
            conv_bc,
            tokens,
            w_bc,
            normed,
            ranks,
        )
    )
    order.follow(*MOVES[2])
    gain_part = jnp.sum(gain_first + gain_second, axis=0, keepdims=True) / rows_table[0:1]
    order.add("sh", sum_tensor_steps(order.mark(gain_part)))
    order.follow(*MOVES[3])
    packed_halves = run_pack(
        low_bits,
        bc_rows,
        step_rows,
        channel_grads,
        gain_rows,
        order.results["sh"],
        conv_bc_grads,
        head_grads,
        head_count,
    )
    order.add("sm", sum_steps(*packed_halves, bits))
    order.follow(*MOVES[4])
    own_hidden, own_cotan, both_own = order.mark(
        lax.dynamic_slice_in_dim(hidden_in, row_start, own_rows, 0),
        lax.dynamic_slice_in_dim(cotangent, row_start, own_rows, 0),
        both_own,
    )
    own_hidden = own_hidden.astype(F32)
    block_out = (own_hidden + both_own[:, width:].astype(F32)).astype(BF16)
    own_inv = lax.rsqrt(jnp.mean(own_hidden * own_hidden, axis=-1, keepdims=True) + EPS)
    gain_scaled = (both_own[:, :width].astype(F32) + pair_part) * pre_gain
    own_dot = jnp.sum(gain_scaled * own_hidden, axis=-1, keepdims=True)
    hidden_grad = (
        own_cotan.astype(F32)
        + own_inv * gain_scaled
        - own_hidden * (own_inv * own_inv * own_inv) * own_dot / width
    )
    block_out, hidden_grad = order.mark(block_out, hidden_grad)
    order.follow(*MOVES[5])
    order.finish_all()
    w_out_sum = jnp.concatenate(order.results["o"]).astype(F32)
    w_gate_sum = jnp.concatenate(order.results["g"]).astype(F32)
    w_value_sum = jnp.concatenate([*order.results["v"], *order.results["w"]]).astype(F32)
    packed = jnp.concatenate(order.results["sm"]).astype(F32)
    at = pair_width + 16
    end = at + CONV + 3
    heads_at = end + CONV + 1
    states = w_bc.shape[1]
    return (
        block_out,
        hidden_grad,
        packed[at + CONV + 2],
        w_gate_sum,
        w_value_sum,
        packed[:pair_width].T,
        packed[pair_width : pair_width + head_count].T,
        packed[at : at + CONV, :channels],
        packed[at + CONV, :channels],
        packed[end : end + CONV, :states],
        packed[end + CONV, :states],
        packed[heads_at, :head_count],
        packed[heads_at + 1, :head_count],
        packed[heads_at + 2, :head_count],
        packed[at + CONV + 1, :channels],
        w_out_sum,
    )


def solution(mesh):
    in_specs = (
        P("dp", None),
        P(),
        P(None, "tensor"),
        P(None, "tensor"),
        P(),
        P(None, "tensor"),
        P(None, "tensor"),
        P("tensor"),
        P(),
        P(),
        P("tensor"),
        P("tensor"),
        P("tensor"),
        P("tensor"),
        P("tensor", None),
        P("dp", None),
        P("dp", None),
    )
    out_specs = (
        P(("dp", "tensor"), None),
        P(("dp", "tensor"), None),
        P(),
        P(None, "tensor"),
        P(None, "tensor"),
        P(None, "tensor"),
        P(None, "tensor"),
        P(None, "tensor"),
        P("tensor"),
        P(),
        P(),
        P("tensor"),
        P("tensor"),
        P("tensor"),
        P("tensor"),
        P("tensor", None),
    )
    return jax.shard_map(shards, mesh=mesh, in_specs=in_specs, out_specs=out_specs, check_vma=False)
```

```python
import functools
import math

import jax
import jax.numpy as jnp
from jax import lax
from jax.experimental import pallas as pl
from jax.experimental.pallas import tpu as pltpu
from jax.sharding import PartitionSpec as P

STATE = 128
CONV = 4
BLOCK = 256
PIECE = 128
OWN_BC = 64
LANES = 128
EPS = 1e-05
HIGH = lax.Precision.HIGHEST
LOG2E = math.log2(math.e)
BF16 = jnp.bfloat16
F32 = jnp.float32


def dot(left, right):
    return jnp.dot(left, right, preferred_element_type=F32)


def dot_last(left, right):
    return lax.dot_general(left, right, (((1,), (1,)), ((), ())), preferred_element_type=F32)


def dot_first(left, right):
    return lax.dot_general(left, right, (((0,), (0,)), ((), ())), preferred_element_type=F32)


def two_terms(array):
    upper = array.astype(BF16)
    return upper, (array - upper.astype(F32)).astype(BF16)


def sigmoid(array):
    return 0.5 * jnp.tanh(0.5 * array) + 0.5


def spread_heads(array, heads_twice):
    upper, rest = two_terms(array)
    return dot(jnp.concatenate([upper, rest], axis=1), heads_twice)


def sum_heads(array, heads):
    upper, rest = two_terms(array)
    return dot_last(upper, heads) + dot_last(rest, heads)


def head_table(channels, head_count):
    head_width = channels // head_count
    channel = lax.broadcasted_iota(jnp.int32, (LANES, channels), 1)
    head = lax.broadcasted_iota(jnp.int32, (LANES, channels), 0)
    first = head * head_width
    return ((channel >= first) & (channel < first + head_width)).astype(F32).astype(BF16)


def head_rows(head_ref, heads):
    upper, rest = two_terms(head_ref[...])
    return dot(upper, heads) + dot(rest, heads)


def table_kernel(
    segment_ref,
    pre_gain_ref,
    bias_x_ref,
    gate_gain_ref,
    bias_bc_ref,
    dt_bias_ref,
    a_log_ref,
    d_skip_ref,
    token_ref,
    row_ref,
    head_ref,
):
    seq_count, length = segment_ref.shape
    place = lax.broadcasted_iota(jnp.int32, (8, length), 1)
    at_row = lax.broadcasted_iota(jnp.int32, (8, length), 0)
    for seq in range(seq_count):
        documents = jnp.broadcast_to(segment_ref[seq : seq + 1, :], (8, length)).astype(F32)
        padded = jnp.where(at_row == 0, documents, 0.0)

        def moved(by):
            other = pltpu.roll(documents, by % length, 1)
            return other, (place >= by) & (place < length + by)

        for k in range(1, CONV):
            before, inside = moved(k)
            padded = jnp.where((at_row == k) & inside & (before == documents), 1.0, padded)
        ends = []
        for piece in range(length // PIECE):
            here = slice(piece * PIECE, (piece + 1) * PIECE)
            ends.append(jnp.broadcast_to(documents[:, (piece + 1) * PIECE - 1 : (piece + 1) * PIECE], (8, PIECE)))
        starts = [jnp.full((8, PIECE), -1.0, F32)] + ends[:-1]
        padded = jnp.where((at_row == 4) & (jnp.concatenate(starts, axis=1) == documents), 1.0, padded)
        padded = jnp.where((at_row == 5) & (jnp.concatenate(ends, axis=1) == documents), 1.0, padded)
        lower = jnp.zeros((8, length), F32)
        for k in range(1, CONV):
            after, inside = moved(-k)
            hit = inside & (after == documents)
            if 5 + k < 8:
                padded = jnp.where((at_row == 5 + k) & hit, 1.0, padded)
            else:
                lower = jnp.where((at_row == 5 + k - 8) & hit, 1.0, lower)
        columns = slice(seq * length, (seq + 1) * length)
        token_ref[0:8, columns] = padded + jnp.where(at_row == 0, 64.0 * seq, 0.0)
        token_ref[8:16, columns] = lower
    row_ref[...] = jnp.zeros(row_ref.shape, F32)
    for at, ref in enumerate((pre_gain_ref, bias_x_ref, gate_gain_ref, bias_bc_ref)):
        row_ref[at : at + 1, 0 : ref.shape[0]] = ref[...].reshape(1, -1)
    head_ref[...] = jnp.zeros(head_ref.shape, F32)
    count = dt_bias_ref.shape[0]
    head_ref[0:1, 0:count] = dt_bias_ref[...].reshape(1, -1)
    head_ref[1:2, 0:count] = -jnp.exp(a_log_ref[...].reshape(1, -1))
    head_ref[2:3, 0:count] = d_skip_ref[...].reshape(1, -1)


def forward_kernel(
    hidden_ref,
    cotan_ref,
    w_gate_ref,
    w_value_ref,
    w_bc_ref,
    w_dt_ref,
    w_out_ref,
    conv_x_ref,
    conv_bc_ref,
    row_ref,
    head_ref,
    token_ref,
    normed_ref,
    mixed_ref,
    act_ref,
    turn_ref,
    grad_ref,
    scan_ref,
    value_ref,
    slope_ref,
    inner_ref,
    step_ref,
    cum_ref,
    bc_ref,
    bc_slope_ref,
    state_ref,
    enter_ref,
    sums_ref,
    tail_x,
    tail_bc,
    carried,
    wide_dt,
    gate_all,
    grad_all,
):
    block = pl.program_id(0)

    @pl.when(block == 0)
    def _():
        tail_x[0:8, :] = jnp.zeros((8, tail_x.shape[1]), F32)
        tail_bc[0:8, :] = jnp.zeros((8, tail_bc.shape[1]), F32)
        carried[...] = jnp.zeros(carried.shape, F32)
        wide_dt[...] = jnp.zeros(wide_dt.shape, BF16)
        wide_dt[0 : w_dt_ref.shape[0], :] = w_dt_ref[...]

    channels = tail_x.shape[1]
    heads = head_table(channels, w_dt_ref.shape[0])
    skips = head_rows(head_ref, heads)[2:3, :]
    side = token_ref[...].T
    hidden = hidden_ref[...].astype(F32)
    inv_rms = lax.rsqrt(jnp.mean(hidden * hidden, axis=-1, keepdims=True) + EPS)
    normed = (hidden * inv_rms * row_ref[0:1, :]).astype(BF16)
    normed_ref[...] = normed
    tail_x[8:, :] = dot(normed, w_value_ref[...])
    tail_bc[8:, :] = dot(normed, w_bc_ref[...])
    step_in = dot_last(normed, wide_dt[...]) + head_ref[0:1, :]
    step_ref[...] = step_in
    step = jnp.maximum(step_in, 0.0) + jnp.log1p(jnp.exp(-jnp.abs(step_in)))
    rate = head_ref[1:2, :] * step * LOG2E
    gate_all[...] = dot(normed, w_gate_ref[...])
    grad_all[...] = dot_last(cotan_ref[...], w_out_ref[...])
    masks = [None] + [side[:, k : k + 1] for k in range(1, CONV)]

    def conv(tail, taps_ref, bias_at, lanes):
        result = row_ref[bias_at : bias_at + 1, lanes] + taps_ref[CONV - 1 : CONV, lanes] * tail[8:, lanes]
        for k in range(1, CONV):
            shifted = tail[8 - k : 8 - k + BLOCK, lanes]
            result = result + taps_ref[CONV - 1 - k : CONV - k, lanes] * shifted * masks[k]
        return result

    for at in range(0, channels, LANES):
        lanes = slice(at, at + LANES)
        before = conv(tail_x, conv_x_ref, 1, lanes)
        half = sigmoid(before)
        value_ref[:, lanes] = (before * half).astype(BF16)
        slope_ref[:, lanes] = (half * (1.0 + before * (1.0 - half))).astype(BF16)
        inner_ref[:, lanes] = tail_x[8:, lanes].astype(BF16)
    for at in range(0, 2 * STATE, LANES):
        lanes = slice(at, at + LANES)
        before = conv(tail_bc, conv_bc_ref, 3, lanes)
        half = sigmoid(before)
        bc_ref[:, lanes] = (before * half).astype(BF16)
        bc_slope_ref[:, lanes] = half * (1.0 + before * (1.0 - half))
        state_ref[:, lanes] = tail_bc[8:, lanes]
    tail_x[0:8, :] = tail_x[BLOCK:, :]
    tail_bc[0:8, :] = tail_bc[BLOCK:, :]

    row_at = lax.broadcasted_iota(jnp.int32, (PIECE, PIECE), 0)
    col_at = lax.broadcasted_iota(jnp.int32, (PIECE, PIECE), 1)
    lower = (row_at >= col_at).astype(F32)
    first_half = lax.broadcasted_iota(jnp.int32, (PIECE, LANES), 1) < LANES // 2
    heads_twice = jnp.concatenate([heads, heads], axis=0)
    for piece in range(BLOCK // PIECE):
        rows = slice(piece * PIECE, (piece + 1) * PIECE)
        cum = jnp.dot(lower, rate[rows], precision=HIGH, preferred_element_type=F32)
        cum_ref[rows, :] = cum
        cum_t = cum.T
        same = (side[rows, 0:1] == token_ref[0:1, rows]) & (row_at >= col_at)
        bias = jnp.where(same, 0.0, -1e30)
        reach = jnp.exp2(cum) * side[rows, 4:5]
        tail = jnp.exp2(cum[PIECE - 1 : PIECE, :] - cum) * side[rows, 5:6]
        wide = spread_heads(jnp.concatenate([step[rows], reach, tail], axis=0), heads_twice)
        b_low = bc_ref[rows, 0:STATE]
        c_low = bc_ref[rows, STATE : 2 * STATE]
        scores = dot_last(c_low, b_low)
        enter = carried[...].astype(BF16)
        enter_ref[piece] = enter
        for pair in range(channels // LANES):
            lanes = slice(pair * LANES, (pair + 1) * LANES)
            values = value_ref[rows, lanes].astype(F32)
            scaled = wide[0:PIECE, lanes] * values
            low = scaled.astype(BF16)
            weights = []
            for head in (2 * pair, 2 * pair + 1):
                gaps = (cum[:, head : head + 1] - cum_t[head : head + 1, :]) + bias
                weights.append((scores * jnp.exp2(gaps)).astype(BF16))
            zero = jnp.zeros_like(low)
            both = jnp.concatenate(
                [jnp.where(first_half, low, zero), jnp.where(first_half, zero, low)], axis=0
            )
            out = dot(jnp.concatenate(weights, axis=1), both)
            out = out + dot(c_low, enter[:, lanes]) * wide[PIECE : 2 * PIECE, lanes]
            scan_ref[rows, lanes] = out + skips[:, lanes] * values
            tailed = (wide[2 * PIECE :, lanes] * scaled).astype(BF16)
            kept = wide[2 * PIECE - 1 : 2 * PIECE, lanes]
            carried[:, lanes] = kept * carried[:, lanes] + dot_first(b_low, tailed)

    ones = jnp.ones((8, LANES), BF16)
    square_part = jnp.zeros((BLOCK, LANES), F32)
    cross_part = jnp.zeros((BLOCK, LANES), F32)
    for at in range(0, channels, LANES):
        lanes = slice(at, at + LANES)
        gate = gate_all[:, lanes]
        scan = scan_ref[:, lanes]
        grad = grad_all[:, lanes]
        half = sigmoid(gate)
        act = gate * half
        mixed = scan * act
        mixed_ref[:, lanes] = mixed.astype(BF16)
        act_ref[:, lanes] = act.astype(BF16)
        turn_ref[:, lanes] = (scan * (half * (1.0 + gate * (1.0 - half)))).astype(BF16)
        grad_ref[:, lanes] = grad.astype(BF16)
        square_part = square_part + mixed * mixed
        cross_part = cross_part + mixed * (grad * row_ref[2:3, lanes])
    upper, rest = two_terms(square_part)
    squares = dot_last(ones, upper) + dot_last(ones, rest)
    upper, rest = two_terms(cross_part)
    crosses = dot_last(ones, upper) + dot_last(ones, rest)
    is_first = lax.broadcasted_iota(jnp.int32, (8, BLOCK), 0) == 0
    sums_ref[...] = jnp.where(is_first, squares, crosses)


def store_halves(total, columns, mine, sent_ref, kept_ref, at=0):
    half = total.shape[0] // 2
    to = slice(at, at + half)
    for which, ref in ((1 - mine, sent_ref), (mine, kept_ref)):
        ref[to, :] = total[pl.ds(pl.multiple_of(which * half, 8), half), columns].astype(BF16)


def gate_kernel(
    low_ref,
    mixed_ref,
    act_ref,
    turn_ref,
    grad_ref,
    sums_ref,
    row_ref,
    cotan_ref,
    normed_ref,
    gated_ref,
    gate_low_ref,
    dscan_ref,
    gain_ref,
    sent_ref,
    kept_ref,
    out_total,
    gate_total,
):
    block = pl.program_id(0)

    @pl.when(block == 0)
    def _():
        gain_ref[...] = jnp.zeros(gain_ref.shape, F32)
        out_total[...] = jnp.zeros(out_total.shape, F32)
        gate_total[...] = jnp.zeros(gate_total.shape, F32)

    row_at = lax.broadcasted_iota(jnp.int32, (8, LANES), 0)

    def column(which):
        pick = (row_at == which).astype(F32)
        return lax.dot_general(
            sums_ref[...], pick, (((0,), (0,)), ((), ())), precision=HIGH, preferred_element_type=F32
        )

    channels = mixed_ref.shape[1]
    inv_gate = lax.rsqrt(column(0) + EPS)
    pull = inv_gate * inv_gate * column(1)
    for at in range(0, channels, LANES):
        lanes = slice(at, at + LANES)
        mixed = mixed_ref[:, lanes].astype(F32)
        grad = grad_ref[:, lanes].astype(F32)
        gain = row_ref[2:3, lanes]
        normal = mixed * inv_gate
        gated_ref[:, lanes] = (normal * gain).astype(BF16)
        gain_ref[:, lanes] += jnp.sum((grad * normal).reshape(-1, 8, LANES), axis=0)
        mixed_grad = inv_gate * (grad * gain - mixed * pull)
        gate_low_ref[:, lanes] = (mixed_grad * turn_ref[:, lanes].astype(F32)).astype(BF16)
        dscan_ref[:, lanes] = (mixed_grad * act_ref[:, lanes].astype(F32)).astype(BF16)
    out_total[...] += dot_first(gated_ref[...], cotan_ref[...])
    gate_total[...] += dot_first(normed_ref[...], gate_low_ref[...])

    @pl.when(block == pl.num_programs(0) - 1)
    def _():
        rows, width = out_total.shape
        for at in range(width // channels):
            columns = slice(at * channels, (at + 1) * channels)
            store_halves(out_total, columns, low_ref[0], sent_ref, kept_ref, at * rows // 2)
        store_halves(gate_total, slice(None), low_ref[0], sent_ref, kept_ref, width // 2)


def weight_kernel(low_ref, normed_ref, grad_ref, after_ref, sent_ref, kept_ref, total):
    block = pl.program_id(0)
    part = dot_first(normed_ref[...], grad_ref[...])

    @pl.when(block == 0)
    def _():
        total[...] = part

    @pl.when(block > 0)
    def _():
        total[...] += part

    @pl.when(block == pl.num_programs(0) - 1)
    def _():
        store_halves(total, slice(None), low_ref[0], sent_ref, kept_ref)


def backward_kernel(
    head_count,
    dscan_ref,
    scan_ref,
    value_ref,
    slope_ref,
    inner_ref,
    step_ref,
    cum_ref,
    bc_ref,
    enter_ref,
    normed_ref,
    bc_slope_ref,
    state_ref,
    conv_x_ref,
    conv_bc_ref,
    head_ref,
    token_ref,
    after_ref,
    state_low_ref,
    inner_low_ref,
    step_low_ref,
    channel_grad_ref,
    conv_bc_grad_ref,
    head_grad_ref,
    step_rows_ref,
    bc_rows_ref,
    later,
    later_bc,
    leaving,
    step_total,
):
    block = pl.program_id(0)

    @pl.when(block == 0)
    def _():
        later[PIECE:, :] = jnp.zeros((8, later.shape[1]), F32)
        later_bc[PIECE:, :] = jnp.zeros((8, later_bc.shape[1]), F32)
        conv_bc_grad_ref[...] = jnp.zeros(conv_bc_grad_ref.shape, F32)
        bc_rows_ref[...] = jnp.zeros(bc_rows_ref.shape, F32)
        leaving[...] = jnp.zeros(leaving.shape, F32)
        channel_grad_ref[...] = jnp.zeros(channel_grad_ref.shape, F32)
        head_grad_ref[...] = jnp.zeros(head_grad_ref.shape, F32)
        step_total[...] = jnp.zeros(step_total.shape, F32)

    channels = inner_ref.shape[1]
    row_at = lax.broadcasted_iota(jnp.int32, (PIECE, PIECE), 0)
    col_at = lax.broadcasted_iota(jnp.int32, (PIECE, PIECE), 1)
    upper_ones = (row_at <= col_at).astype(F32)
    first_half = lax.broadcasted_iota(jnp.int32, (PIECE, LANES), 1) < LANES // 2
    heads = head_table(channels, head_count)
    skips = head_rows(head_ref, heads)[2:3, :]
    side_all = token_ref[...].T
    heads_twice = jnp.concatenate([heads, heads], axis=0)
    for piece in reversed(range(BLOCK // PIECE)):
        rows = slice(piece * PIECE, (piece + 1) * PIECE)
        side = side_all[rows]
        step_in = step_ref[rows, :]
        step = jnp.maximum(step_in, 0.0) + jnp.log1p(jnp.exp(-jnp.abs(step_in)))
        cum = cum_ref[rows, :]
        cum_t = cum.T
        same = (side[:, 0:1] == token_ref[0:1, rows]) & (row_at <= col_at)
        bias = jnp.where(same, 0.0, -1e30)
        reach = jnp.exp2(cum) * side[:, 4:5]
        tail = jnp.exp2(cum[PIECE - 1 : PIECE, :] - cum) * side[:, 5:6]
        wide = spread_heads(jnp.concatenate([step, reach, tail], axis=0), heads_twice)
        b_low = bc_ref[rows, 0:STATE]
        c_low = bc_ref[rows, STATE : 2 * STATE]
        scores = dot_last(b_low, c_low)
        score_grad = jnp.zeros((PIECE, PIECE), F32)
        b_grad = jnp.zeros((PIECE, STATE), F32)
        c_grad = jnp.zeros((PIECE, STATE), F32)
        row_sum = jnp.zeros((PIECE, LANES), F32)
        value_sum = jnp.zeros((PIECE, LANES), F32)
        last_sum = jnp.zeros((8, LANES), F32)
        masks = [None] + [side[:, 5 + k : 6 + k] for k in range(1, CONV)]
        for pair in range(channels // LANES):
            lanes = slice(pair * LANES, (pair + 1) * LANES)
            own_heads = heads[:, lanes]
            values = value_ref[rows, lanes].astype(F32)
            dy_low = dscan_ref[rows, lanes]
            dy = dy_low.astype(F32)
            wide_step = wide[0:PIECE, lanes]
            wide_reach = wide[PIECE : 2 * PIECE, lanes]
            wide_tail = wide[2 * PIECE :, lanes]
            low = (wide_step * values).astype(BF16)
            low_wide = low.astype(F32)
            leave = leaving[:, lanes]
            leave_low = leave.astype(BF16)
            enter = enter_ref[piece, :, lanes]
            reached = (wide_reach * dy).astype(BF16)
            tailed = (wide_tail * low_wide).astype(BF16)
            c_grad = c_grad + dot_last(reached, enter)
            b_grad = b_grad + dot_last(tailed, leave_low)
            from_state = wide_tail * dot(b_low, leave_low)
            zero = jnp.zeros_like(low)
            dy_first = jnp.where(first_half, dy_low, zero)
            dy_second = jnp.where(first_half, zero, dy_low)
            weights = []
            for head, own in ((2 * pair, dy_first), (2 * pair + 1, dy_second)):
                gaps = (cum_t[head : head + 1, :] - cum[:, head : head + 1]) + bias
                decay = jnp.exp2(gaps)
                weights.append((scores * decay).astype(BF16))
                score_grad = score_grad + dot_last(low, own) * decay
            dx = dot(jnp.concatenate(weights, axis=1), jnp.concatenate([dy_first, dy_second], axis=0))
            dx = dx + from_state
            out = scan_ref[rows, lanes] - skips[:, lanes] * values
            row_sum = row_sum + sum_heads(dy * out - low_wide * dx, own_heads)
            value_sum = value_sum + sum_heads(values * dx, own_heads)
            kept = wide[2 * PIECE - 1 : 2 * PIECE, lanes]
            last = jnp.sum(low_wide * from_state, axis=0, keepdims=True) + kept * jnp.sum(
                enter.astype(F32) * leave, axis=0, keepdims=True
            )
            last_sum = last_sum + sum_heads(jnp.broadcast_to(last, (8, LANES)), own_heads)
            leaving[:, lanes] = kept * leave + dot_first(c_low, reached)
            dvalue = wide_step * dx + skips[:, lanes] * dy
            dbefore = dvalue * slope_ref[rows, lanes].astype(F32)
            later[0:PIECE, lanes] = dbefore
            inner = inner_ref[rows, lanes].astype(F32)
            inner_grad = conv_x_ref[CONV - 1 : CONV, lanes] * dbefore
            channel_grad_ref[CONV - 1 : CONV, lanes] += jnp.sum(inner * dbefore, axis=0, keepdims=True)
            channel_grad_ref[CONV : CONV + 1, lanes] += jnp.sum(dbefore, axis=0, keepdims=True)
            channel_grad_ref[CONV + 1 : CONV + 2, lanes] += jnp.sum(dy * values, axis=0, keepdims=True)
            for k in range(1, CONV):
                shifted = later[k : k + PIECE, lanes] * masks[k]
                inner_grad = inner_grad + conv_x_ref[CONV - 1 - k : CONV - k, lanes] * shifted
                channel_grad_ref[CONV - 1 - k : CONV - k, lanes] += jnp.sum(
                    inner * shifted, axis=0, keepdims=True
                )
            inner_low_ref[rows, lanes] = inner_grad.astype(BF16)
        later[PIECE:, :] = later[0:8, :]
        grad_low = score_grad.astype(BF16)
        state_parts = (b_grad + dot(grad_low, c_low), c_grad + dot_first(grad_low, b_low))
        for at, state_part in enumerate(state_parts):
            lanes = slice(at * STATE, (at + 1) * STATE)
            dbefore = state_part * bc_slope_ref[rows, lanes]
            later_bc[0:PIECE, lanes] = dbefore
            state = state_ref[rows, lanes]
            state_grad = conv_bc_ref[CONV - 1 : CONV, lanes] * dbefore
            conv_bc_grad_ref[CONV - 1 : CONV, lanes] += jnp.sum(state * dbefore, axis=0, keepdims=True)
            conv_bc_grad_ref[CONV : CONV + 1, lanes] += jnp.sum(dbefore, axis=0, keepdims=True)
            for k in range(1, CONV):
                shifted = later_bc[k : k + PIECE, lanes] * masks[k]
                state_grad = state_grad + conv_bc_ref[CONV - 1 - k : CONV - k, lanes] * shifted
                conv_bc_grad_ref[CONV - 1 - k : CONV - k, lanes] += jnp.sum(
                    state * shifted, axis=0, keepdims=True
                )
            state_low_ref[rows, lanes] = state_grad.astype(BF16)
        later_bc[PIECE:, :] = later_bc[0:8, :]
        rate_grad = (
            jnp.dot(upper_ones, row_sum, precision=HIGH, preferred_element_type=F32) + last_sum[0:1, :]
        )
        coefficient = head_ref[1:2, :]
        step_grad = (value_sum + coefficient * rate_grad) / (1.0 + jnp.exp(-step_in))
        step_low_ref[rows, :] = step_grad.astype(BF16)
        head_grad_ref[0:1, :] += jnp.sum(step_grad, axis=0, keepdims=True)
        head_grad_ref[1:2, :] += jnp.sum(rate_grad * step, axis=0, keepdims=True) * coefficient
    step_total[...] += dot_first(step_low_ref[...], normed_ref[...])
    bc_rows_ref[...] += dot_first(state_low_ref[...], normed_ref[...])

    @pl.when(block == pl.num_programs(0) - 1)
    def _():
        step_rows_ref[...] = step_total[0 : step_rows_ref.shape[0], :]


def merge_kernel(
    core_ref,
    gate_low_ref,
    inner_low_ref,
    step_low_ref,
    state_low_ref,
    gated_ref,
    normed_ref,
    w_gate_ref,
    w_value_ref,
    w_dt_ref,
    w_bc_ref,
    w_out_ref,
    row_ref,
    after_ref,
    sent_ref,
    kept_ref,
    gain_ref,
    wide_dt,
):
    block = pl.program_id(0)
    last = pl.num_programs(0) - 1

    @pl.when(block == 0)
    def _():
        gain_ref[...] = jnp.zeros(gain_ref.shape, F32)
        wide_dt[...] = jnp.zeros(wide_dt.shape, BF16)
        wide_dt[0 : w_dt_ref.shape[0], :] = w_dt_ref[...]

    width = normed_ref.shape[1]
    total = dot_last(inner_low_ref[...], w_value_ref[...]) + dot_last(gate_low_ref[...], w_gate_ref[...])
    total = total + dot_last(state_low_ref[...], w_bc_ref[...]) + dot(step_low_ref[...], wide_dt[...])
    gain_ref[...] += jnp.sum((total * normed_ref[...].astype(F32)).reshape(-1, 8, width), axis=0)
    branch = dot(gated_ref[...], w_out_ref[...]).astype(BF16)

    @pl.when(2 * block < last)
    def _():
        sent_ref[:, 0:width] = total.astype(BF16)
        sent_ref[:, width:] = branch

    @pl.when(2 * block > last)
    def _():
        kept_ref[:, 0:width] = total.astype(BF16)
        kept_ref[:, width:] = branch

    @pl.when(block == last)
    def _():
        gain = jnp.sum(gain_ref[...], axis=0, keepdims=True) / row_ref[0:1, :]
        gain_ref[...] = jnp.broadcast_to(gain, gain_ref.shape)


def pack_kernel(
    head_count,
    core_ref,
    bc_rows_ref,
    step_rows_ref,
    channel_ref,
    gate_gain_ref,
    gain_ref,
    conv_bc_ref,
    head_ref,
    sent_ref,
    kept_ref,
    own_ref,
):
    core = core_ref[0]
    channels = channel_ref.shape[1]
    states, width = bc_rows_ref.shape
    folds = width // channels
    groups = (kept_ref.shape[0] - 16) // (OWN_BC * folds)
    for which, ref in ((1 - core, sent_ref), (core, kept_ref)):
        for group in range(groups):
            found = bc_rows_ref[pl.ds(pl.multiple_of((2 * group + which) * OWN_BC, 8), OWN_BC), :].astype(BF16)
            for fold in range(folds):
                at = (group * folds + fold) * OWN_BC
                ref[at : at + OWN_BC, :] = found[:, fold * channels : (fold + 1) * channels]
        shared = [gain_ref[0:1, fold * channels : (fold + 1) * channels] for fold in range(folds)]
        conv = conv_bc_ref[0 : CONV + 1, :]
        shared.append(jnp.concatenate([conv, jnp.zeros((CONV + 1, channels - states), F32)], axis=1))
        shared.append(jnp.zeros((16 - folds - CONV - 1, channels), F32))
        ref[ref.shape[0] - 16 :, :] = jnp.concatenate(shared).astype(BF16)
    own_ref[...] = jnp.zeros(own_ref.shape, F32)
    for fold in range(folds):
        own_ref[16 * fold : 16 * fold + 16, :] = step_rows_ref[:, fold * channels : (fold + 1) * channels]
    at = 16 * folds
    own_ref[at : at + CONV + 1, :] = channel_ref[0 : CONV + 1, :]
    own_ref[at + CONV + 1 : at + CONV + 2, :] = jnp.sum(gate_gain_ref[...], axis=0, keepdims=True)
    skips = sum_heads(channel_ref[...], head_table(channels, head_count))
    own_ref[at + CONV + 2 : at + CONV + 4, 0:LANES] = head_ref[0:2, :]
    own_ref[at + CONV + 4 : at + CONV + 5, 0:LANES] = skips[CONV + 1 : CONV + 2, :]


def unpack_kernel(
    one_ref,
    two_ref,
    pre_gain_ref,
    bc_ref,
    dt_ref,
    conv_x_ref,
    bias_x_ref,
    conv_bc_ref,
    bias_bc_ref,
    dt_bias_ref,
    a_log_ref,
    d_skip_ref,
    gate_gain_ref,
    total,
):
    total[...] = one_ref[...].astype(F32) + two_ref[...].astype(F32)
    channels = total.shape[1]
    own_bc, width = bc_ref.shape
    folds = width // channels
    for fold in range(folds):
        bc_ref[:, fold * channels : (fold + 1) * channels] = total[fold * own_bc : (fold + 1) * own_bc, :]
    at = folds * own_bc
    pre_gain_ref[...] = jnp.concatenate([total[at + fold : at + fold + 1, :] for fold in range(folds)], axis=1).reshape(-1)
    at += folds
    states = conv_bc_ref.shape[1]
    conv_bc_ref[...] = total[at : at + CONV, 0:states]
    bias_bc_ref[...] = total[at + CONV : at + CONV + 1, 0:states].reshape(-1)
    at += 16 - folds
    count = dt_ref.shape[0]
    for fold in range(folds):
        dt_ref[:, fold * channels : (fold + 1) * channels] = total[at + 16 * fold : at + 16 * fold + count, :]
    at += 16 * folds
    conv_x_ref[...] = total[at : at + CONV, :]
    bias_x_ref[...] = total[at + CONV : at + CONV + 1, :].reshape(-1)
    gate_gain_ref[...] = total[at + CONV + 1 : at + CONV + 2, :].reshape(-1)
    at += CONV + 2
    for row, ref in enumerate((dt_bias_ref, a_log_ref, d_skip_ref)):
        ref[...] = total[at + row : at + row + 1, 0:LANES].reshape(-1)[0 : ref.shape[0]]


def hidden_kernel(rank_ref, hidden_ref, cotan_ref, kept_ref, got_ref, row_ref, out_ref, grad_ref):
    width = hidden_ref.shape[1]
    hidden = hidden_ref[...].astype(F32)
    branch = kept_ref[:, width:].astype(F32) + got_ref[:, width:].astype(F32)
    out_ref[...] = (hidden + branch).astype(BF16)
    inv_rms = lax.rsqrt(jnp.mean(hidden * hidden, axis=-1, keepdims=True) + EPS)
    scaled = (kept_ref[:, 0:width].astype(F32) + got_ref[:, 0:width].astype(F32)) * row_ref[0:1, :]
    pull = inv_rms * inv_rms * jnp.mean(scaled * hidden, axis=-1, keepdims=True)
    grad_ref[...] = cotan_ref[...].astype(F32) + inv_rms * (scaled - hidden * pull)


def pass_kernel(*refs):
    pass


def finish_kernel(which_ref, own_ref, got_ref, after_ref, out_ref):
    which = which_ref[0]
    out_ref[pl.ds(which, 1)] = own_ref[...].astype(F32)[None]
    out_ref[pl.ds(1 - which, 1)] = got_ref[...].astype(F32)[None]


def finish_pair_kernel(which_ref, own_ref, got_ref, after_ref, out_ref, gate_ref):
    half = pl.program_id(0)

    def store(ref):
        rows, width = out_ref.shape
        channels = gate_ref.shape[1]
        for at in range(width // channels):
            out_ref[:, at * channels : (at + 1) * channels] = ref[at * rows : (at + 1) * rows, :].astype(F32)
        gate_ref[...] = ref[gate_ref.shape[0] :, :].astype(F32)

    @pl.when(half == which_ref[0])
    def _():
        store(own_ref)

    @pl.when(half != which_ref[0])
    def _():
        store(got_ref)


def split_kernel(which_ref, sent_one, sent_two, kept_one, kept_two, sent_ref, kept_ref):
    sent_ref[...] = (sent_one[...].astype(F32) + sent_two[...].astype(F32)).astype(BF16)
    kept_ref[...] = (kept_one[...].astype(F32) + kept_two[...].astype(F32)).astype(BF16)


def whole(shape):
    return pl.BlockSpec(shape, lambda i: (0,) * len(shape), pipeline_mode=pl.Buffered(1))


def no_cost():
    return pl.CostEstimate(flops=0, bytes_accessed=0, transcendentals=0)


def params():
    return pltpu.CompilerParams(vmem_limit_bytes=60 << 20)


def run_tables(segments, pre_gain, bias_x, gate_gain, bias_bc, dt_bias, a_log, d_skip):
    inputs = (segments, pre_gain, bias_x, gate_gain, bias_bc, dt_bias, a_log, d_skip)
    in_vmem = pl.BlockSpec(memory_space=pltpu.VMEM)
    return pl.pallas_call(
        table_kernel,
        in_specs=[in_vmem] * len(inputs),
        out_specs=[in_vmem] * 3,
        out_shape=[
            jax.ShapeDtypeStruct((16, segments.size), F32),
            jax.ShapeDtypeStruct((8, pre_gain.shape[0]), F32),
            jax.ShapeDtypeStruct((8, LANES), F32),
        ],
        compiler_params=params(),
        name="tables",
    )(*inputs)


def run_forward(hidden_in, cotangent, weights, tables, tokens):
    rows, width = hidden_in.shape
    channels = weights[0].shape[1]
    states = weights[2].shape[1]
    constants = (*weights, *tables)

    def block(columns):
        return pl.BlockSpec((BLOCK, columns), lambda i: (i, 0))

    def out(columns, kind=BF16):
        return jax.ShapeDtypeStruct((rows, columns), kind)

    return pl.pallas_call(
        forward_kernel,
        grid=(rows // BLOCK,),
        in_specs=[block(width), block(width)]
        + [whole(array.shape) for array in constants]
        + [pl.BlockSpec((tokens.shape[0], BLOCK), lambda i: (0, i))],
        out_specs=[block(width)]
        + [block(channels)] * 8
        + [block(LANES)] * 2
        + [block(states)] * 3
        + [
            pl.BlockSpec((BLOCK // PIECE, STATE, channels), lambda i: (i, 0, 0)),
            pl.BlockSpec((8, BLOCK), lambda i: (0, i)),
        ],
        out_shape=[
            out(width),
            out(channels),
            out(channels),
            out(channels),
            out(channels),
            out(channels, F32),
            out(channels),
            out(channels),
            out(channels),
            out(LANES, F32),
            out(LANES, F32),
            out(states),
            out(states, F32),
            out(states, F32),
            jax.ShapeDtypeStruct((rows // PIECE, STATE, channels), BF16),
            jax.ShapeDtypeStruct((8, rows), F32),
        ],
        scratch_shapes=[
            pltpu.VMEM((BLOCK + 8, channels), F32),
            pltpu.VMEM((BLOCK + 8, states), F32),
            pltpu.VMEM((STATE, channels), F32),
            pltpu.VMEM((LANES, width), BF16),
            pltpu.VMEM((BLOCK, channels), F32),
            pltpu.VMEM((BLOCK, channels), F32),
        ],
        compiler_params=params(),
        cost_estimate=no_cost(),
        name="forward",
    )(hidden_in, cotangent, *constants, tokens)


def scalar_spec():
    return pl.BlockSpec(memory_space=pltpu.SMEM)


def half_shapes(rows, columns):
    return [jax.ShapeDtypeStruct((rows // 2, columns), BF16)] * 2


def in_place():
    return pl.BlockSpec(memory_space=pl.ANY)


def run_gate(low, forward, sums, rows_table, cotangent, normed):
    rows, channels = forward[0].shape
    width = cotangent.shape[1]
    size = 2 * BLOCK

    def block(columns):
        return pl.BlockSpec((size, columns), lambda i: (i, 0))

    shape = jax.ShapeDtypeStruct((rows, channels), BF16)
    halves = [jax.ShapeDtypeStruct((width // 2 + width // 2, channels), BF16)] * 2
    out = pl.pallas_call(
        gate_kernel,
        grid=(rows // size,),
        in_specs=[scalar_spec()]
        + [block(channels)] * 4
        + [pl.BlockSpec((8, size), lambda i: (0, i)), whole(rows_table.shape), block(width), block(width)],
        out_specs=[block(channels)] * 3 + [whole((8, channels))] + [whole(half.shape) for half in halves],
        out_shape=[shape, shape, shape, jax.ShapeDtypeStruct((8, channels), F32)] + halves,
        scratch_shapes=[pltpu.VMEM((channels, width), F32), pltpu.VMEM((width, channels), F32)],
        compiler_params=params(),
        cost_estimate=no_cost(),
        name="gate",
    )(low, *forward, sums, rows_table, cotangent, normed)
    return out[:4], out[4:]


def run_weight(low, normed, grad, after):
    rows, width = normed.shape
    channels = grad.shape[1]
    size = 2 * BLOCK
    halves = half_shapes(width, channels)
    return pl.pallas_call(
        weight_kernel,
        grid=(rows // size,),
        in_specs=[
            scalar_spec(),
            pl.BlockSpec((size, width), lambda i: (i, 0)),
            pl.BlockSpec((size, channels), lambda i: (i, 0)),
            in_place(),
        ],
        out_specs=[whole(half.shape) for half in halves],
        out_shape=halves,
        scratch_shapes=[pltpu.VMEM((width, channels), F32)],
        compiler_params=params(),
        cost_estimate=no_cost(),
        name="weight",
    )(low, normed, grad, after)


def run_backward(by_channel, step_in, cum, bc_low, enter, normed, by_state, tables, after, head_count):
    rows, channels = by_channel[0].shape
    width = normed.shape[1]
    count = rows // BLOCK
    states = bc_low.shape[1]
    conv_x, conv_bc, head_values, tokens = tables

    def block(columns):
        return pl.BlockSpec((BLOCK, columns), lambda i: (count - 1 - i, 0))

    def low_rows(columns):
        return jax.ShapeDtypeStruct((rows, columns), BF16)

    sums = [
        jax.ShapeDtypeStruct(shape, F32)
        for shape in ((8, channels), (8, states), (8, LANES), (16, width), (states, width))
    ]
    return pl.pallas_call(
        functools.partial(backward_kernel, head_count),
        grid=(count,),
        in_specs=[block(channels)] * 5
        + [block(LANES), block(LANES), block(states)]
        + [pl.BlockSpec((BLOCK // PIECE, STATE, channels), lambda i: (count - 1 - i, 0, 0))]
        + [block(width), block(states), block(states)]
        + [whole(conv_x.shape), whole(conv_bc.shape), whole(head_values.shape)]
        + [pl.BlockSpec((tokens.shape[0], BLOCK), lambda i: (0, count - 1 - i)), in_place()],
        out_specs=[block(states), block(channels), block(LANES)]
        + [whole(shape.shape) for shape in sums],
        out_shape=[low_rows(states), low_rows(channels), low_rows(LANES)] + sums,
        scratch_shapes=[
            pltpu.VMEM((PIECE + 8, channels), F32),
            pltpu.VMEM((PIECE + 8, states), F32),
            pltpu.VMEM((STATE, channels), F32),
            pltpu.VMEM((LANES, width), F32),
        ],
        compiler_params=params(),
        cost_estimate=no_cost(),
        name="backward",
    )(*by_channel, step_in, cum, bc_low, enter, normed, *by_state, conv_x, conv_bc, head_values, tokens, after)


def run_merge(core, blocked, weights, rows_table, after, ranks):
    normed = blocked[-1]
    rows, width = normed.shape
    size = rows // ranks
    half = ranks // 2

    def block(columns):
        return pl.BlockSpec(
            (size, columns),
            lambda i, c: (jnp.where(i < half, 2 * i + 1 - c[0], 2 * (i - half) + c[0]), 0),
        )

    def constant(shape):
        return pl.BlockSpec(shape, lambda i, c: (0,) * len(shape), pipeline_mode=pl.Buffered(1))

    out = jax.ShapeDtypeStruct((rows // 2, 2 * width), BF16)
    return pl.pallas_call(
        merge_kernel,
        grid_spec=pltpu.PrefetchScalarGridSpec(
            num_scalar_prefetch=1,
            grid=(ranks,),
            in_specs=[block(array.shape[1]) for array in blocked]
            + [constant(array.shape) for array in (*weights, rows_table)]
            + [in_place()],
            out_specs=[
                pl.BlockSpec((size, 2 * width), lambda i, c: (jnp.minimum(i, half - 1), 0)),
                pl.BlockSpec((size, 2 * width), lambda i, c: (jnp.maximum(i - half, 0), 0)),
                constant((8, width)),
            ],
            scratch_shapes=[pltpu.VMEM((LANES, width), BF16)],
        ),
        out_shape=[out, out, jax.ShapeDtypeStruct((8, width), F32)],
        compiler_params=params(),
        cost_estimate=no_cost(),
        name="merge",
    )(core, *blocked, *weights, rows_table, after)


def run_pack(core, bc_rows, step_rows, channel_grads, gain_rows, gain, conv_bc_grads, head_grads, head_count):
    states, width = bc_rows.shape
    channels = channel_grads.shape[1]
    folds = width // channels
    in_vmem = pl.BlockSpec(memory_space=pltpu.VMEM)
    shared = jax.ShapeDtypeStruct((states // 2 * folds + 16, channels), BF16)
    return pl.pallas_call(
        functools.partial(pack_kernel, head_count),
        in_specs=[scalar_spec()] + [in_vmem] * 7,
        out_specs=[in_vmem] * 3,
        out_shape=[shared, shared, jax.ShapeDtypeStruct((16 * folds + 16, channels), F32)],
        compiler_params=params(),
        cost_estimate=no_cost(),
        name="pack",
    )(core, bc_rows, step_rows, channel_grads, gain_rows, gain, conv_bc_grads, head_grads)


def run_unpack(one, two, width, states, head_count):
    rows, channels = one.shape
    last = two.shape[0] // rows - 1
    in_vmem = pl.BlockSpec(memory_space=pltpu.VMEM)
    shapes = (
        (width,),
        (OWN_BC, width),
        (head_count, width),
        (CONV, channels),
        (channels,),
        (CONV, states),
        (states,),
        (head_count,),
        (head_count,),
        (head_count,),
        (channels,),
    )
    return pl.pallas_call(
        unpack_kernel,
        grid=(1,),
        in_specs=[
            pl.BlockSpec((rows, channels), lambda i: (0, 0)),
            pl.BlockSpec((rows, channels), lambda i: (last, 0)),
        ],
        out_specs=[pl.BlockSpec(shape, lambda i, rank=len(shape): (0,) * rank) for shape in shapes],
        out_shape=[jax.ShapeDtypeStruct(shape, F32) for shape in shapes],
        scratch_shapes=[pltpu.VMEM(one.shape, F32)],
        compiler_params=params(),
        cost_estimate=no_cost(),
        name="unpack",
    )(one, two)


def run_hidden(rank, hidden_in, cotangent, kept, got, rows_table):
    own_rows = kept.shape[0]
    width = hidden_in.shape[1]
    count = 2
    size = own_rows // count

    def own(columns):
        return pl.BlockSpec((size, columns), lambda i, r: (r[0] * count + i, 0))

    def block(columns):
        return pl.BlockSpec((size, columns), lambda i, r: (i, 0))

    return pl.pallas_call(
        hidden_kernel,
        grid_spec=pltpu.PrefetchScalarGridSpec(
            num_scalar_prefetch=1,
            grid=(count,),
            in_specs=[
                own(width),
                own(width),
                block(2 * width),
                block(2 * width),
                pl.BlockSpec(rows_table.shape, lambda i, r: (0, 0)),
            ],
            out_specs=[block(width), block(width)],
        ),
        out_shape=[
            jax.ShapeDtypeStruct((own_rows, width), BF16),
            jax.ShapeDtypeStruct((own_rows, width), F32),
        ],
        compiler_params=params(),
        cost_estimate=no_cost(),
        name="hidden",
    )(rank, hidden_in, cotangent, kept, got, rows_table)


def run_pass(arrays, after):
    count = len(arrays)
    return pl.pallas_call(
        pass_kernel,
        in_specs=[in_place()] * (count + 1),
        out_specs=[in_place()] * count,
        out_shape=[jax.ShapeDtypeStruct(array.shape, array.dtype) for array in arrays],
        input_output_aliases={at: at for at in range(count)},
        cost_estimate=no_cost(),
        name="pass",
    )(*arrays, after)


def run_finish(which, own, got, after):
    rows, columns = own.shape
    size = rows // 2
    block = pl.BlockSpec((size, columns), lambda i, w: (i, 0))
    out = pl.pallas_call(
        finish_kernel,
        grid_spec=pltpu.PrefetchScalarGridSpec(
            num_scalar_prefetch=1,
            grid=(rows // size,),
            in_specs=[block, block, in_place()],
            out_specs=pl.BlockSpec((2, size, columns), lambda i, w: (0, i, 0)),
        ),
        out_shape=jax.ShapeDtypeStruct((2, rows, columns), F32),
        compiler_params=params(),
        cost_estimate=no_cost(),
        name="finish",
    )(jnp.reshape(which, (1,)), own, got, after)
    return out.reshape(2 * rows, columns)


def run_finish_pair(which, own, got, after, shape):
    rows, channels = own.shape
    out_rows, width = shape
    in_vmem = pl.BlockSpec((rows, channels), lambda i, w: (0, 0), pipeline_mode=pl.Buffered(1))
    return pl.pallas_call(
        finish_pair_kernel,
        grid_spec=pltpu.PrefetchScalarGridSpec(
            num_scalar_prefetch=1,
            grid=(2,),
            in_specs=[in_vmem, in_vmem, in_place()],
            out_specs=[
                pl.BlockSpec((out_rows // 2, width), lambda i, w: (i, 0)),
                pl.BlockSpec((width // 2, channels), lambda i, w: (i, 0)),
            ],
        ),
        out_shape=[
            jax.ShapeDtypeStruct((out_rows, width), F32),
            jax.ShapeDtypeStruct((width, channels), F32),
        ],
        compiler_params=params(),
        cost_estimate=no_cost(),
        name="finish_pair",
    )(jnp.reshape(which, (1,)), own, got, after)


def run_split(one, two, which):
    half, columns = one.shape[0] // 2, one.shape[1]
    count = 2
    size = half // count
    sent = pl.BlockSpec((size, columns), lambda i, w: ((1 - w[0]) * count + i, 0))
    kept = pl.BlockSpec((size, columns), lambda i, w: (w[0] * count + i, 0))
    out = pl.BlockSpec((size, columns), lambda i, w: (i, 0))
    return pl.pallas_call(
        split_kernel,
        grid_spec=pltpu.PrefetchScalarGridSpec(
            num_scalar_prefetch=1,
            grid=(count,),
            in_specs=[sent, sent, kept, kept],
            out_specs=[out, out],
        ),
        out_shape=[jax.ShapeDtypeStruct((half, columns), BF16)] * 2,
        compiler_params=params(),
        cost_estimate=no_cost(),
        name="split",
    )(jnp.reshape(which.astype(jnp.int32), (1,)), one, two, one, two)


def swap(array, axis, bit):
    size = lax.axis_size(axis)
    return lax.ppermute(array, axis, [(source, source ^ bit) for source in range(size)])


def axis_bits(axis):
    size = lax.axis_size(axis)
    return [1 << place for place in range(size.bit_length() - 1)]


def half_of(array, which):
    half = array.shape[0] // 2
    return lax.dynamic_slice_in_dim(array, which * half, half, 0)


def sum_tensor(array):
    for bit in axis_bits("tensor"):
        array = array + swap(array, "tensor", bit)
    return array


def dp_bits(step):
    bits = axis_bits("dp")
    swapped = [bits[1], bits[0]] + bits[2:]
    return bits[step], swapped[step]


def own_bit(step):
    first, second = dp_bits(step)
    place = lax.axis_index("dp").astype(jnp.int32)
    core = lax.axis_index("tensor") % 2
    return jnp.where(core == 0, (place // first) % 2, (place // second) % 2)


def dp_pairs(step):
    ranks = lax.axis_size("tensor")
    pairs = dp_bits(step)
    return [
        (at * ranks + rank, (at ^ pairs[rank % 2]) * ranks + rank)
        for at in range(lax.axis_size("dp"))
        for rank in range(ranks)
    ]


def in_order(which, own, got):
    place = lax.broadcasted_iota(jnp.int32, (2, 1, 1), 0)
    return jnp.where(place == which, own[None], got[None])


def sum_steps(sent, kept, rider=None):
    axes = ("dp", "tensor")
    steps = range(1, len(axis_bits("dp")))
    terms = [kept]
    got = yield sent, axes, dp_pairs(0)

    def total(which):
        return sum(half_of(term, which).astype(F32) for term in terms)

    for step in steps:
        which = own_bit(step)
        terms.append(got)
        sent = total(1 - which).astype(BF16)
        terms = [half_of(term, which) for term in terms]
        got = yield sent, axes, dp_pairs(step)
    part = sum((term.astype(F32) for term in terms), got.astype(F32)).astype(BF16)
    extra = None
    for step in reversed((0, *steps)):
        if step == 1 and rider is not None:
            extra = rider().astype(BF16)
        rows = part.shape[0]
        got = yield part if extra is None else jnp.concatenate([part, extra]), axes, dp_pairs(step)
        if extra is not None:
            extra = (extra.astype(F32) + got[rows:].astype(F32)).astype(BF16)
        if step:
            part = in_order(own_bit(step), part, got[:rows]).reshape(2 * rows, -1)
    return own_bit(0), part, got, extra


def rest_steps(rows):
    axes = ("dp", "tensor")
    for step in range(2, len(axis_bits("dp"))):
        got = yield rows, axes, dp_pairs(step)
        total = rows.astype(F32) + got.astype(F32)
        last, rows = (rows, got), total.astype(BF16)
    return last


def both_steps(sent, kept):
    size = lax.axis_size("tensor")
    rank = lax.axis_index("tensor")
    got = yield sent, "tensor", [(i, i ^ 1) for i in range(size)]
    for bit in axis_bits("tensor")[1:]:
        sent, kept = run_split(kept, got, (rank // bit) % 2)
        got = yield sent, "tensor", [(i, i ^ bit) for i in range(size)]
    return kept, got


def small_steps(sent, kept, own):
    size = lax.axis_size("tensor")
    rank = lax.axis_index("tensor")
    got = yield sent, "tensor", [(i, i ^ 1) for i in range(size)]
    total = kept.astype(F32) + got.astype(F32)
    for bit in axis_bits("tensor")[1:]:
        which = (rank // bit) % 2
        shared = total[-16:].astype(BF16)
        rows = total[:-16]
        got = yield jnp.concatenate([half_of(rows, 1 - which).astype(BF16), shared]), "tensor", [
            (i, i ^ bit) for i in range(size)
        ]
        total = jnp.concatenate([half_of(rows, which), shared.astype(F32)]) + got.astype(F32)
    return jnp.concatenate([total, own])


class Order:
    def __init__(self, last):
        self.last = last
        self.waiting = {}
        self.flying = {}
        self.results = {}

    def advance(self, name, steps, got):
        try:
            request = steps.send(got)
            self.waiting[name] = (steps, request)
            self.last = request[0]
        except StopIteration as end:
            self.results[name] = end.value

    def add(self, name, steps):
        last = self.last
        self.advance(name, steps, None)
        self.last = last

    def go(self, *names):
        for name in names:
            if name in self.waiting:
                steps, (sent, axis, moves) = self.waiting.pop(name)
                self.flying[name] = (steps, lax.ppermute(sent, axis, moves))

    def land(self, *names):
        found = [(name, *self.flying.pop(name)) for name in names if name in self.flying]
        if found:
            passed = run_pass([got for _, _, got in found], self.last)
            self.last = passed[0]
            for at, ((name, steps, _), got) in enumerate(zip(found, passed)):
                self.advance(name, steps, self.hold(got) if at else got)
                if name in self.waiting:
                    self.last = self.waiting[name][1][0]

    def hold(self, array):
        return run_pass([array], self.last)[0]

    def step(self, *names):
        for name in names:
            self.land(name)
            self.go(name)

    def result(self, name):
        while name not in self.results:
            self.go(name)
            self.land(name)
        return self.results[name]


def shards(
    hidden_in,
    pre_gain,
    w_gate,
    w_value,
    w_bc,
    w_dt,
    conv_x,
    conv_x_bias,
    conv_bc,
    conv_bc_bias,
    dt_bias,
    a_log,
    d_skip,
    gate_gain,
    w_out,
    cotangent,
    segments,
):
    row_count, width = hidden_in.shape
    channels = w_gate.shape[1]
    head_count = dt_bias.shape[0]
    head_width = channels // head_count
    ranks = lax.axis_size("tensor")
    my_rank = lax.axis_index("tensor")
    own_rows = row_count // ranks
    row_start = my_rank * own_rows
    pair_width = w_bc.shape[1] // ranks
    low = jnp.reshape(own_bit(0), (1,))
    w_dt_rows = w_dt.T
    tokens, rows_table, head_values = run_tables(
        segments, pre_gain, conv_x_bias, gate_gain, conv_bc_bias, dt_bias, a_log, d_skip
    )
    (
        normed,
        mixed,
        act,
        turn,
        gated_grad,
        scan,
        values,
        slope,
        inner_pre,
        step_in,
        cum,
        bc_low,
        bc_slope,
        state_pre,
        enter,
        sums,
    ) = run_forward(
        hidden_in,
        cotangent,
        (w_gate, w_value, w_bc, w_dt_rows, w_out),
        (conv_x, conv_bc, rows_table, head_values),
        tokens,
    )
    sums = sum_tensor(sums) / (channels * ranks)
    (gated, gate_low, dscan, gain_rows), halves = run_gate(
        low, (mixed, act, turn, gated_grad), sums, rows_table, cotangent, normed
    )
    order = Order(gate_low)
    order.add("first", sum_steps(*halves, lambda: order.result("small")))
    order.go("first")
    (
        state_low,
        inner_low,
        step_low,
        channel_grads,
        conv_bc_grads,
        head_grads,
        step_rows,
        bc_rows,
    ) = run_backward(
        (dscan, scan, values, slope, inner_pre),
        step_in,
        cum,
        bc_low,
        enter,
        normed,
        (bc_slope, state_pre),
        (conv_x, conv_bc, head_values, tokens),
        halves[0],
        head_count,
    )
    order.last = inner_low
    order.step("first")
    sent, kept = run_weight(low, normed, inner_low, order.last)
    order.last = kept
    order.step("first")
    order.add("second", sum_steps(order.hold(sent), kept))
    order.go("second")
    core = jnp.reshape((my_rank % 2).astype(jnp.int32), (1,))
    both_sent, both_kept, gain = run_merge(
        core,
        (gate_low, inner_low, step_low, state_low, gated, normed),
        (w_gate, w_value, w_dt_rows, w_bc, w_out),
        rows_table,
        order.last,
        ranks,
    )
    order.last = both_kept
    order.land("second", "first")
    order.go("second", "first")
    small = run_pack(
        core, bc_rows, step_rows, channel_grads, gain_rows, order.hold(gain), conv_bc_grads, head_grads, head_count
    )
    order.add("small", small_steps(*small))
    order.go("small")
    order.add("both", both_steps(order.hold(both_sent), both_kept))
    order.go("both")
    order.step("small")
    order.land("small")
    order.land("second", "first")
    order.go("second", "first")
    order.step("both")
    order.step("second")
    order.land("second")
    order.land("first")
    order.go("second", "first")
    order.step("second")
    which, own, got, rows = order.result("first")
    order.add("rest", rest_steps(rows))
    order.go("rest")
    w_out_sum, w_gate_sum = run_finish_pair(which, own, got, order.last, w_out.shape)
    order.last = w_out_sum
    order.step("second")
    kept, got = order.result("both")
    block_out, hidden_grad = run_hidden(
        jnp.reshape(my_rank.astype(jnp.int32), (1,)), hidden_in, cotangent, kept, got, rows_table
    )
    order.last = hidden_grad
    one, two = order.result("rest")
    small = run_unpack(one, two, width, w_bc.shape[1], head_count)
    order.last = small[0]
    which, own, got, _ = order.result("second")
    w_value_sum = run_finish(which, own, got, order.last)
    (
        pre_gain_grad,
        w_bc_rows,
        dt_rows,
        conv_x_grad,
        conv_x_bias_grad,
        conv_bc_grad,
        conv_bc_bias_grad,
        dt_bias_grad,
        a_log_grad,
        d_skip_grad,
        gate_gain_grad,
    ) = small
    return (
        block_out,
        hidden_grad,
        pre_gain_grad,
        w_gate_sum,
        w_value_sum,
        w_bc_rows.T,
        dt_rows.T,
        conv_x_grad,
        conv_x_bias_grad,
        conv_bc_grad,
        conv_bc_bias_grad,
        dt_bias_grad,
        a_log_grad,
        d_skip_grad,
        gate_gain_grad,
        w_out_sum,
    )


def solution(mesh):
    in_specs = (
        P("dp", None),
        P(),
        P(None, "tensor"),
        P(None, "tensor"),
        P(),
        P(None, "tensor"),
        P(None, "tensor"),
        P("tensor"),
        P(),
        P(),
        P("tensor"),
        P("tensor"),
        P("tensor"),
        P("tensor"),
        P("tensor", None),
        P("dp", None),
        P("dp", None),
    )
    out_specs = (
        P(("dp", "tensor"), None),
        P(("dp", "tensor"), None),
        P(),
        P(None, "tensor"),
        P(None, "tensor"),
        P(None, "tensor"),
        P(None, "tensor"),
        P(None, "tensor"),
        P("tensor"),
        P(),
        P(),
        P("tensor"),
        P("tensor"),
        P("tensor"),
        P("tensor"),
        P("tensor", None),
    )
    return jax.shard_map(shards, mesh=mesh, in_specs=in_specs, out_specs=out_specs, check_vma=False)
```

```python
import functools
import math

import jax
import jax.numpy as jnp
from jax import lax
from jax.experimental import pallas as pl
from jax.experimental.pallas import tpu as pltpu
from jax.sharding import PartitionSpec as P

STATE = 128
CONV = 4
BLOCK = 256
PIECE = 128
OWN_BC = 64
LANES = 128
EPS = 1e-05
HIGH = lax.Precision.HIGHEST
LOG2E = math.log2(math.e)
BF16 = jnp.bfloat16
F32 = jnp.float32


def dot(left, right):
    return jnp.dot(left, right, preferred_element_type=F32)


def dot_last(left, right):
    return lax.dot_general(left, right, (((1,), (1,)), ((), ())), preferred_element_type=F32)


def dot_first(left, right):
    return lax.dot_general(left, right, (((0,), (0,)), ((), ())), preferred_element_type=F32)


def two_terms(array):
    upper = array.astype(BF16)
    return upper, (array - upper.astype(F32)).astype(BF16)


def sigmoid(array):
    return 0.5 * jnp.tanh(0.5 * array) + 0.5


def spread_heads(array, heads_twice):
    upper, rest = two_terms(array)
    return dot(jnp.concatenate([upper, rest], axis=1), heads_twice)


def sum_heads(array, heads):
    upper, rest = two_terms(array)
    return dot_last(upper, heads) + dot_last(rest, heads)


def head_table(channels, head_count):
    head_width = channels // head_count
    channel = lax.broadcasted_iota(jnp.int32, (LANES, channels), 1)
    head = lax.broadcasted_iota(jnp.int32, (LANES, channels), 0)
    first = head * head_width
    return ((channel >= first) & (channel < first + head_width)).astype(F32).astype(BF16)


def head_rows(head_ref, heads):
    upper, rest = two_terms(head_ref[...])
    return dot(upper, heads) + dot(rest, heads)


def table_kernel(
    segment_ref,
    pre_gain_ref,
    bias_x_ref,
    gate_gain_ref,
    bias_bc_ref,
    dt_bias_ref,
    a_log_ref,
    d_skip_ref,
    token_ref,
    row_ref,
    head_ref,
):
    seq_count, length = segment_ref.shape
    place = lax.broadcasted_iota(jnp.int32, (8, length), 1)
    at_row = lax.broadcasted_iota(jnp.int32, (8, length), 0)
    for seq in range(seq_count):
        documents = jnp.broadcast_to(segment_ref[seq : seq + 1, :], (8, length)).astype(F32)
        padded = jnp.where(at_row == 0, documents, 0.0)

        def moved(by):
            other = pltpu.roll(documents, by % length, 1)
            return other, (place >= by) & (place < length + by)

        for k in range(1, CONV):
            before, inside = moved(k)
            padded = jnp.where((at_row == k) & inside & (before == documents), 1.0, padded)
        ends = []
        for piece in range(length // PIECE):
            here = slice(piece * PIECE, (piece + 1) * PIECE)
            ends.append(jnp.broadcast_to(documents[:, (piece + 1) * PIECE - 1 : (piece + 1) * PIECE], (8, PIECE)))
        starts = [jnp.full((8, PIECE), -1.0, F32)] + ends[:-1]
        padded = jnp.where((at_row == 4) & (jnp.concatenate(starts, axis=1) == documents), 1.0, padded)
        padded = jnp.where((at_row == 5) & (jnp.concatenate(ends, axis=1) == documents), 1.0, padded)
        lower = jnp.zeros((8, length), F32)
        for k in range(1, CONV):
            after, inside = moved(-k)
            hit = inside & (after == documents)
            if 5 + k < 8:
                padded = jnp.where((at_row == 5 + k) & hit, 1.0, padded)
            else:
                lower = jnp.where((at_row == 5 + k - 8) & hit, 1.0, lower)
        columns = slice(seq * length, (seq + 1) * length)
        token_ref[0:8, columns] = padded + jnp.where(at_row == 0, 64.0 * seq, 0.0)
        token_ref[8:16, columns] = lower
    row_ref[...] = jnp.zeros(row_ref.shape, F32)
    for at, ref in enumerate((pre_gain_ref, bias_x_ref, gate_gain_ref, bias_bc_ref)):
        row_ref[at : at + 1, 0 : ref.shape[0]] = ref[...].reshape(1, -1)
    head_ref[...] = jnp.zeros(head_ref.shape, F32)
    count = dt_bias_ref.shape[0]
    head_ref[0:1, 0:count] = dt_bias_ref[...].reshape(1, -1)
    head_ref[1:2, 0:count] = -jnp.exp(a_log_ref[...].reshape(1, -1))
    head_ref[2:3, 0:count] = d_skip_ref[...].reshape(1, -1)


def forward_kernel(
    hidden_ref,
    cotan_ref,
    w_gate_ref,
    w_value_ref,
    w_bc_ref,
    w_dt_ref,
    w_out_ref,
    conv_x_ref,
    conv_bc_ref,
    row_ref,
    head_ref,
    token_ref,
    normed_ref,
    mixed_ref,
    act_ref,
    turn_ref,
    grad_ref,
    scan_ref,
    value_ref,
    slope_ref,
    inner_ref,
    step_ref,
    cum_ref,
    bc_ref,
    bc_slope_ref,
    state_ref,
    enter_ref,
    sums_ref,
    tail_x,
    tail_bc,
    carried,
    wide_dt,
    gate_all,
    grad_all,
    tailed,
):
    block = pl.program_id(0)

    @pl.when(block == 0)
    def _():
        tail_x[0:8, :] = jnp.zeros((8, tail_x.shape[1]), F32)
        tail_bc[0:8, :] = jnp.zeros((8, tail_bc.shape[1]), F32)
        carried[...] = jnp.zeros(carried.shape, F32)
        wide_dt[...] = jnp.zeros(wide_dt.shape, BF16)
        wide_dt[0 : w_dt_ref.shape[0], :] = w_dt_ref[...]

    channels = tail_x.shape[1]
    heads = head_table(channels, w_dt_ref.shape[0])
    skips = head_rows(head_ref, heads)[2:3, :]
    side = token_ref[...].T
    hidden = hidden_ref[...].astype(F32)
    inv_rms = lax.rsqrt(jnp.mean(hidden * hidden, axis=-1, keepdims=True) + EPS)
    normed = (hidden * inv_rms * row_ref[0:1, :]).astype(BF16)
    normed_ref[...] = normed
    tail_x[8:, :] = dot(normed, w_value_ref[...])
    tail_bc[8:, :] = dot(normed, w_bc_ref[...])
    step_in = dot_last(normed, wide_dt[...]) + head_ref[0:1, :]
    step_ref[...] = step_in
    step = jnp.maximum(step_in, 0.0) + jnp.log1p(jnp.exp(-jnp.abs(step_in)))
    rate = head_ref[1:2, :] * step * LOG2E
    gate_all[...] = dot(normed, w_gate_ref[...])
    grad_all[...] = dot_last(cotan_ref[...], w_out_ref[...])
    masks = [None] + [side[:, k : k + 1] for k in range(1, CONV)]

    def conv(tail, taps_ref, bias_at, lanes):
        result = row_ref[bias_at : bias_at + 1, lanes] + taps_ref[CONV - 1 : CONV, lanes] * tail[8:, lanes]
        for k in range(1, CONV):
            shifted = tail[8 - k : 8 - k + BLOCK, lanes]
            result = result + taps_ref[CONV - 1 - k : CONV - k, lanes] * shifted * masks[k]
        return result

    for at in range(0, channels, LANES):
        lanes = slice(at, at + LANES)
        before = conv(tail_x, conv_x_ref, 1, lanes)
        half = sigmoid(before)
        value_ref[:, lanes] = (before * half).astype(BF16)
        slope_ref[:, lanes] = (half * (1.0 + before * (1.0 - half))).astype(BF16)
        inner_ref[:, lanes] = tail_x[8:, lanes].astype(BF16)
    for at in range(0, 2 * STATE, LANES):
        lanes = slice(at, at + LANES)
        before = conv(tail_bc, conv_bc_ref, 3, lanes)
        half = sigmoid(before)
        bc_ref[:, lanes] = (before * half).astype(BF16)
        bc_slope_ref[:, lanes] = half * (1.0 + before * (1.0 - half))
        state_ref[:, lanes] = tail_bc[8:, lanes]
    tail_x[0:8, :] = tail_x[BLOCK:, :]
    tail_bc[0:8, :] = tail_bc[BLOCK:, :]

    row_at = lax.broadcasted_iota(jnp.int32, (PIECE, PIECE), 0)
    col_at = lax.broadcasted_iota(jnp.int32, (PIECE, PIECE), 1)
    lower = (row_at >= col_at).astype(F32)
    first_half = lax.broadcasted_iota(jnp.int32, (PIECE, LANES), 1) < LANES // 2
    heads_twice = jnp.concatenate([heads, heads], axis=0)
    for piece in range(BLOCK // PIECE):
        rows = slice(piece * PIECE, (piece + 1) * PIECE)
        cum = jnp.dot(lower, rate[rows], precision=HIGH, preferred_element_type=F32)
        cum_ref[rows, :] = cum
        cum_t = cum.T
        same = (side[rows, 0:1] == token_ref[0:1, rows]) & (row_at >= col_at)
        bias = jnp.where(same, 0.0, -1e30)
        reach = jnp.exp2(cum) * side[rows, 4:5]
        tail = jnp.exp2(cum[PIECE - 1 : PIECE, :] - cum) * side[rows, 5:6]
        wide = spread_heads(jnp.concatenate([step[rows], reach, tail], axis=0), heads_twice)
        b_low = bc_ref[rows, 0:STATE]
        c_low = bc_ref[rows, STATE : 2 * STATE]
        scores = dot_last(c_low, b_low)
        enter = carried[...].astype(BF16)
        enter_ref[piece] = enter
        from_state = dot(c_low, enter)
        for pair in range(channels // LANES):
            lanes = slice(pair * LANES, (pair + 1) * LANES)
            values = value_ref[rows, lanes].astype(F32)
            scaled = wide[0:PIECE, lanes] * values
            low = scaled.astype(BF16)
            weights = []
            for head in (2 * pair, 2 * pair + 1):
                gaps = (cum[:, head : head + 1] - cum_t[head : head + 1, :]) + bias
                weights.append((scores * jnp.exp2(gaps)).astype(BF16))
            zero = jnp.zeros_like(low)
            both = jnp.concatenate(
                [jnp.where(first_half, low, zero), jnp.where(first_half, zero, low)], axis=0
            )
            out = dot(jnp.concatenate(weights, axis=1), both)
            out = out + from_state[:, lanes] * wide[PIECE : 2 * PIECE, lanes]
            scan_ref[rows, lanes] = out + skips[:, lanes] * values
            tailed[:, lanes] = (wide[2 * PIECE :, lanes] * scaled).astype(BF16)
        kept = wide[2 * PIECE - 1 : 2 * PIECE, :]
        carried[...] = kept * carried[...] + dot_first(b_low, tailed[...])

    ones = jnp.ones((8, LANES), BF16)
    square_part = jnp.zeros((BLOCK, LANES), F32)
    cross_part = jnp.zeros((BLOCK, LANES), F32)
    for at in range(0, channels, LANES):
        lanes = slice(at, at + LANES)
        gate = gate_all[:, lanes]
        scan = scan_ref[:, lanes]
        grad = grad_all[:, lanes]
        half = sigmoid(gate)
        act = gate * half
        mixed = scan * act
        mixed_ref[:, lanes] = mixed.astype(BF16)
        act_ref[:, lanes] = act.astype(BF16)
        turn_ref[:, lanes] = (scan * (half * (1.0 + gate * (1.0 - half)))).astype(BF16)
        grad_ref[:, lanes] = grad.astype(BF16)
        square_part = square_part + mixed * mixed
        cross_part = cross_part + mixed * (grad * row_ref[2:3, lanes])
    upper, rest = two_terms(square_part)
    squares = dot_last(ones, upper) + dot_last(ones, rest)
    upper, rest = two_terms(cross_part)
    crosses = dot_last(ones, upper) + dot_last(ones, rest)
    is_first = lax.broadcasted_iota(jnp.int32, (8, BLOCK), 0) == 0
    sums_ref[...] = jnp.where(is_first, squares, crosses)


def store_halves(total, columns, mine, sent_ref, kept_ref, at=0):
    half = total.shape[0] // 2
    to = slice(at, at + half)
    for which, ref in ((1 - mine, sent_ref), (mine, kept_ref)):
        ref[to, :] = total[pl.ds(pl.multiple_of(which * half, 8), half), columns].astype(BF16)


def gate_columns(sums_ref):
    row_at = lax.broadcasted_iota(jnp.int32, (8, LANES), 0)

    def column(which):
        pick = (row_at == which).astype(F32)
        return lax.dot_general(
            sums_ref[...], pick, (((0,), (0,)), ((), ())), precision=HIGH, preferred_element_type=F32
        )

    inv_gate = lax.rsqrt(column(0) + EPS)
    return inv_gate, inv_gate * inv_gate * column(1)


def gate_kernel(
    low_ref,
    mixed_ref,
    turn_ref,
    grad_ref,
    sums_ref,
    row_ref,
    cotan_ref,
    normed_ref,
    gate_low_ref,
    gain_ref,
    sent_ref,
    kept_ref,
    gated,
    out_total,
    gate_total,
):
    block = pl.program_id(0)

    @pl.when(block == 0)
    def _():
        gain_ref[...] = jnp.zeros(gain_ref.shape, F32)
        out_total[...] = jnp.zeros(out_total.shape, F32)
        gate_total[...] = jnp.zeros(gate_total.shape, F32)

    channels = mixed_ref.shape[1]
    inv_gate, pull = gate_columns(sums_ref)
    for at in range(0, channels, LANES):
        lanes = slice(at, at + LANES)
        mixed = mixed_ref[:, lanes].astype(F32)
        grad = grad_ref[:, lanes].astype(F32)
        gain = row_ref[2:3, lanes]
        normal = mixed * inv_gate
        gated[:, lanes] = (normal * gain).astype(BF16)
        gain_ref[:, lanes] += jnp.sum((grad * normal).reshape(-1, 8, LANES), axis=0)
        mixed_grad = inv_gate * (grad * gain - mixed * pull)
        gate_low_ref[:, lanes] = (mixed_grad * turn_ref[:, lanes].astype(F32)).astype(BF16)
    out_total[...] += dot_first(gated[...], cotan_ref[...])
    gate_total[...] += dot_first(normed_ref[...], gate_low_ref[...])

    @pl.when(block == pl.num_programs(0) - 1)
    def _():
        rows, width = out_total.shape
        for at in range(width // channels):
            columns = slice(at * channels, (at + 1) * channels)
            store_halves(out_total, columns, low_ref[0], sent_ref, kept_ref, at * rows // 2)
        store_halves(gate_total, slice(None), low_ref[0], sent_ref, kept_ref, width // 2)


def weight_kernel(low_ref, normed_ref, grad_ref, after_ref, sent_ref, kept_ref, total):
    block = pl.program_id(0)
    part = dot_first(normed_ref[...], grad_ref[...])

    @pl.when(block == 0)
    def _():
        total[...] = part

    @pl.when(block > 0)
    def _():
        total[...] += part

    @pl.when(block == pl.num_programs(0) - 1)
    def _():
        store_halves(total, slice(None), low_ref[0], sent_ref, kept_ref)


def backward_kernel(
    head_count,
    mixed_ref,
    grad_ref,
    act_ref,
    sums_ref,
    row_ref,
    scan_ref,
    value_ref,
    slope_ref,
    inner_ref,
    step_ref,
    cum_ref,
    bc_ref,
    enter_ref,
    normed_ref,
    bc_slope_ref,
    state_ref,
    conv_x_ref,
    conv_bc_ref,
    head_ref,
    token_ref,
    after_ref,
    state_low_ref,
    inner_low_ref,
    step_low_ref,
    channel_grad_ref,
    conv_bc_grad_ref,
    head_grad_ref,
    step_rows_ref,
    bc_rows_ref,
    later,
    later_bc,
    leaving,
    step_total,
    dys,
    lows,
    reached,
    tailed,
    products,
):
    block = pl.program_id(0)

    @pl.when(block == 0)
    def _():
        later[PIECE:, :] = jnp.zeros((8, later.shape[1]), F32)
        later_bc[PIECE:, :] = jnp.zeros((8, later_bc.shape[1]), F32)
        conv_bc_grad_ref[...] = jnp.zeros(conv_bc_grad_ref.shape, F32)
        bc_rows_ref[...] = jnp.zeros(bc_rows_ref.shape, F32)
        leaving[...] = jnp.zeros(leaving.shape, F32)
        channel_grad_ref[...] = jnp.zeros(channel_grad_ref.shape, F32)
        head_grad_ref[...] = jnp.zeros(head_grad_ref.shape, F32)
        step_total[...] = jnp.zeros(step_total.shape, F32)

    channels = inner_ref.shape[1]
    row_at = lax.broadcasted_iota(jnp.int32, (PIECE, PIECE), 0)
    col_at = lax.broadcasted_iota(jnp.int32, (PIECE, PIECE), 1)
    upper_ones = (row_at <= col_at).astype(F32)
    first_half = lax.broadcasted_iota(jnp.int32, (PIECE, LANES), 1) < LANES // 2
    heads = head_table(channels, head_count)
    skips = head_rows(head_ref, heads)[2:3, :]
    side_all = token_ref[...].T
    inv_gate, pull = gate_columns(sums_ref)
    heads_twice = jnp.concatenate([heads, heads], axis=0)
    for piece in reversed(range(BLOCK // PIECE)):
        rows = slice(piece * PIECE, (piece + 1) * PIECE)
        side = side_all[rows]
        step_in = step_ref[rows, :]
        step = jnp.maximum(step_in, 0.0) + jnp.log1p(jnp.exp(-jnp.abs(step_in)))
        cum = cum_ref[rows, :]
        cum_t = cum.T
        same = (side[:, 0:1] == token_ref[0:1, rows]) & (row_at <= col_at)
        bias = jnp.where(same, 0.0, -1e30)
        reach = jnp.exp2(cum) * side[:, 4:5]
        tail = jnp.exp2(cum[PIECE - 1 : PIECE, :] - cum) * side[:, 5:6]
        wide = spread_heads(jnp.concatenate([step, reach, tail], axis=0), heads_twice)
        b_low = bc_ref[rows, 0:STATE]
        c_low = bc_ref[rows, STATE : 2 * STATE]
        scores = dot_last(b_low, c_low)
        score_grad = jnp.zeros((PIECE, PIECE), F32)
        masks = [None] + [side[:, 5 + k : 6 + k] for k in range(1, CONV)]
        for at in range(0, channels, LANES):
            lanes = slice(at, at + LANES)
            mixed = mixed_ref[rows, lanes].astype(F32)
            grad = grad_ref[rows, lanes].astype(F32)
            mixed_grad = inv_gate[rows] * (grad * row_ref[2:3, lanes] - mixed * pull[rows])
            dy_low = (mixed_grad * act_ref[rows, lanes].astype(F32)).astype(BF16)
            dys[:, lanes] = dy_low
            dy = dy_low.astype(F32)
            low = (wide[0:PIECE, lanes] * value_ref[rows, lanes].astype(F32)).astype(BF16)
            lows[:, lanes] = low
            reached[:, lanes] = (wide[PIECE : 2 * PIECE, lanes] * dy).astype(BF16)
            tailed[:, lanes] = (wide[2 * PIECE :, lanes] * low.astype(F32)).astype(BF16)
        leave = leaving[...]
        leave_low = leave.astype(BF16)
        enter_low = enter_ref[piece]
        kept = wide[2 * PIECE - 1 : 2 * PIECE, :]
        c_grad = dot_last(reached[...], enter_low)
        b_grad = dot_last(tailed[...], leave_low)
        from_states = dot(b_low, leave_low)
        kept_sum = kept * jnp.sum(enter_low.astype(F32) * leave, axis=0, keepdims=True)
        leaving[...] = kept * leave + dot_first(c_low, reached[...])
        for pair in range(channels // LANES):
            lanes = slice(pair * LANES, (pair + 1) * LANES)
            values = value_ref[rows, lanes].astype(F32)
            dy_low = dys[:, lanes]
            dy = dy_low.astype(F32)
            wide_step = wide[0:PIECE, lanes]
            low = lows[:, lanes]
            low_wide = low.astype(F32)
            from_state = wide[2 * PIECE :, lanes] * from_states[:, lanes]
            zero = jnp.zeros_like(low)
            own = jnp.concatenate(
                [jnp.where(first_half, dy_low, zero), jnp.where(first_half, zero, dy_low)], axis=0
            )
            weight_grads = dot_last(low, own)
            weights = []
            for at, head in enumerate((2 * pair, 2 * pair + 1)):
                gaps = (cum_t[head : head + 1, :] - cum[:, head : head + 1]) + bias
                decay = jnp.exp2(gaps)
                weights.append((scores * decay).astype(BF16))
                score_grad = score_grad + weight_grads[:, at * PIECE : (at + 1) * PIECE] * decay
            dx = dot(jnp.concatenate(weights, axis=1), own)
            dx = dx + from_state
            out = scan_ref[rows, lanes] - skips[:, lanes] * values
            last = jnp.sum(low_wide * from_state, axis=0, keepdims=True) + kept_sum[:, lanes]
            for at, product in enumerate(
                (dy * out - low_wide * dx, values * dx, jnp.broadcast_to(last, (16, LANES)))
            ):
                upper, rest = two_terms(product)
                products[2 * at * PIECE : 2 * at * PIECE + upper.shape[0], lanes] = upper
                products[2 * at * PIECE + upper.shape[0] : 2 * (at * PIECE + upper.shape[0]), lanes] = rest
            dvalue = wide_step * dx + skips[:, lanes] * dy
            dbefore = dvalue * slope_ref[rows, lanes].astype(F32)
            later[0:PIECE, lanes] = dbefore
            inner = inner_ref[rows, lanes].astype(F32)
            inner_grad = conv_x_ref[CONV - 1 : CONV, lanes] * dbefore
            channel_grad_ref[CONV - 1 : CONV, lanes] += jnp.sum(inner * dbefore, axis=0, keepdims=True)
            channel_grad_ref[CONV : CONV + 1, lanes] += jnp.sum(dbefore, axis=0, keepdims=True)
            channel_grad_ref[CONV + 1 : CONV + 2, lanes] += jnp.sum(dy * values, axis=0, keepdims=True)
            for k in range(1, CONV):
                shifted = later[k : k + PIECE, lanes] * masks[k]
                inner_grad = inner_grad + conv_x_ref[CONV - 1 - k : CONV - k, lanes] * shifted
                channel_grad_ref[CONV - 1 - k : CONV - k, lanes] += jnp.sum(
                    inner * shifted, axis=0, keepdims=True
                )
            inner_low_ref[rows, lanes] = inner_grad.astype(BF16)
        sums = dot_last(products[...], heads)
        row_sum = sums[0:PIECE] + sums[PIECE : 2 * PIECE]
        value_sum = sums[2 * PIECE : 3 * PIECE] + sums[3 * PIECE : 4 * PIECE]
        last_sum = sums[4 * PIECE : 4 * PIECE + 16] + sums[4 * PIECE + 16 : 4 * PIECE + 32]
        later[PIECE:, :] = later[0:8, :]
        grad_low = score_grad.astype(BF16)
        state_parts = (b_grad + dot(grad_low, c_low), c_grad + dot_first(grad_low, b_low))
        for at, state_part in enumerate(state_parts):
            lanes = slice(at * STATE, (at + 1) * STATE)
            dbefore = state_part * bc_slope_ref[rows, lanes]
            later_bc[0:PIECE, lanes] = dbefore
            state = state_ref[rows, lanes]
            state_grad = conv_bc_ref[CONV - 1 : CONV, lanes] * dbefore
            conv_bc_grad_ref[CONV - 1 : CONV, lanes] += jnp.sum(state * dbefore, axis=0, keepdims=True)
            conv_bc_grad_ref[CONV : CONV + 1, lanes] += jnp.sum(dbefore, axis=0, keepdims=True)
            for k in range(1, CONV):
                shifted = later_bc[k : k + PIECE, lanes] * masks[k]
                state_grad = state_grad + conv_bc_ref[CONV - 1 - k : CONV - k, lanes] * shifted
                conv_bc_grad_ref[CONV - 1 - k : CONV - k, lanes] += jnp.sum(
                    state * shifted, axis=0, keepdims=True
                )
            state_low_ref[rows, lanes] = state_grad.astype(BF16)
        later_bc[PIECE:, :] = later_bc[0:8, :]
        rate_grad = (
            jnp.dot(upper_ones, row_sum, precision=HIGH, preferred_element_type=F32) + last_sum[0:1, :]
        )
        coefficient = head_ref[1:2, :]
        step_grad = (value_sum + coefficient * rate_grad) / (1.0 + jnp.exp(-step_in))
        step_low_ref[rows, :] = step_grad.astype(BF16)
        head_grad_ref[0:1, :] += jnp.sum(step_grad, axis=0, keepdims=True)
        head_grad_ref[1:2, :] += jnp.sum(rate_grad * step, axis=0, keepdims=True) * coefficient
    step_total[...] += dot_first(step_low_ref[...], normed_ref[...])
    bc_rows_ref[...] += dot_first(state_low_ref[...], normed_ref[...])

    @pl.when(block == pl.num_programs(0) - 1)
    def _():
        step_rows_ref[...] = step_total[0 : step_rows_ref.shape[0], :]


def merge_kernel(
    core_ref,
    gate_low_ref,
    inner_low_ref,
    step_low_ref,
    state_low_ref,
    mixed_ref,
    normed_ref,
    sums_ref,
    w_gate_ref,
    w_value_ref,
    w_dt_ref,
    w_bc_ref,
    w_out_ref,
    row_ref,
    after_ref,
    sent_ref,
    kept_ref,
    gain_ref,
    wide_dt,
    gated,
):
    block = pl.program_id(0)
    last = pl.num_programs(0) - 1

    @pl.when(block == 0)
    def _():
        gain_ref[...] = jnp.zeros(gain_ref.shape, F32)
        wide_dt[...] = jnp.zeros(wide_dt.shape, BF16)
        wide_dt[0 : w_dt_ref.shape[0], :] = w_dt_ref[...]

    width = normed_ref.shape[1]
    total = dot_last(inner_low_ref[...], w_value_ref[...]) + dot_last(gate_low_ref[...], w_gate_ref[...])
    total = total + dot_last(state_low_ref[...], w_bc_ref[...]) + dot(step_low_ref[...], wide_dt[...])
    gain_ref[...] += jnp.sum((total * normed_ref[...].astype(F32)).reshape(-1, 8, width), axis=0)
    inv_gate, _ = gate_columns(sums_ref)
    for at in range(0, mixed_ref.shape[1], LANES):
        lanes = slice(at, at + LANES)
        normal = mixed_ref[:, lanes].astype(F32) * inv_gate
        gated[:, lanes] = (normal * row_ref[2:3, lanes]).astype(BF16)
    branch = dot(gated[...], w_out_ref[...]).astype(BF16)

    @pl.when(2 * block < last)
    def _():
        sent_ref[:, 0:width] = total.astype(BF16)
        sent_ref[:, width:] = branch

    @pl.when(2 * block > last)
    def _():
        kept_ref[:, 0:width] = total.astype(BF16)
        kept_ref[:, width:] = branch

    @pl.when(block == last)
    def _():
        gain = jnp.sum(gain_ref[...], axis=0, keepdims=True) / row_ref[0:1, :]
        gain_ref[...] = jnp.broadcast_to(gain, gain_ref.shape)


def pack_kernel(
    head_count,
    core_ref,
    bc_rows_ref,
    step_rows_ref,
    channel_ref,
    gate_gain_ref,
    gain_ref,
    conv_bc_ref,
    head_ref,
    sent_ref,
    kept_ref,
    own_ref,
):
    core = core_ref[0]
    channels = channel_ref.shape[1]
    states, width = bc_rows_ref.shape
    folds = width // channels
    groups = (kept_ref.shape[0] - 16) // (OWN_BC * folds)
    for which, ref in ((1 - core, sent_ref), (core, kept_ref)):
        for group in range(groups):
            found = bc_rows_ref[pl.ds(pl.multiple_of((2 * group + which) * OWN_BC, 8), OWN_BC), :].astype(BF16)
            for fold in range(folds):
                at = (group * folds + fold) * OWN_BC
                ref[at : at + OWN_BC, :] = found[:, fold * channels : (fold + 1) * channels]
        shared = [gain_ref[0:1, fold * channels : (fold + 1) * channels] for fold in range(folds)]
        conv = conv_bc_ref[0 : CONV + 1, :]
        shared.append(jnp.concatenate([conv, jnp.zeros((CONV + 1, channels - states), F32)], axis=1))
        shared.append(jnp.zeros((16 - folds - CONV - 1, channels), F32))
        ref[ref.shape[0] - 16 :, :] = jnp.concatenate(shared).astype(BF16)
    own_ref[...] = jnp.zeros(own_ref.shape, F32)
    for fold in range(folds):
        own_ref[16 * fold : 16 * fold + 16, :] = step_rows_ref[:, fold * channels : (fold + 1) * channels]
    at = 16 * folds
    own_ref[at : at + CONV + 1, :] = channel_ref[0 : CONV + 1, :]
    own_ref[at + CONV + 1 : at + CONV + 2, :] = jnp.sum(gate_gain_ref[...], axis=0, keepdims=True)
    skips = sum_heads(channel_ref[...], head_table(channels, head_count))
    own_ref[at + CONV + 2 : at + CONV + 4, 0:LANES] = head_ref[0:2, :]
    own_ref[at + CONV + 4 : at + CONV + 5, 0:LANES] = skips[CONV + 1 : CONV + 2, :]


def unpack_kernel(
    one_ref,
    two_ref,
    pre_gain_ref,
    bc_ref,
    dt_ref,
    conv_x_ref,
    bias_x_ref,
    conv_bc_ref,
    bias_bc_ref,
    dt_bias_ref,
    a_log_ref,
    d_skip_ref,
    gate_gain_ref,
    total,
):
    total[...] = one_ref[...].astype(F32) + two_ref[...].astype(F32)
    channels = total.shape[1]
    own_bc, width = bc_ref.shape
    folds = width // channels
    for fold in range(folds):
        bc_ref[:, fold * channels : (fold + 1) * channels] = total[fold * own_bc : (fold + 1) * own_bc, :]
    at = folds * own_bc
    pre_gain_ref[...] = jnp.concatenate([total[at + fold : at + fold + 1, :] for fold in range(folds)], axis=1).reshape(-1)
    at += folds
    states = conv_bc_ref.shape[1]
    conv_bc_ref[...] = total[at : at + CONV, 0:states]
    bias_bc_ref[...] = total[at + CONV : at + CONV + 1, 0:states].reshape(-1)
    at += 16 - folds
    count = dt_ref.shape[0]
    for fold in range(folds):
        dt_ref[:, fold * channels : (fold + 1) * channels] = total[at + 16 * fold : at + 16 * fold + count, :]
    at += 16 * folds
    conv_x_ref[...] = total[at : at + CONV, :]
    bias_x_ref[...] = total[at + CONV : at + CONV + 1, :].reshape(-1)
    gate_gain_ref[...] = total[at + CONV + 1 : at + CONV + 2, :].reshape(-1)
    at += CONV + 2
    for row, ref in enumerate((dt_bias_ref, a_log_ref, d_skip_ref)):
        ref[...] = total[at + row : at + row + 1, 0:LANES].reshape(-1)[0 : ref.shape[0]]


def hidden_kernel(rank_ref, hidden_ref, cotan_ref, kept_ref, got_ref, row_ref, out_ref, grad_ref):
    width = hidden_ref.shape[1]
    hidden = hidden_ref[...].astype(F32)
    branch = kept_ref[:, width:].astype(F32) + got_ref[:, width:].astype(F32)
    out_ref[...] = (hidden + branch).astype(BF16)
    inv_rms = lax.rsqrt(jnp.mean(hidden * hidden, axis=-1, keepdims=True) + EPS)
    scaled = (kept_ref[:, 0:width].astype(F32) + got_ref[:, 0:width].astype(F32)) * row_ref[0:1, :]
    pull = inv_rms * inv_rms * jnp.mean(scaled * hidden, axis=-1, keepdims=True)
    grad_ref[...] = cotan_ref[...].astype(F32) + inv_rms * (scaled - hidden * pull)


def pass_kernel(*refs):
    pass


def finish_kernel(which_ref, part_ref, after_ref, out_ref):
    out_ref[...] = part_ref[...].astype(F32)


def finish_pair_kernel(which_ref, part_ref, after_ref, *refs):
    out_ref, gate_ref = refs[-2:]
    rows, width = out_ref.shape
    channels = gate_ref.shape[1]
    for at in range(width // channels):
        out_ref[:, at * channels : (at + 1) * channels] = part_ref[at * rows : (at + 1) * rows, :].astype(F32)
    gate_ref[...] = part_ref[gate_ref.shape[0] :, :].astype(F32)


def finish_into_kernel(which_ref, part_ref, after_ref, whole_ref, out_ref):
    finish_kernel(which_ref, part_ref, after_ref, out_ref)


def split_kernel(which_ref, sent_one, sent_two, kept_one, kept_two, sent_ref, kept_ref):
    sent_ref[...] = (sent_one[...].astype(F32) + sent_two[...].astype(F32)).astype(BF16)
    kept_ref[...] = (kept_one[...].astype(F32) + kept_two[...].astype(F32)).astype(BF16)


def join_kernel(which_ref, own_ref, got_ref, own_extra_ref, got_extra_ref, out_ref):
    which = which_ref[0]
    rows = own_ref.shape[0]
    out_ref[pl.ds(pl.multiple_of(which * rows, 16), rows), :] = own_ref[...]
    out_ref[pl.ds(pl.multiple_of((1 - which) * rows, 16), rows), :] = got_ref[...]
    extra = own_extra_ref[...].astype(F32) + got_extra_ref[...].astype(F32)
    out_ref[2 * rows :, :] = extra.astype(BF16)


def whole(shape):
    return pl.BlockSpec(shape, lambda i: (0,) * len(shape), pipeline_mode=pl.Buffered(1))


def no_cost():
    return pl.CostEstimate(flops=0, bytes_accessed=0, transcendentals=0)


def params():
    return pltpu.CompilerParams(vmem_limit_bytes=60 << 20)


def run_tables(segments, pre_gain, bias_x, gate_gain, bias_bc, dt_bias, a_log, d_skip):
    inputs = (segments, pre_gain, bias_x, gate_gain, bias_bc, dt_bias, a_log, d_skip)
    in_vmem = pl.BlockSpec(memory_space=pltpu.VMEM)
    return pl.pallas_call(
        table_kernel,
        in_specs=[in_vmem] * len(inputs),
        out_specs=[in_vmem] * 3,
        out_shape=[
            jax.ShapeDtypeStruct((16, segments.size), F32),
            jax.ShapeDtypeStruct((8, pre_gain.shape[0]), F32),
            jax.ShapeDtypeStruct((8, LANES), F32),
        ],
        compiler_params=params(),
        name="tables",
    )(*inputs)


def in_place():
    return pl.BlockSpec(memory_space=pl.ANY)


def run_forward(hidden_in, cotangent, weights, tables, tokens):
    rows, width = hidden_in.shape
    channels = weights[0].shape[1]
    states = weights[2].shape[1]
    constants = (*weights, *tables)

    def block(columns):
        return pl.BlockSpec((BLOCK, columns), lambda i: (i, 0))

    def out(columns, kind=BF16):
        return jax.ShapeDtypeStruct((rows, columns), kind)

    return pl.pallas_call(
        forward_kernel,
        grid=(rows // BLOCK,),
        in_specs=[block(width), block(width)]
        + [whole(array.shape) for array in constants]
        + [pl.BlockSpec((tokens.shape[0], BLOCK), lambda i: (0, i))],
        out_specs=[block(width)]
        + [block(channels)] * 8
        + [block(LANES)] * 2
        + [block(states)] * 3
        + [
            pl.BlockSpec((BLOCK // PIECE, STATE, channels), lambda i: (i, 0, 0)),
            pl.BlockSpec((8, BLOCK), lambda i: (0, i)),
        ],
        out_shape=[
            out(width),
            out(channels),
            out(channels),
            out(channels),
            out(channels),
            out(channels, F32),
            out(channels),
            out(channels),
            out(channels),
            out(LANES, F32),
            out(LANES, F32),
            out(states),
            out(states, F32),
            out(states, F32),
            jax.ShapeDtypeStruct((rows // PIECE, STATE, channels), BF16),
            jax.ShapeDtypeStruct((8, rows), F32),
        ],
        scratch_shapes=[
            pltpu.VMEM((BLOCK + 8, channels), F32),
            pltpu.VMEM((BLOCK + 8, states), F32),
            pltpu.VMEM((STATE, channels), F32),
            pltpu.VMEM((LANES, width), BF16),
            pltpu.VMEM((BLOCK, channels), F32),
            pltpu.VMEM((BLOCK, channels), F32),
            pltpu.VMEM((PIECE, channels), BF16),
        ],
        compiler_params=params(),
        cost_estimate=no_cost(),
        name="forward",
    )(hidden_in, cotangent, *constants, tokens)


def scalar_spec():
    return pl.BlockSpec(memory_space=pltpu.SMEM)


def half_shapes(rows, columns):
    return [jax.ShapeDtypeStruct((rows // 2, columns), BF16)] * 2


def run_gate(low, forward, sums, rows_table, cotangent, normed):
    rows, channels = forward[0].shape
    width = cotangent.shape[1]

    def block(columns):
        return pl.BlockSpec((BLOCK, columns), lambda i: (i, 0))

    halves = [jax.ShapeDtypeStruct((width // 2 + width // 2, channels), BF16)] * 2
    out = pl.pallas_call(
        gate_kernel,
        grid=(rows // BLOCK,),
        in_specs=[scalar_spec()]
        + [block(channels)] * 3
        + [pl.BlockSpec((8, BLOCK), lambda i: (0, i)), whole(rows_table.shape), block(width), block(width)],
        out_specs=[block(channels), whole((8, channels))] + [whole(half.shape) for half in halves],
        out_shape=[jax.ShapeDtypeStruct((rows, channels), BF16), jax.ShapeDtypeStruct((8, channels), F32)]
        + halves,
        scratch_shapes=[
            pltpu.VMEM((BLOCK, channels), BF16),
            pltpu.VMEM((channels, width), F32),
            pltpu.VMEM((width, channels), F32),
        ],
        compiler_params=params(),
        cost_estimate=no_cost(),
        name="gate",
    )(low, *forward, sums, rows_table, cotangent, normed)
    return out[:2], out[2:]


def run_weight(low, normed, grad, after):
    rows, width = normed.shape
    channels = grad.shape[1]
    size = 2 * BLOCK
    halves = half_shapes(width, channels)
    return pl.pallas_call(
        weight_kernel,
        grid=(rows // size,),
        in_specs=[
            scalar_spec(),
            pl.BlockSpec((size, width), lambda i: (i, 0)),
            pl.BlockSpec((size, channels), lambda i: (i, 0)),
            in_place(),
        ],
        out_specs=[whole(half.shape) for half in halves],
        out_shape=halves,
        scratch_shapes=[pltpu.VMEM((width, channels), F32)],
        compiler_params=params(),
        cost_estimate=no_cost(),
        name="weight",
    )(low, normed, grad, after)


def run_backward(gate_inputs, sums, rows_table, by_channel, step_in, cum, bc_low, enter, normed, by_state, tables, after, head_count):
    rows, channels = by_channel[0].shape
    width = normed.shape[1]
    count = rows // BLOCK
    states = bc_low.shape[1]
    conv_x, conv_bc, head_values, tokens = tables

    def block(columns):
        return pl.BlockSpec((BLOCK, columns), lambda i: (count - 1 - i, 0))

    def low_rows(columns):
        return jax.ShapeDtypeStruct((rows, columns), BF16)

    totals = [
        jax.ShapeDtypeStruct(shape, F32)
        for shape in ((8, channels), (8, states), (8, LANES), (16, width), (states, width))
    ]
    return pl.pallas_call(
        functools.partial(backward_kernel, head_count),
        grid=(count,),
        in_specs=[block(channels)] * 3
        + [pl.BlockSpec((8, BLOCK), lambda i: (0, count - 1 - i)), whole(rows_table.shape)]
        + [block(channels)] * 4
        + [block(LANES), block(LANES), block(states)]
        + [pl.BlockSpec((BLOCK // PIECE, STATE, channels), lambda i: (count - 1 - i, 0, 0))]
        + [block(width), block(states), block(states)]
        + [whole(conv_x.shape), whole(conv_bc.shape), whole(head_values.shape)]
        + [pl.BlockSpec((tokens.shape[0], BLOCK), lambda i: (0, count - 1 - i)), in_place()],
        out_specs=[block(states), block(channels), block(LANES)]
        + [whole(shape.shape) for shape in totals],
        out_shape=[low_rows(states), low_rows(channels), low_rows(LANES)] + totals,
        scratch_shapes=[
            pltpu.VMEM((PIECE + 8, channels), F32),
            pltpu.VMEM((PIECE + 8, states), F32),
            pltpu.VMEM((STATE, channels), F32),
            pltpu.VMEM((LANES, width), F32),
            pltpu.VMEM((PIECE, channels), BF16),
            pltpu.VMEM((PIECE, channels), BF16),
            pltpu.VMEM((PIECE, channels), BF16),
            pltpu.VMEM((PIECE, channels), BF16),
            pltpu.VMEM((4 * PIECE + 32, channels), BF16),
        ],
        compiler_params=params(),
        cost_estimate=no_cost(),
        name="backward",
    )(*gate_inputs, sums, rows_table, *by_channel, step_in, cum, bc_low, enter, normed, *by_state, conv_x, conv_bc, head_values, tokens, after)


def run_merge(core, blocked, sums, weights, rows_table, after, ranks):
    normed = blocked[-1]
    rows, width = normed.shape
    channels = weights[0].shape[1]
    size = rows // ranks
    half = ranks // 2

    def rank_at(i, c):
        return jnp.where(i < half, 2 * i + 1 - c[0], 2 * (i - half) + c[0])

    def block(columns):
        return pl.BlockSpec((size, columns), lambda i, c: (rank_at(i, c), 0))

    def constant(shape):
        return pl.BlockSpec(shape, lambda i, c: (0,) * len(shape), pipeline_mode=pl.Buffered(1))

    out = jax.ShapeDtypeStruct((rows // 2, 2 * width), BF16)
    return pl.pallas_call(
        merge_kernel,
        grid_spec=pltpu.PrefetchScalarGridSpec(
            num_scalar_prefetch=1,
            grid=(ranks,),
            in_specs=[block(array.shape[1]) for array in blocked]
            + [pl.BlockSpec((8, size), lambda i, c: (0, rank_at(i, c)))]
            + [constant(array.shape) for array in (*weights, rows_table)]
            + [in_place()],
            out_specs=[
                pl.BlockSpec((size, 2 * width), lambda i, c: (jnp.minimum(i, half - 1), 0)),
                pl.BlockSpec((size, 2 * width), lambda i, c: (jnp.maximum(i - half, 0), 0)),
                constant((8, width)),
            ],
            scratch_shapes=[pltpu.VMEM((LANES, width), BF16), pltpu.VMEM((size, channels), BF16)],
        ),
        out_shape=[out, out, jax.ShapeDtypeStruct((8, width), F32)],
        compiler_params=params(),
        cost_estimate=no_cost(),
        name="merge",
    )(core, *blocked, sums, *weights, rows_table, after)


def run_pack(core, bc_rows, step_rows, channel_grads, gain_rows, gain, conv_bc_grads, head_grads, head_count):
    states, width = bc_rows.shape
    channels = channel_grads.shape[1]
    folds = width // channels
    in_vmem = pl.BlockSpec(memory_space=pltpu.VMEM)
    shared = jax.ShapeDtypeStruct((states // 2 * folds + 16, channels), BF16)
    return pl.pallas_call(
        functools.partial(pack_kernel, head_count),
        in_specs=[scalar_spec()] + [in_vmem] * 7,
        out_specs=[in_vmem] * 3,
        out_shape=[shared, shared, jax.ShapeDtypeStruct((16 * folds + 16, channels), F32)],
        compiler_params=params(),
        cost_estimate=no_cost(),
        name="pack",
    )(core, bc_rows, step_rows, channel_grads, gain_rows, gain, conv_bc_grads, head_grads)


def run_unpack(one, two, width, states, head_count):
    rows, channels = one.shape
    last = two.shape[0] // rows - 1
    in_vmem = pl.BlockSpec(memory_space=pltpu.VMEM)
    shapes = (
        (width,),
        (OWN_BC, width),
        (head_count, width),
        (CONV, channels),
        (channels,),
        (CONV, states),
        (states,),
        (head_count,),
        (head_count,),
        (head_count,),
        (channels,),
    )
    return pl.pallas_call(
        unpack_kernel,
        grid=(1,),
        in_specs=[
            pl.BlockSpec((rows, channels), lambda i: (0, 0)),
            pl.BlockSpec((rows, channels), lambda i: (last, 0)),
        ],
        out_specs=[pl.BlockSpec(shape, lambda i, rank=len(shape): (0,) * rank) for shape in shapes],
        out_shape=[jax.ShapeDtypeStruct(shape, F32) for shape in shapes],
        scratch_shapes=[pltpu.VMEM(one.shape, F32)],
        compiler_params=params(),
        cost_estimate=no_cost(),
        name="unpack",
    )(one, two)


def run_hidden(rank, hidden_in, cotangent, kept, got, rows_table):
    own_rows = kept.shape[0]
    width = hidden_in.shape[1]
    count = 2
    size = own_rows // count

    def own(columns):
        return pl.BlockSpec((size, columns), lambda i, r: (r[0] * count + i, 0))

    def block(columns):
        return pl.BlockSpec((size, columns), lambda i, r: (i, 0))

    return pl.pallas_call(
        hidden_kernel,
        grid_spec=pltpu.PrefetchScalarGridSpec(
            num_scalar_prefetch=1,
            grid=(count,),
            in_specs=[
                own(width),
                own(width),
                block(2 * width),
                block(2 * width),
                pl.BlockSpec(rows_table.shape, lambda i, r: (0, 0)),
            ],
            out_specs=[block(width), block(width)],
        ),
        out_shape=[
            jax.ShapeDtypeStruct((own_rows, width), BF16),
            jax.ShapeDtypeStruct((own_rows, width), F32),
        ],
        compiler_params=params(),
        cost_estimate=no_cost(),
        name="hidden",
    )(rank, hidden_in, cotangent, kept, got, rows_table)


def run_pass(arrays, after):
    count = len(arrays)
    return pl.pallas_call(
        pass_kernel,
        in_specs=[in_place()] * (count + 1),
        out_specs=[in_place()] * count,
        out_shape=[jax.ShapeDtypeStruct(array.shape, array.dtype) for array in arrays],
        input_output_aliases={at: at for at in range(count)},
        cost_estimate=no_cost(),
        name="pass",
    )(*arrays, after)


def run_finish(which, part, after, rows, into=None):
    columns = part.shape[1]
    count = 2
    size = rows // count
    inputs = [part, after] + ([] if into is None else [into])
    return pl.pallas_call(
        finish_kernel if into is None else finish_into_kernel,
        grid_spec=pltpu.PrefetchScalarGridSpec(
            num_scalar_prefetch=1,
            grid=(count,),
            in_specs=[pl.BlockSpec((size, columns), lambda i, w: (i, 0))] + [in_place()] * (len(inputs) - 1),
            out_specs=pl.BlockSpec((size, columns), lambda i, w: (w[0] * count + i, 0)),
        ),
        out_shape=jax.ShapeDtypeStruct((2 * rows, columns), F32),
        input_output_aliases={} if into is None else {3: 0},
        compiler_params=params(),
        cost_estimate=no_cost(),
        name="finish",
    )(jnp.reshape(which, (1,)), *inputs)


def run_finish_pair(which, part, after, out_shape, gate_shape, into=()):
    out_rows, out_columns = out_shape
    gate_rows, gate_columns = gate_shape
    return pl.pallas_call(
        finish_pair_kernel,
        grid_spec=pltpu.PrefetchScalarGridSpec(
            num_scalar_prefetch=1,
            grid=(1,),
            in_specs=[pl.BlockSpec((gate_rows, gate_columns), lambda i, w: (0, 0))]
            + [in_place()] * (1 + len(into)),
            out_specs=[
                pl.BlockSpec((out_rows // 2, out_columns), lambda i, w: (w[0], 0)),
                pl.BlockSpec((gate_rows // 2, gate_columns), lambda i, w: (w[0], 0)),
            ],
        ),
        out_shape=[jax.ShapeDtypeStruct(out_shape, F32), jax.ShapeDtypeStruct(gate_shape, F32)],
        input_output_aliases={3 + at: at for at in range(len(into))},
        compiler_params=params(),
        cost_estimate=no_cost(),
        name="finish_pair",
    )(jnp.reshape(which, (1,)), part, after, *into)


def run_split(one, two, which):
    half, columns = one.shape[0] // 2, one.shape[1]
    count = 2
    size = half // count
    sent = pl.BlockSpec((size, columns), lambda i, w: ((1 - w[0]) * count + i, 0))
    kept = pl.BlockSpec((size, columns), lambda i, w: (w[0] * count + i, 0))
    out = pl.BlockSpec((size, columns), lambda i, w: (i, 0))
    return pl.pallas_call(
        split_kernel,
        grid_spec=pltpu.PrefetchScalarGridSpec(
            num_scalar_prefetch=1,
            grid=(count,),
            in_specs=[sent, sent, kept, kept],
            out_specs=[out, out],
        ),
        out_shape=[jax.ShapeDtypeStruct((half, columns), BF16)] * 2,
        compiler_params=params(),
        cost_estimate=no_cost(),
        name="split",
    )(jnp.reshape(which.astype(jnp.int32), (1,)), one, two, one, two)


def run_join(which, own, got, extra_rows):
    rows = own.shape[0] - extra_rows
    columns = own.shape[1]
    matrix = pl.BlockSpec((rows, columns), lambda i, w: (0, 0))
    extra = pl.BlockSpec((extra_rows, columns), lambda i, w: (rows // extra_rows, 0))
    shape = (2 * rows + extra_rows, columns)
    return pl.pallas_call(
        join_kernel,
        grid_spec=pltpu.PrefetchScalarGridSpec(
            num_scalar_prefetch=1,
            grid=(1,),
            in_specs=[matrix, matrix, extra, extra],
            out_specs=pl.BlockSpec(shape, lambda i, w: (0, 0)),
        ),
        out_shape=jax.ShapeDtypeStruct(shape, BF16),
        compiler_params=params(),
        cost_estimate=no_cost(),
        name="join",
    )(jnp.reshape(which, (1,)), own, got, own, got)


def swap(array, axis, bit):
    size = lax.axis_size(axis)
    return lax.ppermute(array, axis, [(source, source ^ bit) for source in range(size)])


def axis_bits(axis):
    size = lax.axis_size(axis)
    return [1 << place for place in range(size.bit_length() - 1)]


def half_of(array, which):
    half = array.shape[0] // 2
    return lax.dynamic_slice_in_dim(array, which * half, half, 0)


def sum_tensor(array):
    for bit in axis_bits("tensor"):
        array = array + swap(array, "tensor", bit)
    return array


def dp_bits(step):
    bits = axis_bits("dp")
    swapped = [bits[1], bits[0]] + bits[2:]
    return bits[step], swapped[step]


def own_bit(step):
    first, second = dp_bits(step)
    place = lax.axis_index("dp").astype(jnp.int32)
    core = lax.axis_index("tensor") % 2
    return jnp.where(core == 0, (place // first) % 2, (place // second) % 2)


def dp_pairs(step):
    ranks = lax.axis_size("tensor")
    pairs = dp_bits(step)
    return [
        (at * ranks + rank, (at ^ pairs[rank % 2]) * ranks + rank)
        for at in range(lax.axis_size("dp"))
        for rank in range(ranks)
    ]


def in_order(which, own, got):
    place = lax.broadcasted_iota(jnp.int32, (2, 1, 1), 0)
    return jnp.where(place == which, own[None], got[None])


def sum_steps(sent, kept, rider=None, own=None):
    axes = ("dp", "tensor")
    steps = range(1, len(axis_bits("dp")))
    terms = [kept]
    got = yield sent, axes, dp_pairs(0)

    def total(which):
        return sum(half_of(term, which).astype(F32) for term in terms)

    for step in steps:
        which = own_bit(step)
        terms.append(got)
        sent = total(1 - which).astype(BF16)
        terms = [half_of(term, which) for term in terms]
        got = yield sent, axes, dp_pairs(step)
    part = sum((term.astype(F32) for term in terms), got.astype(F32)).astype(BF16)
    extra = 0
    for step in reversed((0, *steps)):
        if step == 1 and rider is not None:
            rows = rider().astype(BF16)
            extra = rows.shape[0]
            part = jnp.concatenate([part, rows])
        if step == 0 and own is not None:
            own.append(part)
        got = yield part, axes, dp_pairs(step)
        if step and extra:
            part = run_join(own_bit(step), part, got, extra)
        elif step:
            part = in_order(own_bit(step), part, got).reshape(2 * part.shape[0], -1)
    if extra:
        extra = (part[-extra:].astype(F32) + got[-extra:].astype(F32)).astype(BF16)
    return own_bit(0), part, got, extra


def rest_steps(rows):
    axes = ("dp", "tensor")
    for step in range(2, len(axis_bits("dp"))):
        got = yield rows, axes, dp_pairs(step)
        total = rows.astype(F32) + got.astype(F32)
        last, rows = (rows, got), total.astype(BF16)
    return last


def both_steps(sent, kept):
    size = lax.axis_size("tensor")
    rank = lax.axis_index("tensor")
    got = yield sent, "tensor", [(i, i ^ 1) for i in range(size)]
    for bit in axis_bits("tensor")[1:]:
        sent, kept = run_split(kept, got, (rank // bit) % 2)
        got = yield sent, "tensor", [(i, i ^ bit) for i in range(size)]
    return kept, got


def small_steps(sent, kept, own):
    size = lax.axis_size("tensor")
    rank = lax.axis_index("tensor")
    got = yield sent, "tensor", [(i, i ^ 1) for i in range(size)]
    total = kept.astype(F32) + got.astype(F32)
    for bit in axis_bits("tensor")[1:]:
        which = (rank // bit) % 2
        shared = total[-16:].astype(BF16)
        rows = total[:-16]
        got = yield jnp.concatenate([half_of(rows, 1 - which).astype(BF16), shared]), "tensor", [
            (i, i ^ bit) for i in range(size)
        ]
        total = jnp.concatenate([half_of(rows, which), shared.astype(F32)]) + got.astype(F32)
    return jnp.concatenate([total, own])


class Order:
    def __init__(self, last):
        self.last = last
        self.waiting = {}
        self.flying = {}
        self.arrived = {}
        self.results = {}

    def advance(self, name, steps, got):
        try:
            request = steps.send(got)
            self.waiting[name] = (steps, request)
            self.last = request[0]
        except StopIteration as end:
            self.results[name] = end.value

    def add(self, name, steps):
        last = self.last
        self.advance(name, steps, None)
        self.last = last

    def go(self, *names):
        for name in names:
            if name in self.waiting:
                steps, (sent, axis, moves) = self.waiting.pop(name)
                self.flying[name] = (steps, lax.ppermute(sent, axis, moves))

    def arrive(self, *names):
        found = [(name, *self.flying.pop(name)) for name in names if name in self.flying]
        if found:
            passed = run_pass([got for _, _, got in found], self.last)
            self.last = passed[0]
            for (name, steps, _), got in zip(found, passed):
                self.arrived[name] = (steps, got)

    def take(self, *names):
        for name in names:
            if name in self.arrived:
                steps, got = self.arrived.pop(name)
                self.advance(name, steps, got if got is self.last else self.hold(got))
                if name in self.waiting:
                    self.last = self.waiting[name][1][0]

    def land(self, *names):
        self.arrive(*names)
        self.take(*names)

    def hold(self, array):
        return run_pass([array], self.last)[0]

    def step(self, *names):
        for name in names:
            self.land(name)
            self.go(name)

    def until(self, name, found):
        while not found:
            self.step(name)
        return found[0]

    def result(self, name):
        while name not in self.results:
            self.go(name)
            self.land(name)
        return self.results[name]


def shards(
    hidden_in,
    pre_gain,
    w_gate,
    w_value,
    w_bc,
    w_dt,
    conv_x,
    conv_x_bias,
    conv_bc,
    conv_bc_bias,
    dt_bias,
    a_log,
    d_skip,
    gate_gain,
    w_out,
    cotangent,
    segments,
):
    row_count, width = hidden_in.shape
    channels = w_gate.shape[1]
    head_count = dt_bias.shape[0]
    head_width = channels // head_count
    ranks = lax.axis_size("tensor")
    my_rank = lax.axis_index("tensor")
    own_rows = row_count // ranks
    row_start = my_rank * own_rows
    pair_width = w_bc.shape[1] // ranks
    low = jnp.reshape(own_bit(0), (1,))
    w_dt_rows = w_dt.T
    tokens, rows_table, head_values = run_tables(
        segments, pre_gain, conv_x_bias, gate_gain, conv_bc_bias, dt_bias, a_log, d_skip
    )
    (
        normed,
        mixed,
        act,
        turn,
        gated_grad,
        scan,
        values,
        slope,
        inner_pre,
        step_in,
        cum,
        bc_low,
        bc_slope,
        state_pre,
        enter,
        sums,
    ) = run_forward(
        hidden_in,
        cotangent,
        (w_gate, w_value, w_bc, w_dt_rows, w_out),
        (conv_x, conv_bc, rows_table, head_values),
        tokens,
    )
    sums = sum_tensor(sums) / (channels * ranks)
    (gate_low, gain_rows), halves = run_gate(
        low, (mixed, turn, gated_grad), sums, rows_table, cotangent, normed
    )
    order = Order(gate_low)
    first_own, second_own = [], []
    order.add("first", sum_steps(*halves, lambda: order.result("small"), first_own))
    order.go("first")
    (
        state_low,
        inner_low,
        step_low,
        channel_grads,
        conv_bc_grads,
        head_grads,
        step_rows,
        bc_rows,
    ) = run_backward(
        (mixed, gated_grad, act),
        sums,
        rows_table,
        (scan, values, slope, inner_pre),
        step_in,
        cum,
        bc_low,
        enter,
        normed,
        (bc_slope, state_pre),
        (conv_x, conv_bc, head_values, tokens),
        halves[0],
        head_count,
    )
    order.last = inner_low
    order.step("first")
    sent, kept = run_weight(low, normed, inner_low, order.last)
    order.last = kept
    order.step("first")
    order.add("second", sum_steps(order.hold(sent), kept, None, second_own))
    order.go("second")
    core = jnp.reshape((my_rank % 2).astype(jnp.int32), (1,))
    both_sent, both_kept, gain = run_merge(
        core,
        (gate_low, inner_low, step_low, state_low, mixed, normed),
        sums,
        (w_gate, w_value, w_dt_rows, w_bc, w_out),
        rows_table,
        order.last,
        ranks,
    )
    order.last = both_kept
    order.land("second", "first")
    order.go("second", "first")
    small = run_pack(
        core, bc_rows, step_rows, channel_grads, gain_rows, order.hold(gain), conv_bc_grads, head_grads, head_count
    )
    order.add("small", small_steps(*small))
    order.go("small")
    order.add("both", both_steps(order.hold(both_sent), both_kept))
    order.go("both")
    order.step("small")
    order.land("small")
    order.land("second", "first")
    order.go("second", "first")
    order.step("second")
    order.step("both")
    order.land("second")
    order.land("first")
    order.go("second", "first")
    order.step("second")
    which = own_bit(0)
    sums_first = run_finish_pair(which, order.until("first", first_own), order.last, w_out.shape, w_gate.shape)
    order.last = sums_first[0]
    own = order.until("second", second_own)
    w_value_sum = run_finish(which, own, order.last, own.shape[0])
    order.last = w_value_sum
    _, _, got, rows = order.result("first")
    order.add("rest", rest_steps(rows))
    order.go("rest")
    w_out_sum, w_gate_sum = run_finish_pair(
        1 - which, got, order.last, w_out.shape, w_gate.shape, sums_first
    )
    order.last = w_out_sum
    kept, got = order.result("both")
    block_out, hidden_grad = run_hidden(
        jnp.reshape(my_rank.astype(jnp.int32), (1,)), hidden_in, cotangent, kept, got, rows_table
    )
    order.last = hidden_grad
    one, two = order.result("rest")
    small = run_unpack(one, two, width, w_bc.shape[1], head_count)
    order.last = small[0]
    _, own, got, _ = order.result("second")
    w_value_sum = run_finish(1 - which, got, order.last, own.shape[0], w_value_sum)
    (
        pre_gain_grad,
        w_bc_rows,
        dt_rows,
        conv_x_grad,
        conv_x_bias_grad,
        conv_bc_grad,
        conv_bc_bias_grad,
        dt_bias_grad,
        a_log_grad,
        d_skip_grad,
        gate_gain_grad,
    ) = small
    return (
        block_out,
        hidden_grad,
        pre_gain_grad,
        w_gate_sum,
        w_value_sum,
        w_bc_rows.T,
        dt_rows.T,
        conv_x_grad,
        conv_x_bias_grad,
        conv_bc_grad,
        conv_bc_bias_grad,
        dt_bias_grad,
        a_log_grad,
        d_skip_grad,
        gate_gain_grad,
        w_out_sum,
    )


def solution(mesh):
    in_specs = (
        P("dp", None),
        P(),
        P(None, "tensor"),
        P(None, "tensor"),
        P(),
        P(None, "tensor"),
        P(None, "tensor"),
        P("tensor"),
        P(),
        P(),
        P("tensor"),
        P("tensor"),
        P("tensor"),
        P("tensor"),
        P("tensor", None),
        P("dp", None),
        P("dp", None),
    )
    out_specs = (
        P(("dp", "tensor"), None),
        P(("dp", "tensor"), None),
        P(),
        P(None, "tensor"),
        P(None, "tensor"),
        P(None, "tensor"),
        P(None, "tensor"),
        P(None, "tensor"),
        P("tensor"),
        P(),
        P(),
        P("tensor"),
        P("tensor"),
        P("tensor"),
        P("tensor"),
        P("tensor", None),
    )
    return jax.shard_map(shards, mesh=mesh, in_specs=in_specs, out_specs=out_specs, check_vma=False)
```

```python
import functools
import math

import jax
import jax.numpy as jnp
from jax import lax
from jax.experimental import pallas as pl
from jax.experimental.pallas import tpu as pltpu
from jax.sharding import PartitionSpec as P

STATE = 128
CONV = 4
BLOCK = 256
PIECE = 128
OWN_BC = 64
SHARED_AT = 128
LANES = 128
EPS = 1e-05
HIGH = lax.Precision.HIGHEST
LOG2E = math.log2(math.e)
BF16 = jnp.bfloat16
F32 = jnp.float32


def dot(left, right):
    return jnp.dot(left, right, preferred_element_type=F32)


def dot_last(left, right):
    return lax.dot_general(left, right, (((1,), (1,)), ((), ())), preferred_element_type=F32)


def dot_first(left, right):
    return lax.dot_general(left, right, (((0,), (0,)), ((), ())), preferred_element_type=F32)


def two_terms(array):
    upper = array.astype(BF16)
    return upper, (array - upper.astype(F32)).astype(BF16)


def sum_rows(ones, array):
    first = array.astype(BF16)
    second, third = two_terms(array - first.astype(F32))
    sums = dot(ones.astype(BF16), jnp.concatenate([first, second, third], axis=1))
    columns = array.shape[1]
    return sums[:, 0:columns] + sums[:, columns : 2 * columns] + sums[:, 2 * columns :]


def sigmoid(array):
    return 0.5 * jnp.tanh(0.5 * array) + 0.5


def spread_heads(array, heads_twice):
    upper, rest = two_terms(array)
    return dot(jnp.concatenate([upper, rest], axis=1), heads_twice)


def sum_heads(array, heads):
    upper, rest = two_terms(array)
    return dot_last(upper, heads) + dot_last(rest, heads)


def head_table(channels, head_count):
    head_width = channels // head_count
    channel = lax.broadcasted_iota(jnp.int32, (LANES, channels), 1)
    head = lax.broadcasted_iota(jnp.int32, (LANES, channels), 0)
    first = head * head_width
    return ((channel >= first) & (channel < first + head_width)).astype(F32).astype(BF16)


def head_rows(head_ref, heads):
    upper, rest = two_terms(head_ref[...])
    return dot(upper, heads) + dot(rest, heads)


def table_kernel(
    segment_ref,
    pre_gain_ref,
    bias_x_ref,
    gate_gain_ref,
    bias_bc_ref,
    dt_bias_ref,
    a_log_ref,
    d_skip_ref,
    token_ref,
    row_ref,
    head_ref,
):
    seq_count, length = segment_ref.shape
    place = lax.broadcasted_iota(jnp.int32, (8, length), 1)
    at_row = lax.broadcasted_iota(jnp.int32, (8, length), 0)
    for seq in range(seq_count):
        documents = jnp.broadcast_to(segment_ref[seq : seq + 1, :], (8, length)).astype(F32)
        padded = jnp.where(at_row == 0, documents, 0.0)

        def moved(by):
            other = pltpu.roll(documents, by % length, 1)
            return other, (place >= by) & (place < length + by)

        for k in range(1, CONV):
            before, inside = moved(k)
            padded = jnp.where((at_row == k) & inside & (before == documents), 1.0, padded)
        ends = []
        for piece in range(length // PIECE):
            here = slice(piece * PIECE, (piece + 1) * PIECE)
            ends.append(jnp.broadcast_to(documents[:, (piece + 1) * PIECE - 1 : (piece + 1) * PIECE], (8, PIECE)))
        starts = [jnp.full((8, PIECE), -1.0, F32)] + ends[:-1]
        padded = jnp.where((at_row == 4) & (jnp.concatenate(starts, axis=1) == documents), 1.0, padded)
        padded = jnp.where((at_row == 5) & (jnp.concatenate(ends, axis=1) == documents), 1.0, padded)
        lower = jnp.zeros((8, length), F32)
        for k in range(1, CONV):
            after, inside = moved(-k)
            hit = inside & (after == documents)
            if 5 + k < 8:
                padded = jnp.where((at_row == 5 + k) & hit, 1.0, padded)
            else:
                lower = jnp.where((at_row == 5 + k - 8) & hit, 1.0, lower)
        columns = slice(seq * length, (seq + 1) * length)
        token_ref[0:8, columns] = padded + jnp.where(at_row == 0, 64.0 * seq, 0.0)
        token_ref[8:16, columns] = lower
    row_ref[...] = jnp.zeros(row_ref.shape, F32)
    for at, ref in enumerate((pre_gain_ref, bias_x_ref, gate_gain_ref, bias_bc_ref)):
        row_ref[at : at + 1, 0 : ref.shape[0]] = ref[...].reshape(1, -1)
    head_ref[...] = jnp.zeros(head_ref.shape, F32)
    count = dt_bias_ref.shape[0]
    head_ref[0:1, 0:count] = dt_bias_ref[...].reshape(1, -1)
    head_ref[1:2, 0:count] = -jnp.exp(a_log_ref[...].reshape(1, -1))
    head_ref[2:3, 0:count] = d_skip_ref[...].reshape(1, -1)


def forward_kernel(
    hidden_ref,
    cotan_ref,
    w_gate_ref,
    w_value_ref,
    w_bc_ref,
    w_dt_ref,
    w_out_ref,
    conv_x_ref,
    conv_bc_ref,
    row_ref,
    head_ref,
    token_ref,
    normed_ref,
    mixed_ref,
    act_ref,
    turn_ref,
    grad_ref,
    scan_ref,
    value_ref,
    slope_ref,
    inner_ref,
    step_ref,
    cum_ref,
    bc_ref,
    bc_slope_ref,
    state_ref,
    enter_ref,
    sums_ref,
    tail_x,
    tail_bc,
    carried,
    wide_dt,
    gate_all,
    grad_all,
    tailed,
):
    block = pl.program_id(0)

    @pl.when(block == 0)
    def _():
        tail_x[0:8, :] = jnp.zeros((8, tail_x.shape[1]), F32)
        tail_bc[0:8, :] = jnp.zeros((8, tail_bc.shape[1]), F32)
        carried[...] = jnp.zeros(carried.shape, F32)
        wide_dt[...] = jnp.zeros(wide_dt.shape, BF16)
        wide_dt[0 : w_dt_ref.shape[0], :] = w_dt_ref[...]

    channels = tail_x.shape[1]
    heads = head_table(channels, w_dt_ref.shape[0])
    skips = head_rows(head_ref, heads)[2:3, :]
    side = token_ref[...].T
    hidden = hidden_ref[...].astype(F32)
    inv_rms = lax.rsqrt(jnp.mean(hidden * hidden, axis=-1, keepdims=True) + EPS)
    normed = (hidden * inv_rms * row_ref[0:1, :]).astype(BF16)
    normed_ref[...] = normed
    tail_x[8:, :] = dot(normed, w_value_ref[...])
    tail_bc[8:, :] = dot(normed, w_bc_ref[...])
    step_in = dot_last(normed, wide_dt[...]) + head_ref[0:1, :]
    step_ref[...] = step_in
    step = jnp.maximum(step_in, 0.0) + jnp.log1p(jnp.exp(-jnp.abs(step_in)))
    rate = head_ref[1:2, :] * step * LOG2E
    gate_all[...] = dot(normed, w_gate_ref[...])
    grad_all[...] = dot_last(cotan_ref[...], w_out_ref[...])
    masks = [None] + [side[:, k : k + 1] for k in range(1, CONV)]

    def conv(tail, taps_ref, bias_at, lanes):
        result = row_ref[bias_at : bias_at + 1, lanes] + taps_ref[CONV - 1 : CONV, lanes] * tail[8:, lanes]
        for k in range(1, CONV):
            shifted = tail[8 - k : 8 - k + BLOCK, lanes]
            result = result + taps_ref[CONV - 1 - k : CONV - k, lanes] * shifted * masks[k]
        return result

    for at in range(0, channels, LANES):
        lanes = slice(at, at + LANES)
        before = conv(tail_x, conv_x_ref, 1, lanes)
        half = sigmoid(before)
        value_ref[:, lanes] = (before * half).astype(BF16)
        slope_ref[:, lanes] = (half * (1.0 + before * (1.0 - half))).astype(BF16)
        inner_ref[:, lanes] = tail_x[8:, lanes].astype(BF16)
    for at in range(0, 2 * STATE, LANES):
        lanes = slice(at, at + LANES)
        before = conv(tail_bc, conv_bc_ref, 3, lanes)
        half = sigmoid(before)
        bc_ref[:, lanes] = (before * half).astype(BF16)
        bc_slope_ref[:, lanes] = half * (1.0 + before * (1.0 - half))
        state_ref[:, lanes] = tail_bc[8:, lanes]
    tail_x[0:8, :] = tail_x[BLOCK:, :]
    tail_bc[0:8, :] = tail_bc[BLOCK:, :]

    row_at = lax.broadcasted_iota(jnp.int32, (PIECE, PIECE), 0)
    col_at = lax.broadcasted_iota(jnp.int32, (PIECE, PIECE), 1)
    first_half = lax.broadcasted_iota(jnp.int32, (PIECE, LANES), 1) < LANES // 2
    heads_twice = jnp.concatenate([heads, heads], axis=0)
    block_row = lax.broadcasted_iota(jnp.int32, (BLOCK, BLOCK), 0)
    block_col = lax.broadcasted_iota(jnp.int32, (BLOCK, BLOCK), 1)
    lower = (block_row >= block_col) & (block_row // PIECE == block_col // PIECE)
    cums = sum_rows(lower.astype(F32), rate)
    cum_ref[...] = cums
    cums_t = cums.T
    lasts = [
        jnp.broadcast_to(cums[at + PIECE - 1 : at + PIECE, :], (PIECE, LANES)) for at in range(0, BLOCK, PIECE)
    ]
    reach = jnp.exp2(cums) * side[:, 4:5]
    tail = jnp.exp2(jnp.concatenate(lasts) - cums) * side[:, 5:6]
    wides = spread_heads(jnp.concatenate([step, reach, tail], axis=0), heads_twice)
    for piece in range(BLOCK // PIECE):
        rows = slice(piece * PIECE, (piece + 1) * PIECE)
        cum = cums[rows]
        cum_t = cums_t[:, rows]
        same = (side[rows, 0:1] == token_ref[0:1, rows]) & (row_at >= col_at)
        bias = jnp.where(same, 0.0, -1e30)
        wide = jnp.concatenate([wides[at + piece * PIECE : at + (piece + 1) * PIECE] for at in range(0, 3 * BLOCK, BLOCK)])
        b_low = bc_ref[rows, 0:STATE]
        c_low = bc_ref[rows, STATE : 2 * STATE]
        scores = dot_last(c_low, b_low)
        enter = carried[...].astype(BF16)
        enter_ref[piece] = enter
        from_state = dot(c_low, enter)
        for pair in range(channels // LANES):
            lanes = slice(pair * LANES, (pair + 1) * LANES)
            values = value_ref[rows, lanes].astype(F32)
            scaled = wide[0:PIECE, lanes] * values
            low = scaled.astype(BF16)
            weights = []
            for head in (2 * pair, 2 * pair + 1):
                gaps = (cum[:, head : head + 1] - cum_t[head : head + 1, :]) + bias
                weights.append((scores * jnp.exp2(gaps)).astype(BF16))
            zero = jnp.zeros_like(low)
            both = jnp.concatenate(
                [jnp.where(first_half, low, zero), jnp.where(first_half, zero, low)], axis=0
            )
            out = dot(jnp.concatenate(weights, axis=1), both)
            out = out + from_state[:, lanes] * wide[PIECE : 2 * PIECE, lanes]
            scan_ref[rows, lanes] = out + skips[:, lanes] * values
            tailed[:, lanes] = (wide[2 * PIECE :, lanes] * scaled).astype(BF16)
        kept = wide[2 * PIECE - 1 : 2 * PIECE, :]
        carried[...] = kept * carried[...] + dot_first(b_low, tailed[...])

    ones = jnp.ones((8, LANES), BF16)
    square_part = jnp.zeros((BLOCK, LANES), F32)
    cross_part = jnp.zeros((BLOCK, LANES), F32)
    for at in range(0, channels, LANES):
        lanes = slice(at, at + LANES)
        gate = gate_all[:, lanes]
        scan = scan_ref[:, lanes]
        grad = grad_all[:, lanes]
        half = sigmoid(gate)
        act = gate * half
        mixed = scan * act
        mixed_ref[:, lanes] = mixed.astype(BF16)
        act_ref[:, lanes] = act.astype(BF16)
        turn_ref[:, lanes] = (scan * (half * (1.0 + gate * (1.0 - half)))).astype(BF16)
        grad_ref[:, lanes] = grad.astype(BF16)
        square_part = square_part + mixed * mixed
        cross_part = cross_part + mixed * (grad * row_ref[2:3, lanes])
    upper, rest = two_terms(square_part)
    squares = dot_last(ones, upper) + dot_last(ones, rest)
    upper, rest = two_terms(cross_part)
    crosses = dot_last(ones, upper) + dot_last(ones, rest)
    is_first = lax.broadcasted_iota(jnp.int32, (8, BLOCK), 0) == 0
    sums_ref[...] = jnp.where(is_first, squares, crosses)


def store_halves(total, columns, mine, sent_ref, kept_ref, at=0):
    half = total.shape[0] // 2
    to = slice(at, at + half)
    for which, ref in ((1 - mine, sent_ref), (mine, kept_ref)):
        ref[to, :] = total[pl.ds(pl.multiple_of(which * half, 8), half), columns].astype(BF16)


def gate_columns(sums_ref):
    row_at = lax.broadcasted_iota(jnp.int32, (8, LANES), 0)

    def column(which):
        pick = (row_at == which).astype(F32)
        return lax.dot_general(
            sums_ref[...], pick, (((0,), (0,)), ((), ())), precision=HIGH, preferred_element_type=F32
        )

    inv_gate = lax.rsqrt(column(0) + EPS)
    return inv_gate, inv_gate * inv_gate * column(1)


def gate_kernel(
    low_ref,
    mixed_ref,
    turn_ref,
    grad_ref,
    sums_ref,
    row_ref,
    cotan_ref,
    normed_ref,
    gate_low_ref,
    gain_ref,
    sent_ref,
    kept_ref,
    gated,
    out_total,
    gate_total,
):
    block = pl.program_id(0)

    @pl.when(block == 0)
    def _():
        gain_ref[...] = jnp.zeros(gain_ref.shape, F32)
        out_total[...] = jnp.zeros(out_total.shape, F32)
        gate_total[...] = jnp.zeros(gate_total.shape, F32)

    channels = mixed_ref.shape[1]
    inv_gate, pull = gate_columns(sums_ref)
    for at in range(0, channels, LANES):
        lanes = slice(at, at + LANES)
        mixed = mixed_ref[:, lanes].astype(F32)
        grad = grad_ref[:, lanes].astype(F32)
        gain = row_ref[2:3, lanes]
        normal = mixed * inv_gate
        gated[:, lanes] = (normal * gain).astype(BF16)
        gain_ref[:, lanes] += jnp.sum((grad * normal).reshape(-1, 8, LANES), axis=0)
        mixed_grad = inv_gate * (grad * gain - mixed * pull)
        gate_low_ref[:, lanes] = (mixed_grad * turn_ref[:, lanes].astype(F32)).astype(BF16)
    out_total[...] += dot_first(gated[...], cotan_ref[...])
    gate_total[...] += dot_first(normed_ref[...], gate_low_ref[...])

    @pl.when(block == pl.num_programs(0) - 1)
    def _():
        rows, width = out_total.shape
        for at in range(width // channels):
            columns = slice(at * channels, (at + 1) * channels)
            store_halves(out_total, columns, low_ref[0], sent_ref, kept_ref, at * rows // 2)
        store_halves(gate_total, slice(None), low_ref[0], sent_ref, kept_ref, width // 2)


def weight_kernel(low_ref, normed_ref, grad_ref, after_ref, sent_ref, kept_ref, total):
    block = pl.program_id(0)
    part = dot_first(normed_ref[...], grad_ref[...])

    @pl.when(block == 0)
    def _():
        total[...] = part

    @pl.when(block > 0)
    def _():
        total[...] += part

    @pl.when(block == pl.num_programs(0) - 1)
    def _():
        store_halves(total, slice(None), low_ref[0], sent_ref, kept_ref)


def backward_kernel(
    head_count,
    mixed_ref,
    grad_ref,
    act_ref,
    sums_ref,
    row_ref,
    scan_ref,
    value_ref,
    slope_ref,
    inner_ref,
    step_ref,
    cum_ref,
    bc_ref,
    enter_ref,
    normed_ref,
    bc_slope_ref,
    state_ref,
    conv_x_ref,
    conv_bc_ref,
    head_ref,
    token_ref,
    after_ref,
    state_low_ref,
    inner_low_ref,
    step_low_ref,
    channel_grad_ref,
    conv_bc_grad_ref,
    head_grad_ref,
    step_rows_ref,
    bc_rows_ref,
    later,
    later_bc,
    leaving,
    step_total,
    dys,
    lows,
    reached,
    tailed,
    products,
):
    block = pl.program_id(0)

    @pl.when(block == 0)
    def _():
        later[PIECE:, :] = jnp.zeros((8, later.shape[1]), F32)
        later_bc[PIECE:, :] = jnp.zeros((8, later_bc.shape[1]), F32)
        conv_bc_grad_ref[...] = jnp.zeros(conv_bc_grad_ref.shape, F32)
        bc_rows_ref[...] = jnp.zeros(bc_rows_ref.shape, F32)
        leaving[...] = jnp.zeros(leaving.shape, F32)
        channel_grad_ref[...] = jnp.zeros(channel_grad_ref.shape, F32)
        head_grad_ref[...] = jnp.zeros(head_grad_ref.shape, F32)
        step_total[...] = jnp.zeros(step_total.shape, F32)

    channels = inner_ref.shape[1]
    row_at = lax.broadcasted_iota(jnp.int32, (PIECE, PIECE), 0)
    col_at = lax.broadcasted_iota(jnp.int32, (PIECE, PIECE), 1)
    upper_ones = (row_at <= col_at).astype(F32)
    first_half = lax.broadcasted_iota(jnp.int32, (PIECE, LANES), 1) < LANES // 2
    heads = head_table(channels, head_count)
    skips = head_rows(head_ref, heads)[2:3, :]
    side_all = token_ref[...].T
    inv_gate, pull = gate_columns(sums_ref)
    heads_twice = jnp.concatenate([heads, heads], axis=0)
    for piece in reversed(range(BLOCK // PIECE)):
        rows = slice(piece * PIECE, (piece + 1) * PIECE)
        side = side_all[rows]
        step_in = step_ref[rows, :]
        step = jnp.maximum(step_in, 0.0) + jnp.log1p(jnp.exp(-jnp.abs(step_in)))
        cum = cum_ref[rows, :]
        cum_t = cum.T
        same = (side[:, 0:1] == token_ref[0:1, rows]) & (row_at <= col_at)
        bias = jnp.where(same, 0.0, -1e30)
        reach = jnp.exp2(cum) * side[:, 4:5]
        tail = jnp.exp2(cum[PIECE - 1 : PIECE, :] - cum) * side[:, 5:6]
        wide = spread_heads(jnp.concatenate([step, reach, tail], axis=0), heads_twice)
        b_low = bc_ref[rows, 0:STATE]
        c_low = bc_ref[rows, STATE : 2 * STATE]
        scores = dot_last(b_low, c_low)
        score_grad = jnp.zeros((PIECE, PIECE), F32)
        masks = [None] + [side[:, 5 + k : 6 + k] for k in range(1, CONV)]
        for at in range(0, channels, LANES):
            lanes = slice(at, at + LANES)
            mixed = mixed_ref[rows, lanes].astype(F32)
            grad = grad_ref[rows, lanes].astype(F32)
            mixed_grad = inv_gate[rows] * (grad * row_ref[2:3, lanes] - mixed * pull[rows])
            dy_low = (mixed_grad * act_ref[rows, lanes].astype(F32)).astype(BF16)
            dys[:, lanes] = dy_low
            dy = dy_low.astype(F32)
            low = (wide[0:PIECE, lanes] * value_ref[rows, lanes].astype(F32)).astype(BF16)
            lows[:, lanes] = low
            reached[:, lanes] = (wide[PIECE : 2 * PIECE, lanes] * dy).astype(BF16)
            tailed[:, lanes] = (wide[2 * PIECE :, lanes] * low.astype(F32)).astype(BF16)
        leave = leaving[...]
        leave_low = leave.astype(BF16)
        enter_low = enter_ref[piece]
        kept = wide[2 * PIECE - 1 : 2 * PIECE, :]
        c_grad = dot_last(reached[...], enter_low)
        b_grad = dot_last(tailed[...], leave_low)
        from_states = dot(b_low, leave_low)
        kept_sum = kept * jnp.sum(enter_low.astype(F32) * leave, axis=0, keepdims=True)
        leaving[...] = kept * leave + dot_first(c_low, reached[...])
        for pair in range(channels // LANES):
            lanes = slice(pair * LANES, (pair + 1) * LANES)
            values = value_ref[rows, lanes].astype(F32)
            dy_low = dys[:, lanes]
            dy = dy_low.astype(F32)
            wide_step = wide[0:PIECE, lanes]
            low = lows[:, lanes]
            low_wide = low.astype(F32)
            from_state = wide[2 * PIECE :, lanes] * from_states[:, lanes]
            zero = jnp.zeros_like(low)
            own = jnp.concatenate(
                [jnp.where(first_half, dy_low, zero), jnp.where(first_half, zero, dy_low)], axis=0
            )
            weight_grads = dot_last(low, own)
            weights = []
            for at, head in enumerate((2 * pair, 2 * pair + 1)):
                gaps = (cum_t[head : head + 1, :] - cum[:, head : head + 1]) + bias
                decay = jnp.exp2(gaps)
                weights.append((scores * decay).astype(BF16))
                score_grad = score_grad + weight_grads[:, at * PIECE : (at + 1) * PIECE] * decay
            dx = dot(jnp.concatenate(weights, axis=1), own)
            dx = dx + from_state
            out = scan_ref[rows, lanes] - skips[:, lanes] * values
            last = jnp.sum(low_wide * from_state, axis=0, keepdims=True) + kept_sum[:, lanes]
            for at, product in enumerate(
                (dy * out - low_wide * dx, values * dx, jnp.broadcast_to(last, (16, LANES)))
            ):
                upper, rest = two_terms(product)
                products[2 * at * PIECE : 2 * at * PIECE + upper.shape[0], lanes] = upper
                products[2 * at * PIECE + upper.shape[0] : 2 * (at * PIECE + upper.shape[0]), lanes] = rest
            dvalue = wide_step * dx + skips[:, lanes] * dy
            dbefore = dvalue * slope_ref[rows, lanes].astype(F32)
            later[0:PIECE, lanes] = dbefore
            inner = inner_ref[rows, lanes].astype(F32)
            inner_grad = conv_x_ref[CONV - 1 : CONV, lanes] * dbefore
            channel_grad_ref[CONV - 1 : CONV, lanes] += jnp.sum(inner * dbefore, axis=0, keepdims=True)
            channel_grad_ref[CONV : CONV + 1, lanes] += jnp.sum(dbefore, axis=0, keepdims=True)
            channel_grad_ref[CONV + 1 : CONV + 2, lanes] += jnp.sum(dy * values, axis=0, keepdims=True)
            for k in range(1, CONV):
                shifted = later[k : k + PIECE, lanes] * masks[k]
                inner_grad = inner_grad + conv_x_ref[CONV - 1 - k : CONV - k, lanes] * shifted
                channel_grad_ref[CONV - 1 - k : CONV - k, lanes] += jnp.sum(
                    inner * shifted, axis=0, keepdims=True
                )
            inner_low_ref[rows, lanes] = inner_grad.astype(BF16)
        sums = dot_last(products[...], heads)
        row_sum = sums[0:PIECE] + sums[PIECE : 2 * PIECE]
        value_sum = sums[2 * PIECE : 3 * PIECE] + sums[3 * PIECE : 4 * PIECE]
        last_sum = sums[4 * PIECE : 4 * PIECE + 16] + sums[4 * PIECE + 16 : 4 * PIECE + 32]
        later[PIECE:, :] = later[0:8, :]
        grad_low = score_grad.astype(BF16)
        state_parts = (b_grad + dot(grad_low, c_low), c_grad + dot_first(grad_low, b_low))
        for at, state_part in enumerate(state_parts):
            lanes = slice(at * STATE, (at + 1) * STATE)
            dbefore = state_part * bc_slope_ref[rows, lanes]
            later_bc[0:PIECE, lanes] = dbefore
            state = state_ref[rows, lanes]
            state_grad = conv_bc_ref[CONV - 1 : CONV, lanes] * dbefore
            conv_bc_grad_ref[CONV - 1 : CONV, lanes] += jnp.sum(state * dbefore, axis=0, keepdims=True)
            conv_bc_grad_ref[CONV : CONV + 1, lanes] += jnp.sum(dbefore, axis=0, keepdims=True)
            for k in range(1, CONV):
                shifted = later_bc[k : k + PIECE, lanes] * masks[k]
                state_grad = state_grad + conv_bc_ref[CONV - 1 - k : CONV - k, lanes] * shifted
                conv_bc_grad_ref[CONV - 1 - k : CONV - k, lanes] += jnp.sum(
                    state * shifted, axis=0, keepdims=True
                )
            state_low_ref[rows, lanes] = state_grad.astype(BF16)
        later_bc[PIECE:, :] = later_bc[0:8, :]
        rate_grad = (
            jnp.dot(upper_ones, row_sum, precision=HIGH, preferred_element_type=F32) + last_sum[0:1, :]
        )
        coefficient = head_ref[1:2, :]
        step_grad = (value_sum + coefficient * rate_grad) / (1.0 + jnp.exp(-step_in))
        step_low_ref[rows, :] = step_grad.astype(BF16)
        head_grad_ref[0:1, :] += jnp.sum(step_grad, axis=0, keepdims=True)
        head_grad_ref[1:2, :] += jnp.sum(rate_grad * step, axis=0, keepdims=True) * coefficient
    step_total[...] += dot_first(step_low_ref[...], normed_ref[...])
    bc_rows_ref[...] += dot_first(state_low_ref[...], normed_ref[...])

    @pl.when(block == pl.num_programs(0) - 1)
    def _():
        step_rows_ref[...] = step_total[0 : step_rows_ref.shape[0], :]


def merge_kernel(
    core_ref,
    gate_low_ref,
    inner_low_ref,
    step_low_ref,
    state_low_ref,
    mixed_ref,
    normed_ref,
    sums_ref,
    w_gate_ref,
    w_value_ref,
    w_dt_ref,
    w_bc_ref,
    w_out_ref,
    row_ref,
    after_ref,
    sent_ref,
    kept_ref,
    gain_ref,
    wide_dt,
    gated,
):
    block = pl.program_id(0)
    last = pl.num_programs(0) - 1

    @pl.when(block == 0)
    def _():
        gain_ref[...] = jnp.zeros(gain_ref.shape, F32)
        wide_dt[...] = jnp.zeros(wide_dt.shape, BF16)
        wide_dt[0 : w_dt_ref.shape[0], :] = w_dt_ref[...]

    width = normed_ref.shape[1]
    total = dot_last(inner_low_ref[...], w_value_ref[...]) + dot_last(gate_low_ref[...], w_gate_ref[...])
    total = total + dot_last(state_low_ref[...], w_bc_ref[...]) + dot(step_low_ref[...], wide_dt[...])
    gain_ref[...] += jnp.sum((total * normed_ref[...].astype(F32)).reshape(-1, 8, width), axis=0)
    inv_gate, _ = gate_columns(sums_ref)
    for at in range(0, mixed_ref.shape[1], LANES):
        lanes = slice(at, at + LANES)
        normal = mixed_ref[:, lanes].astype(F32) * inv_gate
        gated[:, lanes] = (normal * row_ref[2:3, lanes]).astype(BF16)
    branch = dot(gated[...], w_out_ref[...]).astype(BF16)

    @pl.when(2 * block < last)
    def _():
        sent_ref[:, 0:width] = total.astype(BF16)
        sent_ref[:, width:] = branch

    @pl.when(2 * block > last)
    def _():
        kept_ref[:, 0:width] = total.astype(BF16)
        kept_ref[:, width:] = branch

    @pl.when(block == last)
    def _():
        gain = jnp.sum(gain_ref[...], axis=0, keepdims=True) / row_ref[0:1, :]
        gain_ref[...] = jnp.broadcast_to(gain, gain_ref.shape)


def pack_kernel(
    head_count,
    core_ref,
    bc_rows_ref,
    step_rows_ref,
    channel_ref,
    gate_gain_ref,
    gain_ref,
    conv_bc_ref,
    head_ref,
    sent_ref,
    kept_ref,
    own_ref,
):
    core = core_ref[0]
    channels = channel_ref.shape[1]
    states, width = bc_rows_ref.shape
    folds = width // channels
    groups = (kept_ref.shape[0] - 16) // (OWN_BC * folds)
    for which, ref in ((1 - core, sent_ref), (core, kept_ref)):
        for group in range(groups):
            found = bc_rows_ref[pl.ds(pl.multiple_of((2 * group + which) * OWN_BC, 8), OWN_BC), :].astype(BF16)
            for fold in range(folds):
                at = (group * folds + fold) * OWN_BC
                ref[at : at + OWN_BC, :] = found[:, fold * channels : (fold + 1) * channels]
        shared = [gain_ref[0:1, fold * channels : (fold + 1) * channels] for fold in range(folds)]
        conv = conv_bc_ref[0 : CONV + 1, :]
        shared.append(jnp.concatenate([conv, jnp.zeros((CONV + 1, channels - states), F32)], axis=1))
        shared.append(jnp.zeros((16 - folds - CONV - 1, channels), F32))
        ref[ref.shape[0] - 16 :, :] = jnp.concatenate(shared).astype(BF16)
    own_ref[...] = jnp.zeros(own_ref.shape, F32)
    for fold in range(folds):
        own_ref[16 * fold : 16 * fold + 16, :] = step_rows_ref[:, fold * channels : (fold + 1) * channels]
    at = 16 * folds
    own_ref[at : at + CONV + 1, :] = channel_ref[0 : CONV + 1, :]
    own_ref[at + CONV + 1 : at + CONV + 2, :] = jnp.sum(gate_gain_ref[...], axis=0, keepdims=True)
    skips = sum_heads(channel_ref[...], head_table(channels, head_count))
    own_ref[at + CONV + 2 : at + CONV + 4, 0:LANES] = head_ref[0:2, :]
    own_ref[at + CONV + 4 : at + CONV + 5, 0:LANES] = skips[CONV + 1 : CONV + 2, :]


def unpack_kernel(
    one_ref,
    two_ref,
    pre_gain_ref,
    bc_ref,
    dt_ref,
    conv_x_ref,
    bias_x_ref,
    conv_bc_ref,
    bias_bc_ref,
    dt_bias_ref,
    a_log_ref,
    d_skip_ref,
    gate_gain_ref,
    total,
):
    total[...] = one_ref[...].astype(F32) + two_ref[...].astype(F32)
    channels = total.shape[1]
    own_bc, width = bc_ref.shape
    folds = width // channels
    for fold in range(folds):
        bc_ref[:, fold * channels : (fold + 1) * channels] = total[fold * own_bc : (fold + 1) * own_bc, :]
    at = folds * own_bc
    pre_gain_ref[...] = jnp.concatenate([total[at + fold : at + fold + 1, :] for fold in range(folds)], axis=1).reshape(-1)
    at += folds
    states = conv_bc_ref.shape[1]
    conv_bc_ref[...] = total[at : at + CONV, 0:states]
    bias_bc_ref[...] = total[at + CONV : at + CONV + 1, 0:states].reshape(-1)
    at += 16 - folds
    count = dt_ref.shape[0]
    for fold in range(folds):
        dt_ref[:, fold * channels : (fold + 1) * channels] = total[at + 16 * fold : at + 16 * fold + count, :]
    at += 16 * folds
    conv_x_ref[...] = total[at : at + CONV, :]
    bias_x_ref[...] = total[at + CONV : at + CONV + 1, :].reshape(-1)
    gate_gain_ref[...] = total[at + CONV + 1 : at + CONV + 2, :].reshape(-1)
    at += CONV + 2
    for row, ref in enumerate((dt_bias_ref, a_log_ref, d_skip_ref)):
        ref[...] = total[at + row : at + row + 1, 0:LANES].reshape(-1)[0 : ref.shape[0]]


def hidden_kernel(rank_ref, hidden_ref, cotan_ref, kept_ref, got_ref, row_ref, out_ref, grad_ref):
    width = hidden_ref.shape[1]
    hidden = hidden_ref[...].astype(F32)
    branch = kept_ref[:, width:].astype(F32) + got_ref[:, width:].astype(F32)
    out_ref[...] = (hidden + branch).astype(BF16)
    inv_rms = lax.rsqrt(jnp.mean(hidden * hidden, axis=-1, keepdims=True) + EPS)
    scaled = (kept_ref[:, 0:width].astype(F32) + got_ref[:, 0:width].astype(F32)) * row_ref[0:1, :]
    pull = inv_rms * inv_rms * jnp.mean(scaled * hidden, axis=-1, keepdims=True)
    grad_ref[...] = cotan_ref[...].astype(F32) + inv_rms * (scaled - hidden * pull)


def pass_kernel(*refs):
    pass


def finish_kernel(which_ref, part_ref, after_ref, out_ref):
    out_ref[...] = part_ref[...].astype(F32)


def finish_pair_kernel(which_ref, part_ref, after_ref, *refs):
    out_ref, gate_ref = refs[-2:]
    rows, width = out_ref.shape
    channels = gate_ref.shape[1]
    for at in range(width // channels):
        out_ref[:, at * channels : (at + 1) * channels] = part_ref[at * rows : (at + 1) * rows, :].astype(F32)
    gate_ref[...] = part_ref[gate_ref.shape[0] :, :].astype(F32)


def finish_into_kernel(which_ref, part_ref, after_ref, whole_ref, out_ref):
    finish_kernel(which_ref, part_ref, after_ref, out_ref)


def split_kernel(which_ref, sent_one, sent_two, kept_one, kept_two, sent_ref, kept_ref):
    sent_ref[...] = (sent_one[...].astype(F32) + sent_two[...].astype(F32)).astype(BF16)
    kept_ref[...] = (kept_one[...].astype(F32) + kept_two[...].astype(F32)).astype(BF16)


def join_kernel(which_ref, own_ref, got_ref, own_extra_ref, got_extra_ref, out_ref):
    which = which_ref[0]
    rows = own_ref.shape[0]
    extra_rows = own_extra_ref.shape[0]
    out_ref[pl.ds(pl.multiple_of(which * rows, 16), rows), :] = own_ref[...]
    out_ref[pl.ds(pl.multiple_of((1 - which) * rows, 16), rows), :] = got_ref[...]
    extra = own_extra_ref[...].astype(F32) + got_extra_ref[...].astype(F32)
    at = 2 * rows
    out_ref[at : at + extra_rows, :] = extra.astype(BF16)
    shared = slice(SHARED_AT, SHARED_AT + 16)
    out_ref[at + SHARED_AT : at + SHARED_AT + 16, :] = own_extra_ref[shared, :]
    out_ref[at + extra_rows : at + extra_rows + 16, :] = got_extra_ref[shared, :]
    out_ref[at + extra_rows + 16 :, :] = jnp.zeros((48, out_ref.shape[1]), BF16)


def rider_kernel(core_ref, own_ref, got_ref, out_ref):
    rows = out_ref.shape[0]
    out_ref[...] = (own_ref[0:rows, :].astype(F32) + got_ref[0:rows, :].astype(F32)).astype(BF16)
    shared, second = slice(SHARED_AT, SHARED_AT + 16), slice(rows, rows + 16)
    own, near = own_ref[shared, :].astype(F32), own_ref[second, :].astype(F32)
    other, far = got_ref[shared, :].astype(F32), got_ref[second, :].astype(F32)
    is_first = core_ref[0] == 0
    total = (own + jnp.where(is_first, other, near)) + (jnp.where(is_first, near, other) + far)
    out_ref[shared, :] = total.astype(BF16)


def whole(shape):
    return pl.BlockSpec(shape, lambda i: (0,) * len(shape), pipeline_mode=pl.Buffered(1))


def no_cost():
    return pl.CostEstimate(flops=0, bytes_accessed=0, transcendentals=0)


def params():
    return pltpu.CompilerParams(vmem_limit_bytes=60 << 20)


def run_tables(segments, pre_gain, bias_x, gate_gain, bias_bc, dt_bias, a_log, d_skip):
    inputs = (segments, pre_gain, bias_x, gate_gain, bias_bc, dt_bias, a_log, d_skip)
    in_vmem = pl.BlockSpec(memory_space=pltpu.VMEM)
    return pl.pallas_call(
        table_kernel,
        in_specs=[in_vmem] * len(inputs),
        out_specs=[in_vmem] * 3,
        out_shape=[
            jax.ShapeDtypeStruct((16, segments.size), F32),
            jax.ShapeDtypeStruct((8, pre_gain.shape[0]), F32),
            jax.ShapeDtypeStruct((8, LANES), F32),
        ],
        compiler_params=params(),
        name="tables",
    )(*inputs)


def in_place():
    return pl.BlockSpec(memory_space=pl.ANY)


def run_forward(hidden_in, cotangent, weights, tables, tokens):
    rows, width = hidden_in.shape
    channels = weights[0].shape[1]
    states = weights[2].shape[1]
    constants = (*weights, *tables)

    def block(columns):
        return pl.BlockSpec((BLOCK, columns), lambda i: (i, 0))

    def out(columns, kind=BF16):
        return jax.ShapeDtypeStruct((rows, columns), kind)

    return pl.pallas_call(
        forward_kernel,
        grid=(rows // BLOCK,),
        in_specs=[block(width), block(width)]
        + [whole(array.shape) for array in constants]
        + [pl.BlockSpec((tokens.shape[0], BLOCK), lambda i: (0, i))],
        out_specs=[block(width)]
        + [block(channels)] * 8
        + [block(LANES)] * 2
        + [block(states)] * 3
        + [
            pl.BlockSpec((BLOCK // PIECE, STATE, channels), lambda i: (i, 0, 0)),
            pl.BlockSpec((8, BLOCK), lambda i: (0, i)),
        ],
        out_shape=[
            out(width),
            out(channels),
            out(channels),
            out(channels),
            out(channels),
            out(channels, F32),
            out(channels),
            out(channels),
            out(channels),
            out(LANES, F32),
            out(LANES, F32),
            out(states),
            out(states, F32),
            out(states, F32),
            jax.ShapeDtypeStruct((rows // PIECE, STATE, channels), BF16),
            jax.ShapeDtypeStruct((8, rows), F32),
        ],
        scratch_shapes=[
            pltpu.VMEM((BLOCK + 8, channels), F32),
            pltpu.VMEM((BLOCK + 8, states), F32),
            pltpu.VMEM((STATE, channels), F32),
            pltpu.VMEM((LANES, width), BF16),
            pltpu.VMEM((BLOCK, channels), F32),
            pltpu.VMEM((BLOCK, channels), F32),
            pltpu.VMEM((PIECE, channels), BF16),
        ],
        compiler_params=params(),
        cost_estimate=no_cost(),
        name="forward",
    )(hidden_in, cotangent, *constants, tokens)


def scalar_spec():
    return pl.BlockSpec(memory_space=pltpu.SMEM)


def half_shapes(rows, columns):
    return [jax.ShapeDtypeStruct((rows // 2, columns), BF16)] * 2


def run_gate(low, forward, sums, rows_table, cotangent, normed):
    rows, channels = forward[0].shape
    width = cotangent.shape[1]

    def block(columns):
        return pl.BlockSpec((BLOCK, columns), lambda i: (i, 0))

    halves = [jax.ShapeDtypeStruct((width // 2 + width // 2, channels), BF16)] * 2
    out = pl.pallas_call(
        gate_kernel,
        grid=(rows // BLOCK,),
        in_specs=[scalar_spec()]
        + [block(channels)] * 3
        + [pl.BlockSpec((8, BLOCK), lambda i: (0, i)), whole(rows_table.shape), block(width), block(width)],
        out_specs=[block(channels), whole((8, channels))] + [whole(half.shape) for half in halves],
        out_shape=[jax.ShapeDtypeStruct((rows, channels), BF16), jax.ShapeDtypeStruct((8, channels), F32)]
        + halves,
        scratch_shapes=[
            pltpu.VMEM((BLOCK, channels), BF16),
            pltpu.VMEM((channels, width), F32),
            pltpu.VMEM((width, channels), F32),
        ],
        compiler_params=params(),
        cost_estimate=no_cost(),
        name="gate",
    )(low, *forward, sums, rows_table, cotangent, normed)
    return out[:2], out[2:]


def run_weight(low, normed, grad, after):
    rows, width = normed.shape
    channels = grad.shape[1]
    size = 2 * BLOCK
    halves = half_shapes(width, channels)
    return pl.pallas_call(
        weight_kernel,
        grid=(rows // size,),
        in_specs=[
            scalar_spec(),
            pl.BlockSpec((size, width), lambda i: (i, 0)),
            pl.BlockSpec((size, channels), lambda i: (i, 0)),
            in_place(),
        ],
        out_specs=[whole(half.shape) for half in halves],
        out_shape=halves,
        scratch_shapes=[pltpu.VMEM((width, channels), F32)],
        compiler_params=params(),
        cost_estimate=no_cost(),
        name="weight",
    )(low, normed, grad, after)


def run_backward(gate_inputs, sums, rows_table, by_channel, step_in, cum, bc_low, enter, normed, by_state, tables, after, head_count):
    rows, channels = by_channel[0].shape
    width = normed.shape[1]
    count = rows // BLOCK
    states = bc_low.shape[1]
    conv_x, conv_bc, head_values, tokens = tables

    def block(columns):
        return pl.BlockSpec((BLOCK, columns), lambda i: (count - 1 - i, 0))

    def low_rows(columns):
        return jax.ShapeDtypeStruct((rows, columns), BF16)

    totals = [
        jax.ShapeDtypeStruct(shape, F32)
        for shape in ((8, channels), (8, states), (8, LANES), (16, width), (states, width))
    ]
    return pl.pallas_call(
        functools.partial(backward_kernel, head_count),
        grid=(count,),
        in_specs=[block(channels)] * 3
        + [pl.BlockSpec((8, BLOCK), lambda i: (0, count - 1 - i)), whole(rows_table.shape)]
        + [block(channels)] * 4
        + [block(LANES), block(LANES), block(states)]
        + [pl.BlockSpec((BLOCK // PIECE, STATE, channels), lambda i: (count - 1 - i, 0, 0))]
        + [block(width), block(states), block(states)]
        + [whole(conv_x.shape), whole(conv_bc.shape), whole(head_values.shape)]
        + [pl.BlockSpec((tokens.shape[0], BLOCK), lambda i: (0, count - 1 - i)), in_place()],
        out_specs=[block(states), block(channels), block(LANES)]
        + [whole(shape.shape) for shape in totals],
        out_shape=[low_rows(states), low_rows(channels), low_rows(LANES)] + totals,
        scratch_shapes=[
            pltpu.VMEM((PIECE + 8, channels), F32),
            pltpu.VMEM((PIECE + 8, states), F32),
            pltpu.VMEM((STATE, channels), F32),
            pltpu.VMEM((LANES, width), F32),
            pltpu.VMEM((PIECE, channels), BF16),
            pltpu.VMEM((PIECE, channels), BF16),
            pltpu.VMEM((PIECE, channels), BF16),
            pltpu.VMEM((PIECE, channels), BF16),
            pltpu.VMEM((4 * PIECE + 32, channels), BF16),
        ],
        compiler_params=params(),
        cost_estimate=no_cost(),
        name="backward",
    )(*gate_inputs, sums, rows_table, *by_channel, step_in, cum, bc_low, enter, normed, *by_state, conv_x, conv_bc, head_values, tokens, after)


def run_merge(core, blocked, sums, weights, rows_table, after, ranks):
    normed = blocked[-1]
    rows, width = normed.shape
    channels = weights[0].shape[1]
    size = rows // ranks
    half = ranks // 2

    def rank_at(i, c):
        return jnp.where(i < half, 2 * i + 1 - c[0], 2 * (i - half) + c[0])

    def block(columns):
        return pl.BlockSpec((size, columns), lambda i, c: (rank_at(i, c), 0))

    def constant(shape):
        return pl.BlockSpec(shape, lambda i, c: (0,) * len(shape), pipeline_mode=pl.Buffered(1))

    out = jax.ShapeDtypeStruct((rows // 2, 2 * width), BF16)
    return pl.pallas_call(
        merge_kernel,
        grid_spec=pltpu.PrefetchScalarGridSpec(
            num_scalar_prefetch=1,
            grid=(ranks,),
            in_specs=[block(array.shape[1]) for array in blocked]
            + [pl.BlockSpec((8, size), lambda i, c: (0, rank_at(i, c)))]
            + [constant(array.shape) for array in (*weights, rows_table)]
            + [in_place()],
            out_specs=[
                pl.BlockSpec((size, 2 * width), lambda i, c: (jnp.minimum(i, half - 1), 0)),
                pl.BlockSpec((size, 2 * width), lambda i, c: (jnp.maximum(i - half, 0), 0)),
                constant((8, width)),
            ],
            scratch_shapes=[pltpu.VMEM((LANES, width), BF16), pltpu.VMEM((size, channels), BF16)],
        ),
        out_shape=[out, out, jax.ShapeDtypeStruct((8, width), F32)],
        compiler_params=params(),
        cost_estimate=no_cost(),
        name="merge",
    )(core, *blocked, sums, *weights, rows_table, after)


def run_pack(core, bc_rows, step_rows, channel_grads, gain_rows, gain, conv_bc_grads, head_grads, head_count):
    states, width = bc_rows.shape
    channels = channel_grads.shape[1]
    folds = width // channels
    in_vmem = pl.BlockSpec(memory_space=pltpu.VMEM)
    shared = jax.ShapeDtypeStruct((states // 2 * folds + 16, channels), BF16)
    return pl.pallas_call(
        functools.partial(pack_kernel, head_count),
        in_specs=[scalar_spec()] + [in_vmem] * 7,
        out_specs=[in_vmem] * 3,
        out_shape=[shared, shared, jax.ShapeDtypeStruct((16 * folds + 16, channels), F32)],
        compiler_params=params(),
        cost_estimate=no_cost(),
        name="pack",
    )(core, bc_rows, step_rows, channel_grads, gain_rows, gain, conv_bc_grads, head_grads)


def run_unpack(one, two, width, states, head_count):
    rows, channels = one.shape
    last = two.shape[0] // rows - 1
    in_vmem = pl.BlockSpec(memory_space=pltpu.VMEM)
    shapes = (
        (width,),
        (OWN_BC, width),
        (head_count, width),
        (CONV, channels),
        (channels,),
        (CONV, states),
        (states,),
        (head_count,),
        (head_count,),
        (head_count,),
        (channels,),
    )
    return pl.pallas_call(
        unpack_kernel,
        grid=(1,),
        in_specs=[
            pl.BlockSpec((rows, channels), lambda i: (0, 0)),
            pl.BlockSpec((rows, channels), lambda i: (last, 0)),
        ],
        out_specs=[pl.BlockSpec(shape, lambda i, rank=len(shape): (0,) * rank) for shape in shapes],
        out_shape=[jax.ShapeDtypeStruct(shape, F32) for shape in shapes],
        scratch_shapes=[pltpu.VMEM(one.shape, F32)],
        compiler_params=params(),
        cost_estimate=no_cost(),
        name="unpack",
    )(one, two)


def run_hidden(rank, hidden_in, cotangent, kept, got, rows_table):
    own_rows = kept.shape[0]
    width = hidden_in.shape[1]
    count = 2
    size = own_rows // count

    def own(columns):
        return pl.BlockSpec((size, columns), lambda i, r: (r[0] * count + i, 0))

    def block(columns):
        return pl.BlockSpec((size, columns), lambda i, r: (i, 0))

    return pl.pallas_call(
        hidden_kernel,
        grid_spec=pltpu.PrefetchScalarGridSpec(
            num_scalar_prefetch=1,
            grid=(count,),
            in_specs=[
                own(width),
                own(width),
                block(2 * width),
                block(2 * width),
                pl.BlockSpec(rows_table.shape, lambda i, r: (0, 0)),
            ],
            out_specs=[block(width), block(width)],
        ),
        out_shape=[
            jax.ShapeDtypeStruct((own_rows, width), BF16),
            jax.ShapeDtypeStruct((own_rows, width), F32),
        ],
        compiler_params=params(),
        cost_estimate=no_cost(),
        name="hidden",
    )(rank, hidden_in, cotangent, kept, got, rows_table)


def run_pass(arrays, after):
    count = len(arrays)
    return pl.pallas_call(
        pass_kernel,
        in_specs=[in_place()] * (count + 1),
        out_specs=[in_place()] * count,
        out_shape=[jax.ShapeDtypeStruct(array.shape, array.dtype) for array in arrays],
        input_output_aliases={at: at for at in range(count)},
        cost_estimate=no_cost(),
        name="pass",
    )(*arrays, after)


def run_finish(which, part, after, rows, into=None):
    columns = part.shape[1]
    count = 2
    size = rows // count
    inputs = [part, after] + ([] if into is None else [into])
    return pl.pallas_call(
        finish_kernel if into is None else finish_into_kernel,
        grid_spec=pltpu.PrefetchScalarGridSpec(
            num_scalar_prefetch=1,
            grid=(count,),
            in_specs=[pl.BlockSpec((size, columns), lambda i, w: (i, 0))] + [in_place()] * (len(inputs) - 1),
            out_specs=pl.BlockSpec((size, columns), lambda i, w: (w[0] * count + i, 0)),
        ),
        out_shape=jax.ShapeDtypeStruct((2 * rows, columns), F32),
        input_output_aliases={} if into is None else {3: 0},
        compiler_params=params(),
        cost_estimate=no_cost(),
        name="finish",
    )(jnp.reshape(which, (1,)), *inputs)


def run_finish_pair(which, part, after, out_shape, gate_shape, into=()):
    out_rows, out_columns = out_shape
    gate_rows, gate_columns = gate_shape
    return pl.pallas_call(
        finish_pair_kernel,
        grid_spec=pltpu.PrefetchScalarGridSpec(
            num_scalar_prefetch=1,
            grid=(1,),
            in_specs=[pl.BlockSpec((gate_rows, gate_columns), lambda i, w: (0, 0))]
            + [in_place()] * (1 + len(into)),
            out_specs=[
                pl.BlockSpec((out_rows // 2, out_columns), lambda i, w: (w[0], 0)),
                pl.BlockSpec((gate_rows // 2, gate_columns), lambda i, w: (w[0], 0)),
            ],
        ),
        out_shape=[jax.ShapeDtypeStruct(out_shape, F32), jax.ShapeDtypeStruct(gate_shape, F32)],
        input_output_aliases={3 + at: at for at in range(len(into))},
        compiler_params=params(),
        cost_estimate=no_cost(),
        name="finish_pair",
    )(jnp.reshape(which, (1,)), part, after, *into)


def run_split(one, two, which):
    half, columns = one.shape[0] // 2, one.shape[1]
    count = 2
    size = half // count
    sent = pl.BlockSpec((size, columns), lambda i, w: ((1 - w[0]) * count + i, 0))
    kept = pl.BlockSpec((size, columns), lambda i, w: (w[0] * count + i, 0))
    out = pl.BlockSpec((size, columns), lambda i, w: (i, 0))
    return pl.pallas_call(
        split_kernel,
        grid_spec=pltpu.PrefetchScalarGridSpec(
            num_scalar_prefetch=1,
            grid=(count,),
            in_specs=[sent, sent, kept, kept],
            out_specs=[out, out],
        ),
        out_shape=[jax.ShapeDtypeStruct((half, columns), BF16)] * 2,
        compiler_params=params(),
        cost_estimate=no_cost(),
        name="split",
    )(jnp.reshape(which.astype(jnp.int32), (1,)), one, two, one, two)


def run_join(which, own, got, extra_rows):
    rows = own.shape[0] - extra_rows
    columns = own.shape[1]
    matrix = pl.BlockSpec((rows, columns), lambda i, w: (0, 0))
    extra = pl.BlockSpec((extra_rows, columns), lambda i, w: (rows // extra_rows, 0))
    shape = (2 * rows + extra_rows + 64, columns)
    return pl.pallas_call(
        join_kernel,
        grid_spec=pltpu.PrefetchScalarGridSpec(
            num_scalar_prefetch=1,
            grid=(1,),
            in_specs=[matrix, matrix, extra, extra],
            out_specs=pl.BlockSpec(shape, lambda i, w: (0, 0)),
        ),
        out_shape=jax.ShapeDtypeStruct(shape, BF16),
        compiler_params=params(),
        cost_estimate=no_cost(),
        name="join",
    )(jnp.reshape(which, (1,)), own, got, own, got)


def run_rider(core, own, got, rows):
    columns = own.shape[1]
    held = rows + 64
    last = pl.BlockSpec((held, columns), lambda i: (own.shape[0] // held - 1, 0))
    return pl.pallas_call(
        rider_kernel,
        grid=(1,),
        in_specs=[scalar_spec(), last, last],
        out_specs=pl.BlockSpec((rows, columns), lambda i: (0, 0)),
        out_shape=jax.ShapeDtypeStruct((rows, columns), BF16),
        compiler_params=params(),
        cost_estimate=no_cost(),
        name="rider",
    )(core, own, got)


def swap(array, axis, bit):
    size = lax.axis_size(axis)
    return lax.ppermute(array, axis, [(source, source ^ bit) for source in range(size)])


def axis_bits(axis):
    size = lax.axis_size(axis)
    return [1 << place for place in range(size.bit_length() - 1)]


def half_of(array, which):
    half = array.shape[0] // 2
    return lax.dynamic_slice_in_dim(array, which * half, half, 0)


def sum_tensor(array):
    for bit in axis_bits("tensor"):
        array = array + swap(array, "tensor", bit)
    return array


def dp_bits(step):
    bits = axis_bits("dp")
    swapped = [bits[1], bits[0]] + bits[2:]
    return bits[step], swapped[step]


def own_bit(step):
    first, second = dp_bits(step)
    place = lax.axis_index("dp").astype(jnp.int32)
    core = lax.axis_index("tensor") % 2
    return jnp.where(core == 0, (place // first) % 2, (place // second) % 2)


def dp_pairs(step):
    ranks = lax.axis_size("tensor")
    pairs = dp_bits(step)
    return [
        (at * ranks + rank, (at ^ pairs[rank % 2]) * ranks + rank)
        for at in range(lax.axis_size("dp"))
        for rank in range(ranks)
    ]


def in_order(which, own, got):
    place = lax.broadcasted_iota(jnp.int32, (2, 1, 1), 0)
    return jnp.where(place == which, own[None], got[None])


def sum_steps(sent, kept, rider=None, own=None):
    axes = ("dp", "tensor")
    steps = range(1, len(axis_bits("dp")))
    terms = [kept]
    got = yield sent, axes, dp_pairs(0)

    def total(which):
        return sum(half_of(term, which).astype(F32) for term in terms)

    for step in steps:
        which = own_bit(step)
        terms.append(got)
        sent = total(1 - which).astype(BF16)
        terms = [half_of(term, which) for term in terms]
        got = yield sent, axes, dp_pairs(step)
    part = sum((term.astype(F32) for term in terms), got.astype(F32)).astype(BF16)
    extra = 0
    for step in reversed((0, *steps)):
        if step == 1 and rider is not None:
            rows = rider().astype(BF16)
            extra = rows.shape[0]
            part = jnp.concatenate([part, rows])
        if step == 0 and own is not None:
            own.append(part)
        got = yield part, axes, dp_pairs(step)
        if step and extra:
            part = run_join(own_bit(step), part, got, extra)
        elif step:
            part = in_order(own_bit(step), part, got).reshape(2 * part.shape[0], -1)
    if extra:
        core = (lax.axis_index("tensor") % 2).astype(jnp.int32)
        extra = run_rider(jnp.reshape(core, (1,)), part, got, extra)
    return own_bit(0), part, got, extra


def rest_steps(rows):
    axes = ("dp", "tensor")
    for step in range(2, len(axis_bits("dp"))):
        got = yield rows, axes, dp_pairs(step)
        total = rows.astype(F32) + got.astype(F32)
        last, rows = (rows, got), total.astype(BF16)
    return last


def both_steps(sent, kept):
    size = lax.axis_size("tensor")
    rank = lax.axis_index("tensor")
    got = yield sent, "tensor", [(i, i ^ 1) for i in range(size)]
    for bit in axis_bits("tensor")[1:]:
        sent, kept = run_split(kept, got, (rank // bit) % 2)
        got = yield sent, "tensor", [(i, i ^ bit) for i in range(size)]
    return kept, got


def small_steps(sent, kept, own):
    size = lax.axis_size("tensor")
    rank = lax.axis_index("tensor")
    got = yield sent, "tensor", [(i, i ^ 1) for i in range(size)]
    total = kept.astype(F32) + got.astype(F32)
    for bit in axis_bits("tensor")[1:]:
        which = (rank // bit) % 2
        shared = lax.reduce_precision(total[-16:], 8, 7).astype(BF16)
        rows = total[:-16]
        got = yield jnp.concatenate([half_of(rows, 1 - which).astype(BF16), shared]), "tensor", [
            (i, i ^ bit) for i in range(size)
        ]
        total = jnp.concatenate([half_of(rows, which), shared.astype(F32)]) + got.astype(F32)
    return jnp.concatenate([total, own])


class Order:
    def __init__(self, last):
        self.last = last
        self.waiting = {}
        self.flying = {}
        self.arrived = {}
        self.results = {}

    def advance(self, name, steps, got):
        try:
            request = steps.send(got)
            self.waiting[name] = (steps, request)
            self.last = request[0]
        except StopIteration as end:
            self.results[name] = end.value

    def add(self, name, steps):
        last = self.last
        self.advance(name, steps, None)
        self.last = last

    def go(self, *names):
        for name in names:
            if name in self.waiting:
                steps, (sent, axis, moves) = self.waiting.pop(name)
                self.flying[name] = (steps, lax.ppermute(sent, axis, moves))

    def arrive(self, *names):
        found = [(name, *self.flying.pop(name)) for name in names if name in self.flying]
        if found:
            passed = run_pass([got for _, _, got in found], self.last)
            self.last = passed[0]
            for (name, steps, _), got in zip(found, passed):
                self.arrived[name] = (steps, got)

    def take(self, *names):
        for name in names:
            if name in self.arrived:
                steps, got = self.arrived.pop(name)
                self.advance(name, steps, got if got is self.last else self.hold(got))
                if name in self.waiting:
                    self.last = self.waiting[name][1][0]

    def land(self, *names):
        self.arrive(*names)
        self.take(*names)

    def hold(self, array):
        return run_pass([array], self.last)[0]

    def step(self, *names):
        for name in names:
            self.land(name)
            self.go(name)

    def until(self, name, found):
        while not found:
            self.step(name)
        return found[0]

    def result(self, name):
        while name not in self.results:
            self.go(name)
            self.land(name)
        return self.results[name]


def shards(
    hidden_in,
    pre_gain,
    w_gate,
    w_value,
    w_bc,
    w_dt,
    conv_x,
    conv_x_bias,
    conv_bc,
    conv_bc_bias,
    dt_bias,
    a_log,
    d_skip,
    gate_gain,
    w_out,
    cotangent,
    segments,
):
    row_count, width = hidden_in.shape
    channels = w_gate.shape[1]
    head_count = dt_bias.shape[0]
    head_width = channels // head_count
    ranks = lax.axis_size("tensor")
    my_rank = lax.axis_index("tensor")
    own_rows = row_count // ranks
    row_start = my_rank * own_rows
    pair_width = w_bc.shape[1] // ranks
    low = jnp.reshape(own_bit(0), (1,))
    w_dt_rows = w_dt.T
    tokens, rows_table, head_values = run_tables(
        segments, pre_gain, conv_x_bias, gate_gain, conv_bc_bias, dt_bias, a_log, d_skip
    )
    (
        normed,
        mixed,
        act,
        turn,
        gated_grad,
        scan,
        values,
        slope,
        inner_pre,
        step_in,
        cum,
        bc_low,
        bc_slope,
        state_pre,
        enter,
        sums,
    ) = run_forward(
        hidden_in,
        cotangent,
        (w_gate, w_value, w_bc, w_dt_rows, w_out),
        (conv_x, conv_bc, rows_table, head_values),
        tokens,
    )
    sums = sum_tensor(sums) / (channels * ranks)
    (gate_low, gain_rows), halves = run_gate(
        low, (mixed, turn, gated_grad), sums, rows_table, cotangent, normed
    )
    order = Order(gate_low)
    first_own, second_own = [], []
    order.add("first", sum_steps(*halves, lambda: order.result("small"), first_own))
    order.go("first")
    (
        state_low,
        inner_low,
        step_low,
        channel_grads,
        conv_bc_grads,
        head_grads,
        step_rows,
        bc_rows,
    ) = run_backward(
        (mixed, gated_grad, act),
        sums,
        rows_table,
        (scan, values, slope, inner_pre),
        step_in,
        cum,
        bc_low,
        enter,
        normed,
        (bc_slope, state_pre),
        (conv_x, conv_bc, head_values, tokens),
        halves[0],
        head_count,
    )
    order.last = inner_low
    order.step("first")
    sent, kept = run_weight(low, normed, inner_low, order.last)
    order.last = kept
    order.step("first")
    order.add("second", sum_steps(order.hold(sent), kept, None, second_own))
    order.go("second")
    core = jnp.reshape((my_rank % 2).astype(jnp.int32), (1,))
    both_sent, both_kept, gain = run_merge(
        core,
        (gate_low, inner_low, step_low, state_low, mixed, normed),
        sums,
        (w_gate, w_value, w_dt_rows, w_bc, w_out),
        rows_table,
        order.last,
        ranks,
    )
    order.last = both_kept
    order.land("second", "first")
    order.go("second", "first")
    small = run_pack(
        core, bc_rows, step_rows, channel_grads, gain_rows, order.hold(gain), conv_bc_grads, head_grads, head_count
    )
    order.add("small", small_steps(*small))
    order.go("small")
    order.add("both", both_steps(order.hold(both_sent), both_kept))
    order.go("both")
    order.step("small")
    order.land("small")
    order.land("second", "first")
    order.go("second", "first")
    order.step("second")
    order.step("both")
    order.land("second")
    order.land("first")
    order.go("second", "first")
    order.step("second")
    which = own_bit(0)
    sums_first = run_finish_pair(which, order.until("first", first_own), order.last, w_out.shape, w_gate.shape)
    order.last = sums_first[0]
    own = order.until("second", second_own)
    w_value_sum = run_finish(which, own, order.last, own.shape[0])
    order.last = w_value_sum
    _, _, got, rows = order.result("first")
    order.add("rest", rest_steps(rows))
    order.go("rest")
    w_out_sum, w_gate_sum = run_finish_pair(
        1 - which, got, order.last, w_out.shape, w_gate.shape, sums_first
    )
    order.last = w_out_sum
    kept, got = order.result("both")
    block_out, hidden_grad = run_hidden(
        jnp.reshape(my_rank.astype(jnp.int32), (1,)), hidden_in, cotangent, kept, got, rows_table
    )
    order.last = hidden_grad
    one, two = order.result("rest")
    small = run_unpack(one, two, width, w_bc.shape[1], head_count)
    order.last = small[0]
    _, own, got, _ = order.result("second")
    w_value_sum = run_finish(1 - which, got, order.last, own.shape[0], w_value_sum)
    (
        pre_gain_grad,
        w_bc_rows,
        dt_rows,
        conv_x_grad,
        conv_x_bias_grad,
        conv_bc_grad,
        conv_bc_bias_grad,
        dt_bias_grad,
        a_log_grad,
        d_skip_grad,
        gate_gain_grad,
    ) = small
    return (
        block_out,
        hidden_grad,
        pre_gain_grad,
        w_gate_sum,
        w_value_sum,
        w_bc_rows.T,
        dt_rows.T,
        conv_x_grad,
        conv_x_bias_grad,
        conv_bc_grad,
        conv_bc_bias_grad,
        dt_bias_grad,
        a_log_grad,
        d_skip_grad,
        gate_gain_grad,
        w_out_sum,
    )


def solution(mesh):
    in_specs = (
        P("dp", None),
        P(),
        P(None, "tensor"),
        P(None, "tensor"),
        P(),
        P(None, "tensor"),
        P(None, "tensor"),
        P("tensor"),
        P(),
        P(),
        P("tensor"),
        P("tensor"),
        P("tensor"),
        P("tensor"),
        P("tensor", None),
        P("dp", None),
        P("dp", None),
    )
    out_specs = (
        P(("dp", "tensor"), None),
        P(("dp", "tensor"), None),
        P(),
        P(None, "tensor"),
        P(None, "tensor"),
        P(None, "tensor"),
        P(None, "tensor"),
        P(None, "tensor"),
        P("tensor"),
        P(),
        P(),
        P("tensor"),
        P("tensor"),
        P("tensor"),
        P("tensor"),
        P("tensor", None),
    )
    return jax.shard_map(shards, mesh=mesh, in_specs=in_specs, out_specs=out_specs, check_vma=False)
```

```python
import functools
import math

import jax
import jax.numpy as jnp
from jax import lax
from jax.experimental import pallas as pl
from jax.experimental.pallas import tpu as pltpu
from jax.sharding import PartitionSpec as P

STATE = 128
CONV = 4
BLOCK = 256
PIECE = 128
OWN_BC = 64
SHARED_AT = 128
LANES = 128
EPS = 1e-05
HIGH = lax.Precision.HIGHEST
LOG2E = math.log2(math.e)
BF16 = jnp.bfloat16
F32 = jnp.float32


def dot(left, right):
    return jnp.dot(left, right, preferred_element_type=F32)


def dot_last(left, right):
    return lax.dot_general(left, right, (((1,), (1,)), ((), ())), preferred_element_type=F32)


def dot_first(left, right):
    return lax.dot_general(left, right, (((0,), (0,)), ((), ())), preferred_element_type=F32)


def two_terms(array):
    upper = array.astype(BF16)
    return upper, (array - upper.astype(F32)).astype(BF16)


def sum_rows(ones, array):
    first = array.astype(BF16)
    second, third = two_terms(array - first.astype(F32))
    sums = dot(ones.astype(BF16), jnp.concatenate([first, second, third], axis=1))
    columns = array.shape[1]
    return sums[:, 0:columns] + sums[:, columns : 2 * columns] + sums[:, 2 * columns :]


def sigmoid(array):
    return 0.5 * jnp.tanh(0.5 * array) + 0.5


def spread_heads(array, heads_twice):
    upper, rest = two_terms(array)
    return dot(jnp.concatenate([upper, rest], axis=1), heads_twice)


def sum_heads(array, heads):
    upper, rest = two_terms(array)
    return dot_last(upper, heads) + dot_last(rest, heads)


def head_table(channels, head_count):
    head_width = channels // head_count
    channel = lax.broadcasted_iota(jnp.int32, (LANES, channels), 1)
    head = lax.broadcasted_iota(jnp.int32, (LANES, channels), 0)
    first = head * head_width
    return ((channel >= first) & (channel < first + head_width)).astype(F32).astype(BF16)


def head_rows(head_ref, heads):
    upper, rest = two_terms(head_ref[...])
    return dot(upper, heads) + dot(rest, heads)


def table_kernel(
    segment_ref,
    pre_gain_ref,
    bias_x_ref,
    gate_gain_ref,
    bias_bc_ref,
    dt_bias_ref,
    a_log_ref,
    d_skip_ref,
    token_ref,
    row_ref,
    head_ref,
):
    seq_count, length = segment_ref.shape
    place = lax.broadcasted_iota(jnp.int32, (8, length), 1)
    at_row = lax.broadcasted_iota(jnp.int32, (8, length), 0)
    for seq in range(seq_count):
        documents = jnp.broadcast_to(segment_ref[seq : seq + 1, :], (8, length)).astype(F32)
        padded = jnp.where(at_row == 0, documents, 0.0)

        def moved(by):
            other = pltpu.roll(documents, by % length, 1)
            return other, (place >= by) & (place < length + by)

        for k in range(1, CONV):
            before, inside = moved(k)
            padded = jnp.where((at_row == k) & inside & (before == documents), 1.0, padded)
        ends = []
        for piece in range(length // PIECE):
            here = slice(piece * PIECE, (piece + 1) * PIECE)
            ends.append(jnp.broadcast_to(documents[:, (piece + 1) * PIECE - 1 : (piece + 1) * PIECE], (8, PIECE)))
        starts = [jnp.full((8, PIECE), -1.0, F32)] + ends[:-1]
        padded = jnp.where((at_row == 4) & (jnp.concatenate(starts, axis=1) == documents), 1.0, padded)
        padded = jnp.where((at_row == 5) & (jnp.concatenate(ends, axis=1) == documents), 1.0, padded)
        lower = jnp.zeros((8, length), F32)
        for k in range(1, CONV):
            after, inside = moved(-k)
            hit = inside & (after == documents)
            if 5 + k < 8:
                padded = jnp.where((at_row == 5 + k) & hit, 1.0, padded)
            else:
                lower = jnp.where((at_row == 5 + k - 8) & hit, 1.0, lower)
        columns = slice(seq * length, (seq + 1) * length)
        token_ref[0:8, columns] = padded + jnp.where(at_row == 0, 64.0 * seq, 0.0)
        token_ref[8:16, columns] = lower
    row_ref[...] = jnp.zeros(row_ref.shape, F32)
    for at, ref in enumerate((pre_gain_ref, bias_x_ref, gate_gain_ref, bias_bc_ref)):
        row_ref[at : at + 1, 0 : ref.shape[0]] = ref[...].reshape(1, -1)
    head_ref[...] = jnp.zeros(head_ref.shape, F32)
    count = dt_bias_ref.shape[0]
    head_ref[0:1, 0:count] = dt_bias_ref[...].reshape(1, -1)
    head_ref[1:2, 0:count] = -jnp.exp(a_log_ref[...].reshape(1, -1))
    head_ref[2:3, 0:count] = d_skip_ref[...].reshape(1, -1)


def forward_kernel(
    hidden_ref,
    cotan_ref,
    w_gate_ref,
    w_value_ref,
    w_bc_ref,
    w_dt_ref,
    w_out_ref,
    conv_x_ref,
    conv_bc_ref,
    row_ref,
    head_ref,
    token_ref,
    normed_ref,
    mixed_ref,
    act_ref,
    turn_ref,
    grad_ref,
    scan_ref,
    value_ref,
    slope_ref,
    inner_ref,
    step_ref,
    cum_ref,
    bc_ref,
    bc_slope_ref,
    state_ref,
    enter_ref,
    sums_ref,
    tail_x,
    tail_bc,
    carried,
    wide_dt,
    gate_all,
    grad_all,
    tailed,
):
    block = pl.program_id(0)

    @pl.when(block == 0)
    def _():
        tail_x[0:8, :] = jnp.zeros((8, tail_x.shape[1]), F32)
        tail_bc[0:8, :] = jnp.zeros((8, tail_bc.shape[1]), F32)
        carried[...] = jnp.zeros(carried.shape, F32)
        wide_dt[...] = jnp.zeros(wide_dt.shape, BF16)
        wide_dt[0 : w_dt_ref.shape[0], :] = w_dt_ref[...]

    channels = tail_x.shape[1]
    heads = head_table(channels, w_dt_ref.shape[0])
    skips = head_rows(head_ref, heads)[2:3, :]
    side = token_ref[...].T
    hidden = hidden_ref[...].astype(F32)
    inv_rms = lax.rsqrt(jnp.mean(hidden * hidden, axis=-1, keepdims=True) + EPS)
    normed = (hidden * inv_rms * row_ref[0:1, :]).astype(BF16)
    normed_ref[...] = normed
    tail_x[8:, :] = dot(normed, w_value_ref[...])
    tail_bc[8:, :] = dot(normed, w_bc_ref[...])
    step_in = dot_last(normed, wide_dt[...]) + head_ref[0:1, :]
    step_ref[...] = step_in
    step = jnp.maximum(step_in, 0.0) + jnp.log1p(jnp.exp(-jnp.abs(step_in)))
    rate = head_ref[1:2, :] * step * LOG2E
    gate_all[...] = dot(normed, w_gate_ref[...])
    grad_all[...] = dot_last(cotan_ref[...], w_out_ref[...])
    masks = [None] + [side[:, k : k + 1] for k in range(1, CONV)]

    def conv(tail, taps_ref, bias_at, lanes):
        result = row_ref[bias_at : bias_at + 1, lanes] + taps_ref[CONV - 1 : CONV, lanes] * tail[8:, lanes]
        for k in range(1, CONV):
            shifted = tail[8 - k : 8 - k + BLOCK, lanes]
            result = result + taps_ref[CONV - 1 - k : CONV - k, lanes] * shifted * masks[k]
        return result

    for at in range(0, channels, LANES):
        lanes = slice(at, at + LANES)
        before = conv(tail_x, conv_x_ref, 1, lanes)
        half = sigmoid(before)
        value_ref[:, lanes] = (before * half).astype(BF16)
        slope_ref[:, lanes] = (half * (1.0 + before * (1.0 - half))).astype(BF16)
        inner_ref[:, lanes] = tail_x[8:, lanes].astype(BF16)
    for at in range(0, 2 * STATE, LANES):
        lanes = slice(at, at + LANES)
        before = conv(tail_bc, conv_bc_ref, 3, lanes)
        half = sigmoid(before)
        bc_ref[:, lanes] = (before * half).astype(BF16)
        bc_slope_ref[:, lanes] = half * (1.0 + before * (1.0 - half))
        state_ref[:, lanes] = tail_bc[8:, lanes]
    tail_x[0:8, :] = tail_x[BLOCK:, :]
    tail_bc[0:8, :] = tail_bc[BLOCK:, :]

    row_at = lax.broadcasted_iota(jnp.int32, (PIECE, PIECE), 0)
    col_at = lax.broadcasted_iota(jnp.int32, (PIECE, PIECE), 1)
    first_half = lax.broadcasted_iota(jnp.int32, (PIECE, LANES), 1) < LANES // 2
    heads_twice = jnp.concatenate([heads, heads], axis=0)
    block_row = lax.broadcasted_iota(jnp.int32, (BLOCK, BLOCK), 0)
    block_col = lax.broadcasted_iota(jnp.int32, (BLOCK, BLOCK), 1)
    lower = (block_row >= block_col) & (block_row // PIECE == block_col // PIECE)
    cums = sum_rows(lower.astype(F32), rate)
    cum_ref[...] = cums
    cums_t = cums.T
    lasts = [
        jnp.broadcast_to(cums[at + PIECE - 1 : at + PIECE, :], (PIECE, LANES)) for at in range(0, BLOCK, PIECE)
    ]
    reach = jnp.exp2(cums) * side[:, 4:5]
    tail = jnp.exp2(jnp.concatenate(lasts) - cums) * side[:, 5:6]
    wides = spread_heads(jnp.concatenate([step, reach, tail], axis=0), heads_twice)
    for piece in range(BLOCK // PIECE):
        rows = slice(piece * PIECE, (piece + 1) * PIECE)
        cum = cums[rows]
        cum_t = cums_t[:, rows]
        same = (side[rows, 0:1] == token_ref[0:1, rows]) & (row_at >= col_at)
        bias = jnp.where(same, 0.0, -1e30)
        wide = jnp.concatenate([wides[at + piece * PIECE : at + (piece + 1) * PIECE] for at in range(0, 3 * BLOCK, BLOCK)])
        b_low = bc_ref[rows, 0:STATE]
        c_low = bc_ref[rows, STATE : 2 * STATE]
        scores = dot_last(c_low, b_low)
        enter = carried[...].astype(BF16)
        enter_ref[piece] = enter
        from_state = dot(c_low, enter)
        for pair in range(channels // LANES):
            lanes = slice(pair * LANES, (pair + 1) * LANES)
            values = value_ref[rows, lanes].astype(F32)
            scaled = wide[0:PIECE, lanes] * values
            low = scaled.astype(BF16)
            weights = []
            for head in (2 * pair, 2 * pair + 1):
                gaps = (cum[:, head : head + 1] - cum_t[head : head + 1, :]) + bias
                weights.append((scores * jnp.exp2(gaps)).astype(BF16))
            zero = jnp.zeros_like(low)
            both = jnp.concatenate(
                [jnp.where(first_half, low, zero), jnp.where(first_half, zero, low)], axis=0
            )
            out = dot(jnp.concatenate(weights, axis=1), both)
            out = out + from_state[:, lanes] * wide[PIECE : 2 * PIECE, lanes]
            scan_ref[rows, lanes] = out + skips[:, lanes] * values
            tailed[:, lanes] = (wide[2 * PIECE :, lanes] * scaled).astype(BF16)
        kept = wide[2 * PIECE - 1 : 2 * PIECE, :]
        carried[...] = kept * carried[...] + dot_first(b_low, tailed[...])

    ones = jnp.ones((8, LANES), BF16)
    square_part = jnp.zeros((BLOCK, LANES), F32)
    cross_part = jnp.zeros((BLOCK, LANES), F32)
    for at in range(0, channels, LANES):
        lanes = slice(at, at + LANES)
        gate = gate_all[:, lanes]
        scan = scan_ref[:, lanes]
        grad = grad_all[:, lanes]
        half = sigmoid(gate)
        act = gate * half
        mixed = scan * act
        mixed_ref[:, lanes] = mixed.astype(BF16)
        act_ref[:, lanes] = act.astype(BF16)
        turn_ref[:, lanes] = (scan * (half * (1.0 + gate * (1.0 - half)))).astype(BF16)
        grad_ref[:, lanes] = grad.astype(BF16)
        square_part = square_part + mixed * mixed
        cross_part = cross_part + mixed * (grad * row_ref[2:3, lanes])
    upper, rest = two_terms(square_part)
    squares = dot_last(ones, upper) + dot_last(ones, rest)
    upper, rest = two_terms(cross_part)
    crosses = dot_last(ones, upper) + dot_last(ones, rest)
    is_first = lax.broadcasted_iota(jnp.int32, (8, BLOCK), 0) == 0
    sums_ref[...] = jnp.where(is_first, squares, crosses)


def store_halves(total, columns, mine, sent_ref, kept_ref, at=0):
    half = total.shape[0] // 2
    to = slice(at, at + half)
    for which, ref in ((1 - mine, sent_ref), (mine, kept_ref)):
        ref[to, :] = total[pl.ds(pl.multiple_of(which * half, 8), half), columns].astype(BF16)


def gate_columns(sums_ref):
    row_at = lax.broadcasted_iota(jnp.int32, (8, LANES), 0)

    def column(which):
        pick = (row_at == which).astype(F32)
        return lax.dot_general(
            sums_ref[...], pick, (((0,), (0,)), ((), ())), precision=HIGH, preferred_element_type=F32
        )

    inv_gate = lax.rsqrt(column(0) + EPS)
    return inv_gate, inv_gate * inv_gate * column(1)


def gate_kernel(
    low_ref,
    mixed_ref,
    turn_ref,
    grad_ref,
    sums_ref,
    row_ref,
    cotan_ref,
    normed_ref,
    gate_low_ref,
    gain_ref,
    sent_ref,
    kept_ref,
    gated,
    out_total,
    gate_total,
):
    block = pl.program_id(0)

    @pl.when(block == 0)
    def _():
        gain_ref[...] = jnp.zeros(gain_ref.shape, F32)
        out_total[...] = jnp.zeros(out_total.shape, F32)
        gate_total[...] = jnp.zeros(gate_total.shape, F32)

    channels = mixed_ref.shape[1]
    inv_gate, pull = gate_columns(sums_ref)
    for at in range(0, channels, LANES):
        lanes = slice(at, at + LANES)
        mixed = mixed_ref[:, lanes].astype(F32)
        grad = grad_ref[:, lanes].astype(F32)
        gain = row_ref[2:3, lanes]
        normal = mixed * inv_gate
        gated[:, lanes] = (normal * gain).astype(BF16)
        gain_ref[:, lanes] += jnp.sum((grad * normal).reshape(-1, 8, LANES), axis=0)
        mixed_grad = inv_gate * (grad * gain - mixed * pull)
        gate_low_ref[:, lanes] = (mixed_grad * turn_ref[:, lanes].astype(F32)).astype(BF16)
    out_total[...] += dot_first(gated[...], cotan_ref[...])
    gate_total[...] += dot_first(normed_ref[...], gate_low_ref[...])

    @pl.when(block == pl.num_programs(0) - 1)
    def _():
        rows, width = out_total.shape
        for at in range(width // channels):
            columns = slice(at * channels, (at + 1) * channels)
            store_halves(out_total, columns, low_ref[0], sent_ref, kept_ref, at * rows // 2)
        store_halves(gate_total, slice(None), low_ref[0], sent_ref, kept_ref, width // 2)


def weight_kernel(low_ref, normed_ref, grad_ref, after_ref, sent_ref, kept_ref, total):
    block = pl.program_id(0)
    part = dot_first(normed_ref[...], grad_ref[...])

    @pl.when(block == 0)
    def _():
        total[...] = part

    @pl.when(block > 0)
    def _():
        total[...] += part

    @pl.when(block == pl.num_programs(0) - 1)
    def _():
        store_halves(total, slice(None), low_ref[0], sent_ref, kept_ref)


def backward_kernel(
    head_count,
    mixed_ref,
    grad_ref,
    act_ref,
    sums_ref,
    row_ref,
    scan_ref,
    value_ref,
    slope_ref,
    inner_ref,
    step_ref,
    cum_ref,
    bc_ref,
    enter_ref,
    normed_ref,
    bc_slope_ref,
    state_ref,
    conv_x_ref,
    conv_bc_ref,
    head_ref,
    token_ref,
    after_ref,
    state_low_ref,
    inner_low_ref,
    step_low_ref,
    channel_grad_ref,
    conv_bc_grad_ref,
    head_grad_ref,
    step_rows_ref,
    bc_rows_ref,
    later,
    later_bc,
    leaving,
    step_total,
    dys,
    lows,
    reached,
    tailed,
    products,
):
    block = pl.program_id(0)

    @pl.when(block == 0)
    def _():
        later[PIECE:, :] = jnp.zeros((8, later.shape[1]), F32)
        later_bc[PIECE:, :] = jnp.zeros((8, later_bc.shape[1]), F32)
        conv_bc_grad_ref[...] = jnp.zeros(conv_bc_grad_ref.shape, F32)
        bc_rows_ref[...] = jnp.zeros(bc_rows_ref.shape, F32)
        leaving[...] = jnp.zeros(leaving.shape, F32)
        channel_grad_ref[...] = jnp.zeros(channel_grad_ref.shape, F32)
        head_grad_ref[...] = jnp.zeros(head_grad_ref.shape, F32)
        step_total[...] = jnp.zeros(step_total.shape, F32)

    channels = inner_ref.shape[1]
    row_at = lax.broadcasted_iota(jnp.int32, (PIECE, PIECE), 0)
    col_at = lax.broadcasted_iota(jnp.int32, (PIECE, PIECE), 1)
    upper_ones = (row_at <= col_at).astype(F32)
    first_half = lax.broadcasted_iota(jnp.int32, (PIECE, LANES), 1) < LANES // 2
    heads = head_table(channels, head_count)
    skips = head_rows(head_ref, heads)[2:3, :]
    side_all = token_ref[...].T
    inv_gate, pull = gate_columns(sums_ref)
    heads_twice = jnp.concatenate([heads, heads], axis=0)
    for piece in reversed(range(BLOCK // PIECE)):
        rows = slice(piece * PIECE, (piece + 1) * PIECE)
        side = side_all[rows]
        step_in = step_ref[rows, :]
        step = jnp.maximum(step_in, 0.0) + jnp.log1p(jnp.exp(-jnp.abs(step_in)))
        cum = cum_ref[rows, :]
        cum_t = cum.T
        same = (side[:, 0:1] == token_ref[0:1, rows]) & (row_at <= col_at)
        bias = jnp.where(same, 0.0, -1e30)
        reach = jnp.exp2(cum) * side[:, 4:5]
        tail = jnp.exp2(cum[PIECE - 1 : PIECE, :] - cum) * side[:, 5:6]
        wide = spread_heads(jnp.concatenate([step, reach, tail], axis=0), heads_twice)
        b_low = bc_ref[rows, 0:STATE]
        c_low = bc_ref[rows, STATE : 2 * STATE]
        scores = dot_last(b_low, c_low)
        score_grad = jnp.zeros((PIECE, PIECE), F32)
        masks = [None] + [side[:, 5 + k : 6 + k] for k in range(1, CONV)]
        for at in range(0, channels, LANES):
            lanes = slice(at, at + LANES)
            mixed = mixed_ref[rows, lanes].astype(F32)
            grad = grad_ref[rows, lanes].astype(F32)
            mixed_grad = inv_gate[rows] * (grad * row_ref[2:3, lanes] - mixed * pull[rows])
            dy_low = (mixed_grad * act_ref[rows, lanes].astype(F32)).astype(BF16)
            dys[:, lanes] = dy_low
            dy = dy_low.astype(F32)
            low = (wide[0:PIECE, lanes] * value_ref[rows, lanes].astype(F32)).astype(BF16)
            lows[:, lanes] = low
            reached[:, lanes] = (wide[PIECE : 2 * PIECE, lanes] * dy).astype(BF16)
            tailed[:, lanes] = (wide[2 * PIECE :, lanes] * low.astype(F32)).astype(BF16)
        leave = leaving[...]
        leave_low = leave.astype(BF16)
        enter_low = enter_ref[piece]
        kept = wide[2 * PIECE - 1 : 2 * PIECE, :]
        c_grad = dot_last(reached[...], enter_low)
        b_grad = dot_last(tailed[...], leave_low)
        from_states = dot(b_low, leave_low)
        kept_sum = kept * jnp.sum(enter_low.astype(F32) * leave, axis=0, keepdims=True)
        leaving[...] = kept * leave + dot_first(c_low, reached[...])
        for pair in range(channels // LANES):
            lanes = slice(pair * LANES, (pair + 1) * LANES)
            values = value_ref[rows, lanes].astype(F32)
            dy_low = dys[:, lanes]
            dy = dy_low.astype(F32)
            wide_step = wide[0:PIECE, lanes]
            low = lows[:, lanes]
            low_wide = low.astype(F32)
            from_state = wide[2 * PIECE :, lanes] * from_states[:, lanes]
            zero = jnp.zeros_like(low)
            own = jnp.concatenate(
                [jnp.where(first_half, dy_low, zero), jnp.where(first_half, zero, dy_low)], axis=0
            )
            weight_grads = dot_last(low, own)
            weights = []
            for at, head in enumerate((2 * pair, 2 * pair + 1)):
                gaps = (cum_t[head : head + 1, :] - cum[:, head : head + 1]) + bias
                decay = jnp.exp2(gaps)
                weights.append((scores * decay).astype(BF16))
                score_grad = score_grad + weight_grads[:, at * PIECE : (at + 1) * PIECE] * decay
            dx = dot(jnp.concatenate(weights, axis=1), own)
            dx = dx + from_state
            out = scan_ref[rows, lanes] - skips[:, lanes] * values
            last = jnp.sum(low_wide * from_state, axis=0, keepdims=True) + kept_sum[:, lanes]
            for at, product in enumerate(
                (dy * out - low_wide * dx, values * dx, jnp.broadcast_to(last, (16, LANES)))
            ):
                upper, rest = two_terms(product)
                products[2 * at * PIECE : 2 * at * PIECE + upper.shape[0], lanes] = upper
                products[2 * at * PIECE + upper.shape[0] : 2 * (at * PIECE + upper.shape[0]), lanes] = rest
            dvalue = wide_step * dx + skips[:, lanes] * dy
            dbefore = dvalue * slope_ref[rows, lanes].astype(F32)
            later[0:PIECE, lanes] = dbefore
            inner = inner_ref[rows, lanes].astype(F32)
            inner_grad = conv_x_ref[CONV - 1 : CONV, lanes] * dbefore
            channel_grad_ref[CONV - 1 : CONV, lanes] += jnp.sum(inner * dbefore, axis=0, keepdims=True)
            channel_grad_ref[CONV : CONV + 1, lanes] += jnp.sum(dbefore, axis=0, keepdims=True)
            channel_grad_ref[CONV + 1 : CONV + 2, lanes] += jnp.sum(dy * values, axis=0, keepdims=True)
            for k in range(1, CONV):
                shifted = later[k : k + PIECE, lanes] * masks[k]
                inner_grad = inner_grad + conv_x_ref[CONV - 1 - k : CONV - k, lanes] * shifted
                channel_grad_ref[CONV - 1 - k : CONV - k, lanes] += jnp.sum(
                    inner * shifted, axis=0, keepdims=True
                )
            inner_low_ref[rows, lanes] = inner_grad.astype(BF16)
        sums = dot_last(products[...], heads)
        row_sum = sums[0:PIECE] + sums[PIECE : 2 * PIECE]
        value_sum = sums[2 * PIECE : 3 * PIECE] + sums[3 * PIECE : 4 * PIECE]
        last_sum = sums[4 * PIECE : 4 * PIECE + 16] + sums[4 * PIECE + 16 : 4 * PIECE + 32]
        later[PIECE:, :] = later[0:8, :]
        grad_low = score_grad.astype(BF16)
        state_parts = (b_grad + dot(grad_low, c_low), c_grad + dot_first(grad_low, b_low))
        for at, state_part in enumerate(state_parts):
            lanes = slice(at * STATE, (at + 1) * STATE)
            dbefore = state_part * bc_slope_ref[rows, lanes]
            later_bc[0:PIECE, lanes] = dbefore
            state = state_ref[rows, lanes]
            state_grad = conv_bc_ref[CONV - 1 : CONV, lanes] * dbefore
            conv_bc_grad_ref[CONV - 1 : CONV, lanes] += jnp.sum(state * dbefore, axis=0, keepdims=True)
            conv_bc_grad_ref[CONV : CONV + 1, lanes] += jnp.sum(dbefore, axis=0, keepdims=True)
            for k in range(1, CONV):
                shifted = later_bc[k : k + PIECE, lanes] * masks[k]
                state_grad = state_grad + conv_bc_ref[CONV - 1 - k : CONV - k, lanes] * shifted
                conv_bc_grad_ref[CONV - 1 - k : CONV - k, lanes] += jnp.sum(
                    state * shifted, axis=0, keepdims=True
                )
            state_low_ref[rows, lanes] = state_grad.astype(BF16)
        later_bc[PIECE:, :] = later_bc[0:8, :]
        rate_grad = (
            jnp.dot(upper_ones, row_sum, precision=HIGH, preferred_element_type=F32) + last_sum[0:1, :]
        )
        coefficient = head_ref[1:2, :]
        step_grad = (value_sum + coefficient * rate_grad) / (1.0 + jnp.exp(-step_in))
        step_low_ref[rows, :] = step_grad.astype(BF16)
        head_grad_ref[0:1, :] += jnp.sum(step_grad, axis=0, keepdims=True)
        head_grad_ref[1:2, :] += jnp.sum(rate_grad * step, axis=0, keepdims=True) * coefficient
    step_total[...] += dot_first(step_low_ref[...], normed_ref[...])
    bc_rows_ref[...] += dot_first(state_low_ref[...], normed_ref[...])

    @pl.when(block == pl.num_programs(0) - 1)
    def _():
        step_rows_ref[...] = step_total[0 : step_rows_ref.shape[0], :]


def merge_kernel(
    core_ref,
    gate_low_ref,
    inner_low_ref,
    step_low_ref,
    state_low_ref,
    mixed_ref,
    normed_ref,
    sums_ref,
    w_gate_ref,
    w_value_ref,
    w_dt_ref,
    w_bc_ref,
    w_out_ref,
    row_ref,
    conv_bc_ref,
    after_ref,
    _,
    __,
    sent_ref,
    kept_ref,
    first_shared_ref,
    second_shared_ref,
    gain_ref,
    wide_dt,
    gated,
):
    block = pl.program_id(0)
    last = pl.num_programs(0) - 1

    @pl.when(block == 0)
    def _():
        gain_ref[...] = jnp.zeros(gain_ref.shape, F32)
        wide_dt[...] = jnp.zeros(wide_dt.shape, BF16)
        wide_dt[0 : w_dt_ref.shape[0], :] = w_dt_ref[...]

    width = normed_ref.shape[1]
    total = dot_last(inner_low_ref[...], w_value_ref[...]) + dot_last(gate_low_ref[...], w_gate_ref[...])
    total = total + dot_last(state_low_ref[...], w_bc_ref[...]) + dot(step_low_ref[...], wide_dt[...])
    gain_ref[...] += jnp.sum((total * normed_ref[...].astype(F32)).reshape(-1, 8, width), axis=0)
    inv_gate, _ = gate_columns(sums_ref)
    for at in range(0, mixed_ref.shape[1], LANES):
        lanes = slice(at, at + LANES)
        normal = mixed_ref[:, lanes].astype(F32) * inv_gate
        gated[:, lanes] = (normal * row_ref[2:3, lanes]).astype(BF16)
    branch = dot(gated[...], w_out_ref[...]).astype(BF16)

    @pl.when(2 * block < last)
    def _():
        sent_ref[:, 0:width] = total.astype(BF16)
        sent_ref[:, width:] = branch

    @pl.when(2 * block > last)
    def _():
        kept_ref[:, 0:width] = total.astype(BF16)
        kept_ref[:, width:] = branch

    @pl.when(block == last)
    def _():
        gain = jnp.sum(gain_ref[...], axis=0, keepdims=True) / row_ref[0:1, :]
        channels = first_shared_ref.shape[1]
        states = conv_bc_ref.shape[1]
        rows = [gain[:, at : at + channels] for at in range(0, width, channels)]
        conv = conv_bc_ref[0 : CONV + 1, :]
        rows.append(jnp.concatenate([conv, jnp.zeros((CONV + 1, channels - states), F32)], axis=1))
        rows.append(jnp.zeros((16 - width // channels - CONV - 1, channels), F32))
        shared = jnp.concatenate(rows).astype(BF16)
        first_shared_ref[...] = shared
        second_shared_ref[...] = shared


def pack_kernel(
    head_count,
    core_ref,
    bc_rows_ref,
    step_rows_ref,
    channel_ref,
    gate_gain_ref,
    head_ref,
    sent_ref,
    kept_ref,
    own_ref,
):
    core = core_ref[0]
    channels = channel_ref.shape[1]
    width = bc_rows_ref.shape[1]
    folds = width // channels
    groups = (kept_ref.shape[0] - 16) // (OWN_BC * folds)
    for which, ref in ((1 - core, sent_ref), (core, kept_ref)):
        for group in range(groups):
            found = bc_rows_ref[pl.ds(pl.multiple_of((2 * group + which) * OWN_BC, 8), OWN_BC), :].astype(BF16)
            for fold in range(folds):
                at = (group * folds + fold) * OWN_BC
                ref[at : at + OWN_BC, :] = found[:, fold * channels : (fold + 1) * channels]
    own_ref[...] = jnp.zeros(own_ref.shape, F32)
    for fold in range(folds):
        own_ref[16 * fold : 16 * fold + 16, :] = step_rows_ref[:, fold * channels : (fold + 1) * channels]
    at = 16 * folds
    own_ref[at : at + CONV + 1, :] = channel_ref[0 : CONV + 1, :]
    own_ref[at + CONV + 1 : at + CONV + 2, :] = jnp.sum(gate_gain_ref[...], axis=0, keepdims=True)
    skips = sum_heads(channel_ref[...], head_table(channels, head_count))
    own_ref[at + CONV + 2 : at + CONV + 4, 0:LANES] = head_ref[0:2, :]
    own_ref[at + CONV + 4 : at + CONV + 5, 0:LANES] = skips[CONV + 1 : CONV + 2, :]


def unpack_kernel(
    one_ref,
    two_ref,
    pre_gain_ref,
    bc_ref,
    dt_ref,
    conv_x_ref,
    bias_x_ref,
    conv_bc_ref,
    bias_bc_ref,
    dt_bias_ref,
    a_log_ref,
    d_skip_ref,
    gate_gain_ref,
    total,
):
    total[...] = one_ref[...].astype(F32) + two_ref[...].astype(F32)
    channels = total.shape[1]
    own_bc, width = bc_ref.shape
    folds = width // channels
    for fold in range(folds):
        bc_ref[:, fold * channels : (fold + 1) * channels] = total[fold * own_bc : (fold + 1) * own_bc, :]
    at = folds * own_bc
    pre_gain_ref[...] = jnp.concatenate([total[at + fold : at + fold + 1, :] for fold in range(folds)], axis=1).reshape(-1)
    at += folds
    states = conv_bc_ref.shape[1]
    conv_bc_ref[...] = total[at : at + CONV, 0:states]
    bias_bc_ref[...] = total[at + CONV : at + CONV + 1, 0:states].reshape(-1)
    at += 16 - folds
    count = dt_ref.shape[0]
    for fold in range(folds):
        dt_ref[:, fold * channels : (fold + 1) * channels] = total[at + 16 * fold : at + 16 * fold + count, :]
    at += 16 * folds
    conv_x_ref[...] = total[at : at + CONV, :]
    bias_x_ref[...] = total[at + CONV : at + CONV + 1, :].reshape(-1)
    gate_gain_ref[...] = total[at + CONV + 1 : at + CONV + 2, :].reshape(-1)
    at += CONV + 2
    for row, ref in enumerate((dt_bias_ref, a_log_ref, d_skip_ref)):
        ref[...] = total[at + row : at + row + 1, 0:LANES].reshape(-1)[0 : ref.shape[0]]


def hidden_kernel(rank_ref, hidden_ref, cotan_ref, kept_ref, got_ref, row_ref, out_ref, grad_ref):
    width = hidden_ref.shape[1]
    hidden = hidden_ref[...].astype(F32)
    branch = kept_ref[:, width:].astype(F32) + got_ref[:, width:].astype(F32)
    out_ref[...] = (hidden + branch).astype(BF16)
    inv_rms = lax.rsqrt(jnp.mean(hidden * hidden, axis=-1, keepdims=True) + EPS)
    scaled = (kept_ref[:, 0:width].astype(F32) + got_ref[:, 0:width].astype(F32)) * row_ref[0:1, :]
    pull = inv_rms * inv_rms * jnp.mean(scaled * hidden, axis=-1, keepdims=True)
    grad_ref[...] = cotan_ref[...].astype(F32) + inv_rms * (scaled - hidden * pull)


def pass_kernel(*refs):
    pass


def finish_kernel(which_ref, part_ref, after_ref, out_ref):
    out_ref[...] = part_ref[...].astype(F32)


def finish_pair_kernel(which_ref, part_ref, after_ref, *refs):
    out_ref, gate_ref = refs[-2:]
    rows, width = out_ref.shape
    channels = gate_ref.shape[1]
    for at in range(width // channels):
        out_ref[:, at * channels : (at + 1) * channels] = part_ref[at * rows : (at + 1) * rows, :].astype(F32)
    gate_ref[...] = part_ref[gate_ref.shape[0] :, :].astype(F32)


def finish_into_kernel(which_ref, part_ref, after_ref, whole_ref, out_ref):
    finish_kernel(which_ref, part_ref, after_ref, out_ref)


def split_kernel(which_ref, sent_one, sent_two, kept_one, kept_two, sent_ref, kept_ref):
    sent_ref[...] = (sent_one[...].astype(F32) + sent_two[...].astype(F32)).astype(BF16)
    kept_ref[...] = (kept_one[...].astype(F32) + kept_two[...].astype(F32)).astype(BF16)


def join_kernel(which_ref, own_ref, got_ref, own_extra_ref, got_extra_ref, out_ref):
    which = which_ref[0]
    rows = own_ref.shape[0]
    extra_rows = own_extra_ref.shape[0]
    out_ref[pl.ds(pl.multiple_of(which * rows, 16), rows), :] = own_ref[...]
    out_ref[pl.ds(pl.multiple_of((1 - which) * rows, 16), rows), :] = got_ref[...]
    extra = own_extra_ref[...].astype(F32) + got_extra_ref[...].astype(F32)
    at = 2 * rows
    out_ref[at : at + extra_rows, :] = extra.astype(BF16)
    shared = slice(SHARED_AT, SHARED_AT + 16)
    out_ref[at + SHARED_AT : at + SHARED_AT + 16, :] = own_extra_ref[shared, :]
    out_ref[at + extra_rows : at + extra_rows + 16, :] = got_extra_ref[shared, :]
    out_ref[at + extra_rows + 16 :, :] = jnp.zeros((48, out_ref.shape[1]), BF16)


def rider_kernel(core_ref, own_ref, got_ref, out_ref):
    rows = out_ref.shape[0]
    out_ref[...] = (own_ref[0:rows, :].astype(F32) + got_ref[0:rows, :].astype(F32)).astype(BF16)
    shared, second = slice(SHARED_AT, SHARED_AT + 16), slice(rows, rows + 16)
    own, near = own_ref[shared, :].astype(F32), own_ref[second, :].astype(F32)
    other, far = got_ref[shared, :].astype(F32), got_ref[second, :].astype(F32)
    is_first = core_ref[0] == 0
    total = (own + jnp.where(is_first, other, near)) + (jnp.where(is_first, near, other) + far)
    out_ref[shared, :] = total.astype(BF16)


def whole(shape):
    return pl.BlockSpec(shape, lambda i: (0,) * len(shape), pipeline_mode=pl.Buffered(1))


def no_cost():
    return pl.CostEstimate(flops=0, bytes_accessed=0, transcendentals=0)


def params():
    return pltpu.CompilerParams(vmem_limit_bytes=60 << 20)


def run_tables(segments, pre_gain, bias_x, gate_gain, bias_bc, dt_bias, a_log, d_skip):
    inputs = (segments, pre_gain, bias_x, gate_gain, bias_bc, dt_bias, a_log, d_skip)
    in_vmem = pl.BlockSpec(memory_space=pltpu.VMEM)
    return pl.pallas_call(
        table_kernel,
        in_specs=[in_vmem] * len(inputs),
        out_specs=[in_vmem] * 3,
        out_shape=[
            jax.ShapeDtypeStruct((16, segments.size), F32),
            jax.ShapeDtypeStruct((8, pre_gain.shape[0]), F32),
            jax.ShapeDtypeStruct((8, LANES), F32),
        ],
        compiler_params=params(),
        name="tables",
    )(*inputs)


def in_place():
    return pl.BlockSpec(memory_space=pl.ANY)


def run_forward(hidden_in, cotangent, weights, tables, tokens):
    rows, width = hidden_in.shape
    channels = weights[0].shape[1]
    states = weights[2].shape[1]
    constants = (*weights, *tables)

    def block(columns):
        return pl.BlockSpec((BLOCK, columns), lambda i: (i, 0))

    def out(columns, kind=BF16):
        return jax.ShapeDtypeStruct((rows, columns), kind)

    return pl.pallas_call(
        forward_kernel,
        grid=(rows // BLOCK,),
        in_specs=[block(width), block(width)]
        + [whole(array.shape) for array in constants]
        + [pl.BlockSpec((tokens.shape[0], BLOCK), lambda i: (0, i))],
        out_specs=[block(width)]
        + [block(channels)] * 8
        + [block(LANES)] * 2
        + [block(states)] * 3
        + [
            pl.BlockSpec((BLOCK // PIECE, STATE, channels), lambda i: (i, 0, 0)),
            pl.BlockSpec((8, BLOCK), lambda i: (0, i)),
        ],
        out_shape=[
            out(width),
            out(channels),
            out(channels),
            out(channels),
            out(channels),
            out(channels, F32),
            out(channels),
            out(channels),
            out(channels),
            out(LANES, F32),
            out(LANES, F32),
            out(states),
            out(states, F32),
            out(states, F32),
            jax.ShapeDtypeStruct((rows // PIECE, STATE, channels), BF16),
            jax.ShapeDtypeStruct((8, rows), F32),
        ],
        scratch_shapes=[
            pltpu.VMEM((BLOCK + 8, channels), F32),
            pltpu.VMEM((BLOCK + 8, states), F32),
            pltpu.VMEM((STATE, channels), F32),
            pltpu.VMEM((LANES, width), BF16),
            pltpu.VMEM((BLOCK, channels), F32),
            pltpu.VMEM((BLOCK, channels), F32),
            pltpu.VMEM((PIECE, channels), BF16),
        ],
        compiler_params=params(),
        cost_estimate=no_cost(),
        name="forward",
    )(hidden_in, cotangent, *constants, tokens)


def scalar_spec():
    return pl.BlockSpec(memory_space=pltpu.SMEM)


def half_shapes(rows, columns):
    return [jax.ShapeDtypeStruct((rows // 2, columns), BF16)] * 2


def run_gate(low, forward, sums, rows_table, cotangent, normed):
    rows, channels = forward[0].shape
    width = cotangent.shape[1]

    def block(columns):
        return pl.BlockSpec((BLOCK, columns), lambda i: (i, 0))

    halves = [jax.ShapeDtypeStruct((width // 2 + width // 2, channels), BF16)] * 2
    out = pl.pallas_call(
        gate_kernel,
        grid=(rows // BLOCK,),
        in_specs=[scalar_spec()]
        + [block(channels)] * 3
        + [pl.BlockSpec((8, BLOCK), lambda i: (0, i)), whole(rows_table.shape), block(width), block(width)],
        out_specs=[block(channels), whole((8, channels))] + [whole(half.shape) for half in halves],
        out_shape=[jax.ShapeDtypeStruct((rows, channels), BF16), jax.ShapeDtypeStruct((8, channels), F32)]
        + halves,
        scratch_shapes=[
            pltpu.VMEM((BLOCK, channels), BF16),
            pltpu.VMEM((channels, width), F32),
            pltpu.VMEM((width, channels), F32),
        ],
        compiler_params=params(),
        cost_estimate=no_cost(),
        name="gate",
    )(low, *forward, sums, rows_table, cotangent, normed)
    return out[:2], out[2:]


def run_weight(low, normed, grad, after):
    rows, width = normed.shape
    channels = grad.shape[1]
    size = 2 * BLOCK
    halves = half_shapes(width, channels)
    return pl.pallas_call(
        weight_kernel,
        grid=(rows // size,),
        in_specs=[
            scalar_spec(),
            pl.BlockSpec((size, width), lambda i: (i, 0)),
            pl.BlockSpec((size, channels), lambda i: (i, 0)),
            in_place(),
        ],
        out_specs=[whole(half.shape) for half in halves],
        out_shape=halves,
        scratch_shapes=[pltpu.VMEM((width, channels), F32)],
        compiler_params=params(),
        cost_estimate=no_cost(),
        name="weight",
    )(low, normed, grad, after)


def run_backward(gate_inputs, sums, rows_table, by_channel, step_in, cum, bc_low, enter, normed, by_state, tables, after, head_count):
    rows, channels = by_channel[0].shape
    width = normed.shape[1]
    count = rows // BLOCK
    states = bc_low.shape[1]
    conv_x, conv_bc, head_values, tokens = tables

    def block(columns):
        return pl.BlockSpec((BLOCK, columns), lambda i: (count - 1 - i, 0))

    def low_rows(columns):
        return jax.ShapeDtypeStruct((rows, columns), BF16)

    totals = [
        jax.ShapeDtypeStruct(shape, F32)
        for shape in ((8, channels), (8, states), (8, LANES), (16, width), (states, width))
    ]
    return pl.pallas_call(
        functools.partial(backward_kernel, head_count),
        grid=(count,),
        in_specs=[block(channels)] * 3
        + [pl.BlockSpec((8, BLOCK), lambda i: (0, count - 1 - i)), whole(rows_table.shape)]
        + [block(channels)] * 4
        + [block(LANES), block(LANES), block(states)]
        + [pl.BlockSpec((BLOCK // PIECE, STATE, channels), lambda i: (count - 1 - i, 0, 0))]
        + [block(width), block(states), block(states)]
        + [whole(conv_x.shape), whole(conv_bc.shape), whole(head_values.shape)]
        + [pl.BlockSpec((tokens.shape[0], BLOCK), lambda i: (0, count - 1 - i)), in_place()],
        out_specs=[block(states), block(channels), block(LANES)]
        + [whole(shape.shape) for shape in totals],
        out_shape=[low_rows(states), low_rows(channels), low_rows(LANES)] + totals,
        scratch_shapes=[
            pltpu.VMEM((PIECE + 8, channels), F32),
            pltpu.VMEM((PIECE + 8, states), F32),
            pltpu.VMEM((STATE, channels), F32),
            pltpu.VMEM((LANES, width), F32),
            pltpu.VMEM((PIECE, channels), BF16),
            pltpu.VMEM((PIECE, channels), BF16),
            pltpu.VMEM((PIECE, channels), BF16),
            pltpu.VMEM((PIECE, channels), BF16),
            pltpu.VMEM((4 * PIECE + 32, channels), BF16),
        ],
        compiler_params=params(),
        cost_estimate=no_cost(),
        name="backward",
    )(*gate_inputs, sums, rows_table, *by_channel, step_in, cum, bc_low, enter, normed, *by_state, conv_x, conv_bc, head_values, tokens, after)


def run_merge(core, blocked, sums, weights, rows_table, conv_bc_grads, after, packed, ranks):
    normed = blocked[-1]
    rows, width = normed.shape
    channels = weights[0].shape[1]
    size = rows // ranks
    half = ranks // 2

    def rank_at(i, c):
        return jnp.where(i < half, 2 * i + 1 - c[0], 2 * (i - half) + c[0])

    def block(columns):
        return pl.BlockSpec((size, columns), lambda i, c: (rank_at(i, c), 0))

    def constant(shape):
        return pl.BlockSpec(shape, lambda i, c: (0,) * len(shape), pipeline_mode=pl.Buffered(1))

    out = jax.ShapeDtypeStruct((rows // 2, 2 * width), BF16)
    last = packed[0].shape[0] // 16 - 1
    shared = pl.BlockSpec((16, channels), lambda i, c: (last, 0))
    first = 5 + len(blocked) + len(weights)
    return pl.pallas_call(
        merge_kernel,
        grid_spec=pltpu.PrefetchScalarGridSpec(
            num_scalar_prefetch=1,
            grid=(ranks,),
            in_specs=[block(array.shape[1]) for array in blocked]
            + [pl.BlockSpec((8, size), lambda i, c: (0, rank_at(i, c)))]
            + [constant(array.shape) for array in (*weights, rows_table, conv_bc_grads)]
            + [in_place()] * 3,
            out_specs=[
                pl.BlockSpec((size, 2 * width), lambda i, c: (jnp.minimum(i, half - 1), 0)),
                pl.BlockSpec((size, 2 * width), lambda i, c: (jnp.maximum(i - half, 0), 0)),
                shared,
                shared,
            ],
            scratch_shapes=[
                pltpu.VMEM((8, width), F32),
                pltpu.VMEM((LANES, width), BF16),
                pltpu.VMEM((size, channels), BF16),
            ],
        ),
        out_shape=[out, out] + [jax.ShapeDtypeStruct(array.shape, BF16) for array in packed],
        input_output_aliases={first: 2, first + 1: 3},
        compiler_params=params(),
        cost_estimate=no_cost(),
        name="merge",
    )(core, *blocked, sums, *weights, rows_table, conv_bc_grads, after, *packed)


def run_pack(core, bc_rows, step_rows, channel_grads, gain_rows, head_grads, head_count):
    states, width = bc_rows.shape
    channels = channel_grads.shape[1]
    folds = width // channels
    in_vmem = pl.BlockSpec(memory_space=pltpu.VMEM)
    shared = jax.ShapeDtypeStruct((states // 2 * folds + 16, channels), BF16)
    return pl.pallas_call(
        functools.partial(pack_kernel, head_count),
        in_specs=[scalar_spec()] + [in_vmem] * 5,
        out_specs=[in_vmem] * 3,
        out_shape=[shared, shared, jax.ShapeDtypeStruct((16 * folds + 16, channels), F32)],
        compiler_params=params(),
        cost_estimate=no_cost(),
        name="pack",
    )(core, bc_rows, step_rows, channel_grads, gain_rows, head_grads)


def run_unpack(one, two, width, states, head_count):
    rows, channels = one.shape
    last = two.shape[0] // rows - 1
    in_vmem = pl.BlockSpec(memory_space=pltpu.VMEM)
    shapes = (
        (width,),
        (OWN_BC, width),
        (head_count, width),
        (CONV, channels),
        (channels,),
        (CONV, states),
        (states,),
        (head_count,),
        (head_count,),
        (head_count,),
        (channels,),
    )
    return pl.pallas_call(
        unpack_kernel,
        grid=(1,),
        in_specs=[
            pl.BlockSpec((rows, channels), lambda i: (0, 0)),
            pl.BlockSpec((rows, channels), lambda i: (last, 0)),
        ],
        out_specs=[pl.BlockSpec(shape, lambda i, rank=len(shape): (0,) * rank) for shape in shapes],
        out_shape=[jax.ShapeDtypeStruct(shape, F32) for shape in shapes],
        scratch_shapes=[pltpu.VMEM(one.shape, F32)],
        compiler_params=params(),
        cost_estimate=no_cost(),
        name="unpack",
    )(one, two)


def run_hidden(rank, hidden_in, cotangent, kept, got, rows_table):
    own_rows = kept.shape[0]
    width = hidden_in.shape[1]
    count = 2
    size = own_rows // count

    def own(columns):
        return pl.BlockSpec((size, columns), lambda i, r: (r[0] * count + i, 0))

    def block(columns):
        return pl.BlockSpec((size, columns), lambda i, r: (i, 0))

    return pl.pallas_call(
        hidden_kernel,
        grid_spec=pltpu.PrefetchScalarGridSpec(
            num_scalar_prefetch=1,
            grid=(count,),
            in_specs=[
                own(width),
                own(width),
                block(2 * width),
                block(2 * width),
                pl.BlockSpec(rows_table.shape, lambda i, r: (0, 0)),
            ],
            out_specs=[block(width), block(width)],
        ),
        out_shape=[
            jax.ShapeDtypeStruct((own_rows, width), BF16),
            jax.ShapeDtypeStruct((own_rows, width), F32),
        ],
        compiler_params=params(),
        cost_estimate=no_cost(),
        name="hidden",
    )(rank, hidden_in, cotangent, kept, got, rows_table)


def run_pass(arrays, after):
    count = len(arrays)
    return pl.pallas_call(
        pass_kernel,
        in_specs=[in_place()] * (count + 1),
        out_specs=[in_place()] * count,
        out_shape=[jax.ShapeDtypeStruct(array.shape, array.dtype) for array in arrays],
        input_output_aliases={at: at for at in range(count)},
        cost_estimate=no_cost(),
        name="pass",
    )(*arrays, after)


def run_finish(which, part, after, rows, into=None):
    columns = part.shape[1]
    count = 2
    size = rows // count
    inputs = [part, after] + ([] if into is None else [into])
    return pl.pallas_call(
        finish_kernel if into is None else finish_into_kernel,
        grid_spec=pltpu.PrefetchScalarGridSpec(
            num_scalar_prefetch=1,
            grid=(count,),
            in_specs=[pl.BlockSpec((size, columns), lambda i, w: (i, 0))] + [in_place()] * (len(inputs) - 1),
            out_specs=pl.BlockSpec((size, columns), lambda i, w: (w[0] * count + i, 0)),
        ),
        out_shape=jax.ShapeDtypeStruct((2 * rows, columns), F32),
        input_output_aliases={} if into is None else {3: 0},
        compiler_params=params(),
        cost_estimate=no_cost(),
        name="finish",
    )(jnp.reshape(which, (1,)), *inputs)


def run_finish_pair(which, part, after, out_shape, gate_shape, into=()):
    out_rows, out_columns = out_shape
    gate_rows, gate_columns = gate_shape
    return pl.pallas_call(
        finish_pair_kernel,
        grid_spec=pltpu.PrefetchScalarGridSpec(
            num_scalar_prefetch=1,
            grid=(1,),
            in_specs=[pl.BlockSpec((gate_rows, gate_columns), lambda i, w: (0, 0))]
            + [in_place()] * (1 + len(into)),
            out_specs=[
                pl.BlockSpec((out_rows // 2, out_columns), lambda i, w: (w[0], 0)),
                pl.BlockSpec((gate_rows // 2, gate_columns), lambda i, w: (w[0], 0)),
            ],
        ),
        out_shape=[jax.ShapeDtypeStruct(out_shape, F32), jax.ShapeDtypeStruct(gate_shape, F32)],
        input_output_aliases={3 + at: at for at in range(len(into))},
        compiler_params=params(),
        cost_estimate=no_cost(),
        name="finish_pair",
    )(jnp.reshape(which, (1,)), part, after, *into)


def run_split(one, two, which):
    half, columns = one.shape[0] // 2, one.shape[1]
    count = 2
    size = half // count
    sent = pl.BlockSpec((size, columns), lambda i, w: ((1 - w[0]) * count + i, 0))
    kept = pl.BlockSpec((size, columns), lambda i, w: (w[0] * count + i, 0))
    out = pl.BlockSpec((size, columns), lambda i, w: (i, 0))
    return pl.pallas_call(
        split_kernel,
        grid_spec=pltpu.PrefetchScalarGridSpec(
            num_scalar_prefetch=1,
            grid=(count,),
            in_specs=[sent, sent, kept, kept],
            out_specs=[out, out],
        ),
        out_shape=[jax.ShapeDtypeStruct((half, columns), BF16)] * 2,
        compiler_params=params(),
        cost_estimate=no_cost(),
        name="split",
    )(jnp.reshape(which.astype(jnp.int32), (1,)), one, two, one, two)


def run_join(which, own, got, extra_rows):
    rows = own.shape[0] - extra_rows
    columns = own.shape[1]
    matrix = pl.BlockSpec((rows, columns), lambda i, w: (0, 0))
    extra = pl.BlockSpec((extra_rows, columns), lambda i, w: (rows // extra_rows, 0))
    shape = (2 * rows + extra_rows + 64, columns)
    return pl.pallas_call(
        join_kernel,
        grid_spec=pltpu.PrefetchScalarGridSpec(
            num_scalar_prefetch=1,
            grid=(1,),
            in_specs=[matrix, matrix, extra, extra],
            out_specs=pl.BlockSpec(shape, lambda i, w: (0, 0)),
        ),
        out_shape=jax.ShapeDtypeStruct(shape, BF16),
        compiler_params=params(),
        cost_estimate=no_cost(),
        name="join",
    )(jnp.reshape(which, (1,)), own, got, own, got)


def run_rider(core, own, got, rows):
    columns = own.shape[1]
    held = rows + 64
    last = pl.BlockSpec((held, columns), lambda i: (own.shape[0] // held - 1, 0))
    return pl.pallas_call(
        rider_kernel,
        grid=(1,),
        in_specs=[scalar_spec(), last, last],
        out_specs=pl.BlockSpec((rows, columns), lambda i: (0, 0)),
        out_shape=jax.ShapeDtypeStruct((rows, columns), BF16),
        compiler_params=params(),
        cost_estimate=no_cost(),
        name="rider",
    )(core, own, got)


def swap(array, axis, bit):
    size = lax.axis_size(axis)
    return lax.ppermute(array, axis, [(source, source ^ bit) for source in range(size)])


def axis_bits(axis):
    size = lax.axis_size(axis)
    return [1 << place for place in range(size.bit_length() - 1)]


def half_of(array, which):
    half = array.shape[0] // 2
    return lax.dynamic_slice_in_dim(array, which * half, half, 0)


def sum_tensor(array):
    for bit in axis_bits("tensor"):
        array = array + swap(array, "tensor", bit)
    return array


def dp_bits(step):
    bits = axis_bits("dp")
    swapped = [bits[1], bits[0]] + bits[2:]
    return bits[step], swapped[step]


def own_bit(step):
    first, second = dp_bits(step)
    place = lax.axis_index("dp").astype(jnp.int32)
    core = lax.axis_index("tensor") % 2
    return jnp.where(core == 0, (place // first) % 2, (place // second) % 2)


def dp_pairs(step):
    ranks = lax.axis_size("tensor")
    pairs = dp_bits(step)
    return [
        (at * ranks + rank, (at ^ pairs[rank % 2]) * ranks + rank)
        for at in range(lax.axis_size("dp"))
        for rank in range(ranks)
    ]


def in_order(which, own, got):
    place = lax.broadcasted_iota(jnp.int32, (2, 1, 1), 0)
    return jnp.where(place == which, own[None], got[None])


def sum_steps(sent, kept, rider=None, own=None):
    axes = ("dp", "tensor")
    steps = range(1, len(axis_bits("dp")))
    terms = [kept]
    got = yield sent, axes, dp_pairs(0)

    def total(which):
        return sum(half_of(term, which).astype(F32) for term in terms)

    for step in steps:
        which = own_bit(step)
        terms.append(got)
        sent = total(1 - which).astype(BF16)
        terms = [half_of(term, which) for term in terms]
        got = yield sent, axes, dp_pairs(step)
    part = sum((term.astype(F32) for term in terms), got.astype(F32)).astype(BF16)
    extra = 0
    for step in reversed((0, *steps)):
        if step == 1 and rider is not None:
            rows = rider().astype(BF16)
            extra = rows.shape[0]
            part = jnp.concatenate([part, rows])
        if step == 0 and own is not None:
            own.append(part)
        got = yield part, axes, dp_pairs(step)
        if step and extra:
            part = run_join(own_bit(step), part, got, extra)
        elif step:
            part = in_order(own_bit(step), part, got).reshape(2 * part.shape[0], -1)
    if extra:
        core = (lax.axis_index("tensor") % 2).astype(jnp.int32)
        extra = run_rider(jnp.reshape(core, (1,)), part, got, extra)
    return own_bit(0), part, got, extra


def rest_steps(rows):
    axes = ("dp", "tensor")
    for step in range(2, len(axis_bits("dp"))):
        got = yield rows, axes, dp_pairs(step)
        total = rows.astype(F32) + got.astype(F32)
        last, rows = (rows, got), total.astype(BF16)
    return last


def both_steps(sent, kept):
    size = lax.axis_size("tensor")
    rank = lax.axis_index("tensor")
    got = yield sent, "tensor", [(i, i ^ 1) for i in range(size)]
    for bit in axis_bits("tensor")[1:]:
        sent, kept = run_split(kept, got, (rank // bit) % 2)
        got = yield sent, "tensor", [(i, i ^ bit) for i in range(size)]
    return kept, got


def small_steps(sent, kept, own):
    size = lax.axis_size("tensor")
    rank = lax.axis_index("tensor")
    got = yield sent, "tensor", [(i, i ^ 1) for i in range(size)]
    total = kept.astype(F32) + got.astype(F32)
    for bit in axis_bits("tensor")[1:]:
        which = (rank // bit) % 2
        shared = lax.reduce_precision(total[-16:], 8, 7).astype(BF16)
        rows = total[:-16]
        got = yield jnp.concatenate([half_of(rows, 1 - which).astype(BF16), shared]), "tensor", [
            (i, i ^ bit) for i in range(size)
        ]
        total = jnp.concatenate([half_of(rows, which), shared.astype(F32)]) + got.astype(F32)
    return jnp.concatenate([total, own])


class Order:
    def __init__(self, last):
        self.last = last
        self.waiting = {}
        self.flying = {}
        self.arrived = {}
        self.results = {}

    def advance(self, name, steps, got):
        try:
            request = steps.send(got)
            self.waiting[name] = (steps, request)
            self.last = request[0]
        except StopIteration as end:
            self.results[name] = end.value

    def add(self, name, steps):
        last = self.last
        self.advance(name, steps, None)
        self.last = last

    def go(self, *names):
        for name in names:
            if name in self.waiting:
                steps, (sent, axis, moves) = self.waiting.pop(name)
                self.flying[name] = (steps, lax.ppermute(sent, axis, moves))

    def arrive(self, *names):
        found = [(name, *self.flying.pop(name)) for name in names if name in self.flying]
        if found:
            passed = run_pass([got for _, _, got in found], self.last)
            self.last = passed[0]
            for (name, steps, _), got in zip(found, passed):
                self.arrived[name] = (steps, got)

    def take(self, *names):
        for name in names:
            if name in self.arrived:
                steps, got = self.arrived.pop(name)
                self.advance(name, steps, got if got is self.last else self.hold(got))
                if name in self.waiting:
                    self.last = self.waiting[name][1][0]

    def land(self, *names):
        self.arrive(*names)
        self.take(*names)

    def hold(self, array):
        return run_pass([array], self.last)[0]

    def step(self, *names):
        for name in names:
            self.land(name)
            self.go(name)

    def until(self, name, found):
        while not found:
            self.step(name)
        return found[0]

    def result(self, name):
        while name not in self.results:
            self.go(name)
            self.land(name)
        return self.results[name]


def shards(
    hidden_in,
    pre_gain,
    w_gate,
    w_value,
    w_bc,
    w_dt,
    conv_x,
    conv_x_bias,
    conv_bc,
    conv_bc_bias,
    dt_bias,
    a_log,
    d_skip,
    gate_gain,
    w_out,
    cotangent,
    segments,
):
    row_count, width = hidden_in.shape
    channels = w_gate.shape[1]
    head_count = dt_bias.shape[0]
    head_width = channels // head_count
    ranks = lax.axis_size("tensor")
    my_rank = lax.axis_index("tensor")
    own_rows = row_count // ranks
    row_start = my_rank * own_rows
    pair_width = w_bc.shape[1] // ranks
    low = jnp.reshape(own_bit(0), (1,))
    w_dt_rows = w_dt.T
    tokens, rows_table, head_values = run_tables(
        segments, pre_gain, conv_x_bias, gate_gain, conv_bc_bias, dt_bias, a_log, d_skip
    )
    (
        normed,
        mixed,
        act,
        turn,
        gated_grad,
        scan,
        values,
        slope,
        inner_pre,
        step_in,
        cum,
        bc_low,
        bc_slope,
        state_pre,
        enter,
        sums,
    ) = run_forward(
        hidden_in,
        cotangent,
        (w_gate, w_value, w_bc, w_dt_rows, w_out),
        (conv_x, conv_bc, rows_table, head_values),
        tokens,
    )
    sums = sum_tensor(sums) / (channels * ranks)
    (gate_low, gain_rows), halves = run_gate(
        low, (mixed, turn, gated_grad), sums, rows_table, cotangent, normed
    )
    order = Order(gate_low)
    first_own, second_own = [], []
    order.add("first", sum_steps(*halves, lambda: order.result("small"), first_own))
    order.go("first")
    (
        state_low,
        inner_low,
        step_low,
        channel_grads,
        conv_bc_grads,
        head_grads,
        step_rows,
        bc_rows,
    ) = run_backward(
        (mixed, gated_grad, act),
        sums,
        rows_table,
        (scan, values, slope, inner_pre),
        step_in,
        cum,
        bc_low,
        enter,
        normed,
        (bc_slope, state_pre),
        (conv_x, conv_bc, head_values, tokens),
        halves[0],
        head_count,
    )
    order.last = inner_low
    order.step("first")
    sent, kept = run_weight(low, normed, inner_low, order.last)
    order.last = kept
    order.step("first")
    order.add("second", sum_steps(order.hold(sent), kept, None, second_own))
    order.go("second")
    core = jnp.reshape((my_rank % 2).astype(jnp.int32), (1,))
    small_sent, small_kept, small_own = run_pack(
        core, bc_rows, step_rows, channel_grads, gain_rows, head_grads, head_count
    )
    both_sent, both_kept, small_sent, small_kept = run_merge(
        core,
        (gate_low, inner_low, step_low, state_low, mixed, normed),
        sums,
        (w_gate, w_value, w_dt_rows, w_bc, w_out),
        rows_table,
        conv_bc_grads,
        order.last,
        (small_sent, small_kept),
        ranks,
    )
    order.last = both_kept
    order.land("second", "first")
    order.go("second", "first")
    order.add("small", small_steps(order.hold(small_sent), small_kept, small_own))
    order.go("small")
    order.add("both", both_steps(order.hold(both_sent), both_kept))
    order.go("both")
    order.step("small")
    order.land("small")
    order.land("second", "first")
    order.go("second", "first")
    order.step("second")
    order.step("both")
    order.land("second")
    order.land("first")
    order.go("second", "first")
    order.step("second")
    which = own_bit(0)
    sums_first = run_finish_pair(which, order.until("first", first_own), order.last, w_out.shape, w_gate.shape)
    order.last = sums_first[0]
    own = order.until("second", second_own)
    w_value_sum = run_finish(which, own, order.last, own.shape[0])
    order.last = w_value_sum
    _, _, got, rows = order.result("first")
    order.add("rest", rest_steps(rows))
    order.go("rest")
    w_out_sum, w_gate_sum = run_finish_pair(
        1 - which, got, order.last, w_out.shape, w_gate.shape, sums_first
    )
    order.last = w_out_sum
    kept, got = order.result("both")
    block_out, hidden_grad = run_hidden(
        jnp.reshape(my_rank.astype(jnp.int32), (1,)), hidden_in, cotangent, kept, got, rows_table
    )
    order.last = hidden_grad
    one, two = order.result("rest")
    small = run_unpack(one, two, width, w_bc.shape[1], head_count)
    order.last = small[0]
    _, own, got, _ = order.result("second")
    w_value_sum = run_finish(1 - which, got, order.last, own.shape[0], w_value_sum)
    (
        pre_gain_grad,
        w_bc_rows,
        dt_rows,
        conv_x_grad,
        conv_x_bias_grad,
        conv_bc_grad,
        conv_bc_bias_grad,
        dt_bias_grad,
        a_log_grad,
        d_skip_grad,
        gate_gain_grad,
    ) = small
    return (
        block_out,
        hidden_grad,
        pre_gain_grad,
        w_gate_sum,
        w_value_sum,
        w_bc_rows.T,
        dt_rows.T,
        conv_x_grad,
        conv_x_bias_grad,
        conv_bc_grad,
        conv_bc_bias_grad,
        dt_bias_grad,
        a_log_grad,
        d_skip_grad,
        gate_gain_grad,
        w_out_sum,
    )


def solution(mesh):
    in_specs = (
        P("dp", None),
        P(),
        P(None, "tensor"),
        P(None, "tensor"),
        P(),
        P(None, "tensor"),
        P(None, "tensor"),
        P("tensor"),
        P(),
        P(),
        P("tensor"),
        P("tensor"),
        P("tensor"),
        P("tensor"),
        P("tensor", None),
        P("dp", None),
        P("dp", None),
    )
    out_specs = (
        P(("dp", "tensor"), None),
        P(("dp", "tensor"), None),
        P(),
        P(None, "tensor"),
        P(None, "tensor"),
        P(None, "tensor"),
        P(None, "tensor"),
        P(None, "tensor"),
        P("tensor"),
        P(),
        P(),
        P("tensor"),
        P("tensor"),
        P("tensor"),
        P("tensor"),
        P("tensor", None),
    )
    return jax.shard_map(shards, mesh=mesh, in_specs=in_specs, out_specs=out_specs, check_vma=False)
```

```python
import functools
import math

import jax
import jax.numpy as jnp
from jax import lax
from jax.experimental import pallas as pl
from jax.experimental.pallas import tpu as pltpu
from jax.sharding import PartitionSpec as P

STATE = 128
CONV = 4
BLOCK = 256
PIECE = 128
OWN_BC = 64
SHARED_AT = 128
LANES = 128
EPS = 1e-05
HIGH = lax.Precision.HIGHEST
LOG2E = math.log2(math.e)
BF16 = jnp.bfloat16
F32 = jnp.float32


def dot(left, right):
    return jnp.dot(left, right, preferred_element_type=F32)


def dot_last(left, right):
    return lax.dot_general(left, right, (((1,), (1,)), ((), ())), preferred_element_type=F32)


def dot_first(left, right):
    return lax.dot_general(left, right, (((0,), (0,)), ((), ())), preferred_element_type=F32)


def two_terms(array):
    upper = array.astype(BF16)
    return upper, (array - upper.astype(F32)).astype(BF16)


def sum_rows(ones, array):
    first = array.astype(BF16)
    second, third = two_terms(array - first.astype(F32))
    sums = dot(ones.astype(BF16), jnp.concatenate([first, second, third], axis=1))
    columns = array.shape[1]
    return sums[:, 0:columns] + sums[:, columns : 2 * columns] + sums[:, 2 * columns :]


def sigmoid(array):
    return 0.5 * jnp.tanh(0.5 * array) + 0.5


def spread_heads(array, heads_twice):
    upper, rest = two_terms(array)
    return dot(jnp.concatenate([upper, rest], axis=1), heads_twice)


def sum_heads(array, heads):
    upper, rest = two_terms(array)
    return dot_last(upper, heads) + dot_last(rest, heads)


def head_table(channels, head_count):
    head_width = channels // head_count
    channel = lax.broadcasted_iota(jnp.int32, (LANES, channels), 1)
    head = lax.broadcasted_iota(jnp.int32, (LANES, channels), 0)
    first = head * head_width
    return ((channel >= first) & (channel < first + head_width)).astype(F32).astype(BF16)


def head_rows(head_ref, heads):
    upper, rest = two_terms(head_ref[...])
    return dot(upper, heads) + dot(rest, heads)


def table_kernel(
    segment_ref,
    pre_gain_ref,
    bias_x_ref,
    gate_gain_ref,
    bias_bc_ref,
    dt_bias_ref,
    a_log_ref,
    d_skip_ref,
    token_ref,
    row_ref,
    head_ref,
):
    seq_count, length = segment_ref.shape
    place = lax.broadcasted_iota(jnp.int32, (8, length), 1)
    at_row = lax.broadcasted_iota(jnp.int32, (8, length), 0)
    for seq in range(seq_count):
        documents = jnp.broadcast_to(segment_ref[seq : seq + 1, :], (8, length)).astype(F32)
        padded = jnp.where(at_row == 0, documents, 0.0)

        def moved(by):
            other = pltpu.roll(documents, by % length, 1)
            return other, (place >= by) & (place < length + by)

        for k in range(1, CONV):
            before, inside = moved(k)
            padded = jnp.where((at_row == k) & inside & (before == documents), 1.0, padded)
        ends = []
        for piece in range(length // PIECE):
            here = slice(piece * PIECE, (piece + 1) * PIECE)
            ends.append(jnp.broadcast_to(documents[:, (piece + 1) * PIECE - 1 : (piece + 1) * PIECE], (8, PIECE)))
        starts = [jnp.full((8, PIECE), -1.0, F32)] + ends[:-1]
        padded = jnp.where((at_row == 4) & (jnp.concatenate(starts, axis=1) == documents), 1.0, padded)
        padded = jnp.where((at_row == 5) & (jnp.concatenate(ends, axis=1) == documents), 1.0, padded)
        lower = jnp.zeros((8, length), F32)
        for k in range(1, CONV):
            after, inside = moved(-k)
            hit = inside & (after == documents)
            if 5 + k < 8:
                padded = jnp.where((at_row == 5 + k) & hit, 1.0, padded)
            else:
                lower = jnp.where((at_row == 5 + k - 8) & hit, 1.0, lower)
        columns = slice(seq * length, (seq + 1) * length)
        token_ref[0:8, columns] = padded + jnp.where(at_row == 0, 64.0 * seq, 0.0)
        token_ref[8:16, columns] = lower
    row_ref[...] = jnp.zeros(row_ref.shape, F32)
    for at, ref in enumerate((pre_gain_ref, bias_x_ref, gate_gain_ref, bias_bc_ref)):
        row_ref[at : at + 1, 0 : ref.shape[0]] = ref[...].reshape(1, -1)
    head_ref[...] = jnp.zeros(head_ref.shape, F32)
    count = dt_bias_ref.shape[0]
    head_ref[0:1, 0:count] = dt_bias_ref[...].reshape(1, -1)
    head_ref[1:2, 0:count] = -jnp.exp(a_log_ref[...].reshape(1, -1))
    head_ref[2:3, 0:count] = d_skip_ref[...].reshape(1, -1)


def forward_kernel(
    hidden_ref,
    cotan_ref,
    w_gate_ref,
    w_value_ref,
    w_bc_ref,
    w_dt_ref,
    w_out_ref,
    conv_x_ref,
    conv_bc_ref,
    row_ref,
    head_ref,
    token_ref,
    normed_ref,
    mixed_ref,
    act_ref,
    turn_ref,
    grad_ref,
    scan_ref,
    value_ref,
    slope_ref,
    inner_ref,
    step_ref,
    cum_ref,
    bc_ref,
    bc_slope_ref,
    state_ref,
    enter_ref,
    sums_ref,
    tail_x,
    tail_bc,
    carried,
    wide_dt,
    gate_all,
    grad_all,
    tailed,
):
    block = pl.program_id(0)

    @pl.when(block == 0)
    def _():
        tail_x[0:8, :] = jnp.zeros((8, tail_x.shape[1]), F32)
        tail_bc[0:8, :] = jnp.zeros((8, tail_bc.shape[1]), F32)
        carried[...] = jnp.zeros(carried.shape, F32)
        wide_dt[...] = jnp.zeros(wide_dt.shape, BF16)
        wide_dt[0 : w_dt_ref.shape[0], :] = w_dt_ref[...]

    channels = tail_x.shape[1]
    heads = head_table(channels, w_dt_ref.shape[0])
    skips = head_rows(head_ref, heads)[2:3, :]
    side = token_ref[...].T
    hidden = hidden_ref[...].astype(F32)
    inv_rms = lax.rsqrt(jnp.mean(hidden * hidden, axis=-1, keepdims=True) + EPS)
    normed = (hidden * inv_rms * row_ref[0:1, :]).astype(BF16)
    normed_ref[...] = normed
    tail_x[8:, :] = dot(normed, w_value_ref[...])
    tail_bc[8:, :] = dot(normed, w_bc_ref[...])
    step_in = dot_last(normed, wide_dt[...]) + head_ref[0:1, :]
    step_ref[...] = step_in
    step = jnp.maximum(step_in, 0.0) + jnp.log1p(jnp.exp(-jnp.abs(step_in)))
    rate = head_ref[1:2, :] * step * LOG2E
    gate_all[...] = dot(normed, w_gate_ref[...])
    grad_all[...] = dot_last(cotan_ref[...], w_out_ref[...])
    masks = [None] + [side[:, k : k + 1] for k in range(1, CONV)]

    def conv(tail, taps_ref, bias_at, lanes):
        result = row_ref[bias_at : bias_at + 1, lanes] + taps_ref[CONV - 1 : CONV, lanes] * tail[8:, lanes]
        for k in range(1, CONV):
            shifted = tail[8 - k : 8 - k + BLOCK, lanes]
            result = result + taps_ref[CONV - 1 - k : CONV - k, lanes] * shifted * masks[k]
        return result

    for at in range(0, channels, LANES):
        lanes = slice(at, at + LANES)
        before = conv(tail_x, conv_x_ref, 1, lanes)
        half = sigmoid(before)
        value_ref[:, lanes] = (before * half).astype(BF16)
        slope_ref[:, lanes] = (half * (1.0 + before * (1.0 - half))).astype(BF16)
        inner_ref[:, lanes] = tail_x[8:, lanes].astype(BF16)
    for at in range(0, 2 * STATE, LANES):
        lanes = slice(at, at + LANES)
        before = conv(tail_bc, conv_bc_ref, 3, lanes)
        half = sigmoid(before)
        bc_ref[:, lanes] = (before * half).astype(BF16)
        bc_slope_ref[:, lanes] = half * (1.0 + before * (1.0 - half))
        state_ref[:, lanes] = tail_bc[8:, lanes]
    tail_x[0:8, :] = tail_x[BLOCK:, :]
    tail_bc[0:8, :] = tail_bc[BLOCK:, :]

    row_at = lax.broadcasted_iota(jnp.int32, (PIECE, PIECE), 0)
    col_at = lax.broadcasted_iota(jnp.int32, (PIECE, PIECE), 1)
    first_half = lax.broadcasted_iota(jnp.int32, (PIECE, LANES), 1) < LANES // 2
    heads_twice = jnp.concatenate([heads, heads], axis=0)
    block_row = lax.broadcasted_iota(jnp.int32, (BLOCK, BLOCK), 0)
    block_col = lax.broadcasted_iota(jnp.int32, (BLOCK, BLOCK), 1)
    lower = (block_row >= block_col) & (block_row // PIECE == block_col // PIECE)
    cums = sum_rows(lower.astype(F32), rate)
    cum_ref[...] = cums
    cums_t = cums.T
    lasts = [
        jnp.broadcast_to(cums[at + PIECE - 1 : at + PIECE, :], (PIECE, LANES)) for at in range(0, BLOCK, PIECE)
    ]
    reach = jnp.exp2(cums) * side[:, 4:5]
    tail = jnp.exp2(jnp.concatenate(lasts) - cums) * side[:, 5:6]
    wides = spread_heads(jnp.concatenate([step, reach, tail], axis=0), heads_twice)
    for piece in range(BLOCK // PIECE):
        rows = slice(piece * PIECE, (piece + 1) * PIECE)
        cum = cums[rows]
        cum_t = cums_t[:, rows]
        same = (side[rows, 0:1] == token_ref[0:1, rows]) & (row_at >= col_at)
        bias = jnp.where(same, 0.0, -1e30)
        wide = jnp.concatenate([wides[at + piece * PIECE : at + (piece + 1) * PIECE] for at in range(0, 3 * BLOCK, BLOCK)])
        b_low = bc_ref[rows, 0:STATE]
        c_low = bc_ref[rows, STATE : 2 * STATE]
        scores = dot_last(c_low, b_low)
        enter = carried[...].astype(BF16)
        enter_ref[piece] = enter
        from_state = dot(c_low, enter)
        for pair in range(channels // LANES):
            lanes = slice(pair * LANES, (pair + 1) * LANES)
            values = value_ref[rows, lanes].astype(F32)
            scaled = wide[0:PIECE, lanes] * values
            low = scaled.astype(BF16)
            weights = []
            for head in (2 * pair, 2 * pair + 1):
                gaps = (cum[:, head : head + 1] - cum_t[head : head + 1, :]) + bias
                weights.append((scores * jnp.exp2(gaps)).astype(BF16))
            zero = jnp.zeros_like(low)
            both = jnp.concatenate(
                [jnp.where(first_half, low, zero), jnp.where(first_half, zero, low)], axis=0
            )
            out = dot(jnp.concatenate(weights, axis=1), both)
            out = out + from_state[:, lanes] * wide[PIECE : 2 * PIECE, lanes]
            scan_ref[rows, lanes] = out + skips[:, lanes] * values
            tailed[:, lanes] = (wide[2 * PIECE :, lanes] * scaled).astype(BF16)
        kept = wide[2 * PIECE - 1 : 2 * PIECE, :]
        carried[...] = kept * carried[...] + dot_first(b_low, tailed[...])

    ones = jnp.ones((8, LANES), BF16)
    square_part = jnp.zeros((BLOCK, LANES), F32)
    cross_part = jnp.zeros((BLOCK, LANES), F32)
    for at in range(0, channels, LANES):
        lanes = slice(at, at + LANES)
        gate = gate_all[:, lanes]
        scan = scan_ref[:, lanes]
        grad = grad_all[:, lanes]
        half = sigmoid(gate)
        act = gate * half
        mixed = scan * act
        mixed_ref[:, lanes] = mixed.astype(BF16)
        act_ref[:, lanes] = act.astype(BF16)
        turn_ref[:, lanes] = (scan * (half * (1.0 + gate * (1.0 - half)))).astype(BF16)
        grad_ref[:, lanes] = grad.astype(BF16)
        square_part = square_part + mixed * mixed
        cross_part = cross_part + mixed * (grad * row_ref[2:3, lanes])
    upper, rest = two_terms(square_part)
    squares = dot_last(ones, upper) + dot_last(ones, rest)
    upper, rest = two_terms(cross_part)
    crosses = dot_last(ones, upper) + dot_last(ones, rest)
    is_first = lax.broadcasted_iota(jnp.int32, (8, BLOCK), 0) == 0
    sums_ref[...] = jnp.where(is_first, squares, crosses)


def store_halves(total, columns, mine, sent_ref, kept_ref, at=0):
    half = total.shape[0] // 2
    to = slice(at, at + half)
    for which, ref in ((1 - mine, sent_ref), (mine, kept_ref)):
        ref[to, :] = total[pl.ds(pl.multiple_of(which * half, 8), half), columns].astype(BF16)


def gate_columns(sums_ref):
    row_at = lax.broadcasted_iota(jnp.int32, (8, LANES), 0)

    def column(which):
        pick = (row_at == which).astype(F32)
        return lax.dot_general(
            sums_ref[...], pick, (((0,), (0,)), ((), ())), precision=HIGH, preferred_element_type=F32
        )

    inv_gate = lax.rsqrt(column(0) + EPS)
    return inv_gate, inv_gate * inv_gate * column(1)


def gate_kernel(
    low_ref,
    mixed_ref,
    turn_ref,
    grad_ref,
    sums_ref,
    row_ref,
    cotan_ref,
    normed_ref,
    gate_low_ref,
    gain_ref,
    sent_ref,
    kept_ref,
    gated,
    out_total,
    gate_total,
):
    block = pl.program_id(0)

    @pl.when(block == 0)
    def _():
        gain_ref[...] = jnp.zeros(gain_ref.shape, F32)
        out_total[...] = jnp.zeros(out_total.shape, F32)
        gate_total[...] = jnp.zeros(gate_total.shape, F32)

    channels = mixed_ref.shape[1]
    inv_gate, pull = gate_columns(sums_ref)
    for at in range(0, channels, LANES):
        lanes = slice(at, at + LANES)
        mixed = mixed_ref[:, lanes].astype(F32)
        grad = grad_ref[:, lanes].astype(F32)
        gain = row_ref[2:3, lanes]
        normal = mixed * inv_gate
        gated[:, lanes] = (normal * gain).astype(BF16)
        gain_ref[:, lanes] += jnp.sum((grad * normal).reshape(-1, 8, LANES), axis=0)
        mixed_grad = inv_gate * (grad * gain - mixed * pull)
        gate_low_ref[:, lanes] = (mixed_grad * turn_ref[:, lanes].astype(F32)).astype(BF16)
    out_total[...] += dot_first(gated[...], cotan_ref[...])
    gate_total[...] += dot_first(normed_ref[...], gate_low_ref[...])

    @pl.when(block == pl.num_programs(0) - 1)
    def _():
        rows, width = out_total.shape
        for at in range(width // channels):
            columns = slice(at * channels, (at + 1) * channels)
            store_halves(out_total, columns, low_ref[0], sent_ref, kept_ref, at * rows // 2)
        store_halves(gate_total, slice(None), low_ref[0], sent_ref, kept_ref, width // 2)


def weight_kernel(low_ref, normed_ref, grad_ref, after_ref, sent_ref, kept_ref, total):
    block = pl.program_id(0)
    part = dot_first(normed_ref[...], grad_ref[...])

    @pl.when(block == 0)
    def _():
        total[...] = part

    @pl.when(block > 0)
    def _():
        total[...] += part

    @pl.when(block == pl.num_programs(0) - 1)
    def _():
        store_halves(total, slice(None), low_ref[0], sent_ref, kept_ref)


def backward_kernel(
    head_count,
    mixed_ref,
    grad_ref,
    act_ref,
    sums_ref,
    row_ref,
    scan_ref,
    value_ref,
    slope_ref,
    inner_ref,
    step_ref,
    cum_ref,
    bc_ref,
    enter_ref,
    normed_ref,
    bc_slope_ref,
    state_ref,
    conv_x_ref,
    conv_bc_ref,
    head_ref,
    token_ref,
    after_ref,
    state_low_ref,
    inner_low_ref,
    step_low_ref,
    channel_grad_ref,
    conv_bc_grad_ref,
    head_grad_ref,
    step_rows_ref,
    bc_rows_ref,
    later,
    later_bc,
    leaving,
    step_total,
    dys,
    lows,
    reached,
    tailed,
    products,
):
    block = pl.program_id(0)

    @pl.when(block == 0)
    def _():
        later[PIECE:, :] = jnp.zeros((8, later.shape[1]), F32)
        later_bc[PIECE:, :] = jnp.zeros((8, later_bc.shape[1]), F32)
        conv_bc_grad_ref[...] = jnp.zeros(conv_bc_grad_ref.shape, F32)
        bc_rows_ref[...] = jnp.zeros(bc_rows_ref.shape, F32)
        leaving[...] = jnp.zeros(leaving.shape, F32)
        channel_grad_ref[...] = jnp.zeros(channel_grad_ref.shape, F32)
        head_grad_ref[...] = jnp.zeros(head_grad_ref.shape, F32)
        step_total[...] = jnp.zeros(step_total.shape, F32)

    channels = inner_ref.shape[1]
    row_at = lax.broadcasted_iota(jnp.int32, (PIECE, PIECE), 0)
    col_at = lax.broadcasted_iota(jnp.int32, (PIECE, PIECE), 1)
    upper_ones = (row_at <= col_at).astype(F32)
    first_half = lax.broadcasted_iota(jnp.int32, (PIECE, LANES), 1) < LANES // 2
    heads = head_table(channels, head_count)
    skips = head_rows(head_ref, heads)[2:3, :]
    side_all = token_ref[...].T
    inv_gate, pull = gate_columns(sums_ref)
    heads_twice = jnp.concatenate([heads, heads], axis=0)
    for piece in reversed(range(BLOCK // PIECE)):
        rows = slice(piece * PIECE, (piece + 1) * PIECE)
        side = side_all[rows]
        step_in = step_ref[rows, :]
        step = jnp.maximum(step_in, 0.0) + jnp.log1p(jnp.exp(-jnp.abs(step_in)))
        cum = cum_ref[rows, :]
        cum_t = cum.T
        same = (side[:, 0:1] == token_ref[0:1, rows]) & (row_at <= col_at)
        bias = jnp.where(same, 0.0, -1e30)
        reach = jnp.exp2(cum) * side[:, 4:5]
        tail = jnp.exp2(cum[PIECE - 1 : PIECE, :] - cum) * side[:, 5:6]
        wide = spread_heads(jnp.concatenate([step, reach, tail], axis=0), heads_twice)
        b_low = bc_ref[rows, 0:STATE]
        c_low = bc_ref[rows, STATE : 2 * STATE]
        scores = dot_last(b_low, c_low)
        score_grad = jnp.zeros((PIECE, PIECE), F32)
        masks = [None] + [side[:, 5 + k : 6 + k] for k in range(1, CONV)]
        for at in range(0, channels, LANES):
            lanes = slice(at, at + LANES)
            mixed = mixed_ref[rows, lanes].astype(F32)
            grad = grad_ref[rows, lanes].astype(F32)
            mixed_grad = inv_gate[rows] * (grad * row_ref[2:3, lanes] - mixed * pull[rows])
            dy_low = (mixed_grad * act_ref[rows, lanes].astype(F32)).astype(BF16)
            dys[:, lanes] = dy_low
            dy = dy_low.astype(F32)
            low = (wide[0:PIECE, lanes] * value_ref[rows, lanes].astype(F32)).astype(BF16)
            lows[:, lanes] = low
            reached[:, lanes] = (wide[PIECE : 2 * PIECE, lanes] * dy).astype(BF16)
            tailed[:, lanes] = (wide[2 * PIECE :, lanes] * low.astype(F32)).astype(BF16)
        leave = leaving[...]
        leave_low = leave.astype(BF16)
        enter_low = enter_ref[piece]
        kept = wide[2 * PIECE - 1 : 2 * PIECE, :]
        c_grad = dot_last(reached[...], enter_low)
        b_grad = dot_last(tailed[...], leave_low)
        from_states = dot(b_low, leave_low)
        kept_sum = kept * jnp.sum(enter_low.astype(F32) * leave, axis=0, keepdims=True)
        leaving[...] = kept * leave + dot_first(c_low, reached[...])
        for pair in range(channels // LANES):
            lanes = slice(pair * LANES, (pair + 1) * LANES)
            values = value_ref[rows, lanes].astype(F32)
            dy_low = dys[:, lanes]
            dy = dy_low.astype(F32)
            wide_step = wide[0:PIECE, lanes]
            low = lows[:, lanes]
            low_wide = low.astype(F32)
            from_state = wide[2 * PIECE :, lanes] * from_states[:, lanes]
            zero = jnp.zeros_like(low)
            own = jnp.concatenate(
                [jnp.where(first_half, dy_low, zero), jnp.where(first_half, zero, dy_low)], axis=0
            )
            weight_grads = dot_last(low, own)
            weights = []
            for at, head in enumerate((2 * pair, 2 * pair + 1)):
                gaps = (cum_t[head : head + 1, :] - cum[:, head : head + 1]) + bias
                decay = jnp.exp2(gaps)
                weights.append((scores * decay).astype(BF16))
                score_grad = score_grad + weight_grads[:, at * PIECE : (at + 1) * PIECE] * decay
            dx = dot(jnp.concatenate(weights, axis=1), own)
            dx = dx + from_state
            out = scan_ref[rows, lanes] - skips[:, lanes] * values
            last = jnp.sum(low_wide * from_state, axis=0, keepdims=True) + kept_sum[:, lanes]
            for at, product in enumerate(
                (dy * out - low_wide * dx, values * dx, jnp.broadcast_to(last, (16, LANES)))
            ):
                upper, rest = two_terms(product)
                products[2 * at * PIECE : 2 * at * PIECE + upper.shape[0], lanes] = upper
                products[2 * at * PIECE + upper.shape[0] : 2 * (at * PIECE + upper.shape[0]), lanes] = rest
            dvalue = wide_step * dx + skips[:, lanes] * dy
            dbefore = dvalue * slope_ref[rows, lanes].astype(F32)
            later[0:PIECE, lanes] = dbefore
            inner = inner_ref[rows, lanes].astype(F32)
            inner_grad = conv_x_ref[CONV - 1 : CONV, lanes] * dbefore
            channel_grad_ref[CONV - 1 : CONV, lanes] += jnp.sum(inner * dbefore, axis=0, keepdims=True)
            channel_grad_ref[CONV : CONV + 1, lanes] += jnp.sum(dbefore, axis=0, keepdims=True)
            channel_grad_ref[CONV + 1 : CONV + 2, lanes] += jnp.sum(dy * values, axis=0, keepdims=True)
            for k in range(1, CONV):
                shifted = later[k : k + PIECE, lanes] * masks[k]
                inner_grad = inner_grad + conv_x_ref[CONV - 1 - k : CONV - k, lanes] * shifted
                channel_grad_ref[CONV - 1 - k : CONV - k, lanes] += jnp.sum(
                    inner * shifted, axis=0, keepdims=True
                )
            inner_low_ref[rows, lanes] = inner_grad.astype(BF16)
        sums = dot_last(products[...], heads)
        row_sum = sums[0:PIECE] + sums[PIECE : 2 * PIECE]
        value_sum = sums[2 * PIECE : 3 * PIECE] + sums[3 * PIECE : 4 * PIECE]
        last_sum = sums[4 * PIECE : 4 * PIECE + 16] + sums[4 * PIECE + 16 : 4 * PIECE + 32]
        later[PIECE:, :] = later[0:8, :]
        grad_low = score_grad.astype(BF16)
        state_parts = (b_grad + dot(grad_low, c_low), c_grad + dot_first(grad_low, b_low))
        for at, state_part in enumerate(state_parts):
            lanes = slice(at * STATE, (at + 1) * STATE)
            dbefore = state_part * bc_slope_ref[rows, lanes]
            later_bc[0:PIECE, lanes] = dbefore
            state = state_ref[rows, lanes]
            state_grad = conv_bc_ref[CONV - 1 : CONV, lanes] * dbefore
            conv_bc_grad_ref[CONV - 1 : CONV, lanes] += jnp.sum(state * dbefore, axis=0, keepdims=True)
            conv_bc_grad_ref[CONV : CONV + 1, lanes] += jnp.sum(dbefore, axis=0, keepdims=True)
            for k in range(1, CONV):
                shifted = later_bc[k : k + PIECE, lanes] * masks[k]
                state_grad = state_grad + conv_bc_ref[CONV - 1 - k : CONV - k, lanes] * shifted
                conv_bc_grad_ref[CONV - 1 - k : CONV - k, lanes] += jnp.sum(
                    state * shifted, axis=0, keepdims=True
                )
            state_low_ref[rows, lanes] = state_grad.astype(BF16)
        later_bc[PIECE:, :] = later_bc[0:8, :]
        rate_grad = (
            jnp.dot(upper_ones, row_sum, precision=HIGH, preferred_element_type=F32) + last_sum[0:1, :]
        )
        coefficient = head_ref[1:2, :]
        step_grad = (value_sum + coefficient * rate_grad) / (1.0 + jnp.exp(-step_in))
        step_low_ref[rows, :] = step_grad.astype(BF16)
        head_grad_ref[0:1, :] += jnp.sum(step_grad, axis=0, keepdims=True)
        head_grad_ref[1:2, :] += jnp.sum(rate_grad * step, axis=0, keepdims=True) * coefficient
    step_total[...] += dot_first(step_low_ref[...], normed_ref[...])
    bc_rows_ref[...] += dot_first(state_low_ref[...], normed_ref[...])

    @pl.when(block == pl.num_programs(0) - 1)
    def _():
        step_rows_ref[...] = step_total[0 : step_rows_ref.shape[0], :]


def merge_kernel(
    core_ref,
    gate_low_ref,
    inner_low_ref,
    step_low_ref,
    state_low_ref,
    mixed_ref,
    normed_ref,
    sums_ref,
    w_gate_ref,
    w_value_ref,
    w_dt_ref,
    w_bc_ref,
    w_out_ref,
    row_ref,
    conv_bc_ref,
    after_ref,
    _,
    __,
    sent_ref,
    kept_ref,
    first_shared_ref,
    second_shared_ref,
    gain_ref,
    wide_dt,
    gated,
):
    block = pl.program_id(0)
    last = pl.num_programs(0) - 1

    @pl.when(block == 0)
    def _():
        gain_ref[...] = jnp.zeros(gain_ref.shape, F32)
        wide_dt[...] = jnp.zeros(wide_dt.shape, BF16)
        wide_dt[0 : w_dt_ref.shape[0], :] = w_dt_ref[...]

    width = normed_ref.shape[1]
    total = dot_last(inner_low_ref[...], w_value_ref[...]) + dot_last(gate_low_ref[...], w_gate_ref[...])
    total = total + dot_last(state_low_ref[...], w_bc_ref[...]) + dot(step_low_ref[...], wide_dt[...])
    gain_ref[...] += jnp.sum((total * normed_ref[...].astype(F32)).reshape(-1, 8, width), axis=0)
    inv_gate, _ = gate_columns(sums_ref)
    for at in range(0, mixed_ref.shape[1], LANES):
        lanes = slice(at, at + LANES)
        normal = mixed_ref[:, lanes].astype(F32) * inv_gate
        gated[:, lanes] = (normal * row_ref[2:3, lanes]).astype(BF16)
    branch = dot(gated[...], w_out_ref[...]).astype(BF16)

    @pl.when(2 * block < last)
    def _():
        sent_ref[:, 0:width] = total.astype(BF16)
        sent_ref[:, width:] = branch

    @pl.when(2 * block > last)
    def _():
        kept_ref[:, 0:width] = total.astype(BF16)
        kept_ref[:, width:] = branch

    @pl.when(block == last)
    def _():
        gain = jnp.sum(gain_ref[...], axis=0, keepdims=True) / row_ref[0:1, :]
        channels = first_shared_ref.shape[1]
        states = conv_bc_ref.shape[1]
        rows = [gain[:, at : at + channels] for at in range(0, width, channels)]
        conv = conv_bc_ref[0 : CONV + 1, :]
        rows.append(jnp.concatenate([conv, jnp.zeros((CONV + 1, channels - states), F32)], axis=1))
        rows.append(jnp.zeros((16 - width // channels - CONV - 1, channels), F32))
        shared = jnp.concatenate(rows).astype(BF16)
        first_shared_ref[...] = shared
        second_shared_ref[...] = shared


def pack_kernel(
    head_count,
    core_ref,
    bc_rows_ref,
    step_rows_ref,
    channel_ref,
    gate_gain_ref,
    head_ref,
    sent_ref,
    kept_ref,
    own_ref,
):
    core = core_ref[0]
    channels = channel_ref.shape[1]
    width = bc_rows_ref.shape[1]
    folds = width // channels
    groups = (kept_ref.shape[0] - 16) // (OWN_BC * folds)
    for which, ref in ((1 - core, sent_ref), (core, kept_ref)):
        for group in range(groups):
            found = bc_rows_ref[pl.ds(pl.multiple_of((2 * group + which) * OWN_BC, 8), OWN_BC), :].astype(BF16)
            for fold in range(folds):
                at = (group * folds + fold) * OWN_BC
                ref[at : at + OWN_BC, :] = found[:, fold * channels : (fold + 1) * channels]
    own_ref[...] = jnp.zeros(own_ref.shape, F32)
    for fold in range(folds):
        own_ref[16 * fold : 16 * fold + 16, :] = step_rows_ref[:, fold * channels : (fold + 1) * channels]
    at = 16 * folds
    own_ref[at : at + CONV + 1, :] = channel_ref[0 : CONV + 1, :]
    own_ref[at + CONV + 1 : at + CONV + 2, :] = jnp.sum(gate_gain_ref[...], axis=0, keepdims=True)
    skips = sum_heads(channel_ref[...], head_table(channels, head_count))
    own_ref[at + CONV + 2 : at + CONV + 4, 0:LANES] = head_ref[0:2, :]
    own_ref[at + CONV + 4 : at + CONV + 5, 0:LANES] = skips[CONV + 1 : CONV + 2, :]


def unpack_kernel(
    one_ref,
    two_ref,
    pre_gain_ref,
    bc_ref,
    dt_ref,
    conv_x_ref,
    bias_x_ref,
    conv_bc_ref,
    bias_bc_ref,
    dt_bias_ref,
    a_log_ref,
    d_skip_ref,
    gate_gain_ref,
    total,
):
    total[...] = one_ref[...].astype(F32) + two_ref[...].astype(F32)
    channels = total.shape[1]
    own_bc, width = bc_ref.shape
    folds = width // channels
    for fold in range(folds):
        bc_ref[:, fold * channels : (fold + 1) * channels] = total[fold * own_bc : (fold + 1) * own_bc, :]
    at = folds * own_bc
    pre_gain_ref[...] = jnp.concatenate([total[at + fold : at + fold + 1, :] for fold in range(folds)], axis=1).reshape(-1)
    at += folds
    states = conv_bc_ref.shape[1]
    conv_bc_ref[...] = total[at : at + CONV, 0:states]
    bias_bc_ref[...] = total[at + CONV : at + CONV + 1, 0:states].reshape(-1)
    at += 16 - folds
    count = dt_ref.shape[0]
    for fold in range(folds):
        dt_ref[:, fold * channels : (fold + 1) * channels] = total[at + 16 * fold : at + 16 * fold + count, :]
    at += 16 * folds
    conv_x_ref[...] = total[at : at + CONV, :]
    bias_x_ref[...] = total[at + CONV : at + CONV + 1, :].reshape(-1)
    gate_gain_ref[...] = total[at + CONV + 1 : at + CONV + 2, :].reshape(-1)
    at += CONV + 2
    for row, ref in enumerate((dt_bias_ref, a_log_ref, d_skip_ref)):
        ref[...] = total[at + row : at + row + 1, 0:LANES].reshape(-1)[0 : ref.shape[0]]


def hidden_kernel(rank_ref, hidden_ref, cotan_ref, kept_ref, got_ref, row_ref, out_ref, grad_ref):
    width = hidden_ref.shape[1]
    hidden = hidden_ref[...].astype(F32)
    branch = kept_ref[:, width:].astype(F32) + got_ref[:, width:].astype(F32)
    out_ref[...] = (hidden + branch).astype(BF16)
    inv_rms = lax.rsqrt(jnp.mean(hidden * hidden, axis=-1, keepdims=True) + EPS)
    scaled = (kept_ref[:, 0:width].astype(F32) + got_ref[:, 0:width].astype(F32)) * row_ref[0:1, :]
    pull = inv_rms * inv_rms * jnp.mean(scaled * hidden, axis=-1, keepdims=True)
    grad_ref[...] = cotan_ref[...].astype(F32) + inv_rms * (scaled - hidden * pull)


def pass_kernel(*refs):
    pass


def finish_kernel(which_ref, part_ref, after_ref, out_ref):
    out_ref[...] = part_ref[...].astype(F32)


def finish_pair_kernel(which_ref, part_ref, after_ref, *refs):
    out_ref, gate_ref = refs[-2:]
    rows, width = out_ref.shape
    channels = gate_ref.shape[1]
    for at in range(width // channels):
        out_ref[:, at * channels : (at + 1) * channels] = part_ref[at * rows : (at + 1) * rows, :].astype(F32)
    gate_ref[...] = part_ref[gate_ref.shape[0] :, :].astype(F32)


def finish_into_kernel(which_ref, part_ref, after_ref, whole_ref, out_ref):
    finish_kernel(which_ref, part_ref, after_ref, out_ref)


def split_kernel(which_ref, sent_one, sent_two, kept_one, kept_two, sent_ref, kept_ref):
    sent_ref[...] = (sent_one[...].astype(F32) + sent_two[...].astype(F32)).astype(BF16)
    kept_ref[...] = (kept_one[...].astype(F32) + kept_two[...].astype(F32)).astype(BF16)


def join_kernel(which_ref, own_ref, got_ref, own_extra_ref, got_extra_ref, out_ref):
    which = which_ref[0]
    rows = own_ref.shape[0]
    out_ref[pl.ds(pl.multiple_of(which * rows, 16), rows), :] = own_ref[...]
    out_ref[pl.ds(pl.multiple_of((1 - which) * rows, 16), rows), :] = got_ref[...]
    extra = own_extra_ref[...].astype(F32) + got_extra_ref[...].astype(F32)
    at = 2 * rows
    out_ref[at:, :] = extra.astype(BF16)
    shared = slice(SHARED_AT, SHARED_AT + 16)
    own_rows, got_rows = own_extra_ref[shared, :].astype(F32), got_extra_ref[shared, :].astype(F32)
    both_rows = jnp.concatenate([own_rows[0:8], got_rows[0:8]])
    out_ref[at + SHARED_AT : at + SHARED_AT + 16, :] = both_rows.astype(BF16)


def rider_kernel(core_ref, own_ref, got_ref, out_ref):
    out_ref[...] = (own_ref[...].astype(F32) + got_ref[...].astype(F32)).astype(BF16)
    shared = slice(SHARED_AT, SHARED_AT + 16)
    own, got = own_ref[shared, :].astype(F32), got_ref[shared, :].astype(F32)
    is_first = core_ref[0] == 0
    first = own[0:8] + jnp.where(is_first, got[0:8], own[8:16])
    second = jnp.where(is_first, own[8:16], got[0:8]) + got[8:16]
    out_ref[shared, :] = jnp.concatenate([first + second, jnp.zeros_like(first)]).astype(BF16)


def whole(shape):
    return pl.BlockSpec(shape, lambda i: (0,) * len(shape), pipeline_mode=pl.Buffered(1))


def no_cost():
    return pl.CostEstimate(flops=0, bytes_accessed=0, transcendentals=0)


def params():
    return pltpu.CompilerParams(vmem_limit_bytes=60 << 20)


def run_tables(segments, pre_gain, bias_x, gate_gain, bias_bc, dt_bias, a_log, d_skip):
    inputs = (segments, pre_gain, bias_x, gate_gain, bias_bc, dt_bias, a_log, d_skip)
    in_vmem = pl.BlockSpec(memory_space=pltpu.VMEM)
    return pl.pallas_call(
        table_kernel,
        in_specs=[in_vmem] * len(inputs),
        out_specs=[in_vmem] * 3,
        out_shape=[
            jax.ShapeDtypeStruct((16, segments.size), F32),
            jax.ShapeDtypeStruct((8, pre_gain.shape[0]), F32),
            jax.ShapeDtypeStruct((8, LANES), F32),
        ],
        compiler_params=params(),
        name="tables",
    )(*inputs)


def in_place():
    return pl.BlockSpec(memory_space=pl.ANY)


def run_forward(hidden_in, cotangent, weights, tables, tokens):
    rows, width = hidden_in.shape
    channels = weights[0].shape[1]
    states = weights[2].shape[1]
    constants = (*weights, *tables)

    def block(columns):
        return pl.BlockSpec((BLOCK, columns), lambda i: (i, 0))

    def out(columns, kind=BF16):
        return jax.ShapeDtypeStruct((rows, columns), kind)

    return pl.pallas_call(
        forward_kernel,
        grid=(rows // BLOCK,),
        in_specs=[block(width), block(width)]
        + [whole(array.shape) for array in constants]
        + [pl.BlockSpec((tokens.shape[0], BLOCK), lambda i: (0, i))],
        out_specs=[block(width)]
        + [block(channels)] * 8
        + [block(LANES)] * 2
        + [block(states)] * 3
        + [
            pl.BlockSpec((BLOCK // PIECE, STATE, channels), lambda i: (i, 0, 0)),
            pl.BlockSpec((8, BLOCK), lambda i: (0, i)),
        ],
        out_shape=[
            out(width),
            out(channels),
            out(channels),
            out(channels),
            out(channels),
            out(channels, F32),
            out(channels),
            out(channels),
            out(channels),
            out(LANES, F32),
            out(LANES, F32),
            out(states),
            out(states, F32),
            out(states, F32),
            jax.ShapeDtypeStruct((rows // PIECE, STATE, channels), BF16),
            jax.ShapeDtypeStruct((8, rows), F32),
        ],
        scratch_shapes=[
            pltpu.VMEM((BLOCK + 8, channels), F32),
            pltpu.VMEM((BLOCK + 8, states), F32),
            pltpu.VMEM((STATE, channels), F32),
            pltpu.VMEM((LANES, width), BF16),
            pltpu.VMEM((BLOCK, channels), F32),
            pltpu.VMEM((BLOCK, channels), F32),
            pltpu.VMEM((PIECE, channels), BF16),
        ],
        compiler_params=params(),
        cost_estimate=no_cost(),
        name="forward",
    )(hidden_in, cotangent, *constants, tokens)


def scalar_spec():
    return pl.BlockSpec(memory_space=pltpu.SMEM)


def half_shapes(rows, columns):
    return [jax.ShapeDtypeStruct((rows // 2, columns), BF16)] * 2


def run_gate(low, forward, sums, rows_table, cotangent, normed):
    rows, channels = forward[0].shape
    width = cotangent.shape[1]

    def block(columns):
        return pl.BlockSpec((BLOCK, columns), lambda i: (i, 0))

    halves = [jax.ShapeDtypeStruct((width // 2 + width // 2, channels), BF16)] * 2
    out = pl.pallas_call(
        gate_kernel,
        grid=(rows // BLOCK,),
        in_specs=[scalar_spec()]
        + [block(channels)] * 3
        + [pl.BlockSpec((8, BLOCK), lambda i: (0, i)), whole(rows_table.shape), block(width), block(width)],
        out_specs=[block(channels), whole((8, channels))] + [whole(half.shape) for half in halves],
        out_shape=[jax.ShapeDtypeStruct((rows, channels), BF16), jax.ShapeDtypeStruct((8, channels), F32)]
        + halves,
        scratch_shapes=[
            pltpu.VMEM((BLOCK, channels), BF16),
            pltpu.VMEM((channels, width), F32),
            pltpu.VMEM((width, channels), F32),
        ],
        compiler_params=params(),
        cost_estimate=no_cost(),
        name="gate",
    )(low, *forward, sums, rows_table, cotangent, normed)
    return out[:2], out[2:]


def run_weight(low, normed, grad, after):
    rows, width = normed.shape
    channels = grad.shape[1]
    size = 2 * BLOCK
    halves = half_shapes(width, channels)
    return pl.pallas_call(
        weight_kernel,
        grid=(rows // size,),
        in_specs=[
            scalar_spec(),
            pl.BlockSpec((size, width), lambda i: (i, 0)),
            pl.BlockSpec((size, channels), lambda i: (i, 0)),
            in_place(),
        ],
        out_specs=[whole(half.shape) for half in halves],
        out_shape=halves,
        scratch_shapes=[pltpu.VMEM((width, channels), F32)],
        compiler_params=params(),
        cost_estimate=no_cost(),
        name="weight",
    )(low, normed, grad, after)


def run_backward(gate_inputs, sums, rows_table, by_channel, step_in, cum, bc_low, enter, normed, by_state, tables, after, head_count):
    rows, channels = by_channel[0].shape
    width = normed.shape[1]
    count = rows // BLOCK
    states = bc_low.shape[1]
    conv_x, conv_bc, head_values, tokens = tables

    def block(columns):
        return pl.BlockSpec((BLOCK, columns), lambda i: (count - 1 - i, 0))

    def low_rows(columns):
        return jax.ShapeDtypeStruct((rows, columns), BF16)

    totals = [
        jax.ShapeDtypeStruct(shape, F32)
        for shape in ((8, channels), (8, states), (8, LANES), (16, width), (states, width))
    ]
    return pl.pallas_call(
        functools.partial(backward_kernel, head_count),
        grid=(count,),
        in_specs=[block(channels)] * 3
        + [pl.BlockSpec((8, BLOCK), lambda i: (0, count - 1 - i)), whole(rows_table.shape)]
        + [block(channels)] * 4
        + [block(LANES), block(LANES), block(states)]
        + [pl.BlockSpec((BLOCK // PIECE, STATE, channels), lambda i: (count - 1 - i, 0, 0))]
        + [block(width), block(states), block(states)]
        + [whole(conv_x.shape), whole(conv_bc.shape), whole(head_values.shape)]
        + [pl.BlockSpec((tokens.shape[0], BLOCK), lambda i: (0, count - 1 - i)), in_place()],
        out_specs=[block(states), block(channels), block(LANES)]
        + [whole(shape.shape) for shape in totals],
        out_shape=[low_rows(states), low_rows(channels), low_rows(LANES)] + totals,
        scratch_shapes=[
            pltpu.VMEM((PIECE + 8, channels), F32),
            pltpu.VMEM((PIECE + 8, states), F32),
            pltpu.VMEM((STATE, channels), F32),
            pltpu.VMEM((LANES, width), F32),
            pltpu.VMEM((PIECE, channels), BF16),
            pltpu.VMEM((PIECE, channels), BF16),
            pltpu.VMEM((PIECE, channels), BF16),
            pltpu.VMEM((PIECE, channels), BF16),
            pltpu.VMEM((4 * PIECE + 32, channels), BF16),
        ],
        compiler_params=params(),
        cost_estimate=no_cost(),
        name="backward",
    )(*gate_inputs, sums, rows_table, *by_channel, step_in, cum, bc_low, enter, normed, *by_state, conv_x, conv_bc, head_values, tokens, after)


def run_merge(core, blocked, sums, weights, rows_table, conv_bc_grads, after, packed, ranks):
    normed = blocked[-1]
    rows, width = normed.shape
    channels = weights[0].shape[1]
    size = rows // ranks
    half = ranks // 2

    def rank_at(i, c):
        return jnp.where(i < half, 2 * i + 1 - c[0], 2 * (i - half) + c[0])

    def block(columns):
        return pl.BlockSpec((size, columns), lambda i, c: (rank_at(i, c), 0))

    def constant(shape):
        return pl.BlockSpec(shape, lambda i, c: (0,) * len(shape), pipeline_mode=pl.Buffered(1))

    out = jax.ShapeDtypeStruct((rows // 2, 2 * width), BF16)
    last = packed[0].shape[0] // 16 - 1
    shared = pl.BlockSpec((16, channels), lambda i, c: (last, 0))
    first = 5 + len(blocked) + len(weights)
    return pl.pallas_call(
        merge_kernel,
        grid_spec=pltpu.PrefetchScalarGridSpec(
            num_scalar_prefetch=1,
            grid=(ranks,),
            in_specs=[block(array.shape[1]) for array in blocked]
            + [pl.BlockSpec((8, size), lambda i, c: (0, rank_at(i, c)))]
            + [constant(array.shape) for array in (*weights, rows_table, conv_bc_grads)]
            + [in_place()] * 3,
            out_specs=[
                pl.BlockSpec((size, 2 * width), lambda i, c: (jnp.minimum(i, half - 1), 0)),
                pl.BlockSpec((size, 2 * width), lambda i, c: (jnp.maximum(i - half, 0), 0)),
                shared,
                shared,
            ],
            scratch_shapes=[
                pltpu.VMEM((8, width), F32),
                pltpu.VMEM((LANES, width), BF16),
                pltpu.VMEM((size, channels), BF16),
            ],
        ),
        out_shape=[out, out] + [jax.ShapeDtypeStruct(array.shape, BF16) for array in packed],
        input_output_aliases={first: 2, first + 1: 3},
        compiler_params=params(),
        cost_estimate=no_cost(),
        name="merge",
    )(core, *blocked, sums, *weights, rows_table, conv_bc_grads, after, *packed)


def run_pack(core, bc_rows, step_rows, channel_grads, gain_rows, head_grads, head_count):
    states, width = bc_rows.shape
    channels = channel_grads.shape[1]
    folds = width // channels
    in_vmem = pl.BlockSpec(memory_space=pltpu.VMEM)
    shared = jax.ShapeDtypeStruct((states // 2 * folds + 16, channels), BF16)
    return pl.pallas_call(
        functools.partial(pack_kernel, head_count),
        in_specs=[scalar_spec()] + [in_vmem] * 5,
        out_specs=[in_vmem] * 3,
        out_shape=[shared, shared, jax.ShapeDtypeStruct((16 * folds + 16, channels), F32)],
        compiler_params=params(),
        cost_estimate=no_cost(),
        name="pack",
    )(core, bc_rows, step_rows, channel_grads, gain_rows, head_grads)


def run_unpack(one, two, width, states, head_count):
    rows, channels = one.shape
    last = two.shape[0] // rows - 1
    in_vmem = pl.BlockSpec(memory_space=pltpu.VMEM)
    shapes = (
        (width,),
        (OWN_BC, width),
        (head_count, width),
        (CONV, channels),
        (channels,),
        (CONV, states),
        (states,),
        (head_count,),
        (head_count,),
        (head_count,),
        (channels,),
    )
    return pl.pallas_call(
        unpack_kernel,
        grid=(1,),
        in_specs=[
            pl.BlockSpec((rows, channels), lambda i: (0, 0)),
            pl.BlockSpec((rows, channels), lambda i: (last, 0)),
        ],
        out_specs=[pl.BlockSpec(shape, lambda i, rank=len(shape): (0,) * rank) for shape in shapes],
        out_shape=[jax.ShapeDtypeStruct(shape, F32) for shape in shapes],
        scratch_shapes=[pltpu.VMEM(one.shape, F32)],
        compiler_params=params(),
        cost_estimate=no_cost(),
        name="unpack",
    )(one, two)


def run_hidden(rank, hidden_in, cotangent, kept, got, rows_table):
    own_rows = kept.shape[0]
    width = hidden_in.shape[1]
    count = 2
    size = own_rows // count

    def own(columns):
        return pl.BlockSpec((size, columns), lambda i, r: (r[0] * count + i, 0))

    def block(columns):
        return pl.BlockSpec((size, columns), lambda i, r: (i, 0))

    return pl.pallas_call(
        hidden_kernel,
        grid_spec=pltpu.PrefetchScalarGridSpec(
            num_scalar_prefetch=1,
            grid=(count,),
            in_specs=[
                own(width),
                own(width),
                block(2 * width),
                block(2 * width),
                pl.BlockSpec(rows_table.shape, lambda i, r: (0, 0)),
            ],
            out_specs=[block(width), block(width)],
        ),
        out_shape=[
            jax.ShapeDtypeStruct((own_rows, width), BF16),
            jax.ShapeDtypeStruct((own_rows, width), F32),
        ],
        compiler_params=params(),
        cost_estimate=no_cost(),
        name="hidden",
    )(rank, hidden_in, cotangent, kept, got, rows_table)


def run_pass(arrays, after):
    count = len(arrays)
    return pl.pallas_call(
        pass_kernel,
        in_specs=[in_place()] * (count + 1),
        out_specs=[in_place()] * count,
        out_shape=[jax.ShapeDtypeStruct(array.shape, array.dtype) for array in arrays],
        input_output_aliases={at: at for at in range(count)},
        cost_estimate=no_cost(),
        name="pass",
    )(*arrays, after)


def run_finish(which, part, after, rows, into=None):
    columns = part.shape[1]
    count = 2
    size = rows // count
    inputs = [part, after] + ([] if into is None else [into])
    return pl.pallas_call(
        finish_kernel if into is None else finish_into_kernel,
        grid_spec=pltpu.PrefetchScalarGridSpec(
            num_scalar_prefetch=1,
            grid=(count,),
            in_specs=[pl.BlockSpec((size, columns), lambda i, w: (i, 0))] + [in_place()] * (len(inputs) - 1),
            out_specs=pl.BlockSpec((size, columns), lambda i, w: (w[0] * count + i, 0)),
        ),
        out_shape=jax.ShapeDtypeStruct((2 * rows, columns), F32),
        input_output_aliases={} if into is None else {3: 0},
        compiler_params=params(),
        cost_estimate=no_cost(),
        name="finish",
    )(jnp.reshape(which, (1,)), *inputs)


def run_finish_pair(which, part, after, out_shape, gate_shape, into=()):
    out_rows, out_columns = out_shape
    gate_rows, gate_columns = gate_shape
    return pl.pallas_call(
        finish_pair_kernel,
        grid_spec=pltpu.PrefetchScalarGridSpec(
            num_scalar_prefetch=1,
            grid=(1,),
            in_specs=[pl.BlockSpec((gate_rows, gate_columns), lambda i, w: (0, 0))]
            + [in_place()] * (1 + len(into)),
            out_specs=[
                pl.BlockSpec((out_rows // 2, out_columns), lambda i, w: (w[0], 0)),
                pl.BlockSpec((gate_rows // 2, gate_columns), lambda i, w: (w[0], 0)),
            ],
        ),
        out_shape=[jax.ShapeDtypeStruct(out_shape, F32), jax.ShapeDtypeStruct(gate_shape, F32)],
        input_output_aliases={3 + at: at for at in range(len(into))},
        compiler_params=params(),
        cost_estimate=no_cost(),
        name="finish_pair",
    )(jnp.reshape(which, (1,)), part, after, *into)


def run_split(one, two, which):
    half, columns = one.shape[0] // 2, one.shape[1]
    count = 2
    size = half // count
    sent = pl.BlockSpec((size, columns), lambda i, w: ((1 - w[0]) * count + i, 0))
    kept = pl.BlockSpec((size, columns), lambda i, w: (w[0] * count + i, 0))
    out = pl.BlockSpec((size, columns), lambda i, w: (i, 0))
    return pl.pallas_call(
        split_kernel,
        grid_spec=pltpu.PrefetchScalarGridSpec(
            num_scalar_prefetch=1,
            grid=(count,),
            in_specs=[sent, sent, kept, kept],
            out_specs=[out, out],
        ),
        out_shape=[jax.ShapeDtypeStruct((half, columns), BF16)] * 2,
        compiler_params=params(),
        cost_estimate=no_cost(),
        name="split",
    )(jnp.reshape(which.astype(jnp.int32), (1,)), one, two, one, two)


def run_join(which, own, got, extra_rows):
    rows = own.shape[0] - extra_rows
    columns = own.shape[1]
    matrix = pl.BlockSpec((rows, columns), lambda i, w: (0, 0))
    extra = pl.BlockSpec((extra_rows, columns), lambda i, w: (rows // extra_rows, 0))
    shape = (2 * rows + extra_rows, columns)
    return pl.pallas_call(
        join_kernel,
        grid_spec=pltpu.PrefetchScalarGridSpec(
            num_scalar_prefetch=1,
            grid=(1,),
            in_specs=[matrix, matrix, extra, extra],
            out_specs=pl.BlockSpec(shape, lambda i, w: (0, 0)),
        ),
        out_shape=jax.ShapeDtypeStruct(shape, BF16),
        compiler_params=params(),
        cost_estimate=no_cost(),
        name="join",
    )(jnp.reshape(which, (1,)), own, got, own, got)


def run_rider(core, own, got, rows):
    columns = own.shape[1]
    last = pl.BlockSpec((rows, columns), lambda i: (own.shape[0] // rows - 1, 0))
    return pl.pallas_call(
        rider_kernel,
        grid=(1,),
        in_specs=[scalar_spec(), last, last],
        out_specs=pl.BlockSpec((rows, columns), lambda i: (0, 0)),
        out_shape=jax.ShapeDtypeStruct((rows, columns), BF16),
        compiler_params=params(),
        cost_estimate=no_cost(),
        name="rider",
    )(core, own, got)


def swap(array, axis, bit):
    size = lax.axis_size(axis)
    return lax.ppermute(array, axis, [(source, source ^ bit) for source in range(size)])


def axis_bits(axis):
    size = lax.axis_size(axis)
    return [1 << place for place in range(size.bit_length() - 1)]


def half_of(array, which):
    half = array.shape[0] // 2
    return lax.dynamic_slice_in_dim(array, which * half, half, 0)


def sum_tensor(array):
    for bit in axis_bits("tensor"):
        array = array + swap(array, "tensor", bit)
    return array


def dp_bits(step):
    bits = axis_bits("dp")
    swapped = [bits[1], bits[0]] + bits[2:]
    return bits[step], swapped[step]


def own_bit(step):
    first, second = dp_bits(step)
    place = lax.axis_index("dp").astype(jnp.int32)
    core = lax.axis_index("tensor") % 2
    return jnp.where(core == 0, (place // first) % 2, (place // second) % 2)


def dp_pairs(step):
    ranks = lax.axis_size("tensor")
    pairs = dp_bits(step)
    return [
        (at * ranks + rank, (at ^ pairs[rank % 2]) * ranks + rank)
        for at in range(lax.axis_size("dp"))
        for rank in range(ranks)
    ]


def in_order(which, own, got):
    place = lax.broadcasted_iota(jnp.int32, (2, 1, 1), 0)
    return jnp.where(place == which, own[None], got[None])


def sum_steps(sent, kept, rider=None, own=None):
    axes = ("dp", "tensor")
    steps = range(1, len(axis_bits("dp")))
    terms = [kept]
    got = yield sent, axes, dp_pairs(0)

    def total(which):
        return sum(half_of(term, which).astype(F32) for term in terms)

    for step in steps:
        which = own_bit(step)
        terms.append(got)
        sent = total(1 - which).astype(BF16)
        terms = [half_of(term, which) for term in terms]
        got = yield sent, axes, dp_pairs(step)
    part = sum((term.astype(F32) for term in terms), got.astype(F32)).astype(BF16)
    extra = 0
    for step in reversed((0, *steps)):
        if step == 1 and rider is not None:
            rows = rider().astype(BF16)
            extra = rows.shape[0]
            part = jnp.concatenate([part, rows])
        if step == 0 and own is not None:
            own.append(part)
        got = yield part, axes, dp_pairs(step)
        if step and extra:
            part = run_join(own_bit(step), part, got, extra)
        elif step:
            part = in_order(own_bit(step), part, got).reshape(2 * part.shape[0], -1)
    if extra:
        core = (lax.axis_index("tensor") % 2).astype(jnp.int32)
        extra = run_rider(jnp.reshape(core, (1,)), part, got, extra)
    return own_bit(0), part, got, extra


def rest_steps(rows):
    axes = ("dp", "tensor")
    for step in range(2, len(axis_bits("dp"))):
        got = yield rows, axes, dp_pairs(step)
        total = rows.astype(F32) + got.astype(F32)
        last, rows = (rows, got), total.astype(BF16)
    return last


def both_steps(sent, kept):
    size = lax.axis_size("tensor")
    rank = lax.axis_index("tensor")
    got = yield sent, "tensor", [(i, i ^ 1) for i in range(size)]
    for bit in axis_bits("tensor")[1:]:
        sent, kept = run_split(kept, got, (rank // bit) % 2)
        got = yield sent, "tensor", [(i, i ^ bit) for i in range(size)]
    return kept, got


def small_steps(sent, kept, own):
    size = lax.axis_size("tensor")
    rank = lax.axis_index("tensor")
    got = yield sent, "tensor", [(i, i ^ 1) for i in range(size)]
    total = kept.astype(F32) + got.astype(F32)
    for bit in axis_bits("tensor")[1:]:
        which = (rank // bit) % 2
        shared = lax.reduce_precision(total[-16:], 8, 7).astype(BF16)
        rows = total[:-16]
        got = yield jnp.concatenate([half_of(rows, 1 - which).astype(BF16), shared]), "tensor", [
            (i, i ^ bit) for i in range(size)
        ]
        total = jnp.concatenate([half_of(rows, which), shared.astype(F32)]) + got.astype(F32)
    return jnp.concatenate([total, own])


class Order:
    def __init__(self, last):
        self.last = last
        self.waiting = {}
        self.flying = {}
        self.arrived = {}
        self.results = {}

    def advance(self, name, steps, got):
        try:
            request = steps.send(got)
            self.waiting[name] = (steps, request)
            self.last = request[0]
        except StopIteration as end:
            self.results[name] = end.value

    def add(self, name, steps):
        last = self.last
        self.advance(name, steps, None)
        self.last = last

    def go(self, *names):
        for name in names:
            if name in self.waiting:
                steps, (sent, axis, moves) = self.waiting.pop(name)
                self.flying[name] = (steps, lax.ppermute(sent, axis, moves))

    def arrive(self, *names):
        found = [(name, *self.flying.pop(name)) for name in names if name in self.flying]
        if found:
            passed = run_pass([got for _, _, got in found], self.last)
            self.last = passed[0]
            for (name, steps, _), got in zip(found, passed):
                self.arrived[name] = (steps, got)

    def take(self, *names):
        for name in names:
            if name in self.arrived:
                steps, got = self.arrived.pop(name)
                self.advance(name, steps, got if got is self.last else self.hold(got))
                if name in self.waiting:
                    self.last = self.waiting[name][1][0]

    def land(self, *names):
        self.arrive(*names)
        self.take(*names)

    def hold(self, array):
        return run_pass([array], self.last)[0]

    def step(self, *names):
        for name in names:
            self.land(name)
            self.go(name)

    def until(self, name, found):
        while not found:
            self.step(name)
        return found[0]

    def result(self, name):
        while name not in self.results:
            self.go(name)
            self.land(name)
        return self.results[name]


def shards(
    hidden_in,
    pre_gain,
    w_gate,
    w_value,
    w_bc,
    w_dt,
    conv_x,
    conv_x_bias,
    conv_bc,
    conv_bc_bias,
    dt_bias,
    a_log,
    d_skip,
    gate_gain,
    w_out,
    cotangent,
    segments,
):
    row_count, width = hidden_in.shape
    channels = w_gate.shape[1]
    head_count = dt_bias.shape[0]
    head_width = channels // head_count
    ranks = lax.axis_size("tensor")
    my_rank = lax.axis_index("tensor")
    own_rows = row_count // ranks
    row_start = my_rank * own_rows
    pair_width = w_bc.shape[1] // ranks
    low = jnp.reshape(own_bit(0), (1,))
    w_dt_rows = w_dt.T
    tokens, rows_table, head_values = run_tables(
        segments, pre_gain, conv_x_bias, gate_gain, conv_bc_bias, dt_bias, a_log, d_skip
    )
    (
        normed,
        mixed,
        act,
        turn,
        gated_grad,
        scan,
        values,
        slope,
        inner_pre,
        step_in,
        cum,
        bc_low,
        bc_slope,
        state_pre,
        enter,
        sums,
    ) = run_forward(
        hidden_in,
        cotangent,
        (w_gate, w_value, w_bc, w_dt_rows, w_out),
        (conv_x, conv_bc, rows_table, head_values),
        tokens,
    )
    sums = sum_tensor(sums) / (channels * ranks)
    (gate_low, gain_rows), halves = run_gate(
        low, (mixed, turn, gated_grad), sums, rows_table, cotangent, normed
    )
    order = Order(gate_low)
    first_own, second_own = [], []
    order.add("first", sum_steps(*halves, lambda: order.result("small"), first_own))
    order.go("first")
    (
        state_low,
        inner_low,
        step_low,
        channel_grads,
        conv_bc_grads,
        head_grads,
        step_rows,
        bc_rows,
    ) = run_backward(
        (mixed, gated_grad, act),
        sums,
        rows_table,
        (scan, values, slope, inner_pre),
        step_in,
        cum,
        bc_low,
        enter,
        normed,
        (bc_slope, state_pre),
        (conv_x, conv_bc, head_values, tokens),
        halves[0],
        head_count,
    )
    order.last = inner_low
    order.step("first")
    sent, kept = run_weight(low, normed, inner_low, order.last)
    order.last = kept
    order.step("first")
    order.add("second", sum_steps(order.hold(sent), kept, None, second_own))
    order.go("second")
    core = jnp.reshape((my_rank % 2).astype(jnp.int32), (1,))
    small_sent, small_kept, small_own = run_pack(
        core, bc_rows, step_rows, channel_grads, gain_rows, head_grads, head_count
    )
    both_sent, both_kept, small_sent, small_kept = run_merge(
        core,
        (gate_low, inner_low, step_low, state_low, mixed, normed),
        sums,
        (w_gate, w_value, w_dt_rows, w_bc, w_out),
        rows_table,
        conv_bc_grads,
        order.last,
        (small_sent, small_kept),
        ranks,
    )
    order.last = both_kept
    order.land("second", "first")
    order.go("second", "first")
    order.add("small", small_steps(order.hold(small_sent), small_kept, small_own))
    order.go("small")
    order.add("both", both_steps(order.hold(both_sent), both_kept))
    order.go("both")
    order.step("small")
    order.land("small")
    order.land("second", "first")
    order.go("second", "first")
    order.step("second")
    order.step("both")
    order.land("second")
    order.land("first")
    order.go("second", "first")
    order.step("second")
    which = own_bit(0)
    sums_first = run_finish_pair(which, order.until("first", first_own), order.last, w_out.shape, w_gate.shape)
    order.last = sums_first[0]
    own = order.until("second", second_own)
    w_value_sum = run_finish(which, own, order.last, own.shape[0])
    order.last = w_value_sum
    _, _, got, rows = order.result("first")
    order.add("rest", rest_steps(rows))
    order.go("rest")
    w_out_sum, w_gate_sum = run_finish_pair(
        1 - which, got, order.last, w_out.shape, w_gate.shape, sums_first
    )
    order.last = w_out_sum
    kept, got = order.result("both")
    block_out, hidden_grad = run_hidden(
        jnp.reshape(my_rank.astype(jnp.int32), (1,)), hidden_in, cotangent, kept, got, rows_table
    )
    order.last = hidden_grad
    one, two = order.result("rest")
    small = run_unpack(one, two, width, w_bc.shape[1], head_count)
    order.last = small[0]
    _, own, got, _ = order.result("second")
    w_value_sum = run_finish(1 - which, got, order.last, own.shape[0], w_value_sum)
    (
        pre_gain_grad,
        w_bc_rows,
        dt_rows,
        conv_x_grad,
        conv_x_bias_grad,
        conv_bc_grad,
        conv_bc_bias_grad,
        dt_bias_grad,
        a_log_grad,
        d_skip_grad,
        gate_gain_grad,
    ) = small
    return (
        block_out,
        hidden_grad,
        pre_gain_grad,
        w_gate_sum,
        w_value_sum,
        w_bc_rows.T,
        dt_rows.T,
        conv_x_grad,
        conv_x_bias_grad,
        conv_bc_grad,
        conv_bc_bias_grad,
        dt_bias_grad,
        a_log_grad,
        d_skip_grad,
        gate_gain_grad,
        w_out_sum,
    )


def solution(mesh):
    in_specs = (
        P("dp", None),
        P(),
        P(None, "tensor"),
        P(None, "tensor"),
        P(),
        P(None, "tensor"),
        P(None, "tensor"),
        P("tensor"),
        P(),
        P(),
        P("tensor"),
        P("tensor"),
        P("tensor"),
        P("tensor"),
        P("tensor", None),
        P("dp", None),
        P("dp", None),
    )
    out_specs = (
        P(("dp", "tensor"), None),
        P(("dp", "tensor"), None),
        P(),
        P(None, "tensor"),
        P(None, "tensor"),
        P(None, "tensor"),
        P(None, "tensor"),
        P(None, "tensor"),
        P("tensor"),
        P(),
        P(),
        P("tensor"),
        P("tensor"),
        P("tensor"),
        P("tensor"),
        P("tensor", None),
    )
    return jax.shard_map(shards, mesh=mesh, in_specs=in_specs, out_specs=out_specs, check_vma=False)
```

```python
import functools
import math

import jax
import jax.numpy as jnp
from jax import lax
from jax.experimental import pallas as pl
from jax.experimental.pallas import tpu as pltpu
from jax.sharding import PartitionSpec as P

STATE = 128
CONV = 4
BLOCK = 256
PIECE = 128
OWN_BC = 64
SHARED_AT = 128
LANES = 128
EPS = 1e-05
HIGH = lax.Precision.HIGHEST
LOG2E = math.log2(math.e)
BF16 = jnp.bfloat16
F32 = jnp.float32


def dot(left, right):
    return jnp.dot(left, right, preferred_element_type=F32)


def dot_last(left, right):
    return lax.dot_general(left, right, (((1,), (1,)), ((), ())), preferred_element_type=F32)


def dot_first(left, right):
    return lax.dot_general(left, right, (((0,), (0,)), ((), ())), preferred_element_type=F32)


def two_terms(array):
    upper = array.astype(BF16)
    return upper, (array - upper.astype(F32)).astype(BF16)


def sum_rows(ones, array):
    first = array.astype(BF16)
    second, third = two_terms(array - first.astype(F32))
    sums = dot(ones.astype(BF16), jnp.concatenate([first, second, third], axis=1))
    columns = array.shape[1]
    return sums[:, 0:columns] + sums[:, columns : 2 * columns] + sums[:, 2 * columns :]


def sigmoid(array):
    return 0.5 * jnp.tanh(0.5 * array) + 0.5


def spread_heads(array, heads_twice):
    upper, rest = two_terms(array)
    return dot(jnp.concatenate([upper, rest], axis=1), heads_twice)


def sum_heads(array, heads):
    upper, rest = two_terms(array)
    return dot_last(upper, heads) + dot_last(rest, heads)


def head_table(channels, head_count):
    head_width = channels // head_count
    channel = lax.broadcasted_iota(jnp.int32, (LANES, channels), 1)
    head = lax.broadcasted_iota(jnp.int32, (LANES, channels), 0)
    first = head * head_width
    return ((channel >= first) & (channel < first + head_width)).astype(F32).astype(BF16)


def head_rows(head_ref, heads):
    upper, rest = two_terms(head_ref[...])
    return dot(upper, heads) + dot(rest, heads)


def table_kernel(
    segment_ref,
    pre_gain_ref,
    bias_x_ref,
    gate_gain_ref,
    bias_bc_ref,
    dt_bias_ref,
    a_log_ref,
    d_skip_ref,
    token_ref,
    row_ref,
    head_ref,
):
    seq_count, length = segment_ref.shape
    place = lax.broadcasted_iota(jnp.int32, (8, length), 1)
    at_row = lax.broadcasted_iota(jnp.int32, (8, length), 0)
    for seq in range(seq_count):
        documents = jnp.broadcast_to(segment_ref[seq : seq + 1, :], (8, length)).astype(F32)
        padded = jnp.where(at_row == 0, documents, 0.0)

        def moved(by):
            other = pltpu.roll(documents, by % length, 1)
            return other, (place >= by) & (place < length + by)

        for k in range(1, CONV):
            before, inside = moved(k)
            padded = jnp.where((at_row == k) & inside & (before == documents), 1.0, padded)
        ends = []
        for piece in range(length // PIECE):
            here = slice(piece * PIECE, (piece + 1) * PIECE)
            ends.append(jnp.broadcast_to(documents[:, (piece + 1) * PIECE - 1 : (piece + 1) * PIECE], (8, PIECE)))
        starts = [jnp.full((8, PIECE), -1.0, F32)] + ends[:-1]
        padded = jnp.where((at_row == 4) & (jnp.concatenate(starts, axis=1) == documents), 1.0, padded)
        padded = jnp.where((at_row == 5) & (jnp.concatenate(ends, axis=1) == documents), 1.0, padded)
        lower = jnp.zeros((8, length), F32)
        for k in range(1, CONV):
            after, inside = moved(-k)
            hit = inside & (after == documents)
            if 5 + k < 8:
                padded = jnp.where((at_row == 5 + k) & hit, 1.0, padded)
            else:
                lower = jnp.where((at_row == 5 + k - 8) & hit, 1.0, lower)
        columns = slice(seq * length, (seq + 1) * length)
        token_ref[0:8, columns] = padded + jnp.where(at_row == 0, 64.0 * seq, 0.0)
        token_ref[8:16, columns] = lower
    row_ref[...] = jnp.zeros(row_ref.shape, F32)
    for at, ref in enumerate((pre_gain_ref, bias_x_ref, gate_gain_ref, bias_bc_ref)):
        row_ref[at : at + 1, 0 : ref.shape[0]] = ref[...].reshape(1, -1)
    head_ref[...] = jnp.zeros(head_ref.shape, F32)
    count = dt_bias_ref.shape[0]
    head_ref[0:1, 0:count] = dt_bias_ref[...].reshape(1, -1)
    head_ref[1:2, 0:count] = -jnp.exp(a_log_ref[...].reshape(1, -1))
    head_ref[2:3, 0:count] = d_skip_ref[...].reshape(1, -1)


def forward_kernel(
    hidden_ref,
    cotan_ref,
    w_gate_ref,
    w_value_ref,
    w_bc_ref,
    w_dt_ref,
    w_out_ref,
    conv_x_ref,
    conv_bc_ref,
    row_ref,
    head_ref,
    token_ref,
    normed_ref,
    mixed_ref,
    act_ref,
    turn_ref,
    grad_ref,
    scan_ref,
    value_ref,
    slope_ref,
    inner_ref,
    step_ref,
    cum_ref,
    bc_ref,
    bc_slope_ref,
    state_ref,
    enter_ref,
    sums_ref,
    tail_x,
    tail_bc,
    carried,
    wide_dt,
    gate_all,
    grad_all,
    tailed,
):
    block = pl.program_id(0)

    @pl.when(block == 0)
    def _():
        tail_x[0:8, :] = jnp.zeros((8, tail_x.shape[1]), F32)
        tail_bc[0:8, :] = jnp.zeros((8, tail_bc.shape[1]), F32)
        carried[...] = jnp.zeros(carried.shape, F32)
        wide_dt[...] = jnp.zeros(wide_dt.shape, BF16)
        wide_dt[0 : w_dt_ref.shape[0], :] = w_dt_ref[...]

    channels = tail_x.shape[1]
    heads = head_table(channels, w_dt_ref.shape[0])
    skips = head_rows(head_ref, heads)[2:3, :]
    side = token_ref[...].T
    hidden = hidden_ref[...].astype(F32)
    inv_rms = lax.rsqrt(jnp.mean(hidden * hidden, axis=-1, keepdims=True) + EPS)
    normed = (hidden * inv_rms * row_ref[0:1, :]).astype(BF16)
    normed_ref[...] = normed
    tail_x[8:, :] = dot(normed, w_value_ref[...])
    tail_bc[8:, :] = dot(normed, w_bc_ref[...])
    step_in = dot_last(normed, wide_dt[...]) + head_ref[0:1, :]
    step_ref[...] = step_in
    step = jnp.maximum(step_in, 0.0) + jnp.log1p(jnp.exp(-jnp.abs(step_in)))
    rate = head_ref[1:2, :] * step * LOG2E
    gate_all[...] = dot(normed, w_gate_ref[...])
    grad_all[...] = dot_last(cotan_ref[...], w_out_ref[...])
    masks = [None] + [side[:, k : k + 1] for k in range(1, CONV)]

    def conv(tail, taps_ref, bias_at, lanes):
        result = row_ref[bias_at : bias_at + 1, lanes] + taps_ref[CONV - 1 : CONV, lanes] * tail[8:, lanes]
        for k in range(1, CONV):
            shifted = tail[8 - k : 8 - k + BLOCK, lanes]
            result = result + taps_ref[CONV - 1 - k : CONV - k, lanes] * shifted * masks[k]
        return result

    for at in range(0, channels, LANES):
        lanes = slice(at, at + LANES)
        before = conv(tail_x, conv_x_ref, 1, lanes)
        half = sigmoid(before)
        value_ref[:, lanes] = (before * half).astype(BF16)
        slope_ref[:, lanes] = (half * (1.0 + before * (1.0 - half))).astype(BF16)
        inner_ref[:, lanes] = tail_x[8:, lanes].astype(BF16)
    for at in range(0, 2 * STATE, LANES):
        lanes = slice(at, at + LANES)
        before = conv(tail_bc, conv_bc_ref, 3, lanes)
        half = sigmoid(before)
        bc_ref[:, lanes] = (before * half).astype(BF16)
        bc_slope_ref[:, lanes] = half * (1.0 + before * (1.0 - half))
        state_ref[:, lanes] = tail_bc[8:, lanes]
    tail_x[0:8, :] = tail_x[BLOCK:, :]
    tail_bc[0:8, :] = tail_bc[BLOCK:, :]

    row_at = lax.broadcasted_iota(jnp.int32, (PIECE, PIECE), 0)
    col_at = lax.broadcasted_iota(jnp.int32, (PIECE, PIECE), 1)
    first_half = lax.broadcasted_iota(jnp.int32, (PIECE, LANES), 1) < LANES // 2
    heads_twice = jnp.concatenate([heads, heads], axis=0)
    block_row = lax.broadcasted_iota(jnp.int32, (BLOCK, BLOCK), 0)
    block_col = lax.broadcasted_iota(jnp.int32, (BLOCK, BLOCK), 1)
    lower = (block_row >= block_col) & (block_row // PIECE == block_col // PIECE)
    cums = sum_rows(lower.astype(F32), rate)
    cum_ref[...] = cums
    cums_t = cums.T
    lasts = [
        jnp.broadcast_to(cums[at + PIECE - 1 : at + PIECE, :], (PIECE, LANES)) for at in range(0, BLOCK, PIECE)
    ]
    reach = jnp.exp2(cums) * side[:, 4:5]
    tail = jnp.exp2(jnp.concatenate(lasts) - cums) * side[:, 5:6]
    wides = spread_heads(jnp.concatenate([step, reach, tail], axis=0), heads_twice)
    for piece in range(BLOCK // PIECE):
        rows = slice(piece * PIECE, (piece + 1) * PIECE)
        cum = cums[rows]
        cum_t = cums_t[:, rows]
        same = (side[rows, 0:1] == token_ref[0:1, rows]) & (row_at >= col_at)
        bias = jnp.where(same, 0.0, -1e30)
        wide = jnp.concatenate([wides[at + piece * PIECE : at + (piece + 1) * PIECE] for at in range(0, 3 * BLOCK, BLOCK)])
        b_low = bc_ref[rows, 0:STATE]
        c_low = bc_ref[rows, STATE : 2 * STATE]
        scores = dot_last(c_low, b_low)
        enter = carried[...].astype(BF16)
        enter_ref[piece] = enter
        from_state = dot(c_low, enter)
        for pair in range(channels // LANES):
            lanes = slice(pair * LANES, (pair + 1) * LANES)
            values = value_ref[rows, lanes].astype(F32)
            scaled = wide[0:PIECE, lanes] * values
            low = scaled.astype(BF16)
            weights = []
            for head in (2 * pair, 2 * pair + 1):
                gaps = (cum[:, head : head + 1] - cum_t[head : head + 1, :]) + bias
                weights.append((scores * jnp.exp2(gaps)).astype(BF16))
            zero = jnp.zeros_like(low)
            both = jnp.concatenate(
                [jnp.where(first_half, low, zero), jnp.where(first_half, zero, low)], axis=0
            )
            out = dot(jnp.concatenate(weights, axis=1), both)
            out = out + from_state[:, lanes] * wide[PIECE : 2 * PIECE, lanes]
            scan_ref[rows, lanes] = out + skips[:, lanes] * values
            tailed[:, lanes] = (wide[2 * PIECE :, lanes] * scaled).astype(BF16)
        kept = wide[2 * PIECE - 1 : 2 * PIECE, :]
        carried[...] = kept * carried[...] + dot_first(b_low, tailed[...])

    ones = jnp.ones((8, LANES), BF16)
    square_part = jnp.zeros((BLOCK, LANES), F32)
    cross_part = jnp.zeros((BLOCK, LANES), F32)
    for at in range(0, channels, LANES):
        lanes = slice(at, at + LANES)
        gate = gate_all[:, lanes]
        scan = scan_ref[:, lanes]
        grad = grad_all[:, lanes]
        half = sigmoid(gate)
        act = gate * half
        mixed = scan * act
        mixed_ref[:, lanes] = mixed.astype(BF16)
        act_ref[:, lanes] = act.astype(BF16)
        turn_ref[:, lanes] = (scan * (half * (1.0 + gate * (1.0 - half)))).astype(BF16)
        grad_ref[:, lanes] = grad.astype(BF16)
        square_part = square_part + mixed * mixed
        cross_part = cross_part + mixed * (grad * row_ref[2:3, lanes])
    upper, rest = two_terms(square_part)
    squares = dot_last(ones, upper) + dot_last(ones, rest)
    upper, rest = two_terms(cross_part)
    crosses = dot_last(ones, upper) + dot_last(ones, rest)
    is_first = lax.broadcasted_iota(jnp.int32, (8, BLOCK), 0) == 0
    sums_ref[...] = jnp.where(is_first, squares, crosses)


def store_halves(total, columns, mine, sent_ref, kept_ref, at=0):
    half = total.shape[0] // 2
    to = slice(at, at + half)
    for which, ref in ((1 - mine, sent_ref), (mine, kept_ref)):
        ref[to, :] = total[pl.ds(pl.multiple_of(which * half, 8), half), columns].astype(BF16)


def gate_columns(sums_ref):
    row_at = lax.broadcasted_iota(jnp.int32, (8, LANES), 0)

    def column(which):
        pick = (row_at == which).astype(F32)
        return lax.dot_general(
            sums_ref[...], pick, (((0,), (0,)), ((), ())), precision=HIGH, preferred_element_type=F32
        )

    inv_gate = lax.rsqrt(column(0) + EPS)
    return inv_gate, inv_gate * inv_gate * column(1)


def gate_kernel(
    low_ref,
    mixed_ref,
    turn_ref,
    grad_ref,
    sums_ref,
    row_ref,
    cotan_ref,
    normed_ref,
    gate_low_ref,
    gain_ref,
    sent_ref,
    kept_ref,
    gated,
    out_total,
    gate_total,
):
    block = pl.program_id(0)

    @pl.when(block == 0)
    def _():
        gain_ref[...] = jnp.zeros(gain_ref.shape, F32)
        out_total[...] = jnp.zeros(out_total.shape, F32)
        gate_total[...] = jnp.zeros(gate_total.shape, F32)

    channels = mixed_ref.shape[1]
    inv_gate, pull = gate_columns(sums_ref)
    for at in range(0, channels, LANES):
        lanes = slice(at, at + LANES)
        mixed = mixed_ref[:, lanes].astype(F32)
        grad = grad_ref[:, lanes].astype(F32)
        gain = row_ref[2:3, lanes]
        normal = mixed * inv_gate
        gated[:, lanes] = (normal * gain).astype(BF16)
        gain_ref[:, lanes] += jnp.sum((grad * normal).reshape(-1, 8, LANES), axis=0)
        mixed_grad = inv_gate * (grad * gain - mixed * pull)
        gate_low_ref[:, lanes] = (mixed_grad * turn_ref[:, lanes].astype(F32)).astype(BF16)
    out_total[...] += dot_first(gated[...], cotan_ref[...])
    gate_total[...] += dot_first(normed_ref[...], gate_low_ref[...])

    @pl.when(block == pl.num_programs(0) - 1)
    def _():
        rows, width = out_total.shape
        for at in range(width // channels):
            columns = slice(at * channels, (at + 1) * channels)
            store_halves(out_total, columns, low_ref[0], sent_ref, kept_ref, at * rows // 2)
        store_halves(gate_total, slice(None), low_ref[0], sent_ref, kept_ref, width // 2)


def weight_kernel(low_ref, normed_ref, grad_ref, after_ref, sent_ref, kept_ref, total):
    block = pl.program_id(0)
    part = dot_first(normed_ref[...], grad_ref[...])

    @pl.when(block == 0)
    def _():
        total[...] = part

    @pl.when(block > 0)
    def _():
        total[...] += part

    @pl.when(block == pl.num_programs(0) - 1)
    def _():
        store_halves(total, slice(None), low_ref[0], sent_ref, kept_ref)


def backward_kernel(
    head_count,
    mixed_ref,
    grad_ref,
    act_ref,
    sums_ref,
    row_ref,
    scan_ref,
    value_ref,
    slope_ref,
    inner_ref,
    step_ref,
    cum_ref,
    bc_ref,
    enter_ref,
    normed_ref,
    bc_slope_ref,
    state_ref,
    conv_x_ref,
    conv_bc_ref,
    head_ref,
    token_ref,
    after_ref,
    state_low_ref,
    inner_low_ref,
    step_low_ref,
    channel_grad_ref,
    conv_bc_grad_ref,
    head_grad_ref,
    step_rows_ref,
    bc_rows_ref,
    later,
    later_bc,
    leaving,
    step_total,
    dys,
    lows,
    reached,
    tailed,
    products,
):
    block = pl.program_id(0)

    @pl.when(block == 0)
    def _():
        later[PIECE:, :] = jnp.zeros((8, later.shape[1]), F32)
        later_bc[PIECE:, :] = jnp.zeros((8, later_bc.shape[1]), F32)
        conv_bc_grad_ref[...] = jnp.zeros(conv_bc_grad_ref.shape, F32)
        bc_rows_ref[...] = jnp.zeros(bc_rows_ref.shape, F32)
        leaving[...] = jnp.zeros(leaving.shape, F32)
        channel_grad_ref[...] = jnp.zeros(channel_grad_ref.shape, F32)
        head_grad_ref[...] = jnp.zeros(head_grad_ref.shape, F32)
        step_total[...] = jnp.zeros(step_total.shape, F32)

    channels = inner_ref.shape[1]
    row_at = lax.broadcasted_iota(jnp.int32, (PIECE, PIECE), 0)
    col_at = lax.broadcasted_iota(jnp.int32, (PIECE, PIECE), 1)
    upper_ones = (row_at <= col_at).astype(F32)
    first_half = lax.broadcasted_iota(jnp.int32, (PIECE, LANES), 1) < LANES // 2
    heads = head_table(channels, head_count)
    skips = head_rows(head_ref, heads)[2:3, :]
    side_all = token_ref[...].T
    inv_gate, pull = gate_columns(sums_ref)
    heads_twice = jnp.concatenate([heads, heads], axis=0)
    for piece in reversed(range(BLOCK // PIECE)):
        rows = slice(piece * PIECE, (piece + 1) * PIECE)
        side = side_all[rows]
        step_in = step_ref[rows, :]
        step = jnp.maximum(step_in, 0.0) + jnp.log1p(jnp.exp(-jnp.abs(step_in)))
        cum = cum_ref[rows, :]
        cum_t = cum.T
        same = (side[:, 0:1] == token_ref[0:1, rows]) & (row_at <= col_at)
        bias = jnp.where(same, 0.0, -1e30)
        reach = jnp.exp2(cum) * side[:, 4:5]
        tail = jnp.exp2(cum[PIECE - 1 : PIECE, :] - cum) * side[:, 5:6]
        wide = spread_heads(jnp.concatenate([step, reach, tail], axis=0), heads_twice)
        b_low = bc_ref[rows, 0:STATE]
        c_low = bc_ref[rows, STATE : 2 * STATE]
        scores = dot_last(b_low, c_low)
        score_grad = jnp.zeros((PIECE, PIECE), F32)
        masks = [None] + [side[:, 5 + k : 6 + k] for k in range(1, CONV)]
        for at in range(0, channels, LANES):
            lanes = slice(at, at + LANES)
            mixed = mixed_ref[rows, lanes].astype(F32)
            grad = grad_ref[rows, lanes].astype(F32)
            mixed_grad = inv_gate[rows] * (grad * row_ref[2:3, lanes] - mixed * pull[rows])
            dy_low = (mixed_grad * act_ref[rows, lanes].astype(F32)).astype(BF16)
            dys[:, lanes] = dy_low
            dy = dy_low.astype(F32)
            low = (wide[0:PIECE, lanes] * value_ref[rows, lanes].astype(F32)).astype(BF16)
            lows[:, lanes] = low
            reached[:, lanes] = (wide[PIECE : 2 * PIECE, lanes] * dy).astype(BF16)
            tailed[:, lanes] = (wide[2 * PIECE :, lanes] * low.astype(F32)).astype(BF16)
        leave = leaving[...]
        leave_low = leave.astype(BF16)
        enter_low = enter_ref[piece]
        kept = wide[2 * PIECE - 1 : 2 * PIECE, :]
        c_grad = dot_last(reached[...], enter_low)
        b_grad = dot_last(tailed[...], leave_low)
        from_states = dot(b_low, leave_low)
        kept_sum = kept * jnp.sum(enter_low.astype(F32) * leave, axis=0, keepdims=True)
        leaving[...] = kept * leave + dot_first(c_low, reached[...])
        for pair in range(channels // LANES):
            lanes = slice(pair * LANES, (pair + 1) * LANES)
            values = value_ref[rows, lanes].astype(F32)
            dy_low = dys[:, lanes]
            dy = dy_low.astype(F32)
            wide_step = wide[0:PIECE, lanes]
            low = lows[:, lanes]
            low_wide = low.astype(F32)
            from_state = wide[2 * PIECE :, lanes] * from_states[:, lanes]
            zero = jnp.zeros_like(low)
            own = jnp.concatenate(
                [jnp.where(first_half, dy_low, zero), jnp.where(first_half, zero, dy_low)], axis=0
            )
            weight_grads = dot_last(low, own)
            weights = []
            for at, head in enumerate((2 * pair, 2 * pair + 1)):
                gaps = (cum_t[head : head + 1, :] - cum[:, head : head + 1]) + bias
                decay = jnp.exp2(gaps)
                weights.append((scores * decay).astype(BF16))
                score_grad = score_grad + weight_grads[:, at * PIECE : (at + 1) * PIECE] * decay
            dx = dot(jnp.concatenate(weights, axis=1), own)
            dx = dx + from_state
            out = scan_ref[rows, lanes] - skips[:, lanes] * values
            last = jnp.sum(low_wide * from_state, axis=0, keepdims=True) + kept_sum[:, lanes]
            for at, product in enumerate(
                (dy * out - low_wide * dx, values * dx, jnp.broadcast_to(last, (16, LANES)))
            ):
                upper, rest = two_terms(product)
                products[2 * at * PIECE : 2 * at * PIECE + upper.shape[0], lanes] = upper
                products[2 * at * PIECE + upper.shape[0] : 2 * (at * PIECE + upper.shape[0]), lanes] = rest
            dvalue = wide_step * dx + skips[:, lanes] * dy
            dbefore = dvalue * slope_ref[rows, lanes].astype(F32)
            later[0:PIECE, lanes] = dbefore
            inner = inner_ref[rows, lanes].astype(F32)
            inner_grad = conv_x_ref[CONV - 1 : CONV, lanes] * dbefore
            channel_grad_ref[CONV - 1 : CONV, lanes] += jnp.sum(inner * dbefore, axis=0, keepdims=True)
            channel_grad_ref[CONV : CONV + 1, lanes] += jnp.sum(dbefore, axis=0, keepdims=True)
            channel_grad_ref[CONV + 1 : CONV + 2, lanes] += jnp.sum(dy * values, axis=0, keepdims=True)
            for k in range(1, CONV):
                shifted = later[k : k + PIECE, lanes] * masks[k]
                inner_grad = inner_grad + conv_x_ref[CONV - 1 - k : CONV - k, lanes] * shifted
                channel_grad_ref[CONV - 1 - k : CONV - k, lanes] += jnp.sum(
                    inner * shifted, axis=0, keepdims=True
                )
            inner_low_ref[rows, lanes] = inner_grad.astype(BF16)
        sums = dot_last(products[...], heads)
        row_sum = sums[0:PIECE] + sums[PIECE : 2 * PIECE]
        value_sum = sums[2 * PIECE : 3 * PIECE] + sums[3 * PIECE : 4 * PIECE]
        last_sum = sums[4 * PIECE : 4 * PIECE + 16] + sums[4 * PIECE + 16 : 4 * PIECE + 32]
        later[PIECE:, :] = later[0:8, :]
        grad_low = score_grad.astype(BF16)
        state_parts = (b_grad + dot(grad_low, c_low), c_grad + dot_first(grad_low, b_low))
        for at, state_part in enumerate(state_parts):
            lanes = slice(at * STATE, (at + 1) * STATE)
            dbefore = state_part * bc_slope_ref[rows, lanes]
            later_bc[0:PIECE, lanes] = dbefore
            state = state_ref[rows, lanes]
            state_grad = conv_bc_ref[CONV - 1 : CONV, lanes] * dbefore
            conv_bc_grad_ref[CONV - 1 : CONV, lanes] += jnp.sum(state * dbefore, axis=0, keepdims=True)
            conv_bc_grad_ref[CONV : CONV + 1, lanes] += jnp.sum(dbefore, axis=0, keepdims=True)
            for k in range(1, CONV):
                shifted = later_bc[k : k + PIECE, lanes] * masks[k]
                state_grad = state_grad + conv_bc_ref[CONV - 1 - k : CONV - k, lanes] * shifted
                conv_bc_grad_ref[CONV - 1 - k : CONV - k, lanes] += jnp.sum(
                    state * shifted, axis=0, keepdims=True
                )
            state_low_ref[rows, lanes] = state_grad.astype(BF16)
        later_bc[PIECE:, :] = later_bc[0:8, :]
        rate_grad = (
            jnp.dot(upper_ones, row_sum, precision=HIGH, preferred_element_type=F32) + last_sum[0:1, :]
        )
        coefficient = head_ref[1:2, :]
        step_grad = (value_sum + coefficient * rate_grad) / (1.0 + jnp.exp(-step_in))
        step_low_ref[rows, :] = step_grad.astype(BF16)
        head_grad_ref[0:1, :] += jnp.sum(step_grad, axis=0, keepdims=True)
        head_grad_ref[1:2, :] += jnp.sum(rate_grad * step, axis=0, keepdims=True) * coefficient
    step_total[...] += dot_first(step_low_ref[...], normed_ref[...])
    bc_rows_ref[...] += dot_first(state_low_ref[...], normed_ref[...])

    @pl.when(block == pl.num_programs(0) - 1)
    def _():
        step_rows_ref[...] = step_total[0 : step_rows_ref.shape[0], :]


def merge_kernel(
    core_ref,
    gate_low_ref,
    inner_low_ref,
    step_low_ref,
    state_low_ref,
    mixed_ref,
    normed_ref,
    sums_ref,
    w_gate_ref,
    w_value_ref,
    w_dt_ref,
    w_bc_ref,
    w_out_ref,
    row_ref,
    conv_bc_ref,
    after_ref,
    _,
    __,
    sent_ref,
    kept_ref,
    first_shared_ref,
    second_shared_ref,
    gain_ref,
    wide_dt,
    gated,
):
    block = pl.program_id(0)
    last = pl.num_programs(0) - 1

    @pl.when(block == 0)
    def _():
        gain_ref[...] = jnp.zeros(gain_ref.shape, F32)
        wide_dt[...] = jnp.zeros(wide_dt.shape, BF16)
        wide_dt[0 : w_dt_ref.shape[0], :] = w_dt_ref[...]

    width = normed_ref.shape[1]
    total = dot_last(inner_low_ref[...], w_value_ref[...]) + dot_last(gate_low_ref[...], w_gate_ref[...])
    total = total + dot_last(state_low_ref[...], w_bc_ref[...]) + dot(step_low_ref[...], wide_dt[...])
    gain_ref[...] += jnp.sum((total * normed_ref[...].astype(F32)).reshape(-1, 8, width), axis=0)
    inv_gate, _ = gate_columns(sums_ref)
    for at in range(0, mixed_ref.shape[1], LANES):
        lanes = slice(at, at + LANES)
        normal = mixed_ref[:, lanes].astype(F32) * inv_gate
        gated[:, lanes] = (normal * row_ref[2:3, lanes]).astype(BF16)
    branch = dot(gated[...], w_out_ref[...]).astype(BF16)

    @pl.when(2 * block < last)
    def _():
        sent_ref[:, 0:width] = total.astype(BF16)
        sent_ref[:, width:] = branch

    @pl.when(2 * block > last)
    def _():
        kept_ref[:, 0:width] = total.astype(BF16)
        kept_ref[:, width:] = branch

    @pl.when(block == last)
    def _():
        gain = jnp.sum(gain_ref[...], axis=0, keepdims=True) / row_ref[0:1, :]
        channels = first_shared_ref.shape[1]
        states = conv_bc_ref.shape[1]
        rows = [gain[:, at : at + channels] for at in range(0, width, channels)]
        conv = conv_bc_ref[0 : CONV + 1, :]
        rows.append(jnp.concatenate([conv, jnp.zeros((CONV + 1, channels - states), F32)], axis=1))
        rows.append(jnp.zeros((16 - width // channels - CONV - 1, channels), F32))
        shared = jnp.concatenate(rows).astype(BF16)
        first_shared_ref[...] = shared
        second_shared_ref[...] = shared


def pack_kernel(
    head_count,
    core_ref,
    bc_rows_ref,
    step_rows_ref,
    channel_ref,
    gate_gain_ref,
    head_ref,
    sent_ref,
    kept_ref,
    own_ref,
):
    core = core_ref[0]
    channels = channel_ref.shape[1]
    width = bc_rows_ref.shape[1]
    folds = width // channels
    groups = (kept_ref.shape[0] - 16) // (OWN_BC * folds)
    for which, ref in ((1 - core, sent_ref), (core, kept_ref)):
        for group in range(groups):
            found = bc_rows_ref[pl.ds(pl.multiple_of((2 * group + which) * OWN_BC, 8), OWN_BC), :].astype(BF16)
            for fold in range(folds):
                at = (group * folds + fold) * OWN_BC
                ref[at : at + OWN_BC, :] = found[:, fold * channels : (fold + 1) * channels]
    own_ref[...] = jnp.zeros(own_ref.shape, F32)
    for fold in range(folds):
        own_ref[16 * fold : 16 * fold + 16, :] = step_rows_ref[:, fold * channels : (fold + 1) * channels]
    at = 16 * folds
    own_ref[at : at + CONV + 1, :] = channel_ref[0 : CONV + 1, :]
    own_ref[at + CONV + 1 : at + CONV + 2, :] = jnp.sum(gate_gain_ref[...], axis=0, keepdims=True)
    skips = sum_heads(channel_ref[...], head_table(channels, head_count))
    own_ref[at + CONV + 2 : at + CONV + 4, 0:LANES] = head_ref[0:2, :]
    own_ref[at + CONV + 4 : at + CONV + 5, 0:LANES] = skips[CONV + 1 : CONV + 2, :]


def unpack_kernel(
    one_ref,
    two_ref,
    pre_gain_ref,
    bc_ref,
    dt_ref,
    conv_x_ref,
    bias_x_ref,
    conv_bc_ref,
    bias_bc_ref,
    dt_bias_ref,
    a_log_ref,
    d_skip_ref,
    gate_gain_ref,
    total,
):
    total[...] = one_ref[...].astype(F32) + two_ref[...].astype(F32)
    channels = total.shape[1]
    own_bc, width = bc_ref.shape
    folds = width // channels
    for fold in range(folds):
        bc_ref[:, fold * channels : (fold + 1) * channels] = total[fold * own_bc : (fold + 1) * own_bc, :]
    at = folds * own_bc
    pre_gain_ref[...] = jnp.concatenate([total[at + fold : at + fold + 1, :] for fold in range(folds)], axis=1).reshape(-1)
    at += folds
    states = conv_bc_ref.shape[1]
    conv_bc_ref[...] = total[at : at + CONV, 0:states]
    bias_bc_ref[...] = total[at + CONV : at + CONV + 1, 0:states].reshape(-1)
    at += 16 - folds
    count = dt_ref.shape[0]
    for fold in range(folds):
        dt_ref[:, fold * channels : (fold + 1) * channels] = total[at + 16 * fold : at + 16 * fold + count, :]
    at += 16 * folds
    conv_x_ref[...] = total[at : at + CONV, :]
    bias_x_ref[...] = total[at + CONV : at + CONV + 1, :].reshape(-1)
    gate_gain_ref[...] = total[at + CONV + 1 : at + CONV + 2, :].reshape(-1)
    at += CONV + 2
    for row, ref in enumerate((dt_bias_ref, a_log_ref, d_skip_ref)):
        ref[...] = total[at + row : at + row + 1, 0:LANES].reshape(-1)[0 : ref.shape[0]]


def hidden_kernel(rank_ref, hidden_ref, cotan_ref, kept_ref, got_ref, row_ref, out_ref, grad_ref):
    width = hidden_ref.shape[1]
    hidden = hidden_ref[...].astype(F32)
    branch = kept_ref[:, width:].astype(F32) + got_ref[:, width:].astype(F32)
    out_ref[...] = (hidden + branch).astype(BF16)
    inv_rms = lax.rsqrt(jnp.mean(hidden * hidden, axis=-1, keepdims=True) + EPS)
    scaled = (kept_ref[:, 0:width].astype(F32) + got_ref[:, 0:width].astype(F32)) * row_ref[0:1, :]
    pull = inv_rms * inv_rms * jnp.mean(scaled * hidden, axis=-1, keepdims=True)
    grad_ref[...] = cotan_ref[...].astype(F32) + inv_rms * (scaled - hidden * pull)


def pass_kernel(*refs):
    pass


def finish_kernel(which_ref, part_ref, after_ref, out_ref):
    out_ref[...] = part_ref[...].astype(F32)


def finish_pair_kernel(which_ref, part_ref, after_ref, *refs):
    out_ref, gate_ref = refs[-2:]
    rows, width = out_ref.shape
    channels = gate_ref.shape[1]
    for at in range(width // channels):
        out_ref[:, at * channels : (at + 1) * channels] = part_ref[at * rows : (at + 1) * rows, :].astype(F32)
    gate_ref[...] = part_ref[gate_ref.shape[0] :, :].astype(F32)


def finish_into_kernel(which_ref, part_ref, after_ref, whole_ref, out_ref):
    finish_kernel(which_ref, part_ref, after_ref, out_ref)


def split_kernel(which_ref, sent_one, sent_two, kept_one, kept_two, sent_ref, kept_ref):
    sent_ref[...] = (sent_one[...].astype(F32) + sent_two[...].astype(F32)).astype(BF16)
    kept_ref[...] = (kept_one[...].astype(F32) + kept_two[...].astype(F32)).astype(BF16)


def join_kernel(which_ref, own_ref, got_ref, own_extra_ref, got_extra_ref, out_ref):
    which = which_ref[0]
    rows = own_ref.shape[0]
    out_ref[pl.ds(pl.multiple_of(which * rows, 16), rows), :] = own_ref[...]
    out_ref[pl.ds(pl.multiple_of((1 - which) * rows, 16), rows), :] = got_ref[...]
    extra = own_extra_ref[...].astype(F32) + got_extra_ref[...].astype(F32)
    at = 2 * rows
    out_ref[at:, :] = extra.astype(BF16)
    shared = slice(SHARED_AT, SHARED_AT + 16)
    own_rows, got_rows = own_extra_ref[shared, :].astype(F32), got_extra_ref[shared, :].astype(F32)
    both_rows = jnp.concatenate([own_rows[0:8], got_rows[0:8]])
    out_ref[at + SHARED_AT : at + SHARED_AT + 16, :] = both_rows.astype(BF16)


def rider_kernel(core_ref, own_ref, got_ref, out_ref):
    out_ref[...] = (own_ref[...].astype(F32) + got_ref[...].astype(F32)).astype(BF16)
    shared = slice(SHARED_AT, SHARED_AT + 16)
    own, got = own_ref[shared, :].astype(F32), got_ref[shared, :].astype(F32)
    is_first = core_ref[0] == 0
    first = own[0:8] + jnp.where(is_first, got[0:8], own[8:16])
    second = jnp.where(is_first, own[8:16], got[0:8]) + got[8:16]
    out_ref[shared, :] = jnp.concatenate([first + second, jnp.zeros_like(first)]).astype(BF16)


def whole(shape):
    return pl.BlockSpec(shape, lambda i: (0,) * len(shape), pipeline_mode=pl.Buffered(1))


def no_cost():
    return pl.CostEstimate(flops=0, bytes_accessed=0, transcendentals=0)


def params():
    return pltpu.CompilerParams(vmem_limit_bytes=60 << 20)


def run_tables(segments, pre_gain, bias_x, gate_gain, bias_bc, dt_bias, a_log, d_skip):
    inputs = (segments, pre_gain, bias_x, gate_gain, bias_bc, dt_bias, a_log, d_skip)
    in_vmem = pl.BlockSpec(memory_space=pltpu.VMEM)
    return pl.pallas_call(
        table_kernel,
        in_specs=[in_vmem] * len(inputs),
        out_specs=[in_vmem] * 3,
        out_shape=[
            jax.ShapeDtypeStruct((16, segments.size), F32),
            jax.ShapeDtypeStruct((8, pre_gain.shape[0]), F32),
            jax.ShapeDtypeStruct((8, LANES), F32),
        ],
        compiler_params=params(),
        name="tables",
    )(*inputs)


def in_place():
    return pl.BlockSpec(memory_space=pl.ANY)


def run_forward(hidden_in, cotangent, weights, tables, tokens):
    rows, width = hidden_in.shape
    channels = weights[0].shape[1]
    states = weights[2].shape[1]
    constants = (*weights, *tables)

    def block(columns):
        return pl.BlockSpec((BLOCK, columns), lambda i: (i, 0))

    def out(columns, kind=BF16):
        return jax.ShapeDtypeStruct((rows, columns), kind)

    return pl.pallas_call(
        forward_kernel,
        grid=(rows // BLOCK,),
        in_specs=[block(width), block(width)]
        + [whole(array.shape) for array in constants]
        + [pl.BlockSpec((tokens.shape[0], BLOCK), lambda i: (0, i))],
        out_specs=[block(width)]
        + [block(channels)] * 8
        + [block(LANES)] * 2
        + [block(states)] * 3
        + [
            pl.BlockSpec((BLOCK // PIECE, STATE, channels), lambda i: (i, 0, 0)),
            pl.BlockSpec((8, BLOCK), lambda i: (0, i)),
        ],
        out_shape=[
            out(width),
            out(channels),
            out(channels),
            out(channels),
            out(channels),
            out(channels, F32),
            out(channels),
            out(channels),
            out(channels),
            out(LANES, F32),
            out(LANES, F32),
            out(states),
            out(states, F32),
            out(states, F32),
            jax.ShapeDtypeStruct((rows // PIECE, STATE, channels), BF16),
            jax.ShapeDtypeStruct((8, rows), F32),
        ],
        scratch_shapes=[
            pltpu.VMEM((BLOCK + 8, channels), F32),
            pltpu.VMEM((BLOCK + 8, states), F32),
            pltpu.VMEM((STATE, channels), F32),
            pltpu.VMEM((LANES, width), BF16),
            pltpu.VMEM((BLOCK, channels), F32),
            pltpu.VMEM((BLOCK, channels), F32),
            pltpu.VMEM((PIECE, channels), BF16),
        ],
        compiler_params=params(),
        cost_estimate=no_cost(),
        name="forward",
    )(hidden_in, cotangent, *constants, tokens)


def scalar_spec():
    return pl.BlockSpec(memory_space=pltpu.SMEM)


def half_shapes(rows, columns):
    return [jax.ShapeDtypeStruct((rows // 2, columns), BF16)] * 2


def run_gate(low, forward, sums, rows_table, cotangent, normed):
    rows, channels = forward[0].shape
    width = cotangent.shape[1]

    def block(columns):
        return pl.BlockSpec((BLOCK, columns), lambda i: (i, 0))

    halves = [jax.ShapeDtypeStruct((width // 2 + width // 2, channels), BF16)] * 2
    out = pl.pallas_call(
        gate_kernel,
        grid=(rows // BLOCK,),
        in_specs=[scalar_spec()]
        + [block(channels)] * 3
        + [pl.BlockSpec((8, BLOCK), lambda i: (0, i)), whole(rows_table.shape), block(width), block(width)],
        out_specs=[block(channels), whole((8, channels))] + [whole(half.shape) for half in halves],
        out_shape=[jax.ShapeDtypeStruct((rows, channels), BF16), jax.ShapeDtypeStruct((8, channels), F32)]
        + halves,
        scratch_shapes=[
            pltpu.VMEM((BLOCK, channels), BF16),
            pltpu.VMEM((channels, width), F32),
            pltpu.VMEM((width, channels), F32),
        ],
        compiler_params=params(),
        cost_estimate=no_cost(),
        name="gate",
    )(low, *forward, sums, rows_table, cotangent, normed)
    return out[:2], out[2:]


def run_weight(low, normed, grad, after):
    rows, width = normed.shape
    channels = grad.shape[1]
    size = 2 * BLOCK
    halves = half_shapes(width, channels)
    return pl.pallas_call(
        weight_kernel,
        grid=(rows // size,),
        in_specs=[
            scalar_spec(),
            pl.BlockSpec((size, width), lambda i: (i, 0)),
            pl.BlockSpec((size, channels), lambda i: (i, 0)),
            in_place(),
        ],
        out_specs=[whole(half.shape) for half in halves],
        out_shape=halves,
        scratch_shapes=[pltpu.VMEM((width, channels), F32)],
        compiler_params=params(),
        cost_estimate=no_cost(),
        name="weight",
    )(low, normed, grad, after)


def run_backward(gate_inputs, sums, rows_table, by_channel, step_in, cum, bc_low, enter, normed, by_state, tables, after, head_count):
    rows, channels = by_channel[0].shape
    width = normed.shape[1]
    count = rows // BLOCK
    states = bc_low.shape[1]
    conv_x, conv_bc, head_values, tokens = tables

    def block(columns):
        return pl.BlockSpec((BLOCK, columns), lambda i: (count - 1 - i, 0))

    def low_rows(columns):
        return jax.ShapeDtypeStruct((rows, columns), BF16)

    totals = [
        jax.ShapeDtypeStruct(shape, F32)
        for shape in ((8, channels), (8, states), (8, LANES), (16, width), (states, width))
    ]
    return pl.pallas_call(
        functools.partial(backward_kernel, head_count),
        grid=(count,),
        in_specs=[block(channels)] * 3
        + [pl.BlockSpec((8, BLOCK), lambda i: (0, count - 1 - i)), whole(rows_table.shape)]
        + [block(channels)] * 4
        + [block(LANES), block(LANES), block(states)]
        + [pl.BlockSpec((BLOCK // PIECE, STATE, channels), lambda i: (count - 1 - i, 0, 0))]
        + [block(width), block(states), block(states)]
        + [whole(conv_x.shape), whole(conv_bc.shape), whole(head_values.shape)]
        + [pl.BlockSpec((tokens.shape[0], BLOCK), lambda i: (0, count - 1 - i)), in_place()],
        out_specs=[block(states), block(channels), block(LANES)]
        + [whole(shape.shape) for shape in totals],
        out_shape=[low_rows(states), low_rows(channels), low_rows(LANES)] + totals,
        scratch_shapes=[
            pltpu.VMEM((PIECE + 8, channels), F32),
            pltpu.VMEM((PIECE + 8, states), F32),
            pltpu.VMEM((STATE, channels), F32),
            pltpu.VMEM((LANES, width), F32),
            pltpu.VMEM((PIECE, channels), BF16),
            pltpu.VMEM((PIECE, channels), BF16),
            pltpu.VMEM((PIECE, channels), BF16),
            pltpu.VMEM((PIECE, channels), BF16),
            pltpu.VMEM((4 * PIECE + 32, channels), BF16),
        ],
        compiler_params=params(),
        cost_estimate=no_cost(),
        name="backward",
    )(*gate_inputs, sums, rows_table, *by_channel, step_in, cum, bc_low, enter, normed, *by_state, conv_x, conv_bc, head_values, tokens, after)


def run_merge(core, blocked, sums, weights, rows_table, conv_bc_grads, after, packed, ranks):
    normed = blocked[-1]
    rows, width = normed.shape
    channels = weights[0].shape[1]
    size = rows // ranks
    half = ranks // 2

    def rank_at(i, c):
        return jnp.where(i < half, 2 * i + 1 - c[0], 2 * (i - half) + c[0])

    def block(columns):
        return pl.BlockSpec((size, columns), lambda i, c: (rank_at(i, c), 0))

    def constant(shape):
        return pl.BlockSpec(shape, lambda i, c: (0,) * len(shape), pipeline_mode=pl.Buffered(1))

    out = jax.ShapeDtypeStruct((rows // 2, 2 * width), BF16)
    last = packed[0].shape[0] // 16 - 1
    shared = pl.BlockSpec((16, channels), lambda i, c: (last, 0))
    first = 5 + len(blocked) + len(weights)
    return pl.pallas_call(
        merge_kernel,
        grid_spec=pltpu.PrefetchScalarGridSpec(
            num_scalar_prefetch=1,
            grid=(ranks,),
            in_specs=[block(array.shape[1]) for array in blocked]
            + [pl.BlockSpec((8, size), lambda i, c: (0, rank_at(i, c)))]
            + [constant(array.shape) for array in (*weights, rows_table, conv_bc_grads)]
            + [in_place()] * 3,
            out_specs=[
                pl.BlockSpec((size, 2 * width), lambda i, c: (jnp.minimum(i, half - 1), 0)),
                pl.BlockSpec((size, 2 * width), lambda i, c: (jnp.maximum(i - half, 0), 0)),
                shared,
                shared,
            ],
            scratch_shapes=[
                pltpu.VMEM((8, width), F32),
                pltpu.VMEM((LANES, width), BF16),
                pltpu.VMEM((size, channels), BF16),
            ],
        ),
        out_shape=[out, out] + [jax.ShapeDtypeStruct(array.shape, BF16) for array in packed],
        input_output_aliases={first: 2, first + 1: 3},
        compiler_params=params(),
        cost_estimate=no_cost(),
        name="merge",
    )(core, *blocked, sums, *weights, rows_table, conv_bc_grads, after, *packed)


def run_pack(core, bc_rows, step_rows, channel_grads, gain_rows, head_grads, head_count):
    states, width = bc_rows.shape
    channels = channel_grads.shape[1]
    folds = width // channels
    in_vmem = pl.BlockSpec(memory_space=pltpu.VMEM)
    shared = jax.ShapeDtypeStruct((states // 2 * folds + 16, channels), BF16)
    return pl.pallas_call(
        functools.partial(pack_kernel, head_count),
        in_specs=[scalar_spec()] + [in_vmem] * 5,
        out_specs=[in_vmem] * 3,
        out_shape=[shared, shared, jax.ShapeDtypeStruct((16 * folds + 16, channels), F32)],
        compiler_params=params(),
        cost_estimate=no_cost(),
        name="pack",
    )(core, bc_rows, step_rows, channel_grads, gain_rows, head_grads)


def run_unpack(one, two, width, states, head_count):
    rows, channels = one.shape
    last = two.shape[0] // rows - 1
    in_vmem = pl.BlockSpec(memory_space=pltpu.VMEM)
    shapes = (
        (width,),
        (OWN_BC, width),
        (head_count, width),
        (CONV, channels),
        (channels,),
        (CONV, states),
        (states,),
        (head_count,),
        (head_count,),
        (head_count,),
        (channels,),
    )
    return pl.pallas_call(
        unpack_kernel,
        grid=(1,),
        in_specs=[
            pl.BlockSpec((rows, channels), lambda i: (0, 0)),
            pl.BlockSpec((rows, channels), lambda i: (last, 0)),
        ],
        out_specs=[pl.BlockSpec(shape, lambda i, rank=len(shape): (0,) * rank) for shape in shapes],
        out_shape=[jax.ShapeDtypeStruct(shape, F32) for shape in shapes],
        scratch_shapes=[pltpu.VMEM(one.shape, F32)],
        compiler_params=params(),
        cost_estimate=no_cost(),
        name="unpack",
    )(one, two)


def run_hidden(rank, hidden_in, cotangent, kept, got, rows_table):
    own_rows = kept.shape[0]
    width = hidden_in.shape[1]
    count = 2
    size = own_rows // count

    def own(columns):
        return pl.BlockSpec((size, columns), lambda i, r: (r[0] * count + i, 0))

    def block(columns):
        return pl.BlockSpec((size, columns), lambda i, r: (i, 0))

    return pl.pallas_call(
        hidden_kernel,
        grid_spec=pltpu.PrefetchScalarGridSpec(
            num_scalar_prefetch=1,
            grid=(count,),
            in_specs=[
                own(width),
                own(width),
                block(2 * width),
                block(2 * width),
                pl.BlockSpec(rows_table.shape, lambda i, r: (0, 0)),
            ],
            out_specs=[block(width), block(width)],
        ),
        out_shape=[
            jax.ShapeDtypeStruct((own_rows, width), BF16),
            jax.ShapeDtypeStruct((own_rows, width), F32),
        ],
        compiler_params=params(),
        cost_estimate=no_cost(),
        name="hidden",
    )(rank, hidden_in, cotangent, kept, got, rows_table)


def run_pass(arrays, after):
    count = len(arrays)
    return pl.pallas_call(
        pass_kernel,
        in_specs=[in_place()] * (count + 1),
        out_specs=[in_place()] * count,
        out_shape=[jax.ShapeDtypeStruct(array.shape, array.dtype) for array in arrays],
        input_output_aliases={at: at for at in range(count)},
        cost_estimate=no_cost(),
        name="pass",
    )(*arrays, after)


def run_finish(which, part, after, rows, into=None):
    columns = part.shape[1]
    count = 2
    size = rows // count
    inputs = [part, after] + ([] if into is None else [into])
    return pl.pallas_call(
        finish_kernel if into is None else finish_into_kernel,
        grid_spec=pltpu.PrefetchScalarGridSpec(
            num_scalar_prefetch=1,
            grid=(count,),
            in_specs=[pl.BlockSpec((size, columns), lambda i, w: (i, 0))] + [in_place()] * (len(inputs) - 1),
            out_specs=pl.BlockSpec((size, columns), lambda i, w: (w[0] * count + i, 0)),
        ),
        out_shape=jax.ShapeDtypeStruct((2 * rows, columns), F32),
        input_output_aliases={} if into is None else {3: 0},
        compiler_params=params(),
        cost_estimate=no_cost(),
        name="finish",
    )(jnp.reshape(which, (1,)), *inputs)


def run_finish_pair(which, part, after, out_shape, gate_shape, into=()):
    out_rows, out_columns = out_shape
    gate_rows, gate_columns = gate_shape
    return pl.pallas_call(
        finish_pair_kernel,
        grid_spec=pltpu.PrefetchScalarGridSpec(
            num_scalar_prefetch=1,
            grid=(1,),
            in_specs=[pl.BlockSpec((gate_rows, gate_columns), lambda i, w: (0, 0))]
            + [in_place()] * (1 + len(into)),
            out_specs=[
                pl.BlockSpec((out_rows // 2, out_columns), lambda i, w: (w[0], 0)),
                pl.BlockSpec((gate_rows // 2, gate_columns), lambda i, w: (w[0], 0)),
            ],
        ),
        out_shape=[jax.ShapeDtypeStruct(out_shape, F32), jax.ShapeDtypeStruct(gate_shape, F32)],
        input_output_aliases={3 + at: at for at in range(len(into))},
        compiler_params=params(),
        cost_estimate=no_cost(),
        name="finish_pair",
    )(jnp.reshape(which, (1,)), part, after, *into)


def run_split(one, two, which):
    half, columns = one.shape[0] // 2, one.shape[1]
    count = 2
    size = half // count
    sent = pl.BlockSpec((size, columns), lambda i, w: ((1 - w[0]) * count + i, 0))
    kept = pl.BlockSpec((size, columns), lambda i, w: (w[0] * count + i, 0))
    out = pl.BlockSpec((size, columns), lambda i, w: (i, 0))
    return pl.pallas_call(
        split_kernel,
        grid_spec=pltpu.PrefetchScalarGridSpec(
            num_scalar_prefetch=1,
            grid=(count,),
            in_specs=[sent, sent, kept, kept],
            out_specs=[out, out],
        ),
        out_shape=[jax.ShapeDtypeStruct((half, columns), BF16)] * 2,
        compiler_params=params(),
        cost_estimate=no_cost(),
        name="split",
    )(jnp.reshape(which.astype(jnp.int32), (1,)), one, two, one, two)


def run_join(which, own, got, extra_rows):
    rows = own.shape[0] - extra_rows
    columns = own.shape[1]
    matrix = pl.BlockSpec((rows, columns), lambda i, w: (0, 0))
    extra = pl.BlockSpec((extra_rows, columns), lambda i, w: (rows // extra_rows, 0))
    shape = (2 * rows + extra_rows, columns)
    return pl.pallas_call(
        join_kernel,
        grid_spec=pltpu.PrefetchScalarGridSpec(
            num_scalar_prefetch=1,
            grid=(1,),
            in_specs=[matrix, matrix, extra, extra],
            out_specs=pl.BlockSpec(shape, lambda i, w: (0, 0)),
        ),
        out_shape=jax.ShapeDtypeStruct(shape, BF16),
        compiler_params=params(),
        cost_estimate=no_cost(),
        name="join",
    )(jnp.reshape(which, (1,)), own, got, own, got)


def run_rider(core, own, got, rows):
    columns = own.shape[1]
    last = pl.BlockSpec((rows, columns), lambda i: (own.shape[0] // rows - 1, 0))
    return pl.pallas_call(
        rider_kernel,
        grid=(1,),
        in_specs=[scalar_spec(), last, last],
        out_specs=pl.BlockSpec((rows, columns), lambda i: (0, 0)),
        out_shape=jax.ShapeDtypeStruct((rows, columns), BF16),
        compiler_params=params(),
        cost_estimate=no_cost(),
        name="rider",
    )(core, own, got)


def swap(array, axis, bit):
    size = lax.axis_size(axis)
    return lax.ppermute(array, axis, [(source, source ^ bit) for source in range(size)])


def axis_bits(axis):
    size = lax.axis_size(axis)
    return [1 << place for place in range(size.bit_length() - 1)]


def half_of(array, which):
    half = array.shape[0] // 2
    return lax.dynamic_slice_in_dim(array, which * half, half, 0)


def sum_tensor(array):
    for bit in axis_bits("tensor"):
        array = array + swap(array, "tensor", bit)
    return array


def dp_bits(step):
    bits = axis_bits("dp")
    swapped = [bits[1], bits[0]] + bits[2:]
    return bits[step], swapped[step]


def own_bit(step):
    first, second = dp_bits(step)
    place = lax.axis_index("dp").astype(jnp.int32)
    core = lax.axis_index("tensor") % 2
    return jnp.where(core == 0, (place // first) % 2, (place // second) % 2)


def dp_pairs(step):
    ranks = lax.axis_size("tensor")
    pairs = dp_bits(step)
    return [
        (at * ranks + rank, (at ^ pairs[rank % 2]) * ranks + rank)
        for at in range(lax.axis_size("dp"))
        for rank in range(ranks)
    ]


def in_order(which, own, got):
    place = lax.broadcasted_iota(jnp.int32, (2, 1, 1), 0)
    return jnp.where(place == which, own[None], got[None])


def sum_steps(sent, kept, rider=None, own=None):
    axes = ("dp", "tensor")
    steps = range(1, len(axis_bits("dp")))
    terms = [kept]
    got = yield sent, axes, dp_pairs(0)

    def total(which):
        return sum(half_of(term, which).astype(F32) for term in terms)

    for step in steps:
        which = own_bit(step)
        terms.append(got)
        sent = total(1 - which).astype(BF16)
        terms = [half_of(term, which) for term in terms]
        got = yield sent, axes, dp_pairs(step)
    part = sum((term.astype(F32) for term in terms), got.astype(F32)).astype(BF16)
    extra = 0
    for step in reversed((0, *steps)):
        if step == 1 and rider is not None:
            rows = rider().astype(BF16)
            extra = rows.shape[0]
            part = jnp.concatenate([part, rows])
        if step == 0 and own is not None:
            own.append(part)
        got = yield part, axes, dp_pairs(step)
        if step and extra:
            part = run_join(own_bit(step), part, got, extra)
        elif step:
            part = in_order(own_bit(step), part, got).reshape(2 * part.shape[0], -1)
    if extra:
        core = (lax.axis_index("tensor") % 2).astype(jnp.int32)
        extra = run_rider(jnp.reshape(core, (1,)), part, got, extra)
    return own_bit(0), part, got, extra


def rest_steps(rows):
    axes = ("dp", "tensor")
    for step in range(2, len(axis_bits("dp"))):
        got = yield rows, axes, dp_pairs(step)
        total = rows.astype(F32) + got.astype(F32)
        last, rows = (rows, got), total.astype(BF16)
    return last


def both_steps(sent, kept):
    size = lax.axis_size("tensor")
    rank = lax.axis_index("tensor")
    got = yield sent, "tensor", [(i, i ^ 1) for i in range(size)]
    for bit in axis_bits("tensor")[1:]:
        sent, kept = run_split(kept, got, (rank // bit) % 2)
        got = yield sent, "tensor", [(i, i ^ bit) for i in range(size)]
    return kept, got


def small_steps(sent, kept, own):
    size = lax.axis_size("tensor")
    rank = lax.axis_index("tensor")
    got = yield sent, "tensor", [(i, i ^ 1) for i in range(size)]
    total = kept.astype(F32) + got.astype(F32)
    for bit in axis_bits("tensor")[1:]:
        which = (rank // bit) % 2
        shared = lax.reduce_precision(total[-16:], 8, 7).astype(BF16)
        rows = total[:-16]
        got = yield jnp.concatenate([half_of(rows, 1 - which).astype(BF16), shared]), "tensor", [
            (i, i ^ bit) for i in range(size)
        ]
        total = jnp.concatenate([half_of(rows, which), shared.astype(F32)]) + got.astype(F32)
    return jnp.concatenate([total, own])


class Order:
    def __init__(self, last):
        self.last = last
        self.waiting = {}
        self.flying = {}
        self.arrived = {}
        self.results = {}

    def advance(self, name, steps, got):
        try:
            request = steps.send(got)
            self.waiting[name] = (steps, request)
            self.last = request[0]
        except StopIteration as end:
            self.results[name] = end.value

    def add(self, name, steps):
        last = self.last
        self.advance(name, steps, None)
        self.last = last

    def go(self, *names):
        for name in names:
            if name in self.waiting:
                steps, (sent, axis, moves) = self.waiting.pop(name)
                self.flying[name] = (steps, lax.ppermute(sent, axis, moves))

    def arrive(self, *names):
        found = [(name, *self.flying.pop(name)) for name in names if name in self.flying]
        if found:
            passed = run_pass([got for _, _, got in found], self.last)
            self.last = passed[0]
            for (name, steps, _), got in zip(found, passed):
                self.arrived[name] = (steps, got)

    def take(self, *names):
        for name in names:
            if name in self.arrived:
                steps, got = self.arrived.pop(name)
                self.advance(name, steps, got if got is self.last else self.hold(got))
                if name in self.waiting:
                    self.last = self.waiting[name][1][0]

    def land(self, *names):
        self.arrive(*names)
        self.take(*names)

    def hold(self, array):
        return run_pass([array], self.last)[0]

    def step(self, *names):
        for name in names:
            self.land(name)
            self.go(name)

    def until(self, name, found):
        while not found:
            self.step(name)
        return found[0]

    def result(self, name):
        while name not in self.results:
            self.go(name)
            self.land(name)
        return self.results[name]


def shards(
    hidden_in,
    pre_gain,
    w_gate,
    w_value,
    w_bc,
    w_dt,
    conv_x,
    conv_x_bias,
    conv_bc,
    conv_bc_bias,
    dt_bias,
    a_log,
    d_skip,
    gate_gain,
    w_out,
    cotangent,
    segments,
):
    row_count, width = hidden_in.shape
    channels = w_gate.shape[1]
    head_count = dt_bias.shape[0]
    head_width = channels // head_count
    ranks = lax.axis_size("tensor")
    my_rank = lax.axis_index("tensor")
    own_rows = row_count // ranks
    row_start = my_rank * own_rows
    pair_width = w_bc.shape[1] // ranks
    low = jnp.reshape(own_bit(0), (1,))
    w_dt_rows = w_dt.T
    tokens, rows_table, head_values = run_tables(
        segments, pre_gain, conv_x_bias, gate_gain, conv_bc_bias, dt_bias, a_log, d_skip
    )
    (
        normed,
        mixed,
        act,
        turn,
        gated_grad,
        scan,
        values,
        slope,
        inner_pre,
        step_in,
        cum,
        bc_low,
        bc_slope,
        state_pre,
        enter,
        sums,
    ) = run_forward(
        hidden_in,
        cotangent,
        (w_gate, w_value, w_bc, w_dt_rows, w_out),
        (conv_x, conv_bc, rows_table, head_values),
        tokens,
    )
    sums = sum_tensor(sums) / (channels * ranks)
    (gate_low, gain_rows), halves = run_gate(
        low, (mixed, turn, gated_grad), sums, rows_table, cotangent, normed
    )
    order = Order(gate_low)
    first_own, second_own = [], []
    order.add("first", sum_steps(*halves, lambda: order.result("small"), first_own))
    order.go("first")
    (
        state_low,
        inner_low,
        step_low,
        channel_grads,
        conv_bc_grads,
        head_grads,
        step_rows,
        bc_rows,
    ) = run_backward(
        (mixed, gated_grad, act),
        sums,
        rows_table,
        (scan, values, slope, inner_pre),
        step_in,
        cum,
        bc_low,
        enter,
        normed,
        (bc_slope, state_pre),
        (conv_x, conv_bc, head_values, tokens),
        halves[0],
        head_count,
    )
    order.last = inner_low
    order.step("first")
    sent, kept = run_weight(low, normed, inner_low, order.last)
    order.last = kept
    order.step("first")
    order.add("second", sum_steps(order.hold(sent), kept, None, second_own))
    order.go("second")
    core = jnp.reshape((my_rank % 2).astype(jnp.int32), (1,))
    small_sent, small_kept, small_own = run_pack(
        core, bc_rows, step_rows, channel_grads, gain_rows, head_grads, head_count
    )
    both_sent, both_kept, small_sent, small_kept = run_merge(
        core,
        (gate_low, inner_low, step_low, state_low, mixed, normed),
        sums,
        (w_gate, w_value, w_dt_rows, w_bc, w_out),
        rows_table,
        conv_bc_grads,
        order.last,
        (small_sent, small_kept),
        ranks,
    )
    order.last = both_kept
    order.land("second", "first")
    order.go("second", "first")
    order.add("small", small_steps(order.hold(small_sent), small_kept, small_own))
    order.go("small")
    order.add("both", both_steps(order.hold(both_sent), both_kept))
    order.go("both")
    order.step("small")
    order.land("small")
    order.land("second", "first")
    order.go("second", "first")
    order.step("second")
    order.step("both")
    order.land("second")
    order.land("first")
    order.go("second", "first")
    order.step("second")
    which = own_bit(0)
    sums_first = run_finish_pair(which, order.until("first", first_own), order.last, w_out.shape, w_gate.shape)
    order.last = sums_first[0]
    own = order.until("second", second_own)
    w_value_sum = run_finish(which, own, order.last, own.shape[0])
    order.last = w_value_sum
    _, _, got, rows = order.result("first")
    order.add("rest", rest_steps(rows))
    order.go("rest")
    w_out_sum, w_gate_sum = run_finish_pair(
        1 - which, got, order.last, w_out.shape, w_gate.shape, sums_first
    )
    order.last = w_out_sum
    kept, got = order.result("both")
    block_out, hidden_grad = run_hidden(
        jnp.reshape(my_rank.astype(jnp.int32), (1,)), hidden_in, cotangent, kept, got, rows_table
    )
    order.last = hidden_grad
    _, own, got, _ = order.result("second")
    w_value_sum = run_finish(1 - which, got, order.last, own.shape[0], w_value_sum)
    order.last = w_value_sum
    one, two = order.result("rest")
    small = run_unpack(one, two, width, w_bc.shape[1], head_count)
    (
        pre_gain_grad,
        w_bc_rows,
        dt_rows,
        conv_x_grad,
        conv_x_bias_grad,
        conv_bc_grad,
        conv_bc_bias_grad,
        dt_bias_grad,
        a_log_grad,
        d_skip_grad,
        gate_gain_grad,
    ) = small
    return (
        block_out,
        hidden_grad,
        pre_gain_grad,
        w_gate_sum,
        w_value_sum,
        w_bc_rows.T,
        dt_rows.T,
        conv_x_grad,
        conv_x_bias_grad,
        conv_bc_grad,
        conv_bc_bias_grad,
        dt_bias_grad,
        a_log_grad,
        d_skip_grad,
        gate_gain_grad,
        w_out_sum,
    )


def solution(mesh):
    in_specs = (
        P("dp", None),
        P(),
        P(None, "tensor"),
        P(None, "tensor"),
        P(),
        P(None, "tensor"),
        P(None, "tensor"),
        P("tensor"),
        P(),
        P(),
        P("tensor"),
        P("tensor"),
        P("tensor"),
        P("tensor"),
        P("tensor", None),
        P("dp", None),
        P("dp", None),
    )
    out_specs = (
        P(("dp", "tensor"), None),
        P(("dp", "tensor"), None),
        P(),
        P(None, "tensor"),
        P(None, "tensor"),
        P(None, "tensor"),
        P(None, "tensor"),
        P(None, "tensor"),
        P("tensor"),
        P(),
        P(),
        P("tensor"),
        P("tensor"),
        P("tensor"),
        P("tensor"),
        P("tensor", None),
    )
    return jax.shard_map(shards, mesh=mesh, in_specs=in_specs, out_specs=out_specs, check_vma=False)
```
